32 devices in a mesh: ctx: 8 (over z, x), head: 4 (over y, core).
Axes of the slice: x: 2, y: 2, z: 4, core: 2. Of those that a mesh axis runs over, the one named last changes fastest.
Arguments:
- queries: bfloat16 [2048, 2048], P('ctx', 'head'), may hold values from -110 to 110
- keys: bfloat16 [32768, 128], P('ctx'), may hold values from -6 to 6
- values: bfloat16 [32768, 128], P('ctx'), may hold values from -6 to 6
- w_out: bfloat16 [2048, 16384], P(None, 'head'), may hold values from -0.125 to 0.125
- new_counts: int32 [8], replicated, may hold values from 1 to 1024, as said below
- prior_lengths: int32 [8], replicated, may hold values from 1 to 15360, as said below
Outputs:
- mixed: bfloat16 [2048, 16384], P('ctx', 'head')
The draws below stay inside these ranges and needn't reach their ends.
Inputs may be any that keep to these rules, and one draw needn't show every extreme that they name: `new_counts`: every request has at least one new token; the counts add up to 2048. `prior_lengths`: every request has at least one cached token; the lengths add up to 30720.
All inputs are finite; a program needn't handle non-finite values.
Results may differ from the reference program's by a relative error of at most 0.011.
Values may be sent and summed in bfloat16 or wider, within the bound.
No kernel may reach another device: no remote copies, remote signals or barrier semaphores. Data moves between devices by JAX's collectives and lax.ppermute only.
A program may use at most 384 MiB of HBM per device.

```python
import jax
import jax.numpy as jnp
from jax import lax

D = 16384
HD = 128
HEADS = 16
QD = 256
CK = 4096
REQS = 8
QTOT = 2048
KTOT = 32768


def draw_queries(key, part):
    key = jax.random.fold_in(key, 11)
    first = jax.random.fold_in(key, 0)
    base = jnp.clip(jax.random.normal(first, (QTOT, HEADS, HD), jnp.float32), -6.0, 6.0)
    return base.reshape(QTOT, HEADS * HD).astype(jnp.bfloat16)


def draw_keys(key, part):
    key = jax.random.fold_in(key, 12)
    base = jnp.clip(jax.random.normal(key, (KTOT, HD), jnp.float32), -6.0, 6.0)
    return base.astype(jnp.bfloat16)


def request_layout(key):
    long_slot = jax.random.randint(jax.random.fold_in(key, 21), (), 1, REQS - 4).astype(jnp.int32)
    slot_index = jnp.arange(REQS, dtype=jnp.int32)
    lead_mask = (slot_index < long_slot).astype(jnp.int32)
    tail_mask = ((slot_index > long_slot) & (slot_index <= long_slot + 3)).astype(jnp.int32)
    trail_mask = (slot_index > long_slot + 3).astype(jnp.int32)
    long_mask = (slot_index == long_slot).astype(jnp.int32)
    return (long_mask, lead_mask, tail_mask, trail_mask)


def share_total(key, amount, slot_mask):
    slot_index = jnp.arange(REQS, dtype=jnp.int32)
    shares = jax.random.randint(key, (REQS,), 1, 9).astype(jnp.int32) * slot_mask
    share_sum = jnp.sum(shares)
    spare = amount - jnp.sum(slot_mask)
    base = spare * shares // share_sum
    leftover = spare - jnp.sum(base)
    first_slot = jnp.min(jnp.where(slot_mask > 0, slot_index, REQS))
    return (slot_mask + base + leftover * (slot_index == first_slot).astype(jnp.int32)).astype(jnp.int32)


def draw_new_counts(key, part):
    long_mask, lead_mask, tail_mask, trail_mask = request_layout(key)
    key = jax.random.fold_in(key, 22)
    first, second, third, fourth, fifth = jax.random.split(key, 5)
    tail_new = jax.random.randint(first, (REQS,), 1, QD // 8 + 1).astype(jnp.int32) * tail_mask
    whole_blocks = jax.random.randint(second, (), 0, QTOT // (2 * QD) - 1).astype(jnp.int32)
    offset = jax.random.randint(third, (), QD // 4, QD // 2 + 1).astype(jnp.int32)
    lead_total = QD * whole_blocks + offset
    lead_new = share_total(fourth, lead_total, lead_mask)
    trail_total = QTOT // 2 - jnp.sum(tail_new) - lead_total
    trail_new = share_total(fifth, trail_total, trail_mask)
    long_new = QTOT // 2 * long_mask
    return (lead_new + long_new + tail_new + trail_new).astype(jnp.int32)


def draw_prior_lengths(key, part):
    long_mask, lead_mask, tail_mask, trail_mask = request_layout(key)
    key = jax.random.fold_in(key, 23)
    first, second = jax.random.split(key, 2)
    side_prior = jax.random.randint(first, (REQS,), 1, CK // 8 + 1).astype(jnp.int32) * (lead_mask + trail_mask)
    long_prior = (KTOT - QTOT) // 2 * long_mask
    tail_total = KTOT - QTOT - (KTOT - QTOT) // 2 - jnp.sum(side_prior)
    tail_prior = share_total(second, tail_total, tail_mask)
    return (side_prior + long_prior + tail_prior).astype(jnp.int32)


def block_scale(key, shape, cuts, smallest, largest):
    level, own = 1.0, jax.random.fold_in(key, 6)
    for axis_at, shards_of in cuts:
        steps = jnp.exp(jax.random.uniform(jax.random.fold_in(own, axis_at), (shards_of,), jnp.float32, smallest / len(cuts), largest / len(cuts)))
        level = level * jnp.repeat(steps, shape[axis_at] // shards_of).reshape([-1 if axis == axis_at else 1 for axis in range(len(shape))])
    return level


def gaussian(rng, shape, width, limit, pieces=(), kind=jnp.bfloat16):
    loudness = block_scale(rng, shape, pieces, -0.22, 0.18) if pieces else 1.0
    entries = jax.random.normal(rng, shape, jnp.float32) * width * loudness
    return jnp.minimum(jnp.maximum(entries, -limit), limit).astype(kind)


def setup_inputs(seed: int = 0) -> dict:
    arg_keys = jax.random.split(jax.random.key(seed), 7)
    queries = draw_queries(jax.random.fold_in(arg_keys[6], 71), 0)
    keys = draw_keys(jax.random.fold_in(arg_keys[6], 71), 0)
    values = gaussian(arg_keys[2], (KTOT, HD), 1.0, 6.0, ((0, 8),))
    w_out = gaussian(arg_keys[3], (HEADS * HD, D), (HEADS * HD) ** -0.5, 0.125, ((1, 4),))
    new_counts = draw_new_counts(jax.random.fold_in(arg_keys[6], 71), 0)
    prior_lengths = draw_prior_lengths(jax.random.fold_in(arg_keys[6], 71), 0)
    return {"queries": queries, "keys": keys, "values": values, "w_out": w_out, "new_counts": new_counts, "prior_lengths": prior_lengths}


NEG = -1e30


def row_info(index, ends, table):
    req = jnp.sum((index[:, None] >= ends[None, :]).astype(jnp.int32), axis=1).astype(jnp.int32)
    onehot = (req[:, None] == jnp.arange(ends.shape[0], dtype=jnp.int32)[None, :]).astype(jnp.int32)
    return req, (index + jnp.sum(onehot * table[None, :], axis=1)).astype(jnp.int32)


def reference(queries, keys, values, w_out, new_counts, prior_lengths):
    q_ends = jnp.cumsum(new_counts).astype(jnp.int32)
    q_table = (prior_lengths - (q_ends - new_counts)).astype(jnp.int32)
    spans = (new_counts + prior_lengths).astype(jnp.int32)
    k_ends = jnp.cumsum(spans).astype(jnp.int32)
    k_table = (spans - k_ends).astype(jnp.int32)
    q_req, q_pos = row_info(jnp.arange(QTOT, dtype=jnp.int32), q_ends, q_table)
    k_req, k_pos = row_info(jnp.arange(KTOT, dtype=jnp.int32), k_ends, k_table)
    keys_wide = keys.astype(jnp.float32)
    values_wide = values.astype(jnp.float32)
    blocks = queries.reshape(QTOT // 64, 64, HEADS, HD)

    def one_block(item):
        q_block, b_req, b_pos = item
        scores = jnp.einsum("nhd,kd->nhk", q_block.astype(jnp.float32), keys_wide) * (HD ** -0.5)
        allowed = ((b_req[:, None] == k_req[None, :]) & (k_pos[None, :] <= b_pos[:, None]))[:, None, :]
        scores = jnp.where(allowed, scores, NEG)
        top = jnp.max(scores, axis=2)
        weights = jnp.where(allowed, jnp.exp(scores - top[:, :, None]), 0.0)
        total = jnp.sum(weights, axis=2)
        rounded = lax.optimization_barrier(weights.astype(jnp.bfloat16))
        summed = jnp.einsum("nhk,kd->nhd", rounded.astype(jnp.float32), values_wide)
        return summed / total[:, :, None]

    attended = lax.map(one_block, (blocks, q_req.reshape(-1, 64), q_pos.reshape(-1, 64)))
    attended = attended.reshape(QTOT, HEADS * HD).astype(jnp.bfloat16)
    return jnp.dot(attended, w_out, preferred_element_type=jnp.float32).astype(jnp.bfloat16)
```

```python
import functools
import math

import jax
import jax.numpy as jnp
from jax import lax
from jax.experimental import pallas as pl
from jax.experimental.pallas import tpu as pltpu
from jax.sharding import PartitionSpec as P

NEG = -1e30
CALM = 60.0
ROW_TILE = 128
KEY_TILE = 512
SIDE = 16
LANES = 128
SMEM = pl.BlockSpec(memory_space=pltpu.SMEM)
VMEM = pl.BlockSpec(memory_space=pltpu.VMEM)


def request_table(new_ref, prior_ref):
    table = []
    row, key = jnp.int32(0), jnp.int32(0)
    for request in range(new_ref.shape[0]):
        new, prior = new_ref[request], prior_ref[request]
        table.append((row, key, key + prior - row))
        row, key = row + new, key + new + prior
    return table


def key_range(table, row):
    first = jnp.broadcast_to(table[0][1], jnp.shape(row))
    shift = jnp.broadcast_to(table[0][2], jnp.shape(row))
    for start, key, ahead in table[1:]:
        own = row >= start
        first = jnp.where(own, key, first)
        shift = jnp.where(own, ahead, shift)
    return first, row + shift


def attend_kernel(slots, chunks, *refs):
    new_ref, prior_ref, row_ref, key_ref = refs[:4]
    q_refs = refs[4:4 + slots]
    kt_refs = refs[4 + slots:4 + slots + chunks]
    v_refs = refs[4 + slots + chunks:4 + slots + 2 * chunks]
    out_refs = refs[4 + slots + 2 * chunks:4 + 2 * slots + 2 * chunks]
    q_all, kt_all, va_all, out_all, logs_all, acc, top, qs = refs[4 + 2 * slots + 2 * chunks:]
    rows = q_refs[0].shape[0]
    width, cache = kt_all.shape
    heads = q_refs[0].shape[1] // width
    tile = min(ROW_TILE, rows)
    step = min(KEY_TILE, min(ref.shape[1] for ref in kt_refs))
    per_slot = rows // tile
    scale = width ** (-0.5)
    factor = scale * math.log2(math.e)
    table = request_table(new_ref, prior_ref)

    for slot in range(slots):
        q_all[slot * rows:(slot + 1) * rows, :] = q_refs[slot][...]
    done = 0
    for kt_ref, v_ref in zip(kt_refs, v_refs):
        count = kt_ref.shape[1]
        kt_all[:, done:done + count] = kt_ref[...]
        va_all[done:done + count, :width] = v_ref[...]
        done += count
    va_all[:, width:] = jnp.ones((cache, width), va_all.dtype)

    def key_norm(at, biggest):
        part = kt_all[:, pl.ds(pl.multiple_of(at * step, step), step)].astype(jnp.float32)
        return jnp.maximum(biggest, jnp.sum(part * part, axis=0, keepdims=True))

    def query_norm(at, biggest):
        for head in range(heads):
            part = q_all[pl.ds(pl.multiple_of(at * tile, tile), tile), head * width:(head + 1) * width].astype(jnp.float32)
            biggest = jnp.maximum(biggest, jnp.sum(part * part, axis=1, keepdims=True))
        return biggest

    key_max = jnp.max(lax.fori_loop(0, cache // step, key_norm, jnp.zeros((1, step), jnp.float32)))
    query_max = jnp.max(lax.fori_loop(0, slots * per_slot, query_norm, jnp.zeros((tile, 1), jnp.float32)))
    calm = query_max * key_max * (scale * scale) <= CALM * CALM

    def one_tile(at, carry):
        local = pl.multiple_of(at * tile, tile)
        row = row_ref[lax.div(at, per_slot)] + lax.rem(at, per_slot) * tile
        first_low, last_low = key_range(table, row)
        first_high, last_high = key_range(table, row + (tile - 1))
        acc[...] = jnp.zeros_like(acc)
        for head in range(heads):
            qs[head * tile:(head + 1) * tile, :] = q_all[pl.ds(local, tile), head * width:(head + 1) * width]
        own_rows = row + lax.broadcasted_iota(jnp.int32, (tile, 1), 0)
        first, last = key_range(table, own_rows)

        def allowed(key):
            index = key + lax.broadcasted_iota(jnp.int32, (tile, step), 1)
            return (index >= first) & (index <= last)

        def scores(part, left):
            return jnp.dot(qs[part, :], kt_all[:, pl.ds(left, step)], preferred_element_type=jnp.float32) * factor

        def add(left, weights):
            return jnp.dot(
                weights.astype(jnp.bfloat16), va_all[pl.ds(left, step), :], preferred_element_type=jnp.float32
            )

        @pl.when(calm)
        def _():
            def turn(at_key, carry):
                left = pl.multiple_of(at_key * step, step)
                key = key_ref[at_key]
                some = (key + step > first_low) & (key <= last_high)
                whole = (key >= first_high) & (key + step - 1 <= last_low)

                @pl.when(whole)
                def _():
                    acc[...] += add(left, jnp.exp2(scores(slice(None), left)))

                @pl.when(some & jnp.logical_not(whole))
                def _():
                    mask = allowed(key)
                    for head in range(heads):
                        part = slice(head * tile, (head + 1) * tile)
                        acc[part, :] += add(left, jnp.where(mask, jnp.exp2(scores(part, left)), 0.0))

                return carry

            lax.fori_loop(0, cache // step, turn, 0)
            top[...] = jnp.zeros_like(top)

        @pl.when(jnp.logical_not(calm))
        def _():
            top[...] = jnp.full_like(top, NEG)

            def turn(at_key, carry):
                left = pl.multiple_of(at_key * step, step)
                key = key_ref[at_key]

                @pl.when((key + step > first_low) & (key <= last_high))
                def _():
                    mask = allowed(key)
                    for head in range(heads):
                        part = slice(head * tile, (head + 1) * tile)
                        score = jnp.where(mask, scores(part, left), NEG)
                        old = top[part, :]
                        new = jnp.maximum(old, jnp.max(score, axis=1, keepdims=True))
                        weights = jnp.where(mask, jnp.exp2(score - new[:, :1]), 0.0)
                        shrink = jnp.exp2(old - new)
                        acc[part, :width] = acc[part, :width] * shrink
                        acc[part, width:] = acc[part, width:] * shrink
                        acc[part, :] += add(left, weights)
                        top[part, :] = new

                return carry

            lax.fori_loop(0, cache // step, turn, 0)

        lane = lax.broadcasted_iota(jnp.int32, (tile, LANES), 1)
        logs = jnp.zeros((tile, LANES), jnp.float32)
        for head in range(heads):
            part = slice(head * tile, (head + 1) * tile)
            total = acc[part, width:]
            live = total > 0.0
            safe = jnp.where(live, total, 1.0)
            out_all[pl.ds(local, tile), head * width:(head + 1) * width] = (acc[part, :width] / safe).astype(jnp.bfloat16)
            logs = jnp.where(lax.rem(lane, heads) == head, jnp.where(live, top[part, :] + jnp.log2(safe), NEG), logs)
        high = logs.astype(jnp.bfloat16).astype(jnp.float32)
        middle = (logs - high).astype(jnp.bfloat16).astype(jnp.float32)
        logs_all[pl.ds(local, tile), :] = jnp.where(
            lane < heads, high, jnp.where(lane < 2 * heads, middle, logs - high - middle)
        )
        return carry

    lax.fori_loop(0, slots * per_slot, one_tile, 0)
    for slot in range(slots):
        out_refs[slot][:rows, :] = out_all[slot * rows:(slot + 1) * rows, :]
        out_refs[slot][rows:, :] = jnp.zeros((SIDE, heads * width), jnp.bfloat16)
        for at in range(0, rows, LANES):
            turned = logs_all[slot * rows + at:slot * rows + at + LANES, :].T
            out_refs[slot][rows:, at:at + LANES] = turned[:SIDE, :].astype(jnp.bfloat16)


def attend(queries, turned_keys, values, new_counts, prior_lengths, row_starts, key_starts):
    slots, chunks = len(queries), len(turned_keys)
    rows = queries[0].shape[0]
    width = values[0].shape[1]
    cache = sum(part.shape[0] for part in values)
    heads = queries[0].shape[1] // width
    tile = min(ROW_TILE, rows)
    return pl.pallas_call(
        functools.partial(attend_kernel, slots, chunks),
        out_shape=tuple(jax.ShapeDtypeStruct((rows + SIDE, heads * width), jnp.bfloat16) for _ in range(slots)),
        in_specs=[SMEM] * 4 + [VMEM] * (slots + 2 * chunks),
        out_specs=(VMEM,) * slots,
        scratch_shapes=[
            pltpu.VMEM((slots * rows, heads * width), jnp.bfloat16),
            pltpu.VMEM((width, cache), jnp.bfloat16),
            pltpu.VMEM((cache, 2 * width), jnp.bfloat16),
            pltpu.VMEM((slots * rows, heads * width), jnp.bfloat16),
            pltpu.VMEM((slots * rows, LANES), jnp.float32),
            pltpu.VMEM((heads * tile, 2 * width), jnp.float32),
            pltpu.VMEM((heads * tile, width), jnp.float32),
            pltpu.VMEM((heads * tile, width), jnp.bfloat16),
        ],
        compiler_params=pltpu.CompilerParams(vmem_limit_bytes=36 * 1024 * 1024),
        cost_estimate=pl.CostEstimate(
            flops=slots * rows * heads * cache * width * 2, bytes_accessed=8 * 1024 * 1024, transcendentals=0
        ),
        name="attend",
    )(new_counts, prior_lengths, row_starts, key_starts, *queries, *turned_keys, *values)


def merge_kernel(heads, *refs):
    parts, out_ref = refs[:-1], refs[-1]
    rows = out_ref.shape[0]
    width = out_ref.shape[1] // heads
    logs = [part[rows:, :rows].astype(jnp.float32) for part in parts]
    spare = LANES - SIDE * len(parts)
    if spare:
        logs.append(jnp.full((spare, rows), NEG, jnp.float32))
    terms = jnp.concatenate(logs, axis=0).T
    total = terms + pltpu.roll(terms, LANES - heads, 1) + pltpu.roll(terms, LANES - 2 * heads, 1)
    lane = lax.broadcasted_iota(jnp.int32, (rows, LANES), 1)
    total = jnp.where((lax.rem(lane, SIDE) < heads) & (lane < SIDE * len(parts)), total, NEG)
    biggest = total
    for shift in (16, 32, 64):
        biggest = jnp.maximum(biggest, pltpu.roll(biggest, shift, 1))
    share = jnp.exp2(total - biggest)
    weight = share
    for shift in (16, 32, 64):
        weight = weight + pltpu.roll(weight, shift, 1)
    share = share / weight
    for head in range(heads):
        own = slice(head * width, (head + 1) * width)
        mixed = jnp.zeros((rows, width), jnp.float32)
        for at, part in enumerate(parts):
            lane_at = at * SIDE + head
            mixed = mixed + part[:rows, own].astype(jnp.float32) * share[:, lane_at:lane_at + 1]
        out_ref[:, own] = mixed.astype(out_ref.dtype)


def merge(parts, heads):
    rows = parts[0].shape[0] - SIDE
    return pl.pallas_call(
        functools.partial(merge_kernel, heads),
        out_shape=jax.ShapeDtypeStruct((rows, parts[0].shape[1]), jnp.bfloat16),
        in_specs=[VMEM] * len(parts),
        out_specs=VMEM,
        compiler_params=pltpu.CompilerParams(vmem_limit_bytes=16 * 1024 * 1024),
        name="merge",
    )(*parts)


def project_kernel(pieces, at_ref, *refs):
    w_ref, out_ref = refs[pieces], refs[pieces + 1]
    deep = refs[0].shape[1]
    total = None
    for at, piece in enumerate(refs[:pieces]):
        start = pl.multiple_of(at_ref[at] * deep, deep)
        term = jnp.dot(piece[...], w_ref[pl.ds(start, deep), :], preferred_element_type=jnp.float32)
        total = term if total is None else total + term
    out_ref[...] = total.astype(out_ref.dtype)


def project(pieces, places, w_out):
    rows, deep = pieces[0].shape
    depth, wide = w_out.shape
    block = min(512, wide)
    return pl.pallas_call(
        functools.partial(project_kernel, len(pieces)),
        out_shape=jax.ShapeDtypeStruct((rows, wide), jnp.bfloat16),
        grid=(wide // block,),
        in_specs=[SMEM]
        + [pl.BlockSpec((rows, deep), lambda at: (0, 0))] * len(pieces)
        + [pl.BlockSpec((depth, block), lambda at: (0, at))],
        out_specs=pl.BlockSpec((rows, block), lambda at: (0, at)),
        compiler_params=pltpu.CompilerParams(vmem_limit_bytes=24 * 1024 * 1024),
        cost_estimate=pl.CostEstimate(
            flops=2 * rows * depth * wide, bytes_accessed=2 * depth * wide, transcendentals=0
        ),
        name="project",
    )(places, *pieces, w_out)


def shift_pairs(count, stride, steps):
    groups = count // stride
    return [
        (group * stride + member, (group + steps) % groups * stride + member)
        for group in range(groups)
        for member in range(stride)
    ]


def swap_pairs(count):
    return [(at, at ^ 1) for at in range(count)]


def body(queries, keys, values, w_out, new_counts, prior_lengths):
    ctx_count, head_count = lax.axis_size("ctx"), lax.axis_size("head")
    device, place = lax.axis_index("ctx"), lax.axis_index("head")
    rows = queries.shape[0]
    cache, width = keys.shape
    heads = queries.shape[1] // width
    groups, half = ctx_count // 2, cache // 2
    group, side, core = device // 2, device % 2, place % 2

    blocks = [queries] + [
        lax.ppermute(queries, "ctx", shift_pairs(ctx_count, 2, steps)) for steps in range(1, groups)
    ]
    row_starts = jnp.stack([(((group - steps) % groups) * 2 + side) * rows for steps in range(groups)]).astype(jnp.int32)

    turned = keys.T
    part_k = lax.dynamic_slice_in_dim(turned, core * half, half, axis=1)
    part_v = lax.dynamic_slice_in_dim(values, core * half, half, axis=0)
    got_k = lax.ppermute(part_k, "ctx", swap_pairs(ctx_count))
    got_v = lax.ppermute(part_v, "ctx", swap_pairs(ctx_count))
    rest_k = lax.ppermute(got_k, "head", swap_pairs(head_count))
    rest_v = lax.ppermute(got_v, "head", swap_pairs(head_count))
    step = min(KEY_TILE, half)
    own_start = device * cache
    other_start = (device ^ 1) * cache
    key_starts = jnp.concatenate([
        own_start + jnp.arange(0, cache, step),
        other_start + core * half + jnp.arange(0, half, step),
        other_start + (1 - core) * half + jnp.arange(0, half, step),
    ]).astype(jnp.int32)

    parts = attend(
        blocks, [turned, got_k, rest_k], [values, got_v, rest_v], new_counts, prior_lengths, row_starts, key_starts
    )
    back = [parts[0]] + [
        lax.ppermute(parts[steps], "ctx", shift_pairs(ctx_count, 2, groups - steps)) for steps in range(1, groups)
    ]
    attended = merge(back, heads)

    chips = head_count // 2
    near = [attended] + [
        lax.ppermute(attended, "head", shift_pairs(head_count, 2, steps)) for steps in range(1, chips)
    ]
    far = [lax.ppermute(piece, "head", swap_pairs(head_count)) for piece in near]
    chip = place // 2
    near_at = [((chip - steps) % chips) * 2 + core for steps in range(chips)]
    far_at = [((chip - steps) % chips) * 2 + (1 - core) for steps in range(chips)]
    return project(near + far, jnp.stack(near_at + far_at).astype(jnp.int32), w_out)


def solution(mesh):
    return jax.shard_map(
        body,
        mesh=mesh,
        in_specs=(P("ctx", "head"), P("ctx", None), P("ctx", None), P(None, "head"), P(), P()),
        out_specs=P("ctx", "head"),
        check_vma=False,
    )
```

```python
import functools
import math

import jax
import jax.numpy as jnp
from jax import lax
from jax.experimental import pallas as pl
from jax.experimental.pallas import tpu as pltpu
from jax.sharding import PartitionSpec as P

NEG = -1e30
CALM = 60.0
ROW_TILE = 128
KEY_TILE = 512
BIG_STEP = 2048
SIDE = 16
LANES = 128
SMEM = pl.BlockSpec(memory_space=pltpu.SMEM)
VMEM = pl.BlockSpec(memory_space=pltpu.VMEM)


def request_table(plan_ref, requests):
    table = []
    row, key = jnp.int32(0), jnp.int32(0)
    for request in range(requests):
        new, prior = plan_ref[request], plan_ref[requests + request]
        table.append((row, key, key + prior - row))
        row, key = row + new, key + new + prior
    return table


def key_range(table, row):
    first = jnp.broadcast_to(table[0][1], jnp.shape(row))
    shift = jnp.broadcast_to(table[0][2], jnp.shape(row))
    for start, key, ahead in table[1:]:
        own = row >= start
        first = jnp.where(own, key, first)
        shift = jnp.where(own, ahead, shift)
    return first, row + shift


def attend_kernel(slots, chunks, carried, final, *refs):
    refs = list(refs)

    def take(count):
        head, refs[:count] = refs[:count], []
        return head

    (plan_ref,) = take(1)
    calm_in = take(1)[0] if carried else None
    q_refs, kt_refs, v_refs = take(slots), take(chunks), take(chunks)
    sums_in, logs_in = (take(slots), take(slots)) if carried else ([], [])
    if final:
        out_refs = take(slots)
    else:
        (calm_out,), sums_out, logs_out = take(1), take(slots), take(slots)
    kt_all, va_all, acc, top, qs, logs_all = refs
    rows = q_refs[0].shape[0]
    width, cache = kt_all.shape
    heads = q_refs[0].shape[1] // width
    tile = min(ROW_TILE, rows)
    big = min(BIG_STEP, min(ref.shape[1] for ref in kt_refs))
    step = min(KEY_TILE, big)
    requests = (plan_ref.shape[0] - slots - cache // step) // 2
    scale = width ** (-0.5)
    factor = scale * math.log2(math.e)
    table = request_table(plan_ref, requests)
    row_at, key_at = 2 * requests, 2 * requests + slots

    done = 0
    for kt_ref, v_ref in zip(kt_refs, v_refs):
        count = kt_ref.shape[1]
        kt_all[:, done:done + count] = kt_ref[...]
        va_all[done:done + count, :width] = v_ref[...]
        done += count
    va_all[:, width:] = jnp.ones((cache, width), va_all.dtype)

    def key_norm(at, biggest):
        part = kt_all[:, pl.ds(pl.multiple_of(at * step, step), step)].astype(jnp.float32)
        return jnp.maximum(biggest, jnp.sum(part * part, axis=0, keepdims=True))

    key_max = jnp.max(lax.fori_loop(0, cache // step, key_norm, jnp.zeros((1, step), jnp.float32)))
    norms = jnp.zeros((rows, 1), jnp.float32)
    for q_ref in q_refs:
        for head in range(heads):
            part = q_ref[:, head * width:(head + 1) * width].astype(jnp.float32)
            norms = jnp.maximum(norms, jnp.sum(part * part, axis=1, keepdims=True))
    calm = jnp.max(norms) * key_max * (scale * scale) <= CALM * CALM
    if carried:
        calm = calm & (calm_in[0] == 1)

    def one_tile(slot, at, carry):
        local = pl.multiple_of(at * tile, tile)
        stack = pl.multiple_of(at * (heads * tile), heads * tile)
        row = plan_ref[row_at + slot] + local
        first_low, last_low = key_range(table, row)
        first_high, last_high = key_range(table, row + (tile - 1))
        for head in range(heads):
            qs[head * tile:(head + 1) * tile, :] = q_refs[slot][pl.ds(local, tile), head * width:(head + 1) * width]
        if carried:
            acc[:, :width] = sums_in[slot][pl.ds(stack, heads * tile), :]
            before = logs_in[slot][pl.ds(stack, heads * tile), :]
            acc[:, width:] = jnp.broadcast_to(before[:, :1], (heads * tile, width))
        else:
            acc[...] = jnp.zeros_like(acc)
        own_rows = row + lax.broadcasted_iota(jnp.int32, (tile, 1), 0)
        first, last = key_range(table, own_rows)

        def allowed(key):
            index = key + lax.broadcasted_iota(jnp.int32, (tile, step), 1)
            return (index >= first) & (index <= last)

        def scores(part, left):
            return jnp.dot(qs[part, :], kt_all[:, pl.ds(left, step)], preferred_element_type=jnp.float32) * factor

        def add(left, weights):
            return jnp.dot(
                weights.astype(jnp.bfloat16), va_all[pl.ds(left, step), :], preferred_element_type=jnp.float32
            )

        def some(key, count):
            return (key + count > first_low) & (key <= last_high)

        @pl.when(calm)
        def _():
            def turn(at_big, carry):
                left = pl.multiple_of(at_big * big, big)
                key = plan_ref[key_at + at_big * (big // step)]
                whole = (key >= first_high) & (key + big - 1 <= last_low)

                @pl.when(whole)
                def _():
                    total = acc[...]
                    ahead = scores(slice(None), left)
                    for part in range(big // step):
                        score = ahead
                        if part + 1 < big // step:
                            ahead = scores(slice(None), left + (part + 1) * step)
                        total = total + add(left + part * step, jnp.exp2(score))
                    acc[...] = total

                @pl.when(some(key, big) & jnp.logical_not(whole))
                def _():
                    def small(at_small, carry):
                        inner = pl.multiple_of(left + at_small * step, step)
                        inner_key = key + at_small * step

                        @pl.when(some(inner_key, step))
                        def _():
                            mask = allowed(inner_key)
                            for head in range(heads):
                                part = slice(head * tile, (head + 1) * tile)
                                acc[part, :] += add(inner, jnp.where(mask, jnp.exp2(scores(part, inner)), 0.0))

                        return carry

                    lax.fori_loop(0, big // step, small, 0)

                return carry

            lax.fori_loop(0, cache // big, turn, 0)
            top[...] = jnp.zeros_like(top)

        @pl.when(jnp.logical_not(calm))
        def _():
            if carried:
                top[...] = jnp.broadcast_to(
                    jnp.where(before[:, :1] > 0.0, before[:, width // 2:width // 2 + 1], NEG), top.shape
                )
            else:
                top[...] = jnp.full_like(top, NEG)

            def turn(at_key, carry):
                left = pl.multiple_of(at_key * step, step)
                key = plan_ref[key_at + at_key]

                @pl.when(some(key, step))
                def _():
                    mask = allowed(key)
                    for head in range(heads):
                        part = slice(head * tile, (head + 1) * tile)
                        score = jnp.where(mask, scores(part, left), NEG)
                        old = top[part, :]
                        new = jnp.maximum(old, jnp.max(score, axis=1, keepdims=True))
                        weights = jnp.where(mask, jnp.exp2(score - new[:, :1]), 0.0)
                        shrink = jnp.exp2(old - new)
                        acc[part, :width] = acc[part, :width] * shrink
                        acc[part, width:] = acc[part, width:] * shrink
                        acc[part, :] += add(left, weights)
                        top[part, :] = new

                return carry

            lax.fori_loop(0, cache // step, turn, 0)

        if not final:
            sums_out[slot][pl.ds(stack, heads * tile), :] = acc[:, :width]
            lane = lax.broadcasted_iota(jnp.int32, (heads * tile, width), 1)
            logs_out[slot][pl.ds(stack, heads * tile), :] = jnp.where(lane < width // 2, acc[:, width:], top[...])
            return carry
        lane = lax.broadcasted_iota(jnp.int32, (tile, LANES), 1)
        logs = jnp.zeros((tile, LANES), jnp.float32)
        for head in range(heads):
            part = slice(head * tile, (head + 1) * tile)
            total = acc[part, width:]
            live = total > 0.0
            safe = jnp.where(live, total, 1.0)
            out_refs[slot][pl.ds(local, tile), head * width:(head + 1) * width] = (acc[part, :width] / safe).astype(jnp.bfloat16)
            logs = jnp.where(lax.rem(lane, heads) == head, jnp.where(live, top[part, :] + jnp.log2(safe), NEG), logs)
        high = logs.astype(jnp.bfloat16).astype(jnp.float32)
        middle = (logs - high).astype(jnp.bfloat16).astype(jnp.float32)
        logs_all[pl.ds(local, tile), :] = jnp.where(
            lane < heads, high, jnp.where(lane < 2 * heads, middle, logs - high - middle)
        )
        return carry

    for slot in range(slots):
        lax.fori_loop(0, rows // tile, functools.partial(one_tile, slot), 0)
        if final:
            out_refs[slot][rows:, :] = jnp.zeros((SIDE, heads * width), jnp.bfloat16)
            for at in range(0, rows, LANES):
                turned = logs_all[at:at + LANES, :].T
                out_refs[slot][rows:, at:at + LANES] = turned[:SIDE, :].astype(jnp.bfloat16)
    if not final:
        calm_out[0] = calm.astype(jnp.int32)


def attend(plan, queries, turned_keys, values, before=None, final=True):
    slots, chunks = len(queries), len(turned_keys)
    rows = queries[0].shape[0]
    width = values[0].shape[1]
    cache = sum(part.shape[0] for part in values)
    heads = queries[0].shape[1] // width
    tile = min(ROW_TILE, rows)
    carried = before is not None
    carry_in = [*before[1], *before[2]] if carried else []
    sums = jax.ShapeDtypeStruct((rows * heads, width), jnp.float32)
    if final:
        out_shape = (jax.ShapeDtypeStruct((rows + SIDE, heads * width), jnp.bfloat16),) * slots
        out_specs = (VMEM,) * slots
    else:
        out_shape = (jax.ShapeDtypeStruct((1,), jnp.int32),) + (sums,) * (2 * slots)
        out_specs = (SMEM,) + (VMEM,) * (2 * slots)
    result = pl.pallas_call(
        functools.partial(attend_kernel, slots, chunks, carried, final),
        out_shape=out_shape,
        in_specs=[SMEM] * (1 + carried) + [VMEM] * (slots + 2 * chunks + len(carry_in)),
        out_specs=out_specs,
        scratch_shapes=[
            pltpu.VMEM((width, cache), jnp.bfloat16),
            pltpu.VMEM((cache, 2 * width), jnp.bfloat16),
            pltpu.VMEM((heads * tile, 2 * width), jnp.float32),
            pltpu.VMEM((heads * tile, width), jnp.float32),
            pltpu.VMEM((heads * tile, width), jnp.bfloat16),
            pltpu.VMEM((rows, LANES), jnp.float32),
        ],
        compiler_params=pltpu.CompilerParams(vmem_limit_bytes=32 * 1024 * 1024),
        cost_estimate=pl.CostEstimate(
            flops=slots * rows * heads * cache * width * 4, bytes_accessed=4 * 1024 * 1024, transcendentals=0
        ),
        name="attend_last" if final else "attend_first",
    )(plan, *([before[0]] if carried else []), *queries, *turned_keys, *values, *carry_in)
    return result if final else (result[0], result[1:1 + slots], result[1 + slots:])


def merge_kernel(heads, *refs):
    parts, out_ref = refs[:-1], refs[-1]
    rows = out_ref.shape[0]
    width = out_ref.shape[1] // heads
    logs = [part[rows:, :rows].astype(jnp.float32) for part in parts]
    spare = LANES - SIDE * len(parts)
    if spare:
        logs.append(jnp.full((spare, rows), NEG, jnp.float32))
    terms = jnp.concatenate(logs, axis=0).T
    total = terms + pltpu.roll(terms, LANES - heads, 1) + pltpu.roll(terms, LANES - 2 * heads, 1)
    lane = lax.broadcasted_iota(jnp.int32, (rows, LANES), 1)
    total = jnp.where((lax.rem(lane, SIDE) < heads) & (lane < SIDE * len(parts)), total, NEG)
    biggest = total
    for shift in (16, 32, 64):
        biggest = jnp.maximum(biggest, pltpu.roll(biggest, shift, 1))
    share = jnp.exp2(total - biggest)
    weight = share
    for shift in (16, 32, 64):
        weight = weight + pltpu.roll(weight, shift, 1)
    share = share / weight
    for head in range(heads):
        own = slice(head * width, (head + 1) * width)
        mixed = jnp.zeros((rows, width), jnp.float32)
        for at, part in enumerate(parts):
            lane_at = at * SIDE + head
            mixed = mixed + part[:rows, own].astype(jnp.float32) * share[:, lane_at:lane_at + 1]
        out_ref[:, own] = mixed.astype(out_ref.dtype)


def merge(parts, heads):
    rows = parts[0].shape[0] - SIDE
    return pl.pallas_call(
        functools.partial(merge_kernel, heads),
        out_shape=jax.ShapeDtypeStruct((rows, parts[0].shape[1]), jnp.bfloat16),
        in_specs=[VMEM] * len(parts),
        out_specs=VMEM,
        compiler_params=pltpu.CompilerParams(vmem_limit_bytes=16 * 1024 * 1024),
        name="merge",
    )(*parts)


def project_kernel(pieces, at_ref, *refs):
    w_ref, out_ref = refs[pieces], refs[pieces + 1]
    deep = refs[0].shape[1]
    total = None
    for at, piece in enumerate(refs[:pieces]):
        start = pl.multiple_of(at_ref[at] * deep, deep)
        term = jnp.dot(piece[...], w_ref[pl.ds(start, deep), :], preferred_element_type=jnp.float32)
        total = term if total is None else total + term
    out_ref[...] = total.astype(out_ref.dtype)


def project(pieces, places, w_out):
    rows, deep = pieces[0].shape
    depth, wide = w_out.shape
    block = min(512, wide)
    return pl.pallas_call(
        functools.partial(project_kernel, len(pieces)),
        out_shape=jax.ShapeDtypeStruct((rows, wide), jnp.bfloat16),
        grid=(wide // block,),
        in_specs=[SMEM]
        + [pl.BlockSpec((rows, deep), lambda at: (0, 0))] * len(pieces)
        + [pl.BlockSpec((depth, block), lambda at: (0, at))],
        out_specs=pl.BlockSpec((rows, block), lambda at: (0, at)),
        compiler_params=pltpu.CompilerParams(vmem_limit_bytes=56 * 1024 * 1024),
        cost_estimate=pl.CostEstimate(
            flops=2 * rows * depth * wide, bytes_accessed=2 * depth * wide, transcendentals=0
        ),
        name="project",
    )(places, *pieces, w_out)


def shift_pairs(count, stride, steps):
    groups = count // stride
    return [
        (group * stride + member, (group + steps) % groups * stride + member)
        for group in range(groups)
        for member in range(stride)
    ]


def swap_pairs(count):
    return [(at, at ^ 1) for at in range(count)]


def body(queries, keys, values, w_out, new_counts, prior_lengths):
    ctx_count, head_count = lax.axis_size("ctx"), lax.axis_size("head")
    device, place = lax.axis_index("ctx"), lax.axis_index("head")
    rows = queries.shape[0]
    cache, width = keys.shape
    heads = queries.shape[1] // width
    groups, half = ctx_count // 2, cache // 2
    group, side, core = device // 2, device % 2, place % 2

    blocks = [queries] + [
        lax.ppermute(queries, "ctx", shift_pairs(ctx_count, 2, steps)) for steps in range(1, groups)
    ]
    row_starts = [(((group - steps) % groups) * 2 + side) * rows for steps in range(groups)]

    turned = keys.T
    part_k = lax.dynamic_slice_in_dim(turned, core * half, half, axis=1)
    part_v = lax.dynamic_slice_in_dim(values, core * half, half, axis=0)
    got_k = lax.ppermute(part_k, "ctx", swap_pairs(ctx_count))
    got_v = lax.ppermute(part_v, "ctx", swap_pairs(ctx_count))
    got_k, got_v, _ = lax.optimization_barrier((got_k, got_v, blocks[1:]))
    rest_k = lax.ppermute(got_k, "head", swap_pairs(head_count))
    rest_v = lax.ppermute(got_v, "head", swap_pairs(head_count))
    step = min(KEY_TILE, half)
    other = (device ^ 1) * cache
    own_keys = device * cache + jnp.arange(0, cache, step)
    other_keys = [
        other + core * half + jnp.arange(0, half, step), other + (1 - core) * half + jnp.arange(0, half, step)
    ]

    def plan(slots, key_starts):
        starts = jnp.stack([row_starts[slot] for slot in slots])
        return jnp.concatenate([new_counts, prior_lengths, starts, *key_starts]).astype(jnp.int32)

    every = list(range(groups))
    calm, sums, logs = attend(plan(every, [own_keys]), blocks, [turned], [values], final=False)
    away = sorted(every[1:], key=lambda steps: -min(steps, groups - steps))
    near_count = len(away) * 2 // 3
    back = [None] * groups
    for slots in (away[:len(away) - near_count], away[len(away) - near_count:], [0]):
        if not slots:
            continue
        before = (calm, [sums[slot] for slot in slots], [logs[slot] for slot in slots])
        parts = attend(
            plan(slots, other_keys), [blocks[slot] for slot in slots], [got_k, rest_k], [got_v, rest_v], before
        )
        for slot, part in zip(slots, parts):
            back[slot] = part if slot == 0 else lax.ppermute(part, "ctx", shift_pairs(ctx_count, 2, groups - slot))
    attended = merge(back, heads)

    chips = head_count // 2
    near = [attended] + [
        lax.ppermute(attended, "head", shift_pairs(head_count, 2, steps)) for steps in range(1, chips)
    ]
    far = [lax.ppermute(piece, "head", swap_pairs(head_count)) for piece in near]
    chip = place // 2
    near_at = [((chip - steps) % chips) * 2 + core for steps in range(chips)]
    far_at = [((chip - steps) % chips) * 2 + (1 - core) for steps in range(chips)]
    return project(near + far, jnp.stack(near_at + far_at).astype(jnp.int32), w_out)


def solution(mesh):
    return jax.shard_map(
        body,
        mesh=mesh,
        in_specs=(P("ctx", "head"), P("ctx", None), P("ctx", None), P(None, "head"), P(), P()),
        out_specs=P("ctx", "head"),
        check_vma=False,
    )
```

```python
import functools
import math

import jax
import jax.numpy as jnp
from jax import lax
from jax.experimental import pallas as pl
from jax.experimental.pallas import tpu as pltpu
from jax.sharding import PartitionSpec as P

NEG = -1e30
CALM = 60.0
ROW_TILE = 128
KEY_TILE = 512
BIG_STEP = 2048
SIDE = 16
LANES = 128
MIB = 1024 * 1024
SMEM = pl.BlockSpec(memory_space=pltpu.SMEM)
VMEM = pl.BlockSpec(memory_space=pltpu.VMEM)


def prepare_kernel(parts, *refs):
    part_refs, (turned_ref, beside_ref, longest_ref) = refs[:parts], refs[parts:]
    width, cache = turned_ref.shape
    step = min(KEY_TILE, part_refs[0].shape[0])
    longest = jnp.zeros((1, step), jnp.float32)
    done = 0
    for part_ref in part_refs:

        def turn(at, longest, part_ref=part_ref, done=done):
            here = pl.multiple_of(at * step, step)
            there = pl.multiple_of(done + at * step, step)
            keys = part_ref[pl.ds(here, step), :width].astype(jnp.float32).T
            turned_ref[:, pl.ds(there, step)] = keys.astype(jnp.bfloat16)
            beside_ref[pl.ds(there, step), :width] = part_ref[pl.ds(here, step), width:]
            return jnp.maximum(longest, jnp.sum(keys * keys, axis=0, keepdims=True))

        longest = lax.fori_loop(0, part_ref.shape[0] // step, turn, longest)
        done += part_ref.shape[0]
    beside_ref[:, width:] = jnp.ones((cache, width), jnp.bfloat16)
    longest_ref[0] = jnp.max(longest)


def prepare(parts):
    width = parts[0].shape[1] // 2
    cache = sum(part.shape[0] for part in parts)
    return pl.pallas_call(
        functools.partial(prepare_kernel, len(parts)),
        out_shape=(
            pltpu.VMEM((width, cache), jnp.bfloat16),
            pltpu.VMEM((cache, 2 * width), jnp.bfloat16),
            jax.ShapeDtypeStruct((1,), jnp.float32),
        ),
        in_specs=[VMEM] * len(parts),
        out_specs=(VMEM, VMEM, SMEM),
        compiler_params=pltpu.CompilerParams(vmem_limit_bytes=12 * MIB),
        name="prepare",
    )(*parts)


def request_table(plan_ref, requests):
    table = []
    row, key = jnp.int32(0), jnp.int32(0)
    for request in range(requests):
        new, prior = plan_ref[request], plan_ref[requests + request]
        table.append((row, key, key + prior - row, row + new, key + new + prior))
        row, key = row + new, key + new + prior
    return table


def key_range(table, row):
    first = jnp.broadcast_to(table[0][1], jnp.shape(row))
    shift = jnp.broadcast_to(table[0][2], jnp.shape(row))
    for start, key, ahead, _, _ in table[1:]:
        own = row >= start
        first = jnp.where(own, key, first)
        shift = jnp.where(own, ahead, shift)
    return first, row + shift


def request_of(table, key):
    entry = table[0]
    for other in table[1:]:
        own = key >= other[1]
        entry = tuple(jnp.where(own, new, old) for new, old in zip(other, entry))
    return entry


def attend_kernel(slots, requests, row_at, key_at, slot_at, carried, *refs):
    refs = list(refs)

    def take(count):
        head, refs[:count] = refs[:count], []
        return head

    plan_ref, longest_ref, turned_ref, beside_ref = take(4)
    if carried:
        calm_in, norm_in, stack_ref, sums_in, logs_in = take(5)
        out_refs = take(slots)
        acc, top, logs_all, out_all = refs
    else:
        q_refs = take(slots)
        calm_out, norm_out, stack_ref, sums_out, logs_out = take(5)
        acc, top = refs
    width, cache = turned_ref.shape
    rows = out_refs[0].shape[0] - SIDE if carried else q_refs[0].shape[0]
    heads = out_refs[0].shape[1] // width if carried else q_refs[0].shape[1] // width
    tile = min(ROW_TILE, rows)
    deep = heads * tile
    big = min(BIG_STEP, cache // 2)
    step = min(KEY_TILE, big)
    scale = width ** (-0.5)
    factor = scale * math.log2(math.e)
    table = request_table(plan_ref, requests)

    if carried:
        norm = norm_in[0]
        calm = (norm * longest_ref[0] * (scale * scale) <= CALM * CALM) & (calm_in[0] == 1)
    else:
        norms = jnp.zeros((tile, 1), jnp.float32)
        for slot in range(slots):
            for at in range(0, rows, tile):
                for head in range(heads):
                    part = q_refs[slot][at:at + tile, head * width:(head + 1) * width]
                    start = slot * rows * heads + at * heads + head * tile
                    stack_ref[start:start + tile, :] = part
                    wide = part.astype(jnp.float32)
                    norms = jnp.maximum(norms, jnp.sum(wide * wide, axis=1, keepdims=True))
        norm = jnp.max(norms)
        norm_out[0] = norm
        calm = norm * longest_ref[0] * (scale * scale) <= CALM * CALM
        calm_out[0] = calm.astype(jnp.int32)

    def one_tile(index, carry):
        order, at = lax.div(index, rows // tile), lax.rem(index, rows // tile)
        slot = plan_ref[slot_at + order]
        row = plan_ref[row_at + slot] + at * tile
        stack = pl.multiple_of((slot * (rows // tile) + at) * deep, deep)
        first_low, last_low = key_range(table, row)
        first_high, last_high = key_range(table, row + (tile - 1))
        if carried:
            acc[:, :width] = sums_in[pl.ds(stack, deep), :]
            acc[:, width:] = jnp.broadcast_to(logs_in[pl.ds(stack, deep), :][:, :1], (deep, width))
        else:
            acc[...] = jnp.zeros_like(acc)
        own_rows = row + lax.broadcasted_iota(jnp.int32, (tile, 1), 0)
        first, last = key_range(table, own_rows)

        def allowed(key):
            place = key + lax.broadcasted_iota(jnp.int32, (tile, step), 1)
            return (place >= first) & (place <= last)

        def scores(part, left):
            return jnp.dot(
                stack_ref[pl.ds(stack + part.start, part.stop - part.start), :],
                turned_ref[:, pl.ds(left, step)],
                preferred_element_type=jnp.float32,
            ) * factor

        def add(left, weights):
            return jnp.dot(
                weights.astype(jnp.bfloat16), beside_ref[pl.ds(left, step), :], preferred_element_type=jnp.float32
            )

        def some(key, count):
            return (key + count > first_low) & (key <= last_high)

        def whole(key, count):
            start, _, ahead, row_end, key_end = request_of(table, key)
            low, high = jnp.maximum(row, start), jnp.minimum(row + tile, row_end)
            return (key + count <= key_end) & (low < high) & (low + ahead >= key + count - 1), low, high

        def pour(left, count, low, high):
            total = None
            ahead = scores(slice(0, deep), left)
            for part in range(count // step):
                score = ahead
                if part + 1 < count // step:
                    ahead = scores(slice(0, deep), left + (part + 1) * step)
                term = add(left + part * step, jnp.exp2(score))
                total = term if total is None else total + term
            own = (own_rows >= low) & (own_rows < high)
            for head in range(heads):
                part = slice(head * tile, (head + 1) * tile)
                acc[part, :] += jnp.where(own, total[part, :], 0.0)

        @pl.when(calm)
        def _():
            def turn(at_big, carry):
                left = pl.multiple_of(at_big * big, big)
                key = plan_ref[key_at + at_big * (big // step)]
                live = some(key, big)
                plain, low, high = whole(key, big)

                @pl.when(live & plain)
                def _():
                    pour(left, big, low, high)

                @pl.when(live & jnp.logical_not(plain))
                def _():
                    def small(at_small, carry):
                        inner = pl.multiple_of(left + at_small * step, step)
                        inner_key = key + at_small * step
                        inner_live = some(inner_key, step)
                        inner_plain, inner_low, inner_high = whole(inner_key, step)

                        @pl.when(inner_live & inner_plain)
                        def _():
                            pour(inner, step, inner_low, inner_high)

                        @pl.when(inner_live & jnp.logical_not(inner_plain))
                        def _():
                            mask = allowed(inner_key)
                            weights = jnp.exp2(scores(slice(0, deep), inner))
                            weights = jnp.concatenate([
                                jnp.where(mask, weights[head * tile:(head + 1) * tile, :], 0.0)
                                for head in range(heads)
                            ])
                            acc[...] += add(inner, weights)

                        return carry

                    lax.fori_loop(0, big // step, small, 0)

                return carry

            lax.fori_loop(0, cache // big, turn, 0)
            top[...] = jnp.zeros_like(top)

        @pl.when(jnp.logical_not(calm))
        def _():
            if carried:
                before = logs_in[pl.ds(stack, deep), :]
                top[...] = jnp.broadcast_to(
                    jnp.where(before[:, :1] > 0.0, before[:, width // 2:width // 2 + 1], NEG), top.shape
                )
            else:
                top[...] = jnp.full_like(top, NEG)

            def turn(at_key, carry):
                left = pl.multiple_of(at_key * step, step)
                key = plan_ref[key_at + at_key]

                @pl.when(some(key, step))
                def _():
                    mask = allowed(key)
                    for head in range(heads):
                        part = slice(head * tile, (head + 1) * tile)
                        score = jnp.where(mask, scores(part, left), NEG)
                        old = top[part, :]
                        new = jnp.maximum(old, jnp.max(score, axis=1, keepdims=True))
                        weights = jnp.where(mask, jnp.exp2(score - new[:, :1]), 0.0)
                        shrink = jnp.exp2(old - new)
                        acc[part, :width] = acc[part, :width] * shrink
                        acc[part, width:] = acc[part, width:] * shrink
                        acc[part, :] += add(left, weights)
                        top[part, :] = new

                return carry

            lax.fori_loop(0, cache // step, turn, 0)

        if not carried:
            sums_out[pl.ds(stack, deep), :] = acc[:, :width]
            lane = lax.broadcasted_iota(jnp.int32, (deep, width), 1)
            logs_out[pl.ds(stack, deep), :] = jnp.where(lane < width // 2, acc[:, width:], top[...])
            return carry
        lane = lax.broadcasted_iota(jnp.int32, (tile, LANES), 1)
        logs = jnp.zeros((tile, LANES), jnp.float32)
        here = pl.multiple_of(index * tile, tile)
        for head in range(heads):
            part = slice(head * tile, (head + 1) * tile)
            total = acc[part, width:]
            live = total > 0.0
            safe = jnp.where(live, total, 1.0)
            out_all[pl.ds(here, tile), head * width:(head + 1) * width] = (acc[part, :width] / safe).astype(jnp.bfloat16)
            logs = jnp.where(lax.rem(lane, heads) == head, jnp.where(live, top[part, :] + jnp.log2(safe), NEG), logs)
        high = logs.astype(jnp.bfloat16).astype(jnp.float32)
        middle = (logs - high).astype(jnp.bfloat16).astype(jnp.float32)
        logs_all[pl.ds(here, tile), :] = jnp.where(
            lane < heads, high, jnp.where(lane < 2 * heads, middle, logs - high - middle)
        )
        return carry

    lax.fori_loop(0, slots * (rows // tile), one_tile, 0)
    if carried:
        for slot, out_ref in enumerate(out_refs):
            out_ref[:rows, :] = out_all[slot * rows:(slot + 1) * rows, :]
            out_ref[rows:, :] = jnp.zeros((SIDE, heads * width), jnp.bfloat16)
            for at in range(0, rows, LANES):
                turned = logs_all[slot * rows + at:slot * rows + at + LANES, :].T
                out_ref[rows:, at:at + LANES] = turned[:SIDE, :].astype(jnp.bfloat16)


def attend(places, plan, cache_side, queries=None, before=None, slots=0, heads=0):
    turned, beside, longest = cache_side
    width, cache = turned.shape
    carried = before is not None
    if not carried:
        slots, rows = len(queries), queries[0].shape[0]
        heads = queries[0].shape[1] // width
    else:
        rows = before[2].shape[0] // heads // places["blocks"]
    tile = min(ROW_TILE, rows)
    kernel = functools.partial(
        attend_kernel, slots, places["requests"], places["rows"], places["keys"], places["slots"], carried
    )
    scratch = [
        pltpu.VMEM((heads * tile, 2 * width), jnp.float32),
        pltpu.VMEM((heads * tile, width), jnp.float32),
    ]
    common = dict(
        compiler_params=pltpu.CompilerParams(vmem_limit_bytes=20 * MIB),
        cost_estimate=pl.CostEstimate(
            flops=slots * rows * heads * cache * width * 4, bytes_accessed=4 * MIB, transcendentals=0
        ),
    )
    if carried:
        return pl.pallas_call(
            kernel,
            out_shape=(jax.ShapeDtypeStruct((rows + SIDE, heads * width), jnp.bfloat16),) * slots,
            in_specs=[SMEM, SMEM, VMEM, VMEM, SMEM, SMEM, VMEM, VMEM, VMEM],
            out_specs=(VMEM,) * slots,
            scratch_shapes=scratch + [
                pltpu.VMEM((slots * rows, LANES), jnp.float32),
                pltpu.VMEM((slots * rows, heads * width), jnp.bfloat16),
            ],
            name="attend_last",
            **common,
        )(plan, longest, turned, beside, *before)
    stacked = slots * rows * heads
    return pl.pallas_call(
        kernel,
        out_shape=(
            jax.ShapeDtypeStruct((1,), jnp.int32),
            jax.ShapeDtypeStruct((1,), jnp.float32),
            pltpu.VMEM((stacked, width), jnp.bfloat16),
            pltpu.VMEM((stacked, width), jnp.float32),
            pltpu.VMEM((stacked, width), jnp.float32),
        ),
        in_specs=[SMEM, SMEM, VMEM, VMEM] + [VMEM] * slots,
        out_specs=(SMEM, SMEM, VMEM, VMEM, VMEM),
        scratch_shapes=scratch,
        name="attend_first",
        **common,
    )(plan, longest, turned, beside, *queries)


def merge_kernel(heads, there_ref, *refs):
    parts, out_ref = refs[:-1], refs[-1]
    rows = out_ref.shape[0]
    width = out_ref.shape[1] // heads
    logs = [
        jnp.where(there_ref[at] == 1, part[rows:, :rows].astype(jnp.float32), NEG) for at, part in enumerate(parts)
    ]
    spare = LANES - SIDE * len(parts)
    if spare:
        logs.append(jnp.full((spare, rows), NEG, jnp.float32))
    terms = jnp.concatenate(logs, axis=0).T
    total = terms + pltpu.roll(terms, LANES - heads, 1) + pltpu.roll(terms, LANES - 2 * heads, 1)
    lane = lax.broadcasted_iota(jnp.int32, (rows, LANES), 1)
    total = jnp.where((lax.rem(lane, SIDE) < heads) & (lane < SIDE * len(parts)), total, NEG)
    biggest = total
    for shift in (16, 32, 64):
        biggest = jnp.maximum(biggest, pltpu.roll(biggest, shift, 1))
    share = jnp.exp2(total - biggest)
    weight = share
    for shift in (16, 32, 64):
        weight = weight + pltpu.roll(weight, shift, 1)
    share = share / weight
    for head in range(heads):
        own = slice(head * width, (head + 1) * width)
        mixed = jnp.zeros((rows, width), jnp.float32)
        for at, part in enumerate(parts):
            lane_at = at * SIDE + head
            mixed = mixed + part[:rows, own].astype(jnp.float32) * share[:, lane_at:lane_at + 1]
        out_ref[:, own] = mixed.astype(out_ref.dtype)


def merge(parts, there, heads):
    rows = parts[0].shape[0] - SIDE
    return pl.pallas_call(
        functools.partial(merge_kernel, heads),
        out_shape=jax.ShapeDtypeStruct((rows, parts[0].shape[1]), jnp.bfloat16),
        in_specs=[SMEM] + [VMEM] * len(parts),
        out_specs=VMEM,
        compiler_params=pltpu.CompilerParams(vmem_limit_bytes=12 * MIB),
        name="merge",
    )(there, *parts)


def fetch_kernel(w_ref, out_ref, sem):
    copy = pltpu.make_async_copy(w_ref, out_ref, sem)
    copy.start()
    copy.wait()


def fetch(w_out):
    return pl.pallas_call(
        fetch_kernel,
        out_shape=pltpu.VMEM(w_out.shape, w_out.dtype),
        in_specs=[pl.BlockSpec(memory_space=pl.ANY)],
        out_specs=VMEM,
        scratch_shapes=[pltpu.SemaphoreType.DMA],
        compiler_params=pltpu.CompilerParams(vmem_limit_bytes=MIB),
        name="fetch",
    )(w_out)


def project_kernel(pieces, at_ref, *refs):
    w_ref, out_ref, whole = refs[pieces:]
    deep = refs[0].shape[1]
    block = out_ref.shape[1]

    @pl.when(pl.program_id(0) == 0)
    def _():
        for at, piece in enumerate(refs[:pieces]):
            whole[:, pl.ds(pl.multiple_of(at_ref[at] * deep, deep), deep)] = piece[...]

    left = pl.multiple_of(pl.program_id(0) * block, block)
    out_ref[...] = jnp.dot(
        whole[...], w_ref[:, pl.ds(left, block)], preferred_element_type=jnp.float32
    ).astype(out_ref.dtype)


def project(pieces, places, w_out):
    rows, deep = pieces[0].shape
    depth, wide = w_out.shape
    block = min(512, wide)
    return pl.pallas_call(
        functools.partial(project_kernel, len(pieces)),
        out_shape=jax.ShapeDtypeStruct((rows, wide), jnp.bfloat16),
        grid=(wide // block,),
        in_specs=[SMEM] + [VMEM] * (len(pieces) + 1),
        out_specs=pl.BlockSpec((rows, block), lambda at: (0, at)),
        scratch_shapes=[pltpu.VMEM((rows, depth), jnp.bfloat16)],
        compiler_params=pltpu.CompilerParams(vmem_limit_bytes=20 * MIB),
        cost_estimate=pl.CostEstimate(
            flops=2 * rows * depth * wide, bytes_accessed=2 * depth * wide, transcendentals=0
        ),
        name="project",
    )(places, *pieces, w_out)


def shift_pairs(count, stride, steps):
    groups = count // stride
    return [
        (group * stride + member, (group + steps) % groups * stride + member)
        for group in range(groups)
        for member in range(stride)
    ]


def swap_pairs(count):
    return [(at, at ^ 1) for at in range(count)]


def is_far(groups, one, two):
    low, high = min(one, two), max(one, two)
    return low < groups // 2 and high >= groups - max(1, groups // 4)


def move(value, groups, steps, far):
    pairs = [
        (source, target)
        for source, target in shift_pairs(2 * groups, 2, steps)
        if is_far(groups, source // 2, target // 2) == far
    ]
    return lax.ppermute(value, "ctx", pairs) if pairs else jnp.zeros_like(value)


def far_needed(groups, rows, cache, new_counts, prior_lengths):
    row_ends = jnp.cumsum(new_counts)
    key_ends = jnp.cumsum(new_counts + prior_lengths)
    key_first = key_ends - new_counts - prior_lengths
    ahead = key_first + prior_lengths - (row_ends - new_counts)

    def at(table, row):
        own = jnp.sum((row[:, None] >= row_ends[None, :]).astype(jnp.int32), axis=1)
        return jnp.sum(jnp.where(own[:, None] == jnp.arange(table.shape[0])[None, :], table[None, :], 0), axis=1)

    pairs = [(s, t) for s in range(groups) for t in range(groups) if is_far(groups, s, t)]
    source = jnp.array([s for s, _ in pairs], jnp.int32) * (2 * rows)
    target = jnp.array([t for _, t in pairs], jnp.int32) * (2 * cache)
    end = source + 2 * rows - 1
    return jnp.any((at(key_first, source) < target + 2 * cache) & (end + at(ahead, end) >= target))


def body(queries, keys, values, w_out, new_counts, prior_lengths):
    ctx_count, head_count = lax.axis_size("ctx"), lax.axis_size("head")
    device, place = lax.axis_index("ctx"), lax.axis_index("head")
    rows = queries.shape[0]
    cache, width = keys.shape
    heads = queries.shape[1] // width
    groups, half = ctx_count // 2, cache // 2
    group, side, core = device // 2, device % 2, place % 2
    every = list(range(groups))

    blocks = [move(queries, groups, steps, False) for steps in every[1:]]

    cached = jnp.concatenate([keys, values], axis=1)
    got = lax.ppermute(
        lax.dynamic_slice_in_dim(cached, core * half, half, axis=0), "ctx", swap_pairs(ctx_count)
    )

    needed = far_needed(groups, rows, cache, new_counts, prior_lengths)
    calls = [[slot for slot in every[1:] if 2 * slot >= groups], [slot for slot in every[1:] if 2 * slot < groups], [0]]
    calls = [slots for slots in calls if slots]
    step = min(KEY_TILE, half)
    other = (device ^ 1) * cache
    starts = jnp.stack([(((group - steps) % groups) * 2 + side) * rows for steps in every])
    pieces = [
        new_counts,
        prior_lengths,
        starts,
        device * cache + jnp.arange(0, cache, step),
        other + core * half + jnp.arange(0, half, step),
        other + (1 - core) * half + jnp.arange(0, half, step),
        jnp.array([slot for slots in calls for slot in slots], jnp.int32),
    ]
    plan = jnp.concatenate(pieces).astype(jnp.int32)
    requests = new_counts.shape[0]
    places = dict(requests=requests, rows=2 * requests, keys=2 * requests + groups, blocks=groups)
    places["slots"] = places["keys"] + 2 * (cache // step)

    own_side = prepare([cached])
    near_w = fetch(w_out)
    got, _ = lax.optimization_barrier((got, blocks))
    rest = lax.ppermute(got, "head", swap_pairs(head_count))
    blocks = lax.cond(
        needed,
        lambda parts: [part + move(queries, groups, steps, True) for steps, part in zip(every[1:], parts)],
        lambda parts: parts,
        blocks,
    )
    sums = attend(places, plan, own_side, queries=[queries] + blocks)
    other_side = prepare([got, rest])
    places["keys"] += cache // step
    parts = [None] * groups
    for slots in calls:
        results = attend(places, plan, other_side, before=sums, slots=len(slots), heads=heads)
        places["slots"] += len(slots)
        for slot, part in zip(slots, results):
            parts[slot] = part
    back = [move(parts[slot], groups, groups - slot, False) for slot in every[1:]]
    back = lax.cond(
        needed,
        lambda near: [
            part + move(parts[slot], groups, groups - slot, True) for slot, part in zip(every[1:], near)
        ],
        lambda near: near,
        back,
    )
    far = jnp.array([[is_far(groups, (g + d) % groups, g) for d in every] for g in every], jnp.int32)
    there = jnp.where(needed, 1, 1 - lax.dynamic_index_in_dim(far, group, 0, keepdims=False)).astype(jnp.int32)
    attended = merge([parts[0]] + back, there, heads)

    chips = head_count // 2
    near = [attended] + [
        lax.ppermute(attended, "head", shift_pairs(head_count, 2, steps)) for steps in range(1, chips)
    ]
    far_core = [lax.ppermute(piece, "head", swap_pairs(head_count)) for piece in near]
    chip = place // 2
    near_at = [((chip - steps) % chips) * 2 + core for steps in range(chips)]
    far_at = [((chip - steps) % chips) * 2 + (1 - core) for steps in range(chips)]
    return project(near + far_core, jnp.stack(near_at + far_at).astype(jnp.int32), near_w)


def solution(mesh):
    return jax.shard_map(
        body,
        mesh=mesh,
        in_specs=(P("ctx", "head"), P("ctx", None), P("ctx", None), P(None, "head"), P(), P()),
        out_specs=P("ctx", "head"),
        check_vma=False,
    )
```

```python
import functools
import math

import jax
import jax.numpy as jnp
from jax import lax
from jax.experimental import pallas as pl
from jax.experimental.pallas import tpu as pltpu
from jax.sharding import PartitionSpec as P

NEG = -1e30
CALM = 60.0
ROW_TILE = 128
KEY_TILE = 512
BIG_STEP = 2048
SIDE = 16
LANES = 128
MIB = 1024 * 1024
SMEM = pl.BlockSpec(memory_space=pltpu.SMEM)
VMEM = pl.BlockSpec(memory_space=pltpu.VMEM)
HBM = pl.BlockSpec(memory_space=pltpu.HBM)


def prepare_kernel(joined, *refs):
    keys_ref, beside_ref, longest_ref = refs[2:]
    cache, width = keys_ref.shape
    sources = [(ref, ref, width) for ref in refs[:2]] if joined else [(refs[0], refs[1], 0)]
    step = min(KEY_TILE, refs[0].shape[0])
    longest = jnp.zeros((step, 1), jnp.float32)
    done = 0
    for from_keys, from_values, value_lane in sources:

        def turn(at, longest, from_keys=from_keys, from_values=from_values, value_lane=value_lane, done=done):
            here = pl.ds(pl.multiple_of(at * step, step), step)
            there = pl.ds(pl.multiple_of(done + at * step, step), step)
            keys = from_keys[here, :width]
            keys_ref[there, :] = keys
            beside_ref[there, :width] = from_values[here, value_lane:value_lane + width]
            beside_ref[there, width:] = jnp.ones((step, width), jnp.bfloat16)
            wide = keys.astype(jnp.float32)
            return jnp.maximum(longest, jnp.sum(wide * wide, axis=1, keepdims=True))

        longest = lax.fori_loop(0, from_keys.shape[0] // step, turn, longest)
        done += from_keys.shape[0]
    longest_ref[0] = jnp.max(longest)


def prepare(one, two, joined):
    width = one.shape[1] // 2 if joined else one.shape[1]
    cache = one.shape[0] + two.shape[0] if joined else one.shape[0]
    return pl.pallas_call(
        functools.partial(prepare_kernel, joined),
        out_shape=(
            pltpu.VMEM((cache, width), jnp.bfloat16),
            pltpu.VMEM((cache, 2 * width), jnp.bfloat16),
            jax.ShapeDtypeStruct((1,), jnp.float32),
        ),
        in_specs=[VMEM] * 2,
        out_specs=(VMEM, VMEM, SMEM),
        compiler_params=pltpu.CompilerParams(vmem_limit_bytes=12 * MIB),
        name="prepare",
    )(one, two)


def request_table(plan_ref, requests):
    table = []
    row, key = jnp.int32(0), jnp.int32(0)
    for request in range(requests):
        new, prior = plan_ref[request], plan_ref[requests + request]
        table.append((row, key, key + prior - row, row + new, key + new + prior))
        row, key = row + new, key + new + prior
    return table


def key_range(table, row):
    first = jnp.broadcast_to(table[0][1], jnp.shape(row))
    shift = jnp.broadcast_to(table[0][2], jnp.shape(row))
    for start, key, ahead, _, _ in table[1:]:
        own = row >= start
        first = jnp.where(own, key, first)
        shift = jnp.where(own, ahead, shift)
    return first, row + shift


def request_of(table, key):
    entry = table[0]
    for other in table[1:]:
        own = key >= other[1]
        entry = tuple(jnp.where(own, new, old) for new, old in zip(other, entry))
    return entry


def attend_kernel(slots, requests, row_at, key_at, slot_at, carried, fetching, *refs):
    refs = list(refs)

    def take(count):
        head, refs[:count] = refs[:count], []
        return head

    plan_ref, longest_ref, keys_ref, beside_ref = take(4)
    if carried:
        calm_in, norm_in, stack_ref, sums_in, logs_in = take(5)
        far_w = take(1) if fetching else []
        out_refs = take(slots)
        near_w = take(1) if fetching else []
        acc, top, logs_all, out_all = take(4)
        fetches = [pltpu.make_async_copy(one, two, refs[0]) for one, two in zip(far_w, near_w)]
        for copy in fetches:
            copy.start()
    else:
        q_refs = take(slots)
        calm_out, norm_out, stack_ref, sums_out, logs_out = take(5)
        acc, top, q_all, q_sem = refs
    cache, width = keys_ref.shape
    rows = out_refs[0].shape[0] - SIDE if carried else q_refs[0].shape[0]
    heads = out_refs[0].shape[1] // width if carried else q_refs[0].shape[1] // width
    tile = min(ROW_TILE, rows)
    deep = heads * tile
    big = min(BIG_STEP, cache // 2)
    step = min(KEY_TILE, big)
    scale = width ** (-0.5)
    factor = scale * math.log2(math.e)
    table = request_table(plan_ref, requests)

    if carried:
        norm = norm_in[0]
        calm = (norm * longest_ref[0] * (scale * scale) <= CALM * CALM) & (calm_in[0] == 1)
    else:
        copies = [pltpu.make_async_copy(q_ref, q_all.at[slot], q_sem.at[slot]) for slot, q_ref in enumerate(q_refs)]
        for copy in copies:
            copy.start()
        for copy in copies:
            copy.wait()
        norms = jnp.zeros((tile, 1), jnp.float32)
        for slot in range(slots):
            for at in range(0, rows, tile):
                for head in range(heads):
                    part = q_all[slot, at:at + tile, head * width:(head + 1) * width]
                    start = slot * rows * heads + at * heads + head * tile
                    stack_ref[start:start + tile, :] = part
                    wide = part.astype(jnp.float32)
                    norms = jnp.maximum(norms, jnp.sum(wide * wide, axis=1, keepdims=True))
        norm = jnp.max(norms)
        norm_out[0] = norm
        calm = norm * longest_ref[0] * (scale * scale) <= CALM * CALM
        calm_out[0] = calm.astype(jnp.int32)

    def one_tile(index, carry):
        order, at = lax.div(index, rows // tile), lax.rem(index, rows // tile)
        slot = plan_ref[slot_at + order]
        row = plan_ref[row_at + slot] + at * tile
        stack = pl.multiple_of((slot * (rows // tile) + at) * deep, deep)
        first_low, last_low = key_range(table, row)
        first_high, last_high = key_range(table, row + (tile - 1))
        if carried:
            acc[:, :width] = sums_in[pl.ds(stack, deep), :]
            acc[:, width:] = jnp.broadcast_to(logs_in[pl.ds(stack, deep), :][:, :1], (deep, width))
        else:
            acc[...] = jnp.zeros_like(acc)
        own_rows = row + lax.broadcasted_iota(jnp.int32, (tile, 1), 0)
        first, last = key_range(table, own_rows)

        def allowed(key):
            place = key + lax.broadcasted_iota(jnp.int32, (tile, step), 1)
            return (place >= first) & (place <= last)

        def scores(part, left):
            return lax.dot_general(
                stack_ref[pl.ds(stack + part.start, part.size), :],
                keys_ref[pl.ds(left, step), :],
                (((1,), (1,)), ((), ())),
                preferred_element_type=jnp.float32,
            ) * factor

        def add(left, weights):
            return jnp.dot(
                weights.astype(jnp.bfloat16), beside_ref[pl.ds(left, step), :], preferred_element_type=jnp.float32
            )

        def some(key, count):
            return (key + count > first_low) & (key <= last_high)

        def whole(key, count):
            start, _, ahead, row_end, key_end = request_of(table, key)
            low, high = jnp.maximum(row, start), jnp.minimum(row + tile, row_end)
            return (key + count <= key_end) & (low < high) & (low + ahead >= key + count - 1), low, high

        def pour(left, count, low, high):
            total = None
            ahead = scores(pl.ds(0, deep), left)
            for part in range(count // step):
                score = ahead
                if part + 1 < count // step:
                    ahead = scores(pl.ds(0, deep), left + (part + 1) * step)
                term = add(left + part * step, jnp.exp2(score))
                total = term if total is None else total + term
            own = (own_rows >= low) & (own_rows < high)
            for head in range(heads):
                part = slice(head * tile, (head + 1) * tile)
                acc[part, :] += jnp.where(own, total[part, :], 0.0)

        @pl.when(calm)
        def _():
            def turn(at_big, carry):
                left = pl.multiple_of(at_big * big, big)
                key = plan_ref[key_at + at_big * (big // step)]
                live = some(key, big)
                plain, low, high = whole(key, big)

                @pl.when(live & plain)
                def _():
                    pour(left, big, low, high)

                @pl.when(live & jnp.logical_not(plain))
                def _():
                    def small(at_small, carry):
                        inner = pl.multiple_of(left + at_small * step, step)
                        inner_key = key + at_small * step
                        inner_live = some(inner_key, step)
                        inner_plain, inner_low, inner_high = whole(inner_key, step)

                        @pl.when(inner_live & inner_plain)
                        def _():
                            pour(inner, step, inner_low, inner_high)

                        @pl.when(inner_live & jnp.logical_not(inner_plain))
                        def _():
                            mask = allowed(inner_key)
                            weights = jnp.exp2(scores(pl.ds(0, deep), inner))
                            weights = jnp.concatenate([
                                jnp.where(mask, weights[head * tile:(head + 1) * tile, :], 0.0)
                                for head in range(heads)
                            ])
                            acc[...] += add(inner, weights)

                        return carry

                    lax.fori_loop(0, big // step, small, 0)

                return carry

            lax.fori_loop(0, cache // big, turn, 0)
            top[...] = jnp.zeros_like(top)

        @pl.when(jnp.logical_not(calm))
        def _():
            if carried:
                before = logs_in[pl.ds(stack, deep), :]
                top[...] = jnp.broadcast_to(
                    jnp.where(before[:, :1] > 0.0, before[:, width // 2:width // 2 + 1], NEG), top.shape
                )
            else:
                top[...] = jnp.full_like(top, NEG)

            def turn(at_key, carry):
                left = pl.multiple_of(at_key * step, step)
                key = plan_ref[key_at + at_key]

                @pl.when(some(key, step))
                def _():
                    mask = allowed(key)

                    def one_head(head, carry):
                        part = pl.ds(pl.multiple_of(head * tile, tile), tile)
                        score = jnp.where(mask, scores(part, left), NEG)
                        old = top[part, :]
                        new = jnp.maximum(old, jnp.max(score, axis=1, keepdims=True))
                        weights = jnp.where(mask, jnp.exp2(score - new[:, :1]), 0.0)
                        shrink = jnp.exp2(old - new)
                        acc[part, :width] = acc[part, :width] * shrink
                        acc[part, width:] = acc[part, width:] * shrink
                        acc[part, :] += add(left, weights)
                        top[part, :] = new
                        return carry

                    lax.fori_loop(0, heads, one_head, 0)

                return carry

            lax.fori_loop(0, cache // step, turn, 0)

        if not carried:
            sums_out[pl.ds(stack, deep), :] = acc[:, :width]
            lane = lax.broadcasted_iota(jnp.int32, (deep, width), 1)
            logs_out[pl.ds(stack, deep), :] = jnp.where(lane < width // 2, acc[:, width:], top[...])
            return carry
        lane = lax.broadcasted_iota(jnp.int32, (tile, LANES), 1)
        logs = jnp.zeros((tile, LANES), jnp.float32)
        here = pl.multiple_of(index * tile, tile)
        for head in range(heads):
            part = slice(head * tile, (head + 1) * tile)
            total = acc[part, width:]
            live = total > 0.0
            safe = jnp.where(live, total, 1.0)
            out_all[pl.ds(here, tile), head * width:(head + 1) * width] = (acc[part, :width] / safe).astype(jnp.bfloat16)
            logs = jnp.where(lax.rem(lane, heads) == head, jnp.where(live, top[part, :] + jnp.log2(safe), NEG), logs)
        high = logs.astype(jnp.bfloat16).astype(jnp.float32)
        middle = (logs - high).astype(jnp.bfloat16).astype(jnp.float32)
        logs_all[pl.ds(here, tile), :] = jnp.where(
            lane < heads, high, jnp.where(lane < 2 * heads, middle, logs - high - middle)
        )
        return carry

    lax.fori_loop(0, slots * (rows // tile), one_tile, 0)
    if carried:
        for slot, out_ref in enumerate(out_refs):
            out_ref[:rows, :] = out_all[slot * rows:(slot + 1) * rows, :]
            out_ref[rows:, :] = jnp.zeros((SIDE, heads * width), jnp.bfloat16)
            for at in range(0, rows, LANES):
                turned = logs_all[slot * rows + at:slot * rows + at + LANES, :].T
                out_ref[rows:, at:at + LANES] = turned[:SIDE, :].astype(jnp.bfloat16)
        for copy in fetches:
            copy.wait()


def attend(places, plan, cache_side, queries=None, before=None, slots=0, heads=0, fetch=None):
    keys, beside, longest = cache_side
    cache, width = keys.shape
    carried = before is not None
    if not carried:
        slots, rows = len(queries), queries[0].shape[0]
        heads = queries[0].shape[1] // width
    else:
        rows = before[2].shape[0] // heads // places["blocks"]
    tile = min(ROW_TILE, rows)
    kernel = functools.partial(
        attend_kernel, slots, places["requests"], places["rows"], places["keys"], places["slots"], carried,
        fetch is not None,
    )
    scratch = [
        pltpu.VMEM((heads * tile, 2 * width), jnp.float32),
        pltpu.VMEM((heads * tile, width), jnp.float32),
    ]
    common = dict(
        compiler_params=pltpu.CompilerParams(vmem_limit_bytes=20 * MIB),
        cost_estimate=pl.CostEstimate(
            flops=slots * rows * heads * cache * width * 4, bytes_accessed=4 * MIB, transcendentals=0
        ),
    )
    fetched = [] if fetch is None else [pltpu.with_memory_space_constraint(fetch, pltpu.HBM)]
    if carried:
        return pl.pallas_call(
            kernel,
            out_shape=(jax.ShapeDtypeStruct((rows + SIDE, heads * width), jnp.bfloat16),) * slots
            + tuple(pltpu.VMEM(array.shape, array.dtype) for array in fetched),
            in_specs=[SMEM, SMEM, VMEM, VMEM, SMEM, SMEM, VMEM, VMEM, VMEM] + [HBM] * len(fetched),
            out_specs=(VMEM,) * (slots + len(fetched)),
            scratch_shapes=scratch + [
                pltpu.VMEM((slots * rows, LANES), jnp.float32),
                pltpu.VMEM((slots * rows, heads * width), jnp.bfloat16),
            ] + [pltpu.SemaphoreType.DMA] * len(fetched),
            name="attend_last",
            **common,
        )(plan, longest, keys, beside, *before, *fetched)
    stacked = slots * rows * heads
    return pl.pallas_call(
        kernel,
        out_shape=(
            jax.ShapeDtypeStruct((1,), jnp.int32),
            jax.ShapeDtypeStruct((1,), jnp.float32),
            pltpu.VMEM((stacked, width), jnp.bfloat16),
            pltpu.VMEM((stacked, width), jnp.float32),
            pltpu.VMEM((stacked, width), jnp.float32),
        ),
        in_specs=[SMEM, SMEM, VMEM, VMEM] + [HBM] * slots,
        out_specs=(SMEM, SMEM, VMEM, VMEM, VMEM),
        scratch_shapes=scratch + [
            pltpu.VMEM((slots, rows, heads * width), jnp.bfloat16),
            pltpu.SemaphoreType.DMA((slots,)),
        ],
        name="attend_first",
        **common,
    )(plan, longest, keys, beside, *queries)


def merge_kernel(heads, there_at, plan_ref, *refs):
    parts, out_ref = refs[:-1], refs[-1]
    rows = out_ref.shape[0]
    width = out_ref.shape[1] // heads
    logs = [
        jnp.where(plan_ref[there_at + at] == 1, part[rows:, :rows].astype(jnp.float32), NEG) for at, part in enumerate(parts)
    ]
    spare = LANES - SIDE * len(parts)
    if spare:
        logs.append(jnp.full((spare, rows), NEG, jnp.float32))
    terms = jnp.concatenate(logs, axis=0).T
    total = terms + pltpu.roll(terms, LANES - heads, 1) + pltpu.roll(terms, LANES - 2 * heads, 1)
    lane = lax.broadcasted_iota(jnp.int32, (rows, LANES), 1)
    total = jnp.where((lax.rem(lane, SIDE) < heads) & (lane < SIDE * len(parts)), total, NEG)
    biggest = total
    for shift in (16, 32, 64):
        biggest = jnp.maximum(biggest, pltpu.roll(biggest, shift, 1))
    share = jnp.exp2(total - biggest)
    weight = share
    for shift in (16, 32, 64):
        weight = weight + pltpu.roll(weight, shift, 1)
    share = share / weight
    for head in range(heads):
        own = slice(head * width, (head + 1) * width)
        mixed = jnp.zeros((rows, width), jnp.float32)
        for at, part in enumerate(parts):
            lane_at = at * SIDE + head
            mixed = mixed + part[:rows, own].astype(jnp.float32) * share[:, lane_at:lane_at + 1]
        out_ref[:, own] = mixed.astype(out_ref.dtype)


def merge(places, plan, parts, heads):
    rows = parts[0].shape[0] - SIDE
    return pl.pallas_call(
        functools.partial(merge_kernel, heads, places["there"]),
        out_shape=jax.ShapeDtypeStruct((rows, parts[0].shape[1]), jnp.bfloat16),
        in_specs=[SMEM] + [VMEM] * len(parts),
        out_specs=VMEM,
        compiler_params=pltpu.CompilerParams(vmem_limit_bytes=12 * MIB),
        name="merge",
    )(plan, *parts)


def project_kernel(pieces, from_at, plan_ref, *refs):
    w_ref, out_ref, whole = refs[pieces:]
    deep = refs[0].shape[1]
    block = out_ref.shape[1]

    @pl.when(pl.program_id(0) == 0)
    def _():
        for at, piece in enumerate(refs[:pieces]):
            whole[:, pl.ds(pl.multiple_of(plan_ref[from_at + at] * deep, deep), deep)] = piece[...]

    left = pl.multiple_of(pl.program_id(0) * block, block)
    out_ref[...] = jnp.dot(
        whole[...], w_ref[:, pl.ds(left, block)], preferred_element_type=jnp.float32
    ).astype(out_ref.dtype)


def project(places, plan, pieces, w_out):
    rows, deep = pieces[0].shape
    depth, wide = w_out.shape
    block = min(1024, wide)
    return pl.pallas_call(
        functools.partial(project_kernel, len(pieces), places["from"]),
        out_shape=pltpu.HBM((rows, wide), jnp.bfloat16),
        grid=(wide // block,),
        in_specs=[SMEM] + [VMEM] * (len(pieces) + 1),
        out_specs=pl.BlockSpec((rows, block), lambda at: (0, at)),
        scratch_shapes=[pltpu.VMEM((rows, depth), jnp.bfloat16)],
        compiler_params=pltpu.CompilerParams(vmem_limit_bytes=20 * MIB),
        cost_estimate=pl.CostEstimate(
            flops=2 * rows * depth * wide, bytes_accessed=2 * depth * wide, transcendentals=0
        ),
        name="project",
    )(plan, *pieces, w_out)


def shift_pairs(count, stride, steps):
    groups = count // stride
    return [
        (group * stride + member, (group + steps) % groups * stride + member)
        for group in range(groups)
        for member in range(stride)
    ]


def swap_pairs(count):
    return [(at, at ^ 1) for at in range(count)]


def is_far(groups, one, two):
    low, high = min(one, two), max(one, two)
    return low < groups // 2 and high >= groups - max(1, groups // 4)


def move(value, groups, steps, far):
    pairs = [
        (source, target)
        for source, target in shift_pairs(2 * groups, 2, steps)
        if far or not is_far(groups, source // 2, target // 2)
    ]
    return lax.ppermute(value, "ctx", pairs) if pairs else jnp.zeros_like(value)


def plan_kernel(shape, places, new_ref, prior_ref, at_ref, plan_ref, far_ref):
    groups, chips, rows, cache, step, calls = shape
    device, place = at_ref[0], at_ref[1]
    group, side, chip, core = lax.div(device, 2), lax.rem(device, 2), lax.div(place, 2), lax.rem(place, 2)
    requests = new_ref.shape[0]
    for request in range(requests):
        plan_ref[places["new"] + request] = new_ref[request]
        plan_ref[places["prior"] + request] = prior_ref[request]
    table = request_table(plan_ref, requests)
    spans = [
        (key_range(table, jnp.int32(2 * rows * at))[0], key_range(table, jnp.int32(2 * rows * (at + 1) - 1))[1])
        for at in range(groups)
    ]
    needed = jnp.int32(0)
    for source in range(groups):
        for target in range(groups):
            if is_far(groups, source, target):
                first, last = spans[source]
                meet = (first < 2 * cache * (target + 1)) & (last >= 2 * cache * target)
                needed = jnp.where(meet, 1, needed)
    far_ref[0] = needed
    for steps in range(groups):
        plan_ref[places["rows"] + steps] = (lax.rem(group + (groups - steps), groups) * 2 + side) * rows
        there = jnp.int32(1)
        for at in range(groups):
            if is_far(groups, (at + steps) % groups, at):
                there = jnp.where(group == at, needed, there)
        plan_ref[places["there"] + steps] = there
    count = cache // step
    other = (device + 1 - 2 * side) * cache
    for at in range(count):
        plan_ref[places["keys"] + at] = device * cache + at * step
        half = core if at < count // 2 else 1 - core
        plan_ref[places["others"] + at] = other + half * (cache // 2) + (at % (count // 2)) * step
    for at, slot in enumerate(calls):
        plan_ref[places["slots"] + at] = jnp.int32(slot)
    for at in range(2 * chips):
        own = core if at < chips else 1 - core
        plan_ref[places["from"] + at] = lax.rem(chip + (chips - at % chips), chips) * 2 + own


def make_plan(shape, new_counts, prior_lengths, at):
    groups, chips, _, cache, step, _ = shape
    requests = new_counts.shape[0]
    sizes = dict(
        new=requests,
        prior=requests,
        rows=groups,
        keys=cache // step,
        others=cache // step,
        slots=groups,
        there=groups,
    )
    sizes["from"] = 2 * chips
    places, total = dict(requests=requests, blocks=groups), 0
    for name, size in sizes.items():
        places[name] = total
        total += size
    plan, far = pl.pallas_call(
        functools.partial(plan_kernel, shape, dict(places)),
        out_shape=(jax.ShapeDtypeStruct((total,), jnp.int32), jax.ShapeDtypeStruct((1,), jnp.int32)),
        in_specs=[SMEM] * 3,
        out_specs=(SMEM, SMEM),
        name="plan",
    )(new_counts, prior_lengths, at)
    return places, plan, far


def body(queries, keys, values, w_out, new_counts, prior_lengths):
    ctx_count, head_count = lax.axis_size("ctx"), lax.axis_size("head")
    rows = queries.shape[0]
    cache = keys.shape[0]
    groups, chips = ctx_count // 2, head_count // 2
    order = list(range(1, groups)) + [0]
    at = jnp.stack([lax.axis_index("ctx"), lax.axis_index("head")]).astype(jnp.int32)
    shape = (groups, chips, rows, cache, min(KEY_TILE, cache // 2), order)
    places, plan, far = make_plan(shape, new_counts, prior_lengths, at)
    arrays = (queries, keys, values, w_out, plan)
    return lax.cond(
        far[0] == 1,
        functools.partial(attend_and_project, places, True),
        functools.partial(attend_and_project, places, False),
        *arrays,
    )


def attend_and_project(places, far, queries, keys, values, w_out, plan):
    places = dict(places)
    ctx_count, head_count = lax.axis_size("ctx"), lax.axis_size("head")
    cache, width = keys.shape
    heads = queries.shape[1] // width
    groups, chips, half = ctx_count // 2, head_count // 2, cache // 2
    core = lax.axis_index("head") % 2
    every = list(range(groups))

    blocks = [move(queries, groups, steps, far) for steps in every[1:]]

    mine = [lax.dynamic_slice_in_dim(array, core * half, half, axis=0) for array in (keys, values)]
    got = lax.ppermute(jnp.concatenate(mine, axis=1), "ctx", swap_pairs(ctx_count))
    own_side = prepare(keys, values, False)
    got, _ = lax.optimization_barrier((got, blocks))
    rest = lax.ppermute(got, "head", swap_pairs(head_count))
    sums = attend(places, plan, own_side, queries=[queries] + blocks)
    other_side = prepare(got, rest, True)
    places["keys"] = places["others"]
    away = attend(places, plan, other_side, before=sums, slots=groups - 1, heads=heads)
    back = [move(part, groups, groups - slot, far) for slot, part in zip(every[1:], away)]
    places["slots"] += groups - 1
    own, near_w = attend(places, plan, other_side, before=sums, slots=1, heads=heads, fetch=w_out)
    attended = merge(places, plan, [own] + back, heads)

    near = [attended] + [
        lax.ppermute(attended, "head", shift_pairs(head_count, 2, steps)) for steps in range(1, chips)
    ]
    far_core = [lax.ppermute(piece, "head", swap_pairs(head_count)) for piece in near]
    return project(places, plan, near + far_core, near_w)


def solution(mesh):
    return jax.shard_map(
        body,
        mesh=mesh,
        in_specs=(P("ctx", "head"), P("ctx", None), P("ctx", None), P(None, "head"), P(), P()),
        out_specs=P("ctx", "head"),
        check_vma=False,
    )
```

```python
import functools
import math

import jax
import jax.numpy as jnp
from jax import lax
from jax.experimental import pallas as pl
from jax.experimental.pallas import tpu as pltpu
from jax.sharding import PartitionSpec as P

NEG = -1e30
CALM = 60.0
KEY_TILE = 512
FEW_ROWS = 64
SIDE = 16
LANES = 128
MIB = 1024 * 1024
SMEM = pl.BlockSpec(memory_space=pltpu.SMEM)
VMEM = pl.BlockSpec(memory_space=pltpu.VMEM)
HBM = pl.BlockSpec(memory_space=pltpu.HBM)


def prepare_kernel(keys_ref, values_ref, beside_ref, longest_ref):
    cache, width = keys_ref.shape
    step = min(KEY_TILE, cache)

    def turn(at, longest):
        here = pl.ds(pl.multiple_of(at * step, step), step)
        beside_ref[here, :width] = values_ref[here, :]
        beside_ref[here, width:] = jnp.ones((step, width), jnp.bfloat16)
        keys = keys_ref[here, :].astype(jnp.float32)
        return jnp.maximum(longest, jnp.sum(keys * keys, axis=1, keepdims=True))

    longest_ref[0] = jnp.max(lax.fori_loop(0, cache // step, turn, jnp.zeros((step, 1), jnp.float32)))


def prepare(keys, values):
    cache, width = keys.shape
    return pl.pallas_call(
        prepare_kernel,
        out_shape=(pltpu.VMEM((cache, 2 * width), jnp.bfloat16), jax.ShapeDtypeStruct((1,), jnp.float32)),
        in_specs=[VMEM] * 2,
        out_specs=(VMEM, SMEM),
        compiler_params=pltpu.CompilerParams(vmem_limit_bytes=8 * MIB),
        name="prepare",
    )(keys, values)


def stack_kernel(slots, group_at, width, plan_ref, *refs):
    q_refs, (stack_ref, longest_ref, q_all, sems) = refs[:slots], refs[slots:]
    rows = q_refs[0].shape[0]
    heads = q_refs[0].shape[1] // width
    local = slots * rows
    copies = [pltpu.make_async_copy(q_ref, q_all.at[slot], sems.at[slot]) for slot, q_ref in enumerate(q_refs)]
    for copy in copies:
        copy.start()
    longest = jnp.zeros((rows, 1), jnp.float32)
    for slot, copy in enumerate(copies):
        copy.wait()
        start = plan_ref[group_at + slot] * rows
        for head in range(heads):
            part = q_all[slot, :, head * width:(head + 1) * width]
            stack_ref[pl.ds(pl.multiple_of(head * local + start, rows), rows), :] = part
            wide = part.astype(jnp.float32)
            longest = jnp.maximum(longest, jnp.sum(wide * wide, axis=1, keepdims=True))
    longest_ref[0] = jnp.max(longest)


def stack_queries(places, plan, queries, width):
    slots, (rows, wide) = len(queries), queries[0].shape
    return pl.pallas_call(
        functools.partial(stack_kernel, slots, places["groups"], width),
        out_shape=(
            pltpu.VMEM((slots * rows * (wide // width), width), jnp.bfloat16),
            jax.ShapeDtypeStruct((1,), jnp.float32),
        ),
        in_specs=[SMEM] + [HBM] * slots,
        out_specs=(VMEM, SMEM),
        scratch_shapes=[pltpu.VMEM((slots, rows, wide), jnp.bfloat16), pltpu.SemaphoreType.DMA((slots,))],
        compiler_params=pltpu.CompilerParams(vmem_limit_bytes=8 * MIB),
        name="stack",
    )(plan, *queries)


def request_table(new_ref, prior_ref):
    table = []
    row, key = jnp.int32(0), jnp.int32(0)
    for request in range(new_ref.shape[0]):
        new, prior = new_ref[request], prior_ref[request]
        table.append((row, key, key + prior - row, row + new, key + new + prior))
        row, key = row + new, key + new + prior
    return table


def key_range(table, row):
    first, shift = table[0][1], table[0][2]
    for start, key, ahead, _, _ in table[1:]:
        own = row >= start
        first = jnp.where(own, key, first)
        shift = jnp.where(own, ahead, shift)
    return first, row + shift


def attend_kernel(shape, places, *refs):
    groups, rows, heads, requests = shape
    plan_ref, key_norm_ref, query_norm_ref, stack_ref, keys_ref, beside_ref, got_ref, rest_ref, far_w = refs[:9]
    out_refs, near_w = refs[9:9 + groups], refs[9 + groups]
    keys_all, beside_all, sums, tops, chunk_q, chunk_sum, chunk_top, sem = refs[10 + groups:]
    cache, width = keys_ref.shape
    local = groups * rows
    step = min(KEY_TILE, cache // 2)
    scale = width ** (-0.5)
    factor = scale * math.log2(math.e)
    fetch = pltpu.make_async_copy(far_w, near_w, sem)
    fetch.start()

    keys_all[:cache, :] = keys_ref[...]
    beside_all[:cache, :] = beside_ref[...]
    longest = jnp.zeros((step, 1), jnp.float32)
    done = cache
    for part_ref in (got_ref, rest_ref):

        def turn(at, longest, part_ref=part_ref, done=done):
            here = pl.ds(pl.multiple_of(at * step, step), step)
            there = pl.ds(pl.multiple_of(done + at * step, step), step)
            keys = part_ref[here, :width]
            keys_all[there, :] = keys
            beside_all[there, :width] = part_ref[here, width:]
            beside_all[there, width:] = jnp.ones((step, width), jnp.bfloat16)
            wide = keys.astype(jnp.float32)
            return jnp.maximum(longest, jnp.sum(wide * wide, axis=1, keepdims=True))

        longest = lax.fori_loop(0, part_ref.shape[0] // step, turn, longest)
        done += part_ref.shape[0]
    key_norm = jnp.maximum(jnp.max(longest), key_norm_ref[0])
    calm = key_norm * query_norm_ref[0] * (scale * scale) <= CALM * CALM
    side = plan_ref[places["side"]]

    def clear(at, carry):
        sums[pl.ds(pl.multiple_of(at * rows, rows), rows), :] = jnp.zeros((rows, 2 * width), jnp.float32)
        return carry

    lax.fori_loop(0, heads * groups, clear, 0)

    def global_row(place):
        whole = place + side * rows
        for group in range(1, groups):
            whole = whole + jnp.where(place >= group * rows, rows, 0)
        return whole

    def one_chunk(count, online, request, begin, end, start):
        first_key = plan_ref[places["first_key"] + request]
        ahead = plan_ref[places["ahead"] + request]
        start = pl.multiple_of(start, SIDE)
        low_key, high_key = global_row(begin) + ahead, global_row(end - 1) + ahead
        total = heads * count
        for head in range(heads):
            chunk_q[head * count:(head + 1) * count, :] = stack_ref[
                pl.ds(pl.multiple_of(head * local + start, SIDE), count), :
            ]
        chunk_sum[:total, :] = jnp.zeros((total, 2 * width), jnp.float32)
        if online:
            chunk_top[:total, :] = jnp.full((total, width), NEG, jnp.float32)
        place = start + lax.broadcasted_iota(jnp.int32, (count, 1), 0)
        last = global_row(place) + ahead

        def scores(part, left):
            return lax.dot_general(
                chunk_q[part, :], keys_all[pl.ds(left, step), :], (((1,), (1,)), ((), ())),
                preferred_element_type=jnp.float32,
            ) * factor

        def add(left, weights):
            return jnp.dot(
                weights.astype(jnp.bfloat16), beside_all[pl.ds(left, step), :], preferred_element_type=jnp.float32
            )

        def one_step(left, key):
            def allowed():
                index = key + lax.broadcasted_iota(jnp.int32, (count, step), 1)
                return (index >= first_key) & (index <= last)

            if online:
                mask = allowed()

                def one_head(head, carry):
                    part = pl.ds(pl.multiple_of(head * count, count), count)
                    score = jnp.where(mask, scores(part, left), NEG)
                    old = chunk_top[part, :]
                    new = jnp.maximum(old, jnp.ceil(jnp.max(score, axis=1, keepdims=True)))
                    weights = jnp.where(mask, jnp.exp2(score - new[:, :1]), 0.0)
                    shrink = jnp.exp2(old - new)
                    chunk_sum[part, :width] = chunk_sum[part, :width] * shrink
                    chunk_sum[part, width:] = chunk_sum[part, width:] * shrink
                    chunk_sum[part, :] += add(left, weights)
                    chunk_top[part, :] = new
                    return carry

                lax.fori_loop(0, heads, one_head, 0)
                return

            plain = (key >= first_key) & (key + step - 1 <= low_key)

            @pl.when(plain)
            def _():
                chunk_sum[:total, :] += add(left, jnp.exp2(scores(pl.ds(0, total), left)))

            @pl.when(jnp.logical_not(plain))
            def _():
                mask = allowed()
                weights = jnp.exp2(scores(pl.ds(0, total), left))
                weights = jnp.concatenate([
                    jnp.where(mask, weights[head * count:(head + 1) * count, :], 0.0) for head in range(heads)
                ])
                chunk_sum[:total, :] += add(left, weights)

        def one_part(part, carry):
            left, key, steps = (plan_ref[places[name] + part] for name in ("lefts", "keys", "steps"))
            low = jnp.clip(lax.div(first_key - key, step), 0, steps)
            high = jnp.clip(lax.div(high_key - key + step, step), 0, steps)

            def turn(at, carry):
                one_step(pl.multiple_of(left + at * step, step), key + at * step)
                return carry

            lax.fori_loop(low, high, turn, 0)
            return carry

        lax.fori_loop(0, 3, one_part, 0)
        own = (place >= begin) & (place < end)
        for head in range(heads):
            here = pl.ds(pl.multiple_of(head * local + start, SIDE), count)
            part = slice(head * count, (head + 1) * count)
            sums[here, :] += jnp.where(own, chunk_sum[part, :], 0.0)
            if online:
                tops[here, :] = jnp.where(own, chunk_top[part, :], tops[here, :])

    def all_chunks(count, online, request, begin, end):
        aligned = lax.div(begin, SIDE) * SIDE

        def turn(at, carry):
            from_row = aligned + at * count
            one_chunk(
                count,
                online,
                request,
                jnp.maximum(begin, from_row),
                jnp.minimum(end, from_row + count),
                jnp.minimum(from_row, local - count),
            )
            return carry

        lax.fori_loop(0, lax.div(end - aligned + (count - 1), count), turn, 0)

    many, few = min(2 * rows + SIDE, local), min(FEW_ROWS, local)

    def one_request(request, carry):
        begin, end = plan_ref[places["begin"] + request], plan_ref[places["end"] + request]
        large = end - lax.div(begin, SIDE) * SIDE > 2 * few

        @pl.when((end > begin) & calm & large)
        def _():
            all_chunks(many, False, request, begin, end)

        @pl.when((end > begin) & calm & jnp.logical_not(large))
        def _():
            all_chunks(few, False, request, begin, end)

        @pl.when((end > begin) & jnp.logical_not(calm))
        def _():
            all_chunks(few, True, request, begin, end)

        return carry

    lax.fori_loop(0, requests, one_request, 0)

    lane = lax.broadcasted_iota(jnp.int32, (LANES, LANES), 1)
    for slot, out_ref in enumerate(out_refs):
        start = plan_ref[places["groups"] + slot] * rows
        out_ref[rows:, :] = jnp.zeros((SIDE, heads * width), jnp.bfloat16)
        for at in range(0, rows, LANES):
            terms = jnp.zeros((LANES, LANES), jnp.float32)
            for head in range(heads):
                here = pl.ds(pl.multiple_of(head * local + start + at, LANES), LANES)
                out_ref[at:at + LANES, head * width:(head + 1) * width] = sums[here, :width].astype(jnp.bfloat16)
                weight = sums[here, width:]
                top = jnp.where(weight > 0.0, jnp.where(calm, 0.0, tops[here, :]), NEG)
                for term, value in enumerate((weight, top)):
                    high = value.astype(jnp.bfloat16).astype(jnp.float32)
                    terms = jnp.where(lane == 2 * term * heads + head, high, terms)
                    terms = jnp.where(lane == (2 * term + 1) * heads + head, value - high, terms)
            out_ref[rows:, at:at + LANES] = terms.T[:SIDE, :].astype(jnp.bfloat16)
    fetch.wait()


def attend(places, plan, norms, stack, sides, w_out, shape):
    groups, rows, heads, _ = shape
    keys, beside, got, rest = sides
    cache, width = keys.shape
    local = groups * rows
    most = heads * min(2 * rows + SIDE, local)
    return pl.pallas_call(
        functools.partial(attend_kernel, shape, dict(places)),
        out_shape=(jax.ShapeDtypeStruct((rows + SIDE, heads * width), jnp.bfloat16),) * groups
        + (pltpu.VMEM(w_out.shape, w_out.dtype),),
        in_specs=[SMEM] * 3 + [VMEM] * 5 + [HBM],
        out_specs=(VMEM,) * (groups + 1),
        scratch_shapes=[
            pltpu.VMEM((2 * cache, width), jnp.bfloat16),
            pltpu.VMEM((2 * cache, 2 * width), jnp.bfloat16),
            pltpu.VMEM((heads * local, 2 * width), jnp.float32),
            pltpu.VMEM((heads * local, width), jnp.float32),
            pltpu.VMEM((most, width), jnp.bfloat16),
            pltpu.VMEM((most, 2 * width), jnp.float32),
            pltpu.VMEM((heads * min(FEW_ROWS, local), width), jnp.float32),
            pltpu.SemaphoreType.DMA,
        ],
        compiler_params=pltpu.CompilerParams(vmem_limit_bytes=36 * MIB),
        cost_estimate=pl.CostEstimate(
            flops=local * heads * cache * width * 4, bytes_accessed=24 * MIB, transcendentals=0
        ),
        name="attend",
    )(plan, *norms, stack, keys, beside, got, rest, pltpu.with_memory_space_constraint(w_out, pltpu.HBM))


def merge_kernel(heads, there_at, plan_ref, *refs):
    parts, out_ref = refs[:-1], refs[-1]
    rows = out_ref.shape[0]
    width = out_ref.shape[1] // heads
    logs = [
        jnp.where(plan_ref[there_at + at] == 1, part[rows:, :rows].astype(jnp.float32), 0.0) for at, part in enumerate(parts)
    ]
    spare = LANES - SIDE * len(parts)
    if spare:
        logs.append(jnp.zeros((spare, rows), jnp.float32))
    terms = jnp.concatenate(logs, axis=0).T
    total = terms + pltpu.roll(terms, LANES - heads, 1)
    top = pltpu.roll(terms, LANES - 2 * heads, 1) + pltpu.roll(terms, LANES - 3 * heads, 1)
    lane = lax.broadcasted_iota(jnp.int32, (rows, LANES), 1)
    used = (lax.rem(lane, SIDE) < heads) & (lane < SIDE * len(parts)) & (total > 0.0)
    top = jnp.where(used, top, NEG)
    biggest = top
    for shift in (16, 32, 64):
        biggest = jnp.maximum(biggest, pltpu.roll(biggest, shift, 1))
    share = jnp.where(used, jnp.exp2(top - biggest), 0.0)
    weight = share * jnp.where(used, total, 0.0)
    for shift in (16, 32, 64):
        weight = weight + pltpu.roll(weight, shift, 1)
    share = share / weight
    for head in range(heads):
        own = slice(head * width, (head + 1) * width)
        mixed = jnp.zeros((rows, width), jnp.float32)
        for at, part in enumerate(parts):
            lane_at = at * SIDE + head
            mixed = mixed + part[:rows, own].astype(jnp.float32) * share[:, lane_at:lane_at + 1]
        out_ref[:, own] = mixed.astype(out_ref.dtype)


def merge(places, plan, parts, heads):
    rows = parts[0].shape[0] - SIDE
    return pl.pallas_call(
        functools.partial(merge_kernel, heads, places["there"]),
        out_shape=jax.ShapeDtypeStruct((rows, parts[0].shape[1]), jnp.bfloat16),
        in_specs=[SMEM] + [VMEM] * len(parts),
        out_specs=VMEM,
        compiler_params=pltpu.CompilerParams(vmem_limit_bytes=12 * MIB),
        name="merge",
    )(plan, *parts)


def project_kernel(pieces, from_at, plan_ref, *refs):
    w_ref, out_ref, whole = refs[pieces:]
    deep = refs[0].shape[1]
    block = out_ref.shape[1]

    @pl.when(pl.program_id(0) == 0)
    def _():
        for at, piece in enumerate(refs[:pieces]):
            whole[:, pl.ds(pl.multiple_of(plan_ref[from_at + at] * deep, deep), deep)] = piece[...]

    left = pl.multiple_of(pl.program_id(0) * block, block)
    out_ref[...] = jnp.dot(
        whole[...], w_ref[:, pl.ds(left, block)], preferred_element_type=jnp.float32
    ).astype(out_ref.dtype)


def project(places, plan, pieces, w_out):
    rows, deep = pieces[0].shape
    depth, wide = w_out.shape
    block = min(1024, wide)
    return pl.pallas_call(
        functools.partial(project_kernel, len(pieces), places["from"]),
        out_shape=pltpu.HBM((rows, wide), jnp.bfloat16),
        grid=(wide // block,),
        in_specs=[SMEM] + [VMEM] * (len(pieces) + 1),
        out_specs=pl.BlockSpec((rows, block), lambda at: (0, at)),
        scratch_shapes=[pltpu.VMEM((rows, depth), jnp.bfloat16)],
        compiler_params=pltpu.CompilerParams(vmem_limit_bytes=20 * MIB),
        cost_estimate=pl.CostEstimate(
            flops=2 * rows * depth * wide, bytes_accessed=2 * depth * wide, transcendentals=0
        ),
        name="project",
    )(plan, *pieces, w_out)


def shift_pairs(count, stride, steps):
    groups = count // stride
    return [
        (group * stride + member, (group + steps) % groups * stride + member)
        for group in range(groups)
        for member in range(stride)
    ]


def swap_pairs(count):
    return [(at, at ^ 1) for at in range(count)]


def is_far(groups, one, two):
    low, high = min(one, two), max(one, two)
    return low < groups // 2 and high >= groups - max(1, groups // 4)


def move(value, groups, steps, far):
    pairs = [
        (source, target)
        for source, target in shift_pairs(2 * groups, 2, steps)
        if far or not is_far(groups, source // 2, target // 2)
    ]
    return lax.ppermute(value, "ctx", pairs) if pairs else jnp.zeros_like(value)


def plan_kernel(shape, places, new_ref, prior_ref, at_ref, plan_ref, far_ref):
    groups, chips, rows, cache, step = shape
    device, place = at_ref[0], at_ref[1]
    group, side, chip, core = lax.div(device, 2), lax.rem(device, 2), lax.div(place, 2), lax.rem(place, 2)
    table = request_table(new_ref, prior_ref)

    def rows_before(row):
        block = lax.div(row, rows)
        odd, inside = lax.rem(block, 2), lax.rem(row, rows)
        return lax.div(block, 2) * rows + jnp.where(odd == side, inside, jnp.where(odd == 1, rows, 0))

    for request, (row, key, ahead, row_end, _) in enumerate(table):
        plan_ref[places["first_key"] + request] = key
        plan_ref[places["ahead"] + request] = ahead
        plan_ref[places["begin"] + request] = rows_before(row)
        plan_ref[places["end"] + request] = rows_before(row_end)
    spans = [
        (key_range(table, jnp.int32(2 * rows * at))[0], key_range(table, jnp.int32(2 * rows * (at + 1) - 1))[1])
        for at in range(groups)
    ]
    needed = jnp.int32(0)
    for source in range(groups):
        for target in range(groups):
            if is_far(groups, source, target):
                first, last = spans[source]
                meet = (first < 2 * cache * (target + 1)) & (last >= 2 * cache * target)
                needed = jnp.where(meet, 1, needed)
    far_ref[0] = needed
    plan_ref[places["side"]] = side
    for steps in range(groups):
        plan_ref[places["groups"] + steps] = lax.rem(group + (groups - steps), groups)
        there = jnp.int32(1)
        for at in range(groups):
            if is_far(groups, (at + steps) % groups, at):
                there = jnp.where(group == at, needed, there)
        plan_ref[places["there"] + steps] = there
    other = (device + 1 - 2 * side) * cache
    half = cache // 2
    stretches = [(0, device * cache, cache), (cache, other + core * half, half), (cache + half, other + (1 - core) * half, half)]
    for part, (left, key, count) in enumerate(stretches):
        plan_ref[places["lefts"] + part] = jnp.int32(left)
        plan_ref[places["keys"] + part] = key
        plan_ref[places["steps"] + part] = jnp.int32(count // step)
    for at in range(2 * chips):
        own = core if at < chips else 1 - core
        plan_ref[places["from"] + at] = lax.rem(chip + (chips - at % chips), chips) * 2 + own


def make_plan(shape, new_counts, prior_lengths, at):
    groups, chips = shape[:2]
    requests = new_counts.shape[0]
    sizes = dict(first_key=requests, ahead=requests, begin=requests, end=requests, side=1)
    sizes.update(groups=groups, there=groups, lefts=3, keys=3, steps=3)
    sizes["from"] = 2 * chips
    places, total = {}, 0
    for name, size in sizes.items():
        places[name] = total
        total += size
    plan, far = pl.pallas_call(
        functools.partial(plan_kernel, shape, dict(places)),
        out_shape=(jax.ShapeDtypeStruct((total,), jnp.int32), jax.ShapeDtypeStruct((1,), jnp.int32)),
        in_specs=[SMEM] * 3,
        out_specs=(SMEM, SMEM),
        name="plan",
    )(new_counts, prior_lengths, at)
    return places, plan, far


def body(queries, keys, values, w_out, new_counts, prior_lengths):
    ctx_count, head_count = lax.axis_size("ctx"), lax.axis_size("head")
    rows = queries.shape[0]
    cache = keys.shape[0]
    groups, chips = ctx_count // 2, head_count // 2
    at = jnp.stack([lax.axis_index("ctx"), lax.axis_index("head")]).astype(jnp.int32)
    shape = (groups, chips, rows, cache, min(KEY_TILE, cache // 2))
    places, plan, far = make_plan(shape, new_counts, prior_lengths, at)
    requests = new_counts.shape[0]
    return lax.cond(
        far[0] == 1,
        functools.partial(attend_and_project, places, requests, True),
        functools.partial(attend_and_project, places, requests, False),
        *(queries, keys, values, w_out, plan),
    )


def attend_and_project(places, requests, far, queries, keys, values, w_out, plan):
    ctx_count, head_count = lax.axis_size("ctx"), lax.axis_size("head")
    rows = queries.shape[0]
    cache, width = keys.shape
    heads = queries.shape[1] // width
    groups, chips, half = ctx_count // 2, head_count // 2, cache // 2
    core = lax.axis_index("head") % 2

    blocks = [move(queries, groups, steps, far) for steps in range(1, groups)]

    mine = [lax.dynamic_slice_in_dim(array, core * half, half, axis=0) for array in (keys, values)]
    got = lax.ppermute(jnp.concatenate(mine, axis=1), "ctx", swap_pairs(ctx_count))
    beside, key_norm = prepare(keys, values)
    got, key_norm, _ = lax.optimization_barrier((got, key_norm, blocks))
    rest = lax.ppermute(got, "head", swap_pairs(head_count))
    stack, query_norm = stack_queries(places, plan, [queries] + blocks, width)
    shape = (groups, rows, heads, requests)
    *parts, near_w = attend(
        places, plan, (key_norm, query_norm), stack, (keys, beside, got, rest), w_out, shape
    )
    back = [parts[0]] + [move(parts[steps], groups, groups - steps, far) for steps in range(1, groups)]
    attended = merge(places, plan, back, heads)

    near = [attended] + [
        lax.ppermute(attended, "head", shift_pairs(head_count, 2, steps)) for steps in range(1, chips)
    ]
    far_core = [lax.ppermute(piece, "head", swap_pairs(head_count)) for piece in near]
    return project(places, plan, near + far_core, near_w)


def solution(mesh):
    return jax.shard_map(
        body,
        mesh=mesh,
        in_specs=(P("ctx", "head"), P("ctx", None), P("ctx", None), P(None, "head"), P(), P()),
        out_specs=P("ctx", "head"),
        check_vma=False,
    )
```

```python
import functools
import math

import jax
import jax.numpy as jnp
from jax import lax
from jax.experimental import pallas as pl
from jax.experimental.pallas import tpu as pltpu
from jax.sharding import PartitionSpec as P

NEG = -1e30
CALM = 60.0
KEY_TILE = 512
FEW_ROWS = 64
SIDE = 16
LANES = 128
MIB = 1024 * 1024
SMEM = pl.BlockSpec(memory_space=pltpu.SMEM)
VMEM = pl.BlockSpec(memory_space=pltpu.VMEM)
HBM = pl.BlockSpec(memory_space=pltpu.HBM)


def prepare_kernel(keys_ref, values_ref, beside_ref, longest_ref):
    cache, width = keys_ref.shape
    step = min(KEY_TILE, cache)

    def turn(at, longest):
        here = pl.ds(pl.multiple_of(at * step, step), step)
        beside_ref[here, :width] = values_ref[here, :]
        beside_ref[here, width:] = jnp.ones((step, width), jnp.bfloat16)
        keys = keys_ref[here, :].astype(jnp.float32)
        return jnp.maximum(longest, jnp.sum(keys * keys, axis=1, keepdims=True))

    longest_ref[0] = jnp.max(lax.fori_loop(0, cache // step, turn, jnp.zeros((step, 1), jnp.float32)))


def prepare(keys, values):
    cache, width = keys.shape
    return pl.pallas_call(
        prepare_kernel,
        out_shape=(pltpu.VMEM((cache, 2 * width), jnp.bfloat16), jax.ShapeDtypeStruct((1,), jnp.float32)),
        in_specs=[VMEM] * 2,
        out_specs=(VMEM, SMEM),
        compiler_params=pltpu.CompilerParams(vmem_limit_bytes=8 * MIB),
        name="prepare",
    )(keys, values)


def join_kernel(got_ref, rest_ref, keys_ref, beside_ref, longest_ref):
    half, width = got_ref.shape[0], keys_ref.shape[1]
    step = min(KEY_TILE, half)
    longest = jnp.zeros((step, 1), jnp.float32)
    for done, part_ref in ((0, got_ref), (half, rest_ref)):

        def turn(at, longest, part_ref=part_ref, done=done):
            here = pl.ds(pl.multiple_of(at * step, step), step)
            there = pl.ds(pl.multiple_of(done + at * step, step), step)
            keys = part_ref[here, :width]
            keys_ref[there, :] = keys
            beside_ref[there, :width] = part_ref[here, width:]
            beside_ref[there, width:] = jnp.ones((step, width), jnp.bfloat16)
            wide = keys.astype(jnp.float32)
            return jnp.maximum(longest, jnp.sum(wide * wide, axis=1, keepdims=True))

        longest = lax.fori_loop(0, half // step, turn, longest)
    longest_ref[0] = jnp.max(longest)


def join(got, rest):
    half, wide = got.shape
    return pl.pallas_call(
        join_kernel,
        out_shape=(
            pltpu.VMEM((2 * half, wide // 2), jnp.bfloat16),
            pltpu.VMEM((2 * half, wide), jnp.bfloat16),
            jax.ShapeDtypeStruct((1,), jnp.float32),
        ),
        in_specs=[VMEM] * 2,
        out_specs=(VMEM, VMEM, SMEM),
        compiler_params=pltpu.CompilerParams(vmem_limit_bytes=8 * MIB),
        name="join",
    )(got, rest)


def stack_kernel(slots, group_at, width, plan_ref, *refs):
    q_refs, (stack_ref, longest_ref, q_all, sems) = refs[:slots], refs[slots:]
    rows = q_refs[0].shape[0]
    heads = q_refs[0].shape[1] // width
    local = slots * rows
    copies = [pltpu.make_async_copy(q_ref, q_all.at[slot], sems.at[slot]) for slot, q_ref in enumerate(q_refs)]
    for copy in copies:
        copy.start()
    longest = jnp.zeros((rows, 1), jnp.float32)
    for slot, copy in enumerate(copies):
        copy.wait()
        start = plan_ref[group_at + slot] * rows
        for head in range(heads):
            part = q_all[slot, :, head * width:(head + 1) * width]
            stack_ref[pl.ds(pl.multiple_of(head * local + start, rows), rows), :] = part
            wide = part.astype(jnp.float32)
            longest = jnp.maximum(longest, jnp.sum(wide * wide, axis=1, keepdims=True))
    longest_ref[0] = jnp.max(longest)


def stack_queries(places, plan, queries, width):
    slots, (rows, wide) = len(queries), queries[0].shape
    return pl.pallas_call(
        functools.partial(stack_kernel, slots, places["groups"], width),
        out_shape=(
            pltpu.VMEM((slots * rows * (wide // width), width), jnp.bfloat16),
            jax.ShapeDtypeStruct((1,), jnp.float32),
        ),
        in_specs=[SMEM] + [HBM] * slots,
        out_specs=(VMEM, SMEM),
        scratch_shapes=[pltpu.VMEM((slots, rows, wide), jnp.bfloat16), pltpu.SemaphoreType.DMA((slots,))],
        compiler_params=pltpu.CompilerParams(vmem_limit_bytes=8 * MIB),
        name="stack",
    )(plan, *queries)


def request_table(new_ref, prior_ref):
    table = []
    row, key = jnp.int32(0), jnp.int32(0)
    for request in range(new_ref.shape[0]):
        new, prior = new_ref[request], prior_ref[request]
        table.append((row, key, key + prior - row, row + new, key + new + prior))
        row, key = row + new, key + new + prior
    return table


def key_range(table, row):
    first, shift = table[0][1], table[0][2]
    for start, key, ahead, _, _ in table[1:]:
        own = row >= start
        first = jnp.where(own, key, first)
        shift = jnp.where(own, ahead, shift)
    return first, row + shift


def attend_kernel(shape, places, first_head, heads, stretches, last_call, fetching, *refs):
    groups, rows, requests, many = shape
    refs = list(refs)

    def take(count):
        taken, refs[:count] = refs[:count], []
        return taken

    plan_ref, key_norm_ref, query_norm_ref, stack_ref, keys_ref, beside_ref = take(6)
    cache, width = keys_ref.shape
    local = groups * rows
    step = min(KEY_TILE, cache // 2)
    scale = width ** (-0.5)
    factor = scale * math.log2(math.e)
    calm = key_norm_ref[0] * query_norm_ref[0] * (scale * scale) <= CALM * CALM
    side = plan_ref[places["side"]]
    if last_call:
        calm_in, sums_in, tops_in = take(3)
        far_w = take(1) if fetching else []
        out_refs = take(groups)
        near_w = take(1) if fetching else []
        chunk_q, chunk_sum, chunk_top, sums, tops = take(5)
        calm_before = calm_in[0] == 1
        calm = calm & calm_before
        fetches = [pltpu.make_async_copy(one, two, refs[0]) for one, two in zip(far_w, near_w)]
        for fetch in fetches:
            fetch.start()
    else:
        calm_out, sums, tops = take(3)
        chunk_q, chunk_sum, chunk_top = take(3)
        calm_out[0] = calm.astype(jnp.int32)

    def begin_sums(at, carry):
        here = pl.ds(pl.multiple_of(at * rows, rows), rows)
        there = pl.ds(pl.multiple_of(first_head * local + at * rows, rows), rows)
        sums[here, :] = sums_in[there, :] if last_call else jnp.zeros((rows, 2 * width), jnp.float32)

        @pl.when(jnp.logical_not(calm))
        def _():
            if last_call:
                before = jnp.where(calm_before, 0.0, tops_in[there, :])
                tops[here, :] = jnp.where(sums_in[there, width:] > 0.0, before, NEG)
            else:
                tops[here, :] = jnp.full((rows, width), NEG, jnp.float32)

        return carry

    lax.fori_loop(0, heads * groups, begin_sums, 0)

    def global_row(place):
        whole = place + side * rows
        for group in range(1, groups):
            whole = whole + jnp.where(place >= group * rows, rows, 0)
        return whole

    def one_chunk(count, online, request, begin, end, start):
        first_key = plan_ref[places["first_key"] + request]
        ahead = plan_ref[places["ahead"] + request]
        start = pl.multiple_of(start, SIDE)
        low_key, high_key = global_row(begin) + ahead, global_row(end - 1) + ahead
        total = heads * count
        for head in range(heads):
            chunk_q[head * count:(head + 1) * count, :] = stack_ref[
                pl.ds(pl.multiple_of((first_head + head) * local + start, SIDE), count), :
            ]
        chunk_sum[:total, :] = jnp.zeros((total, 2 * width), jnp.float32)
        if online:
            chunk_top[:total, :] = jnp.full((total, width), NEG, jnp.float32)
        place = start + lax.broadcasted_iota(jnp.int32, (count, 1), 0)
        last = global_row(place) + ahead

        def scores(part, left):
            return lax.dot_general(
                chunk_q[part, :], keys_ref[pl.ds(left, step), :], (((1,), (1,)), ((), ())),
                preferred_element_type=jnp.float32,
            ) * factor

        def add(left, weights):
            return jnp.dot(
                weights.astype(jnp.bfloat16), beside_ref[pl.ds(left, step), :], preferred_element_type=jnp.float32
            )

        def one_step(left, key):
            def allowed():
                index = key + lax.broadcasted_iota(jnp.int32, (count, step), 1)
                return (index >= first_key) & (index <= last)

            if online:
                mask = allowed()

                def one_head(head, carry):
                    part = pl.ds(pl.multiple_of(head * count, count), count)
                    score = jnp.where(mask, scores(part, left), NEG)
                    old = chunk_top[part, :]
                    new = jnp.maximum(old, jnp.ceil(jnp.max(score, axis=1, keepdims=True)))
                    weights = jnp.where(mask, jnp.exp2(score - new[:, :1]), 0.0)
                    shrink = jnp.exp2(old - new)
                    chunk_sum[part, :width] = chunk_sum[part, :width] * shrink
                    chunk_sum[part, width:] = chunk_sum[part, width:] * shrink
                    chunk_sum[part, :] += add(left, weights)
                    chunk_top[part, :] = new
                    return carry

                lax.fori_loop(0, heads, one_head, 0)
                return

            plain = (key >= first_key) & (key + step - 1 <= low_key)

            @pl.when(plain)
            def _():
                chunk_sum[:total, :] += add(left, jnp.exp2(scores(pl.ds(0, total), left)))

            @pl.when(jnp.logical_not(plain))
            def _():
                mask = allowed()
                weights = jnp.exp2(scores(pl.ds(0, total), left))
                weights = jnp.concatenate([
                    jnp.where(mask, weights[head * count:(head + 1) * count, :], 0.0) for head in range(heads)
                ])
                chunk_sum[:total, :] += add(left, weights)

        def one_part(part, carry):
            left, key, steps = (plan_ref[places[name] + part] for name in ("lefts", "keys", "steps"))
            low = jnp.clip(lax.div(first_key - key, step), 0, steps)
            high = jnp.clip(lax.div(high_key - key + step, step), 0, steps)

            def turn(at, carry):
                one_step(pl.multiple_of(left + at * step, step), key + at * step)
                return carry

            lax.fori_loop(low, high, turn, 0)
            return carry

        lax.fori_loop(*stretches, one_part, 0)
        own = (place >= begin) & (place < end)
        for head in range(heads):
            here = pl.ds(pl.multiple_of(head * local + start, SIDE), count)
            part = slice(head * count, (head + 1) * count)
            if not online:
                sums[here, :] += jnp.where(own, chunk_sum[part, :], 0.0)
                continue
            old = tops[here, :]
            new = jnp.where(own, jnp.maximum(old, chunk_top[part, :]), old)
            grown = jnp.where(own, jnp.exp2(chunk_top[part, :] - new), 0.0)
            shrink = jnp.exp2(old - new)
            sums[here, :width] = sums[here, :width] * shrink + chunk_sum[part, :width] * grown
            sums[here, width:] = sums[here, width:] * shrink + chunk_sum[part, width:] * grown
            tops[here, :] = new

    def all_chunks(count, online, request, begin, end):
        aligned = lax.div(begin, SIDE) * SIDE

        def turn(at, carry):
            from_row = aligned + at * count
            one_chunk(
                count,
                online,
                request,
                jnp.maximum(begin, from_row),
                jnp.minimum(end, from_row + count),
                jnp.minimum(from_row, local - count),
            )
            return carry

        lax.fori_loop(0, lax.div(end - aligned + (count - 1), count), turn, 0)

    few = min(FEW_ROWS, local)

    def one_request(request, carry):
        begin, end = plan_ref[places["begin"] + request], plan_ref[places["end"] + request]
        large = end - lax.div(begin, SIDE) * SIDE > 2 * few

        @pl.when((end > begin) & calm & large)
        def _():
            all_chunks(many, False, request, begin, end)

        @pl.when((end > begin) & calm & jnp.logical_not(large))
        def _():
            all_chunks(few, False, request, begin, end)

        @pl.when((end > begin) & jnp.logical_not(calm))
        def _():
            all_chunks(few, True, request, begin, end)

        return carry

    lax.fori_loop(0, requests, one_request, 0)

    if not last_call:
        return
    lane = lax.broadcasted_iota(jnp.int32, (LANES, LANES), 1)
    for slot, out_ref in enumerate(out_refs):
        start = plan_ref[places["groups"] + slot] * rows
        if heads * width > rows:
            out_ref[rows:, :] = jnp.zeros((out_ref.shape[0] - rows, heads * width), jnp.bfloat16)
        for at in range(0, rows, LANES):
            terms = jnp.zeros((LANES, LANES), jnp.float32)
            for head in range(heads):
                here = pl.ds(pl.multiple_of(head * local + start + at, LANES), LANES)
                out_ref[at:at + LANES, head * width:(head + 1) * width] = sums[here, :width].astype(jnp.bfloat16)
                weight = sums[here, width:]
                top = jnp.where(weight > 0.0, jnp.where(calm, 0.0, tops[here, :]), NEG)
                for term, value in enumerate((weight, top)):
                    high = value.astype(jnp.bfloat16).astype(jnp.float32)
                    terms = jnp.where(lane == 2 * term * heads + head, high, terms)
                    terms = jnp.where(lane == (2 * term + 1) * heads + head, value - high, terms)
            fold, column = at // (heads * width), at % (heads * width)
            out_ref[rows + fold * SIDE:rows + (fold + 1) * SIDE, column:column + LANES] = terms.T[:SIDE, :].astype(
                jnp.bfloat16
            )
    for fetch in fetches:
        fetch.wait()


def side_rows(rows, wide):
    return SIDE * max(1, rows // wide)


def attend(places, plan, norms, stack, cache_side, shape, first_head, heads, stretches, before=None, w_out=None):
    groups, rows, requests = shape
    keys, beside = cache_side
    cache, width = keys.shape
    local, wide = groups * rows, heads * width
    last_call = before is not None
    many = min((1 if heads > 2 else 2) * rows + SIDE, local)
    kernel = functools.partial(
        attend_kernel, (*shape, many), dict(places), first_head, heads, stretches, last_call, w_out is not None
    )
    scratch = [
        pltpu.VMEM((heads * many, width), jnp.bfloat16),
        pltpu.VMEM((heads * many, 2 * width), jnp.float32),
        pltpu.VMEM((heads * min(FEW_ROWS, local), width), jnp.float32),
    ]
    sums = [pltpu.VMEM((heads * local, 2 * width), jnp.float32), pltpu.VMEM((heads * local, width), jnp.float32)]
    fetched = [] if w_out is None else [pltpu.with_memory_space_constraint(w_out, pltpu.HBM)]
    if last_call:
        return pl.pallas_call(
            kernel,
            out_shape=(jax.ShapeDtypeStruct((rows + side_rows(rows, wide), wide), jnp.bfloat16),) * groups
            + tuple(pltpu.VMEM(array.shape, array.dtype) for array in fetched),
            in_specs=[SMEM] * 3 + [VMEM] * 3 + [SMEM, VMEM, VMEM] + [HBM] * len(fetched),
            out_specs=(VMEM,) * (groups + len(fetched)),
            scratch_shapes=scratch + sums + [pltpu.SemaphoreType.DMA] * len(fetched),
            compiler_params=pltpu.CompilerParams(vmem_limit_bytes=22 * MIB),
            cost_estimate=pl.CostEstimate(
                flops=local * heads * cache * width * 2, bytes_accessed=8 * MIB, transcendentals=0
            ),
            name="attend_last",
        )(plan, *norms, stack, keys, beside, *before, *fetched)
    return pl.pallas_call(
        kernel,
        out_shape=(jax.ShapeDtypeStruct((1,), jnp.int32), *sums),
        in_specs=[SMEM] * 3 + [VMEM] * 3,
        out_specs=(SMEM, VMEM, VMEM),
        scratch_shapes=scratch,
        compiler_params=pltpu.CompilerParams(vmem_limit_bytes=16 * MIB),
        cost_estimate=pl.CostEstimate(
            flops=local * heads * cache * width * 2, bytes_accessed=8 * MIB, transcendentals=0
        ),
        name="attend_first",
    )(plan, *norms, stack, keys, beside)


def merge_kernel(heads, there_at, plan_ref, *refs):
    parts, out_ref = refs[:-1], refs[-1]
    rows = out_ref.shape[0]
    width = out_ref.shape[1] // heads
    logs = [
        jnp.where(
            plan_ref[there_at + at] == 1,
            jnp.concatenate([
                part[row:row + SIDE, :min(rows, out_ref.shape[1])] for row in range(rows, part.shape[0], SIDE)
            ], axis=1).astype(jnp.float32),
            0.0,
        )
        for at, part in enumerate(parts)
    ]
    spare = LANES - SIDE * len(parts)
    if spare:
        logs.append(jnp.zeros((spare, rows), jnp.float32))
    terms = jnp.concatenate(logs, axis=0).T
    total = terms + pltpu.roll(terms, LANES - heads, 1)
    top = pltpu.roll(terms, LANES - 2 * heads, 1) + pltpu.roll(terms, LANES - 3 * heads, 1)
    lane = lax.broadcasted_iota(jnp.int32, (rows, LANES), 1)
    used = (lax.rem(lane, SIDE) < heads) & (lane < SIDE * len(parts)) & (total > 0.0)
    top = jnp.where(used, top, NEG)
    biggest = top
    for shift in (16, 32, 64):
        biggest = jnp.maximum(biggest, pltpu.roll(biggest, shift, 1))
    share = jnp.where(used, jnp.exp2(top - biggest), 0.0)
    weight = share * jnp.where(used, total, 0.0)
    for shift in (16, 32, 64):
        weight = weight + pltpu.roll(weight, shift, 1)
    share = share / weight
    for head in range(heads):
        own = slice(head * width, (head + 1) * width)
        mixed = jnp.zeros((rows, width), jnp.float32)
        for at, part in enumerate(parts):
            lane_at = at * SIDE + head
            mixed = mixed + part[:rows, own].astype(jnp.float32) * share[:, lane_at:lane_at + 1]
        out_ref[:, own] = mixed.astype(out_ref.dtype)


def merge(places, plan, parts, rows, heads):
    return pl.pallas_call(
        functools.partial(merge_kernel, heads, places["there"]),
        out_shape=jax.ShapeDtypeStruct((rows, parts[0].shape[1]), jnp.bfloat16),
        in_specs=[SMEM] + [VMEM] * len(parts),
        out_specs=VMEM,
        compiler_params=pltpu.CompilerParams(vmem_limit_bytes=12 * MIB),
        name="merge",
    )(plan, *parts)


def project_kernel(pieces, parts, from_at, plan_ref, *refs):
    w_ref, out_ref, whole = refs[pieces:]
    deep = refs[0].shape[1]
    block = out_ref.shape[1]

    @pl.when(pl.program_id(0) == 0)
    def _():
        for at, piece in enumerate(refs[:pieces]):
            own = plan_ref[from_at + at // parts] * parts + at % parts
            whole[:, pl.ds(pl.multiple_of(own * deep, deep), deep)] = piece[...]

    left = pl.multiple_of(pl.program_id(0) * block, block)
    out_ref[...] = jnp.dot(
        whole[...], w_ref[:, pl.ds(left, block)], preferred_element_type=jnp.float32
    ).astype(out_ref.dtype)


def project(places, plan, pieces, parts, w_out):
    rows, deep = pieces[0].shape
    depth, wide = w_out.shape
    block = min(1024, wide)
    return pl.pallas_call(
        functools.partial(project_kernel, len(pieces), parts, places["from"]),
        out_shape=pltpu.HBM((rows, wide), jnp.bfloat16),
        grid=(wide // block,),
        in_specs=[SMEM] + [VMEM] * (len(pieces) + 1),
        out_specs=pl.BlockSpec((rows, block), lambda at: (0, at)),
        scratch_shapes=[pltpu.VMEM((rows, depth), jnp.bfloat16)],
        compiler_params=pltpu.CompilerParams(vmem_limit_bytes=20 * MIB),
        cost_estimate=pl.CostEstimate(
            flops=2 * rows * depth * wide, bytes_accessed=2 * depth * wide, transcendentals=0
        ),
        name="project",
    )(plan, *pieces, w_out)


def shift_pairs(count, stride, steps):
    groups = count // stride
    return [
        (group * stride + member, (group + steps) % groups * stride + member)
        for group in range(groups)
        for member in range(stride)
    ]


def swap_pairs(count):
    return [(at, at ^ 1) for at in range(count)]


def is_far(groups, one, two):
    low, high = min(one, two), max(one, two)
    return low < groups // 2 and high >= groups - max(1, groups // 4)


def move(value, groups, steps, far):
    pairs = [
        (source, target)
        for source, target in shift_pairs(2 * groups, 2, steps)
        if far or not is_far(groups, source // 2, target // 2)
    ]
    return lax.ppermute(value, "ctx", pairs) if pairs else jnp.zeros_like(value)


def plan_kernel(shape, places, new_ref, prior_ref, at_ref, plan_ref, far_ref):
    groups, chips, rows, cache, step = shape
    device, place = at_ref[0], at_ref[1]
    group, side, chip, core = lax.div(device, 2), lax.rem(device, 2), lax.div(place, 2), lax.rem(place, 2)
    table = request_table(new_ref, prior_ref)

    def rows_before(row):
        block = lax.div(row, rows)
        odd, inside = lax.rem(block, 2), lax.rem(row, rows)
        return lax.div(block, 2) * rows + jnp.where(odd == side, inside, jnp.where(odd == 1, rows, 0))

    for request, (row, key, ahead, row_end, _) in enumerate(table):
        plan_ref[places["first_key"] + request] = key
        plan_ref[places["ahead"] + request] = ahead
        plan_ref[places["begin"] + request] = rows_before(row)
        plan_ref[places["end"] + request] = rows_before(row_end)
    spans = [
        (key_range(table, jnp.int32(2 * rows * at))[0], key_range(table, jnp.int32(2 * rows * (at + 1) - 1))[1])
        for at in range(groups)
    ]
    needed = jnp.int32(0)
    for source in range(groups):
        for target in range(groups):
            if is_far(groups, source, target):
                first, last = spans[source]
                meet = (first < 2 * cache * (target + 1)) & (last >= 2 * cache * target)
                needed = jnp.where(meet, 1, needed)
    far_ref[0] = needed
    plan_ref[places["side"]] = side
    for steps in range(groups):
        plan_ref[places["groups"] + steps] = lax.rem(group + (groups - steps), groups)
        there = jnp.int32(1)
        for at in range(groups):
            if is_far(groups, (at + steps) % groups, at):
                there = jnp.where(group == at, needed, there)
        plan_ref[places["there"] + steps] = there
    other = (device + 1 - 2 * side) * cache
    half = cache // 2
    stretches = [(0, device * cache, cache), (0, other + core * half, half), (half, other + (1 - core) * half, half)]
    for part, (left, key, count) in enumerate(stretches):
        plan_ref[places["lefts"] + part] = jnp.int32(left)
        plan_ref[places["keys"] + part] = key
        plan_ref[places["steps"] + part] = jnp.int32(count // step)
    for at in range(2 * chips):
        own = core if at < chips else 1 - core
        plan_ref[places["from"] + at] = lax.rem(chip + (chips - at % chips), chips) * 2 + own


def make_plan(shape, new_counts, prior_lengths, at):
    groups, chips = shape[:2]
    requests = new_counts.shape[0]
    sizes = dict(first_key=requests, ahead=requests, begin=requests, end=requests, side=1)
    sizes.update(groups=groups, there=groups, lefts=3, keys=3, steps=3)
    sizes["from"] = 2 * chips
    places, total = {}, 0
    for name, size in sizes.items():
        places[name] = total
        total += size
    plan, far = pl.pallas_call(
        functools.partial(plan_kernel, shape, dict(places)),
        out_shape=(jax.ShapeDtypeStruct((total,), jnp.int32), jax.ShapeDtypeStruct((1,), jnp.int32)),
        in_specs=[SMEM] * 3,
        out_specs=(SMEM, SMEM),
        name="plan",
    )(new_counts, prior_lengths, at)
    return places, plan, far


def body(queries, keys, values, w_out, new_counts, prior_lengths):
    ctx_count, head_count = lax.axis_size("ctx"), lax.axis_size("head")
    rows = queries.shape[0]
    cache = keys.shape[0]
    groups, chips = ctx_count // 2, head_count // 2
    at = jnp.stack([lax.axis_index("ctx"), lax.axis_index("head")]).astype(jnp.int32)
    shape = (groups, chips, rows, cache, min(KEY_TILE, cache // 2))
    places, plan, far = make_plan(shape, new_counts, prior_lengths, at)
    requests = new_counts.shape[0]
    return lax.cond(
        far[0] == 1,
        functools.partial(attend_and_project, places, requests, True),
        functools.partial(attend_and_project, places, requests, False),
        *(queries, keys, values, w_out, plan),
    )


def attend_and_project(places, requests, far, queries, keys, values, w_out, plan):
    ctx_count, head_count = lax.axis_size("ctx"), lax.axis_size("head")
    rows = queries.shape[0]
    cache, width = keys.shape
    heads = queries.shape[1] // width
    groups, chips, half = ctx_count // 2, head_count // 2, cache // 2
    core = lax.axis_index("head") % 2

    blocks = [move(queries, groups, steps, far) for steps in range(1, groups)]

    mine = [lax.dynamic_slice_in_dim(array, core * half, half, axis=0) for array in (keys, values)]
    got = lax.ppermute(jnp.concatenate(mine, axis=1), "ctx", swap_pairs(ctx_count))
    beside, key_norm = prepare(keys, values)
    stack, query_norm = stack_queries(places, plan, [queries] + blocks, width)
    shape = (groups, rows, requests)
    calm, sums, tops = attend(
        places, plan, (key_norm, query_norm), stack, (keys, beside), shape, 0, heads, (0, 1)
    )
    got, calm = lax.optimization_barrier((got, calm))
    rest = lax.ppermute(got, "head", swap_pairs(head_count))
    *other_side, other_norm = join(got, rest)

    halves = 2 if heads % 2 == 0 else 1
    few = heads // halves
    back = []
    for part in range(halves):
        *parts, near_w = attend(
            places, plan, (other_norm, query_norm), stack, other_side, shape, part * few, few, (1, 3),
            before=(calm, sums, tops), w_out=w_out if part == halves - 1 else None,
        ) + (() if part == halves - 1 else (None,))
        back.append(
            [parts[0]] + [move(parts[steps], groups, groups - steps, far) for steps in range(1, groups)]
        )
    gathered = []
    for parts in back:
        attended = merge(places, plan, parts, rows, few)
        near = [attended] + [
            lax.ppermute(attended, "head", shift_pairs(head_count, 2, steps)) for steps in range(1, chips)
        ]
        gathered.append(near + [lax.ppermute(piece, "head", swap_pairs(head_count)) for piece in near])
    pieces = [piece for same in zip(*gathered) for piece in same]
    return project(places, plan, pieces, halves, near_w)


def solution(mesh):
    return jax.shard_map(
        body,
        mesh=mesh,
        in_specs=(P("ctx", "head"), P("ctx", None), P("ctx", None), P(None, "head"), P(), P()),
        out_specs=P("ctx", "head"),
        check_vma=False,
    )
```

```python
import functools
import math

import jax
import jax.numpy as jnp
from jax import lax
from jax.experimental import pallas as pl
from jax.experimental.pallas import tpu as pltpu
from jax.sharding import PartitionSpec as P

NEG = -1e30
CALM = 60.0
KEY_TILE = 512
FEW_ROWS = 64
SIDE = 16
SLACK = 1.05
LANES = 128
MIB = 1024 * 1024
SMEM = pl.BlockSpec(memory_space=pltpu.SMEM)
VMEM = pl.BlockSpec(memory_space=pltpu.VMEM)
HBM = pl.BlockSpec(memory_space=pltpu.HBM)


def lengths(rows):
    wide = rows.astype(jnp.float32)
    ones = jnp.ones((rows.shape[1], LANES), jnp.bfloat16)
    return jnp.dot((wide * wide).astype(jnp.bfloat16), ones, preferred_element_type=jnp.float32)


def fill(parts, keys_ref, beside_ref):
    width = keys_ref.shape[1]
    longest = jnp.zeros((KEY_TILE, LANES), jnp.float32)
    for from_keys, from_values, done in parts:
        step = min(KEY_TILE, from_keys.shape[0])

        def turn(at, longest, from_keys=from_keys, from_values=from_values, done=done, step=step):
            here = pl.ds(pl.multiple_of(at * step, step), step)
            there = pl.ds(pl.multiple_of(done + at * step, step), step)
            keys = from_keys[here, :]
            keys_ref[there, :] = keys
            beside_ref[there, :width] = from_values[here, :]
            beside_ref[there, width:] = jnp.ones((step, width), jnp.bfloat16)
            return jnp.maximum(longest, lengths(keys))

        longest = lax.fori_loop(0, from_keys.shape[0] // step, turn, longest)
    return jnp.max(longest)


def prepare_kernel(keys_ref, values_ref, far_w, all_keys, beside_ref, longest_ref, near_w, sem):
    fetch = pltpu.make_async_copy(far_w, near_w, sem)
    fetch.start()
    longest_ref[0] = fill([(keys_ref, values_ref, 0)], all_keys, beside_ref)
    fetch.wait()


def prepare(keys, values, w_out):
    cache, width = keys.shape
    return pl.pallas_call(
        prepare_kernel,
        out_shape=(
            pltpu.VMEM((2 * cache, width), jnp.bfloat16),
            pltpu.VMEM((2 * cache, 2 * width), jnp.bfloat16),
            jax.ShapeDtypeStruct((1,), jnp.float32),
            pltpu.VMEM(w_out.shape, w_out.dtype),
        ),
        in_specs=[VMEM, VMEM, HBM],
        out_specs=(VMEM, VMEM, SMEM, VMEM),
        scratch_shapes=[pltpu.SemaphoreType.DMA],
        compiler_params=pltpu.CompilerParams(vmem_limit_bytes=4 * MIB),
        name="prepare",
    )(keys, values, pltpu.with_memory_space_constraint(w_out, pltpu.HBM))


def join_kernel(got_ref, rest_ref, own_ref, keys_in, beside_in, all_keys, beside_ref, longest_ref):
    del keys_in, beside_in
    half, width = got_ref.shape[0], all_keys.shape[1]
    parts = [
        (ref.at[:, :width], ref.at[:, width:], 2 * half + at * half) for at, ref in enumerate((got_ref, rest_ref))
    ]
    longest_ref[0] = jnp.maximum(own_ref[0], fill(parts, all_keys, beside_ref))


def join(got, rest, own_longest, all_keys, beside):
    return pl.pallas_call(
        join_kernel,
        out_shape=(
            pltpu.VMEM(all_keys.shape, all_keys.dtype),
            pltpu.VMEM(beside.shape, beside.dtype),
            jax.ShapeDtypeStruct((1,), jnp.float32),
        ),
        in_specs=[VMEM, VMEM, SMEM, VMEM, VMEM],
        out_specs=(VMEM, VMEM, SMEM),
        input_output_aliases={3: 0, 4: 1},
        compiler_params=pltpu.CompilerParams(vmem_limit_bytes=4 * MIB),
        name="join",
    )(got, rest, own_longest, all_keys, beside)


def stack_kernel(slots, group_at, width, plan_ref, *refs):
    q_refs, (stack_ref, longest_ref, q_all, sems) = refs[:slots], refs[slots:]
    rows = q_refs[0].shape[0]
    heads = q_refs[0].shape[1] // width
    local = slots * rows
    copies = [pltpu.make_async_copy(q_ref, q_all.at[slot], sems.at[slot]) for slot, q_ref in enumerate(q_refs)]
    for copy in copies:
        copy.start()
    longest = jnp.zeros((rows, LANES), jnp.float32)
    for slot, copy in enumerate(copies):
        copy.wait()
        start = plan_ref[group_at + slot] * rows
        for head in range(heads):
            part = q_all[slot, :, head * width:(head + 1) * width]
            stack_ref[pl.ds(pl.multiple_of(head * local + start, rows), rows), :] = part
            longest = jnp.maximum(longest, lengths(part))
    longest_ref[0] = jnp.max(longest)


def stack_queries(places, plan, queries, width):
    slots, (rows, wide) = len(queries), queries[0].shape
    return pl.pallas_call(
        functools.partial(stack_kernel, slots, places["groups"], width),
        out_shape=(
            pltpu.VMEM((slots * rows * (wide // width), width), jnp.bfloat16),
            jax.ShapeDtypeStruct((1,), jnp.float32),
        ),
        in_specs=[SMEM] + [HBM] * slots,
        out_specs=(VMEM, SMEM),
        scratch_shapes=[pltpu.VMEM((slots, rows, wide), jnp.bfloat16), pltpu.SemaphoreType.DMA((slots,))],
        compiler_params=pltpu.CompilerParams(vmem_limit_bytes=4 * MIB),
        name="stack",
    )(plan, *queries)


def request_table(new_ref, prior_ref):
    table = []
    row, key = jnp.int32(0), jnp.int32(0)
    for request in range(new_ref.shape[0]):
        new, prior = new_ref[request], prior_ref[request]
        table.append((row, key, key + prior - row, row + new, key + new + prior))
        row, key = row + new, key + new + prior
    return table


def key_range(table, row):
    first, shift = table[0][1], table[0][2]
    for start, key, ahead, _, _ in table[1:]:
        own = row >= start
        first = jnp.where(own, key, first)
        shift = jnp.where(own, ahead, shift)
    return first, row + shift


def attend_kernel(shape, places, first_head, heads, *refs):
    groups, rows, requests, many = shape
    plan_ref, key_norm_ref, query_norm_ref, stack_ref, keys_ref, beside_ref = refs[:6]
    out_refs = refs[6:6 + groups]
    sums, tops, chunk_q, chunk_sum, chunk_top = refs[6 + groups:]
    width = keys_ref.shape[1]
    local = groups * rows
    step = min(KEY_TILE, keys_ref.shape[0] // 4)
    scale = width ** (-0.5)
    factor = scale * math.log2(math.e)
    calm = key_norm_ref[0] * query_norm_ref[0] * (SLACK * scale * scale) <= CALM * CALM
    side = plan_ref[places["side"]]

    def clear(at, carry):
        sums[pl.ds(pl.multiple_of(at * rows, rows), rows), :] = jnp.zeros((rows, 2 * width), jnp.float32)
        return carry

    lax.fori_loop(0, heads * groups, clear, 0)

    def global_row(place):
        whole = place + side * rows
        for group in range(1, groups):
            whole = whole + jnp.where(place >= group * rows, rows, 0)
        return whole

    def one_chunk(count, online, request, begin, end, start):
        first_key = plan_ref[places["first_key"] + request]
        ahead = plan_ref[places["ahead"] + request]
        start = pl.multiple_of(start, SIDE)
        low_key, high_key = global_row(begin) + ahead, global_row(end - 1) + ahead
        total = heads * count
        for head in range(heads):
            chunk_q[head * count:(head + 1) * count, :] = stack_ref[
                pl.ds(pl.multiple_of((first_head + head) * local + start, SIDE), count), :
            ]
        chunk_sum[:total, :] = jnp.zeros((total, 2 * width), jnp.float32)
        if online:
            chunk_top[:total, :] = jnp.full((total, width), NEG, jnp.float32)
        place = start + lax.broadcasted_iota(jnp.int32, (count, 1), 0)
        last = global_row(place) + ahead

        def scores(part, left):
            return lax.dot_general(
                chunk_q[part, :], keys_ref[pl.ds(left, step), :], (((1,), (1,)), ((), ())),
                preferred_element_type=jnp.float32,
            ) * factor

        def add(left, weights):
            return jnp.dot(
                weights.astype(jnp.bfloat16), beside_ref[pl.ds(left, step), :], preferred_element_type=jnp.float32
            )

        def one_step(left, key):
            def allowed():
                index = key + lax.broadcasted_iota(jnp.int32, (count, step), 1)
                return (index >= first_key) & (index <= last)

            if online:
                mask = allowed()

                def one_head(head, carry):
                    part = pl.ds(pl.multiple_of(head * count, count), count)
                    score = jnp.where(mask, scores(part, left), NEG)
                    old = chunk_top[part, :]
                    new = jnp.maximum(old, jnp.ceil(jnp.max(score, axis=1, keepdims=True)))
                    weights = jnp.where(mask, jnp.exp2(score - new[:, :1]), 0.0)
                    shrink = jnp.exp2(old - new)
                    chunk_sum[part, :width] = chunk_sum[part, :width] * shrink
                    chunk_sum[part, width:] = chunk_sum[part, width:] * shrink
                    chunk_sum[part, :] += add(left, weights)
                    chunk_top[part, :] = new
                    return carry

                lax.fori_loop(0, heads, one_head, 0)
                return

            plain = (key >= first_key) & (key + step - 1 <= low_key)

            @pl.when(plain)
            def _():
                chunk_sum[:total, :] += add(left, jnp.exp2(scores(pl.ds(0, total), left)))

            @pl.when(jnp.logical_not(plain))
            def _():
                mask = allowed()
                weights = jnp.exp2(scores(pl.ds(0, total), left))
                weights = jnp.concatenate([
                    jnp.where(mask, weights[head * count:(head + 1) * count, :], 0.0) for head in range(heads)
                ])
                chunk_sum[:total, :] += add(left, weights)

        def one_part(part, carry):
            left, key, steps = (plan_ref[places[name] + part] for name in ("lefts", "keys", "steps"))
            low = jnp.clip(lax.div(first_key - key, step), 0, steps)
            high = jnp.clip(lax.div(high_key - key + step, step), 0, steps)

            def turn(at, carry):
                one_step(pl.multiple_of(left + at * step, step), key + at * step)
                return carry

            lax.fori_loop(low, high, turn, 0)
            return carry

        lax.fori_loop(0, 3, one_part, 0)
        own = (place >= begin) & (place < end)
        for head in range(heads):
            here = pl.ds(pl.multiple_of(head * local + start, SIDE), count)
            part = slice(head * count, (head + 1) * count)
            sums[here, :] += jnp.where(own, chunk_sum[part, :], 0.0)
            if online:
                tops[here, :] = jnp.where(own, chunk_top[part, :], tops[here, :])

    def all_chunks(count, online, request, begin, end):
        aligned = lax.div(begin, SIDE) * SIDE

        def turn(at, carry):
            from_row = aligned + at * count
            one_chunk(
                count,
                online,
                request,
                jnp.maximum(begin, from_row),
                jnp.minimum(end, from_row + count),
                jnp.minimum(from_row, local - count),
            )
            return carry

        lax.fori_loop(0, lax.div(end - aligned + (count - 1), count), turn, 0)

    few = min(FEW_ROWS, local)

    def one_request(request, carry):
        begin, end = plan_ref[places["begin"] + request], plan_ref[places["end"] + request]
        large = end - lax.div(begin, SIDE) * SIDE > 2 * few

        @pl.when((end > begin) & calm & large)
        def _():
            all_chunks(many, False, request, begin, end)

        @pl.when((end > begin) & calm & jnp.logical_not(large))
        def _():
            all_chunks(few, False, request, begin, end)

        @pl.when((end > begin) & jnp.logical_not(calm))
        def _():
            all_chunks(few, True, request, begin, end)

        return carry

    lax.fori_loop(0, requests, one_request, 0)

    lane = lax.broadcasted_iota(jnp.int32, (LANES, LANES), 1)
    for slot, out_ref in enumerate(out_refs):
        start = plan_ref[places["groups"] + slot] * rows
        if heads * width > rows:
            out_ref[rows:, :] = jnp.zeros((out_ref.shape[0] - rows, heads * width), jnp.bfloat16)
        for at in range(0, rows, LANES):
            terms = jnp.zeros((LANES, LANES), jnp.float32)
            for head in range(heads):
                here = pl.ds(pl.multiple_of(head * local + start + at, LANES), LANES)
                out_ref[at:at + LANES, head * width:(head + 1) * width] = sums[here, :width].astype(jnp.bfloat16)
                weight = sums[here, width:]
                top = jnp.where(weight > 0.0, jnp.where(calm, 0.0, tops[here, :]), NEG)
                for term, value in enumerate((weight, top)):
                    high = value.astype(jnp.bfloat16).astype(jnp.float32)
                    terms = jnp.where(lane == 2 * term * heads + head, high, terms)
                    terms = jnp.where(lane == (2 * term + 1) * heads + head, value - high, terms)
            fold, column = at // (heads * width), at % (heads * width)
            out_ref[rows + fold * SIDE:rows + (fold + 1) * SIDE, column:column + LANES] = terms.T[:SIDE, :].astype(
                jnp.bfloat16
            )


def side_rows(rows, wide):
    return SIDE * max(1, rows // wide)


def attend(places, plan, norms, stack, keys, beside, shape, first_head, heads):
    groups, rows, _ = shape
    width = keys.shape[1]
    local, wide = groups * rows, heads * width
    many = min(2 * rows + SIDE, local)
    return pl.pallas_call(
        functools.partial(attend_kernel, (*shape, many), dict(places), first_head, heads),
        out_shape=(jax.ShapeDtypeStruct((rows + side_rows(rows, wide), wide), jnp.bfloat16),) * groups,
        in_specs=[SMEM] * 3 + [VMEM] * 3,
        out_specs=(VMEM,) * groups,
        scratch_shapes=[
            pltpu.VMEM((heads * local, 2 * width), jnp.float32),
            pltpu.VMEM((heads * local, width), jnp.float32),
            pltpu.VMEM((heads * many, width), jnp.bfloat16),
            pltpu.VMEM((heads * many, 2 * width), jnp.float32),
            pltpu.VMEM((heads * min(FEW_ROWS, local), width), jnp.float32),
        ],
        compiler_params=pltpu.CompilerParams(vmem_limit_bytes=20 * MIB),
        cost_estimate=pl.CostEstimate(
            flops=local * heads * keys.shape[0] * width * 2, bytes_accessed=8 * MIB, transcendentals=0
        ),
        name="attend",
    )(plan, *norms, stack, keys, beside)


def merge_kernel(heads, there_at, plan_ref, *refs):
    parts, out_ref = refs[:-1], refs[-1]
    rows = out_ref.shape[0]
    width = out_ref.shape[1] // heads
    logs = [
        jnp.where(
            plan_ref[there_at + at] == 1,
            jnp.concatenate([
                part[row:row + SIDE, :min(rows, out_ref.shape[1])] for row in range(rows, part.shape[0], SIDE)
            ], axis=1).astype(jnp.float32),
            0.0,
        )
        for at, part in enumerate(parts)
    ]
    spare = LANES - SIDE * len(parts)
    if spare:
        logs.append(jnp.zeros((spare, rows), jnp.float32))
    terms = jnp.concatenate(logs, axis=0).T
    total = terms + pltpu.roll(terms, LANES - heads, 1)
    top = pltpu.roll(terms, LANES - 2 * heads, 1) + pltpu.roll(terms, LANES - 3 * heads, 1)
    lane = lax.broadcasted_iota(jnp.int32, (rows, LANES), 1)
    used = (lax.rem(lane, SIDE) < heads) & (lane < SIDE * len(parts)) & (total > 0.0)
    top = jnp.where(used, top, NEG)
    biggest = top
    for shift in (16, 32, 64):
        biggest = jnp.maximum(biggest, pltpu.roll(biggest, shift, 1))
    share = jnp.where(used, jnp.exp2(top - biggest), 0.0)
    weight = share * jnp.where(used, total, 0.0)
    for shift in (16, 32, 64):
        weight = weight + pltpu.roll(weight, shift, 1)
    share = share / weight
    for head in range(heads):
        own = slice(head * width, (head + 1) * width)
        mixed = jnp.zeros((rows, width), jnp.float32)
        for at, part in enumerate(parts):
            lane_at = at * SIDE + head
            mixed = mixed + part[:rows, own].astype(jnp.float32) * share[:, lane_at:lane_at + 1]
        out_ref[:, own] = mixed.astype(out_ref.dtype)


def merge(places, plan, parts, rows, heads):
    return pl.pallas_call(
        functools.partial(merge_kernel, heads, places["there"]),
        out_shape=jax.ShapeDtypeStruct((rows, parts[0].shape[1]), jnp.bfloat16),
        in_specs=[SMEM] + [VMEM] * len(parts),
        out_specs=VMEM,
        compiler_params=pltpu.CompilerParams(vmem_limit_bytes=12 * MIB),
        name="merge",
    )(plan, *parts)


def project_kernel(pieces, parts, part, from_at, plan_ref, *refs):
    refs = list(refs)
    before_ref = refs.pop(0) if part else None
    piece_refs, (w_ref, out_ref, token_ref) = refs[:pieces], refs[pieces:]
    token_ref[0] = jnp.int32(part)
    deep = piece_refs[0].shape[1]
    block = out_ref.shape[1]
    left = pl.multiple_of(pl.program_id(0) * block, block)
    total = None
    for at, piece_ref in enumerate(piece_refs):
        own = pl.multiple_of((plan_ref[from_at + at] * parts + part) * deep, deep)
        term = jnp.dot(
            piece_ref[...], w_ref[pl.ds(own, deep), pl.ds(left, block)], preferred_element_type=jnp.float32
        )
        total = term if total is None else total + term
    if part:
        total = total + before_ref[:, pl.ds(left, block)]
    out_ref[...] = total.astype(out_ref.dtype)


def project(places, plan, pieces, parts, part, before, w_out):
    rows, deep = pieces[0].shape
    depth, wide = w_out.shape
    block = min(1024, wide)
    last = part == parts - 1
    return pl.pallas_call(
        functools.partial(project_kernel, len(pieces), parts, part, places["from"]),
        out_shape=(
            pltpu.HBM((rows, wide), jnp.bfloat16) if last else pltpu.VMEM((rows, wide), jnp.float32),
            jax.ShapeDtypeStruct((1,), jnp.int32),
        ),
        grid=(wide // block,),
        in_specs=[SMEM] + [VMEM] * (bool(part) + len(pieces) + 1),
        out_specs=(pl.BlockSpec((rows, block), lambda at: (0, at)), SMEM),
        compiler_params=pltpu.CompilerParams(vmem_limit_bytes=16 * MIB),
        cost_estimate=pl.CostEstimate(
            flops=2 * rows * depth * wide // parts, bytes_accessed=2 * depth * wide // parts, transcendentals=0
        ),
        name="project",
    )(plan, *([before] if part else []), *pieces, w_out)


def shift_pairs(count, stride, steps):
    groups = count // stride
    return [
        (group * stride + member, (group + steps) % groups * stride + member)
        for group in range(groups)
        for member in range(stride)
    ]


def swap_pairs(count):
    return [(at, at ^ 1) for at in range(count)]


def is_far(groups, one, two):
    low, high = min(one, two), max(one, two)
    return low < groups // 2 and high >= groups - max(1, groups // 4)


def move(value, groups, steps, far):
    pairs = [
        (source, target)
        for source, target in shift_pairs(2 * groups, 2, steps)
        if far or not is_far(groups, source // 2, target // 2)
    ]
    return lax.ppermute(value, "ctx", pairs) if pairs else jnp.zeros_like(value)


def plan_kernel(shape, places, new_ref, prior_ref, at_ref, plan_ref, far_ref):
    groups, chips, rows, cache, step = shape
    device, place = at_ref[0], at_ref[1]
    group, side, chip, core = lax.div(device, 2), lax.rem(device, 2), lax.div(place, 2), lax.rem(place, 2)
    table = request_table(new_ref, prior_ref)

    def rows_before(row):
        block = lax.div(row, rows)
        odd, inside = lax.rem(block, 2), lax.rem(row, rows)
        return lax.div(block, 2) * rows + jnp.where(odd == side, inside, jnp.where(odd == 1, rows, 0))

    for request, (row, key, ahead, row_end, _) in enumerate(table):
        plan_ref[places["first_key"] + request] = key
        plan_ref[places["ahead"] + request] = ahead
        plan_ref[places["begin"] + request] = rows_before(row)
        plan_ref[places["end"] + request] = rows_before(row_end)
    spans = [
        (key_range(table, jnp.int32(2 * rows * at))[0], key_range(table, jnp.int32(2 * rows * (at + 1) - 1))[1])
        for at in range(groups)
    ]
    needed = jnp.int32(0)
    for source in range(groups):
        for target in range(groups):
            if is_far(groups, source, target):
                first, last = spans[source]
                meet = (first < 2 * cache * (target + 1)) & (last >= 2 * cache * target)
                needed = jnp.where(meet, 1, needed)
    far_ref[0] = needed
    plan_ref[places["side"]] = side
    for steps in range(groups):
        plan_ref[places["groups"] + steps] = lax.rem(group + (groups - steps), groups)
        there = jnp.int32(1)
        for at in range(groups):
            if is_far(groups, (at + steps) % groups, at):
                there = jnp.where(group == at, needed, there)
        plan_ref[places["there"] + steps] = there
    other = (device + 1 - 2 * side) * cache
    half = cache // 2
    stretches = [(0, device * cache, cache), (cache, other + core * half, half), (cache + half, other + (1 - core) * half, half)]
    for part, (left, key, count) in enumerate(stretches):
        plan_ref[places["lefts"] + part] = jnp.int32(left)
        plan_ref[places["keys"] + part] = key
        plan_ref[places["steps"] + part] = jnp.int32(count // step)
    for at in range(2 * chips):
        own = core if at < chips else 1 - core
        plan_ref[places["from"] + at] = lax.rem(chip + (chips - at % chips), chips) * 2 + own


def make_plan(shape, new_counts, prior_lengths, at):
    groups, chips = shape[:2]
    requests = new_counts.shape[0]
    sizes = dict(first_key=requests, ahead=requests, begin=requests, end=requests, side=1)
    sizes.update(groups=groups, there=groups, lefts=3, keys=3, steps=3)
    sizes["from"] = 2 * chips
    places, total = {}, 0
    for name, size in sizes.items():
        places[name] = total
        total += size
    plan, far = pl.pallas_call(
        functools.partial(plan_kernel, shape, dict(places)),
        out_shape=(jax.ShapeDtypeStruct((total,), jnp.int32), jax.ShapeDtypeStruct((1,), jnp.int32)),
        in_specs=[SMEM] * 3,
        out_specs=(SMEM, SMEM),
        name="plan",
    )(new_counts, prior_lengths, at)
    return places, plan, far


def body(queries, keys, values, w_out, new_counts, prior_lengths):
    ctx_count, head_count = lax.axis_size("ctx"), lax.axis_size("head")
    rows = queries.shape[0]
    cache = keys.shape[0]
    groups, chips = ctx_count // 2, head_count // 2
    at = jnp.stack([lax.axis_index("ctx"), lax.axis_index("head")]).astype(jnp.int32)
    shape = (groups, chips, rows, cache, min(KEY_TILE, cache // 2))
    places, plan, far = make_plan(shape, new_counts, prior_lengths, at)
    requests = new_counts.shape[0]
    return lax.cond(
        far[0] == 1,
        functools.partial(attend_and_project, places, requests, True),
        functools.partial(attend_and_project, places, requests, False),
        *(queries, keys, values, w_out, plan),
    )


def attend_and_project(places, requests, far, queries, keys, values, w_out, plan):
    ctx_count, head_count = lax.axis_size("ctx"), lax.axis_size("head")
    rows = queries.shape[0]
    cache, width = keys.shape
    heads = queries.shape[1] // width
    groups, chips, half = ctx_count // 2, head_count // 2, cache // 2
    core = lax.axis_index("head") % 2

    blocks = [move(queries, groups, steps, far) for steps in range(1, groups)]

    mine = [lax.dynamic_slice_in_dim(array, core * half, half, axis=0) for array in (keys, values)]
    got = lax.ppermute(jnp.concatenate(mine, axis=1), "ctx", swap_pairs(ctx_count))
    all_keys, beside, own_norm, near_w = prepare(keys, values, w_out)
    stack, query_norm = stack_queries(places, plan, [queries] + blocks, width)
    got, query_norm, own_norm = lax.optimization_barrier((got, query_norm, own_norm))
    rest = lax.ppermute(got, "head", swap_pairs(head_count))
    all_keys, beside, key_norm = join(got, rest, own_norm, all_keys, beside)

    parts = 2 if heads % 2 == 0 else 1
    few = heads // parts
    back = []
    for part in range(parts):
        sent = attend(
            places, plan, (key_norm, query_norm), stack, all_keys, beside, (groups, rows, requests), part * few, few
        )
        back.append([sent[0]] + [move(sent[steps], groups, groups - steps, far) for steps in range(1, groups)])
    mixed, pieces, token = None, [], jnp.zeros((1,), jnp.int32)
    for part, arrived in enumerate(back):
        arrived, pieces = lax.optimization_barrier((arrived, pieces))
        attended = merge(places, plan, arrived, rows, few)
        away = [lax.ppermute(attended, "head", shift_pairs(head_count, 2, steps)) for steps in range(1, chips)]
        pair = lax.ppermute(attended, "head", swap_pairs(head_count))
        if part:
            mixed, token = project(places, plan, pieces, parts, part - 1, mixed, near_w)
            away, token = lax.optimization_barrier((away, token))
        pieces = [attended] + away + [pair] + [lax.ppermute(piece, "head", swap_pairs(head_count)) for piece in away]
    mixed, _ = project(places, plan, pieces, parts, parts - 1, mixed, near_w)
    return mixed


def solution(mesh):
    return jax.shard_map(
        body,
        mesh=mesh,
        in_specs=(P("ctx", "head"), P("ctx", None), P("ctx", None), P(None, "head"), P(), P()),
        out_specs=P("ctx", "head"),
        check_vma=False,
    )
```

```python
import functools
import math

import jax
import jax.numpy as jnp
from jax import lax
from jax.experimental import pallas as pl
from jax.experimental.pallas import tpu as pltpu
from jax.sharding import PartitionSpec as P

NEG = -1e30
CALM = 60.0
KEY_TILE = 512
FEW_ROWS = 64
SIDE = 16
LANES = 128
MIB = 1024 * 1024
SMEM = pl.BlockSpec(memory_space=pltpu.SMEM)
VMEM = pl.BlockSpec(memory_space=pltpu.VMEM)
HBM = pl.BlockSpec(memory_space=pltpu.HBM)


def lengths(rows):
    wide = rows.astype(jnp.float32)
    return jnp.sum(wide * wide, axis=1, keepdims=True)


def fill(parts, keys_ref, beside_ref):
    width = keys_ref.shape[1]
    longest = jnp.zeros((min(KEY_TILE, parts[0][0].shape[0]), 1), jnp.float32)
    for from_keys, from_values, done in parts:
        step = min(KEY_TILE, from_keys.shape[0])

        def turn(at, longest, from_keys=from_keys, from_values=from_values, done=done, step=step):
            here = pl.ds(pl.multiple_of(at * step, step), step)
            there = pl.ds(pl.multiple_of(done + at * step, step), step)
            keys = from_keys[here, :]
            keys_ref[there, :] = keys
            beside_ref[there, :width] = from_values[here, :]
            beside_ref[there, width:] = jnp.ones((step, width), jnp.bfloat16)
            return jnp.maximum(longest, lengths(keys))

        longest = lax.fori_loop(0, from_keys.shape[0] // step, turn, longest)
    return jnp.max(longest)


def prepare_kernel(keys_ref, values_ref, far_w, all_keys, beside_ref, longest_ref, near_w, sem):
    fetch = pltpu.make_async_copy(far_w, near_w, sem)
    fetch.start()
    longest_ref[0] = fill([(keys_ref, values_ref, 0)], all_keys, beside_ref)
    fetch.wait()


def prepare(keys, values, w_out):
    cache, width = keys.shape
    return pl.pallas_call(
        prepare_kernel,
        out_shape=(
            pltpu.VMEM((2 * cache, width), jnp.bfloat16),
            pltpu.VMEM((2 * cache, 2 * width), jnp.bfloat16),
            jax.ShapeDtypeStruct((1,), jnp.float32),
            pltpu.VMEM(w_out.shape, w_out.dtype),
        ),
        in_specs=[VMEM, VMEM, HBM],
        out_specs=(VMEM, VMEM, SMEM, VMEM),
        scratch_shapes=[pltpu.SemaphoreType.DMA],
        compiler_params=pltpu.CompilerParams(vmem_limit_bytes=4 * MIB),
        name="prepare",
    )(keys, values, pltpu.with_memory_space_constraint(w_out, pltpu.HBM))


def join_kernel(got_ref, rest_ref, own_ref, keys_in, beside_in, all_keys, beside_ref, longest_ref):
    del keys_in, beside_in
    half, width = got_ref.shape[0], all_keys.shape[1]
    parts = [
        (ref.at[:, :width], ref.at[:, width:], 2 * half + at * half) for at, ref in enumerate((got_ref, rest_ref))
    ]
    longest_ref[0] = jnp.maximum(own_ref[0], fill(parts, all_keys, beside_ref))


def join(got, rest, own_longest, all_keys, beside):
    return pl.pallas_call(
        join_kernel,
        out_shape=(
            pltpu.VMEM(all_keys.shape, all_keys.dtype),
            pltpu.VMEM(beside.shape, beside.dtype),
            jax.ShapeDtypeStruct((1,), jnp.float32),
        ),
        in_specs=[VMEM, VMEM, SMEM, VMEM, VMEM],
        out_specs=(VMEM, VMEM, SMEM),
        input_output_aliases={3: 0, 4: 1},
        compiler_params=pltpu.CompilerParams(vmem_limit_bytes=4 * MIB),
        name="join",
    )(got, rest, own_longest, all_keys, beside)


def stack_kernel(slots, group_at, width, plan_ref, *refs):
    q_refs, (stack_ref, longest_ref, q_all, sems) = refs[:slots], refs[slots:]
    rows = q_refs[0].shape[0]
    heads = q_refs[0].shape[1] // width
    local = slots * rows
    copies = [pltpu.make_async_copy(q_ref, q_all.at[slot], sems.at[slot]) for slot, q_ref in enumerate(q_refs)]
    for copy in copies:
        copy.start()
    longest = jnp.zeros((rows, 1), jnp.float32)
    for slot, copy in enumerate(copies):
        copy.wait()
        start = plan_ref[group_at + slot] * rows
        for head in range(heads):
            part = q_all[slot, :, head * width:(head + 1) * width]
            stack_ref[pl.ds(pl.multiple_of(head * local + start, rows), rows), :] = part
            longest = jnp.maximum(longest, lengths(part))
    longest_ref[0] = jnp.max(longest)


def stack_queries(places, plan, queries, width):
    slots, (rows, wide) = len(queries), queries[0].shape
    return pl.pallas_call(
        functools.partial(stack_kernel, slots, places["groups"], width),
        out_shape=(
            pltpu.VMEM((slots * rows * (wide // width), width), jnp.bfloat16),
            jax.ShapeDtypeStruct((1,), jnp.float32),
        ),
        in_specs=[SMEM] + [HBM] * slots,
        out_specs=(VMEM, SMEM),
        scratch_shapes=[pltpu.VMEM((slots, rows, wide), jnp.bfloat16), pltpu.SemaphoreType.DMA((slots,))],
        compiler_params=pltpu.CompilerParams(vmem_limit_bytes=4 * MIB),
        name="stack",
    )(plan, *queries)


def request_table(new_ref, prior_ref):
    table = []
    row, key = jnp.int32(0), jnp.int32(0)
    for request in range(new_ref.shape[0]):
        new, prior = new_ref[request], prior_ref[request]
        table.append((row, key, key + prior - row, row + new, key + new + prior))
        row, key = row + new, key + new + prior
    return table


def key_range(table, row):
    first, shift = table[0][1], table[0][2]
    for start, key, ahead, _, _ in table[1:]:
        own = row >= start
        first = jnp.where(own, key, first)
        shift = jnp.where(own, ahead, shift)
    return first, row + shift


def attend_kernel(shape, places, first_head, heads, *refs):
    groups, rows, requests, many = shape
    plan_ref, key_norm_ref, query_norm_ref, stack_ref, keys_ref, beside_ref = refs[:6]
    out_refs = refs[6:6 + groups]
    sums, tops, chunk_q, chunk_sum, chunk_top = refs[6 + groups:]
    width = keys_ref.shape[1]
    local = groups * rows
    step = min(KEY_TILE, keys_ref.shape[0] // 4)
    scale = width ** (-0.5)
    factor = scale * math.log2(math.e)
    calm = key_norm_ref[0] * query_norm_ref[0] * (scale * scale) <= CALM * CALM
    side = plan_ref[places["side"]]

    def clear(at, carry):
        sums[pl.ds(pl.multiple_of(at * rows, rows), rows), :] = jnp.zeros((rows, 2 * width), jnp.float32)
        return carry

    lax.fori_loop(0, heads * groups, clear, 0)

    def global_row(place):
        whole = place + side * rows
        for group in range(1, groups):
            whole = whole + jnp.where(place >= group * rows, rows, 0)
        return whole

    def one_chunk(count, online, request, begin, end, start):
        first_key = plan_ref[places["first_key"] + request]
        ahead = plan_ref[places["ahead"] + request]
        start = pl.multiple_of(start, SIDE)
        low_key, high_key = global_row(begin) + ahead, global_row(end - 1) + ahead
        total = heads * count
        for head in range(heads):
            chunk_q[head * count:(head + 1) * count, :] = stack_ref[
                pl.ds(pl.multiple_of((first_head + head) * local + start, SIDE), count), :
            ]
        chunk_sum[:total, :] = jnp.zeros((total, 2 * width), jnp.float32)
        if online:
            chunk_top[:total, :] = jnp.full((total, width), NEG, jnp.float32)
        place = start + lax.broadcasted_iota(jnp.int32, (count, 1), 0)
        last = global_row(place) + ahead

        def scores(part, left):
            return lax.dot_general(
                chunk_q[part, :], keys_ref[pl.ds(left, step), :], (((1,), (1,)), ((), ())),
                preferred_element_type=jnp.float32,
            )

        def add(left, weights):
            return jnp.dot(
                weights.astype(jnp.bfloat16), beside_ref[pl.ds(left, step), :], preferred_element_type=jnp.float32
            )

        def one_step(left, key):
            def allowed():
                index = key + lax.broadcasted_iota(jnp.int32, (count, step), 1)
                return (index >= first_key) & (index <= last)

            if online:
                mask = allowed()

                def one_head(head, carry):
                    part = pl.ds(pl.multiple_of(head * count, count), count)
                    score = jnp.where(mask, scores(part, left) * factor, NEG)
                    old = chunk_top[part, :]
                    new = jnp.maximum(old, jnp.ceil(jnp.max(score, axis=1, keepdims=True)))
                    weights = jnp.where(mask, jnp.exp2(score - new[:, :1]), 0.0)
                    shrink = jnp.exp2(old - new)
                    chunk_sum[part, :width] = chunk_sum[part, :width] * shrink
                    chunk_sum[part, width:] = chunk_sum[part, width:] * shrink
                    chunk_sum[part, :] += add(left, weights)
                    chunk_top[part, :] = new
                    return carry

                lax.fori_loop(0, heads, one_head, 0)
                return

            plain = (key >= first_key) & (key + step - 1 <= low_key)

            @pl.when(plain)
            def _():
                chunk_sum[:total, :] += add(left, jnp.exp(scores(pl.ds(0, total), left) * scale))

            @pl.when(jnp.logical_not(plain))
            def _():
                mask = allowed()
                weights = jnp.exp(scores(pl.ds(0, total), left) * scale)
                weights = jnp.concatenate([
                    jnp.where(mask, weights[head * count:(head + 1) * count, :], 0.0) for head in range(heads)
                ])
                chunk_sum[:total, :] += add(left, weights)

        def one_part(part, carry):
            left, key, steps = (plan_ref[places[name] + part] for name in ("lefts", "keys", "steps"))
            low = jnp.clip(lax.div(first_key - key, step), 0, steps)
            high = jnp.clip(lax.div(high_key - key + step, step), 0, steps)

            def turn(at, carry):
                one_step(pl.multiple_of(left + at * step, step), key + at * step)
                return carry

            lax.fori_loop(low, high, turn, 0)
            return carry

        lax.fori_loop(0, 3, one_part, 0)
        own = (place >= begin) & (place < end)
        for head in range(heads):
            here = pl.ds(pl.multiple_of(head * local + start, SIDE), count)
            part = slice(head * count, (head + 1) * count)
            sums[here, :] += jnp.where(own, chunk_sum[part, :], 0.0)
            if online:
                tops[here, :] = jnp.where(own, chunk_top[part, :], tops[here, :])

    def all_chunks(count, online, request, begin, end):
        aligned = lax.div(begin, SIDE) * SIDE

        def turn(at, carry):
            from_row = aligned + at * count
            one_chunk(
                count,
                online,
                request,
                jnp.maximum(begin, from_row),
                jnp.minimum(end, from_row + count),
                jnp.minimum(from_row, local - count),
            )
            return carry

        lax.fori_loop(0, lax.div(end - aligned + (count - 1), count), turn, 0)

    few = min(FEW_ROWS, local)

    def one_request(request, carry):
        begin, end = plan_ref[places["begin"] + request], plan_ref[places["end"] + request]
        large = end - lax.div(begin, SIDE) * SIDE > 2 * few

        @pl.when((end > begin) & calm & large)
        def _():
            all_chunks(many, False, request, begin, end)

        @pl.when((end > begin) & calm & jnp.logical_not(large))
        def _():
            all_chunks(few, False, request, begin, end)

        @pl.when((end > begin) & jnp.logical_not(calm))
        def _():
            all_chunks(few, True, request, begin, end)

        return carry

    lax.fori_loop(0, requests, one_request, 0)

    lane = lax.broadcasted_iota(jnp.int32, (LANES, LANES), 1)
    for slot, out_ref in enumerate(out_refs):
        start = plan_ref[places["groups"] + slot] * rows
        if heads * width > rows:
            out_ref[rows:, :] = jnp.zeros((out_ref.shape[0] - rows, heads * width), jnp.bfloat16)
        for at in range(0, rows, LANES):
            terms = jnp.zeros((LANES, LANES), jnp.float32)
            for head in range(heads):
                here = pl.ds(pl.multiple_of(head * local + start + at, LANES), LANES)
                out_ref[at:at + LANES, head * width:(head + 1) * width] = sums[here, :width].astype(jnp.bfloat16)
                weight = sums[here, width:]
                top = jnp.where(weight > 0.0, jnp.where(calm, 0.0, tops[here, :]), NEG)
                for term, value in enumerate((weight, top)):
                    high = value.astype(jnp.bfloat16).astype(jnp.float32)
                    terms = jnp.where(lane == 2 * term * heads + head, high, terms)
                    terms = jnp.where(lane == (2 * term + 1) * heads + head, value - high, terms)
            fold, column = at // (heads * width), at % (heads * width)
            out_ref[rows + fold * SIDE:rows + (fold + 1) * SIDE, column:column + LANES] = terms.T[:SIDE, :].astype(
                jnp.bfloat16
            )


def side_rows(rows, wide):
    return SIDE * max(1, rows // wide)


def attend(places, plan, norms, stack, keys, beside, shape, first_head, heads):
    groups, rows, _ = shape
    width = keys.shape[1]
    local, wide = groups * rows, heads * width
    many = min(2 * rows + SIDE, local)
    return pl.pallas_call(
        functools.partial(attend_kernel, (*shape, many), dict(places), first_head, heads),
        out_shape=(jax.ShapeDtypeStruct((rows + side_rows(rows, wide), wide), jnp.bfloat16),) * groups,
        in_specs=[SMEM] * 3 + [VMEM] * 3,
        out_specs=(VMEM,) * groups,
        scratch_shapes=[
            pltpu.VMEM((heads * local, 2 * width), jnp.float32),
            pltpu.VMEM((heads * local, width), jnp.float32),
            pltpu.VMEM((heads * many, width), jnp.bfloat16),
            pltpu.VMEM((heads * many, 2 * width), jnp.float32),
            pltpu.VMEM((heads * min(FEW_ROWS, local), width), jnp.float32),
        ],
        compiler_params=pltpu.CompilerParams(vmem_limit_bytes=20 * MIB),
        cost_estimate=pl.CostEstimate(
            flops=local * heads * keys.shape[0] * width * 12, bytes_accessed=8 * MIB, transcendentals=0
        ),
        name="attend",
    )(plan, *norms, stack, keys, beside)


def merge_kernel(heads, there_at, plan_ref, *refs):
    parts, out_ref = refs[:-1], refs[-1]
    rows = out_ref.shape[0]
    width = out_ref.shape[1] // heads
    logs = [
        jnp.where(
            plan_ref[there_at + at] == 1,
            jnp.concatenate([
                part[row:row + SIDE, :min(rows, out_ref.shape[1])] for row in range(rows, part.shape[0], SIDE)
            ], axis=1).astype(jnp.float32),
            0.0,
        )
        for at, part in enumerate(parts)
    ]
    spare = LANES - SIDE * len(parts)
    if spare:
        logs.append(jnp.zeros((spare, rows), jnp.float32))
    terms = jnp.concatenate(logs, axis=0).T
    total = terms + pltpu.roll(terms, LANES - heads, 1)
    top = pltpu.roll(terms, LANES - 2 * heads, 1) + pltpu.roll(terms, LANES - 3 * heads, 1)
    lane = lax.broadcasted_iota(jnp.int32, (rows, LANES), 1)
    used = (lax.rem(lane, SIDE) < heads) & (lane < SIDE * len(parts)) & (total > 0.0)
    top = jnp.where(used, top, NEG)
    biggest = top
    for shift in (16, 32, 64):
        biggest = jnp.maximum(biggest, pltpu.roll(biggest, shift, 1))
    share = jnp.where(used, jnp.exp2(top - biggest), 0.0)
    weight = share * jnp.where(used, total, 0.0)
    for shift in (16, 32, 64):
        weight = weight + pltpu.roll(weight, shift, 1)
    share = share / weight
    for head in range(heads):
        own = slice(head * width, (head + 1) * width)
        mixed = jnp.zeros((rows, width), jnp.float32)
        for at, part in enumerate(parts):
            lane_at = at * SIDE + head
            mixed = mixed + part[:rows, own].astype(jnp.float32) * share[:, lane_at:lane_at + 1]
        out_ref[:, own] = mixed.astype(out_ref.dtype)


def merge(places, plan, parts, rows, heads):
    return pl.pallas_call(
        functools.partial(merge_kernel, heads, places["there"]),
        out_shape=jax.ShapeDtypeStruct((rows, parts[0].shape[1]), jnp.bfloat16),
        in_specs=[SMEM] + [VMEM] * len(parts),
        out_specs=VMEM,
        compiler_params=pltpu.CompilerParams(vmem_limit_bytes=12 * MIB),
        name="merge",
    )(plan, *parts)


def project_kernel(pieces, parts, part, from_at, plan_ref, *refs):
    refs = list(refs)
    before_ref = refs.pop(0) if part else None
    piece_refs, (w_ref, out_ref, token_ref) = refs[:pieces], refs[pieces:]
    token_ref[0] = jnp.int32(part)
    deep = piece_refs[0].shape[1]
    block = out_ref.shape[1]
    left = pl.multiple_of(pl.program_id(0) * block, block)
    total = None
    for at, piece_ref in enumerate(piece_refs):
        own = pl.multiple_of((plan_ref[from_at + at] * parts + part) * deep, deep)
        term = jnp.dot(
            piece_ref[...], w_ref[pl.ds(own, deep), pl.ds(left, block)], preferred_element_type=jnp.float32
        )
        total = term if total is None else total + term
    if part:
        total = total + before_ref[:, pl.ds(left, block)]
    out_ref[...] = total.astype(out_ref.dtype)


def project(places, plan, pieces, parts, part, before, w_out):
    rows, deep = pieces[0].shape
    depth, wide = w_out.shape
    block = min(1024, wide)
    last = part == parts - 1
    return pl.pallas_call(
        functools.partial(project_kernel, len(pieces), parts, part, places["from"]),
        out_shape=(
            pltpu.HBM((rows, wide), jnp.bfloat16) if last else pltpu.VMEM((rows, wide), jnp.float32),
            jax.ShapeDtypeStruct((1,), jnp.int32),
        ),
        grid=(wide // block,),
        in_specs=[SMEM] + [VMEM] * (bool(part) + len(pieces) + 1),
        out_specs=(pl.BlockSpec((rows, block), lambda at: (0, at)), SMEM),
        compiler_params=pltpu.CompilerParams(vmem_limit_bytes=16 * MIB),
        cost_estimate=pl.CostEstimate(
            flops=2 * rows * depth * wide // parts, bytes_accessed=2 * depth * wide // parts, transcendentals=0
        ),
        name="project",
    )(plan, *([before] if part else []), *pieces, w_out)


def shift_pairs(count, stride, steps):
    groups = count // stride
    return [
        (group * stride + member, (group + steps) % groups * stride + member)
        for group in range(groups)
        for member in range(stride)
    ]


def swap_pairs(count):
    return [(at, at ^ 1) for at in range(count)]


def is_far(groups, one, two):
    low, high = min(one, two), max(one, two)
    return low < groups // 2 and high >= groups - max(1, groups // 4)


def move(value, groups, steps, far):
    pairs = [
        (source, target)
        for source, target in shift_pairs(2 * groups, 2, steps)
        if far or not is_far(groups, source // 2, target // 2)
    ]
    return lax.ppermute(value, "ctx", pairs) if pairs else jnp.zeros_like(value)


def plan_kernel(shape, places, new_ref, prior_ref, at_ref, plan_ref, far_ref):
    groups, chips, rows, cache, step = shape
    device, place = at_ref[0], at_ref[1]
    group, side, chip, core = lax.div(device, 2), lax.rem(device, 2), lax.div(place, 2), lax.rem(place, 2)
    table = request_table(new_ref, prior_ref)

    def rows_before(row):
        block = lax.div(row, rows)
        odd, inside = lax.rem(block, 2), lax.rem(row, rows)
        return lax.div(block, 2) * rows + jnp.where(odd == side, inside, jnp.where(odd == 1, rows, 0))

    for request, (row, key, ahead, row_end, _) in enumerate(table):
        plan_ref[places["first_key"] + request] = key
        plan_ref[places["ahead"] + request] = ahead
        plan_ref[places["begin"] + request] = rows_before(row)
        plan_ref[places["end"] + request] = rows_before(row_end)
    spans = [
        (key_range(table, jnp.int32(2 * rows * at))[0], key_range(table, jnp.int32(2 * rows * (at + 1) - 1))[1])
        for at in range(groups)
    ]
    needed = jnp.int32(0)
    for source in range(groups):
        for target in range(groups):
            if is_far(groups, source, target):
                first, last = spans[source]
                meet = (first < 2 * cache * (target + 1)) & (last >= 2 * cache * target)
                needed = jnp.where(meet, 1, needed)
    far_ref[0] = needed
    plan_ref[places["side"]] = side
    for steps in range(groups):
        plan_ref[places["groups"] + steps] = lax.rem(group + (groups - steps), groups)
        there = jnp.int32(1)
        for at in range(groups):
            if is_far(groups, (at + steps) % groups, at):
                there = jnp.where(group == at, needed, there)
        plan_ref[places["there"] + steps] = there
    other = (device + 1 - 2 * side) * cache
    half = cache // 2
    stretches = [(0, device * cache, cache), (cache, other + core * half, half), (cache + half, other + (1 - core) * half, half)]
    for part, (left, key, count) in enumerate(stretches):
        plan_ref[places["lefts"] + part] = jnp.int32(left)
        plan_ref[places["keys"] + part] = key
        plan_ref[places["steps"] + part] = jnp.int32(count // step)
    for at in range(2 * chips):
        own = core if at < chips else 1 - core
        plan_ref[places["from"] + at] = lax.rem(chip + (chips - at % chips), chips) * 2 + own


def make_plan(shape, new_counts, prior_lengths, at):
    groups, chips = shape[:2]
    requests = new_counts.shape[0]
    sizes = dict(first_key=requests, ahead=requests, begin=requests, end=requests, side=1)
    sizes.update(groups=groups, there=groups, lefts=3, keys=3, steps=3)
    sizes["from"] = 2 * chips
    places, total = {}, 0
    for name, size in sizes.items():
        places[name] = total
        total += size
    plan, far = pl.pallas_call(
        functools.partial(plan_kernel, shape, dict(places)),
        out_shape=(jax.ShapeDtypeStruct((total,), jnp.int32), jax.ShapeDtypeStruct((1,), jnp.int32)),
        in_specs=[SMEM] * 3,
        out_specs=(SMEM, SMEM),
        name="plan",
    )(new_counts, prior_lengths, at)
    return places, plan, far


def body(queries, keys, values, w_out, new_counts, prior_lengths):
    ctx_count, head_count = lax.axis_size("ctx"), lax.axis_size("head")
    rows = queries.shape[0]
    cache = keys.shape[0]
    groups, chips = ctx_count // 2, head_count // 2
    at = jnp.stack([lax.axis_index("ctx"), lax.axis_index("head")]).astype(jnp.int32)
    shape = (groups, chips, rows, cache, min(KEY_TILE, cache // 2))
    places, plan, far = make_plan(shape, new_counts, prior_lengths, at)
    requests = new_counts.shape[0]
    return lax.cond(
        far[0] == 1,
        functools.partial(attend_and_project, places, requests, True),
        functools.partial(attend_and_project, places, requests, False),
        *(queries, keys, values, w_out, plan),
    )


def attend_and_project(places, requests, far, queries, keys, values, w_out, plan):
    ctx_count, head_count = lax.axis_size("ctx"), lax.axis_size("head")
    rows = queries.shape[0]
    cache, width = keys.shape
    heads = queries.shape[1] // width
    groups, chips, half = ctx_count // 2, head_count // 2, cache // 2
    core = lax.axis_index("head") % 2

    blocks = [move(queries, groups, steps, far) for steps in range(1, groups)]

    mine = [lax.dynamic_slice_in_dim(array, core * half, half, axis=0) for array in (keys, values)]
    got = lax.ppermute(jnp.concatenate(mine, axis=1), "ctx", swap_pairs(ctx_count))
    all_keys, beside, own_norm, near_w = prepare(keys, values, w_out)
    stack, query_norm = stack_queries(places, plan, [queries] + blocks, width)
    got, query_norm, own_norm = lax.optimization_barrier((got, query_norm, own_norm))
    rest = lax.ppermute(got, "head", swap_pairs(head_count))
    all_keys, beside, key_norm = join(got, rest, own_norm, all_keys, beside)

    parts = 2 if heads % 2 == 0 else 1
    few = heads // parts
    back = []
    for part in range(parts):
        sent = attend(
            places, plan, (key_norm, query_norm), stack, all_keys, beside, (groups, rows, requests), part * few, few
        )
        back.append([sent[0]] + [move(sent[steps], groups, groups - steps, far) for steps in range(1, groups)])
    back[0], back[-1][0] = lax.optimization_barrier((back[0], back[-1][0]))
    mixed, pieces, token = None, [], jnp.zeros((1,), jnp.int32)
    for part, arrived in enumerate(back):
        arrived, pieces = lax.optimization_barrier((arrived, pieces))
        attended = merge(places, plan, arrived, rows, few)
        away = [lax.ppermute(attended, "head", shift_pairs(head_count, 2, steps)) for steps in range(1, chips)]
        pair = lax.ppermute(attended, "head", swap_pairs(head_count))
        if part:
            mixed, token = project(places, plan, pieces, parts, part - 1, mixed, near_w)
            away, token = lax.optimization_barrier((away, token))
        pieces = [attended] + away + [pair] + [lax.ppermute(piece, "head", swap_pairs(head_count)) for piece in away]
    mixed, _ = project(places, plan, pieces, parts, parts - 1, mixed, near_w)
    return mixed


def solution(mesh):
    return jax.shard_map(
        body,
        mesh=mesh,
        in_specs=(P("ctx", "head"), P("ctx", None), P("ctx", None), P(None, "head"), P(), P()),
        out_specs=P("ctx", "head"),
        check_vma=False,
    )
```

```python
import functools
import math

import jax
import jax.numpy as jnp
from jax import lax
from jax.experimental import pallas as pl
from jax.experimental.pallas import tpu as pltpu
from jax.sharding import PartitionSpec as P

NEG = -1e30
CALM = 60.0
KEY_TILE = 512
FEW_ROWS = 64
SIDE = 16
LANES = 128
MIB = 1024 * 1024
SMEM = pl.BlockSpec(memory_space=pltpu.SMEM)
VMEM = pl.BlockSpec(memory_space=pltpu.VMEM)
HBM = pl.BlockSpec(memory_space=pltpu.HBM)


def lengths(rows):
    wide = rows.astype(jnp.float32)
    return jnp.sum(wide * wide, axis=1, keepdims=True)


def fill(from_keys, from_values, done, keys_ref, beside_ref):
    width = keys_ref.shape[1]
    count = from_keys[0].shape[0]
    step = min(KEY_TILE, count)

    def add_up(sources, here):
        total = sources[0][here, :]
        for source in sources[1:]:
            total = total + source[here, :]
        return total

    def turn(at, longest):
        here = pl.ds(pl.multiple_of(at * step, step), step)
        there = pl.ds(pl.multiple_of(done + at * step, step), step)
        keys, values = add_up(from_keys, here), add_up(from_values, here)
        keys_ref[there, :] = keys
        beside_ref[there, :width] = values
        beside_ref[there, width:] = jnp.ones((step, width), jnp.bfloat16)
        return jnp.maximum(longest, lengths(keys))

    return jnp.max(lax.fori_loop(0, count // step, turn, jnp.zeros((step, 1), jnp.float32)))


def prepare_kernel(keys_ref, values_ref, far_w, all_keys, beside_ref, longest_ref, near_w, sem):
    fetch = pltpu.make_async_copy(far_w, near_w, sem)
    fetch.start()
    longest_ref[0] = fill([keys_ref], [values_ref], 0, all_keys, beside_ref)
    fetch.wait()


def prepare(keys, values, w_out):
    cache, width = keys.shape
    return pl.pallas_call(
        prepare_kernel,
        out_shape=(
            pltpu.VMEM((2 * cache, width), jnp.bfloat16),
            pltpu.VMEM((2 * cache, 2 * width), jnp.bfloat16),
            jax.ShapeDtypeStruct((1,), jnp.float32),
            pltpu.VMEM(w_out.shape, w_out.dtype),
        ),
        in_specs=[VMEM, VMEM, HBM],
        out_specs=(VMEM, VMEM, SMEM, VMEM),
        scratch_shapes=[pltpu.SemaphoreType.DMA],
        compiler_params=pltpu.CompilerParams(vmem_limit_bytes=4 * MIB),
        name="prepare",
    )(keys, values, pltpu.with_memory_space_constraint(w_out, pltpu.HBM))


def stack_kernel(slots, group_at, width, plan_ref, *refs):
    q_refs, (stack_ref, longest_ref, q_all, sems) = refs[:slots], refs[slots:]
    rows = q_refs[0].shape[0]
    heads = q_refs[0].shape[1] // width
    local = slots * rows
    copies = [pltpu.make_async_copy(q_ref, q_all.at[slot], sems.at[slot]) for slot, q_ref in enumerate(q_refs)]
    for copy in copies:
        copy.start()
    longest = jnp.zeros((rows, 1), jnp.float32)
    for slot, copy in enumerate(copies):
        copy.wait()
        start = plan_ref[group_at + slot] * rows
        for head in range(heads):
            part = q_all[slot, :, head * width:(head + 1) * width]
            stack_ref[pl.ds(pl.multiple_of(head * local + start, rows), rows), :] = part
            longest = jnp.maximum(longest, lengths(part))
    longest_ref[0] = jnp.max(longest)


def stack_queries(places, plan, queries, width):
    slots, (rows, wide) = len(queries), queries[0].shape
    return pl.pallas_call(
        functools.partial(stack_kernel, slots, places["groups"], width),
        out_shape=(
            pltpu.VMEM((slots * rows * (wide // width), width), jnp.bfloat16),
            jax.ShapeDtypeStruct((1,), jnp.float32),
        ),
        in_specs=[SMEM] + [HBM] * slots,
        out_specs=(VMEM, SMEM),
        scratch_shapes=[pltpu.VMEM((slots, rows, wide), jnp.bfloat16), pltpu.SemaphoreType.DMA((slots,))],
        compiler_params=pltpu.CompilerParams(vmem_limit_bytes=4 * MIB),
        name="stack",
    )(plan, *queries)


def request_table(new_ref, prior_ref):
    table = []
    row, key = jnp.int32(0), jnp.int32(0)
    for request in range(new_ref.shape[0]):
        new, prior = new_ref[request], prior_ref[request]
        table.append((row, key, key + prior - row, row + new, key + new + prior))
        row, key = row + new, key + new + prior
    return table


def key_range(table, row):
    first, shift = table[0][1], table[0][2]
    for start, key, ahead, _, _ in table[1:]:
        own = row >= start
        first = jnp.where(own, key, first)
        shift = jnp.where(own, ahead, shift)
    return first, row + shift


def attend_kernel(shape, places, *refs):
    groups, rows, heads, requests = shape
    plan_ref, key_norm_ref, query_norm_ref, stack_ref = refs[:4]
    fetched = refs[4:8]
    keys_ref, beside_ref = refs[10:12]
    out_refs = refs[12:12 + groups]
    sums, tops, chunk_q, chunk_sum, chunk_top, arrived, sems = refs[12 + groups:]
    cache, width = fetched[0].shape
    local = groups * rows
    step = min(KEY_TILE, cache // 2)
    scale = width ** (-0.5)
    factor = scale * math.log2(math.e)
    copies = [pltpu.make_async_copy(ref, arrived.at[at], sems.at[at]) for at, ref in enumerate(fetched)]
    for copy in copies:
        copy.start()
    for copy in copies:
        copy.wait()
    other_norm = fill(
        [arrived.at[0], arrived.at[1]], [arrived.at[2], arrived.at[3]], cache, keys_ref, beside_ref
    )
    key_norm = jnp.maximum(other_norm, key_norm_ref[0])
    calm = key_norm * query_norm_ref[0] * (scale * scale) <= CALM * CALM
    side = plan_ref[places["side"]]

    def clear(at, carry):
        sums[pl.ds(pl.multiple_of(at * rows, rows), rows), :] = jnp.zeros((rows, 2 * width), jnp.float32)
        return carry

    lax.fori_loop(0, heads * groups, clear, 0)

    def global_row(place):
        whole = place + side * rows
        for group in range(1, groups):
            whole = whole + jnp.where(place >= group * rows, rows, 0)
        return whole

    def one_chunk(count, online, request, begin, end, start):
        first_key = plan_ref[places["first_key"] + request]
        ahead = plan_ref[places["ahead"] + request]
        start = pl.multiple_of(start, SIDE)
        low_key, high_key = global_row(begin) + ahead, global_row(end - 1) + ahead
        total = heads * count
        for head in range(heads):
            chunk_q[head * count:(head + 1) * count, :] = stack_ref[
                pl.ds(pl.multiple_of(head * local + start, SIDE), count), :
            ]
        chunk_sum[:total, :] = jnp.zeros((total, 2 * width), jnp.float32)
        if online:
            chunk_top[:total, :] = jnp.full((total, width), NEG, jnp.float32)
        place = start + lax.broadcasted_iota(jnp.int32, (count, 1), 0)
        last = global_row(place) + ahead

        def scores(part, left):
            return lax.dot_general(
                chunk_q[part, :], keys_ref[pl.ds(left, step), :], (((1,), (1,)), ((), ())),
                preferred_element_type=jnp.float32,
            ) * factor

        def add(left, weights):
            return jnp.dot(
                weights.astype(jnp.bfloat16), beside_ref[pl.ds(left, step), :], preferred_element_type=jnp.float32
            )

        def one_step(left, key):
            def allowed():
                index = key + lax.broadcasted_iota(jnp.int32, (count, step), 1)
                return (index >= first_key) & (index <= last)

            if online:
                mask = allowed()

                def one_head(head, carry):
                    part = pl.ds(pl.multiple_of(head * count, count), count)
                    score = jnp.where(mask, scores(part, left), NEG)
                    old = chunk_top[part, :]
                    new = jnp.maximum(old, jnp.ceil(jnp.max(score, axis=1, keepdims=True)))
                    weights = jnp.where(mask, jnp.exp2(score - new[:, :1]), 0.0)
                    shrink = jnp.exp2(old - new)
                    chunk_sum[part, :width] = chunk_sum[part, :width] * shrink
                    chunk_sum[part, width:] = chunk_sum[part, width:] * shrink
                    chunk_sum[part, :] += add(left, weights)
                    chunk_top[part, :] = new
                    return carry

                lax.fori_loop(0, heads, one_head, 0)
                return

            plain = (key >= first_key) & (key + step - 1 <= low_key)

            @pl.when(plain)
            def _():
                chunk_sum[:total, :] += add(left, jnp.exp2(scores(pl.ds(0, total), left)))

            @pl.when(jnp.logical_not(plain))
            def _():
                mask = allowed()
                weights = jnp.exp2(scores(pl.ds(0, total), left))
                weights = jnp.concatenate([
                    jnp.where(mask, weights[head * count:(head + 1) * count, :], 0.0) for head in range(heads)
                ])
                chunk_sum[:total, :] += add(left, weights)

        def one_part(part, carry):
            left, key, steps = (plan_ref[places[name] + part] for name in ("lefts", "keys", "steps"))
            low = jnp.clip(lax.div(first_key - key, step), 0, steps)
            high = jnp.clip(lax.div(high_key - key + step, step), 0, steps)

            def turn(at, carry):
                one_step(pl.multiple_of(left + at * step, step), key + at * step)
                return carry

            lax.fori_loop(low, high, turn, 0)
            return carry

        lax.fori_loop(0, 2, one_part, 0)
        own = (place >= begin) & (place < end)
        for head in range(heads):
            here = pl.ds(pl.multiple_of(head * local + start, SIDE), count)
            part = slice(head * count, (head + 1) * count)
            sums[here, :] += jnp.where(own, chunk_sum[part, :], 0.0)
            if online:
                tops[here, :] = jnp.where(own, chunk_top[part, :], tops[here, :])

    def all_chunks(count, online, request, begin, end):
        aligned = lax.div(begin, SIDE) * SIDE

        def turn(at, carry):
            from_row = aligned + at * count
            one_chunk(
                count,
                online,
                request,
                jnp.maximum(begin, from_row),
                jnp.minimum(end, from_row + count),
                jnp.minimum(from_row, local - count),
            )
            return carry

        lax.fori_loop(0, lax.div(end - aligned + (count - 1), count), turn, 0)

    many, few = min(2 * rows + SIDE, local), min(FEW_ROWS, local)

    def one_request(request, carry):
        begin, end = plan_ref[places["begin"] + request], plan_ref[places["end"] + request]
        large = end - lax.div(begin, SIDE) * SIDE > 2 * few

        @pl.when((end > begin) & calm & large)
        def _():
            all_chunks(many, False, request, begin, end)

        @pl.when((end > begin) & calm & jnp.logical_not(large))
        def _():
            all_chunks(few, False, request, begin, end)

        @pl.when((end > begin) & jnp.logical_not(calm))
        def _():
            all_chunks(few, True, request, begin, end)

        return carry

    lax.fori_loop(0, requests, one_request, 0)

    lane = lax.broadcasted_iota(jnp.int32, (LANES, LANES), 1)
    for slot, out_ref in enumerate(out_refs):
        start = plan_ref[places["groups"] + slot] * rows
        out_ref[rows:, :] = jnp.zeros((SIDE, heads * width), jnp.bfloat16)
        for at in range(0, rows, LANES):
            terms = jnp.zeros((LANES, LANES), jnp.float32)
            for head in range(heads):
                here = pl.ds(pl.multiple_of(head * local + start + at, LANES), LANES)
                out_ref[at:at + LANES, head * width:(head + 1) * width] = sums[here, :width].astype(jnp.bfloat16)
                weight = sums[here, width:]
                top = jnp.where(weight > 0.0, jnp.where(calm, 0.0, tops[here, :]), NEG)
                for term, value in enumerate((weight, top)):
                    high = value.astype(jnp.bfloat16).astype(jnp.float32)
                    terms = jnp.where(lane == 2 * term * heads + head, high, terms)
                    terms = jnp.where(lane == (2 * term + 1) * heads + head, value - high, terms)
            out_ref[rows:, at:at + LANES] = terms.T[:SIDE, :].astype(jnp.bfloat16)


def attend(places, plan, norms, stack, fetched, all_keys, beside, shape):
    groups, rows, heads, _ = shape
    cache, width = fetched[0].shape
    local = groups * rows
    most = heads * min(2 * rows + SIDE, local)
    _, _, *payloads = pl.pallas_call(
        functools.partial(attend_kernel, shape, dict(places)),
        out_shape=(pltpu.VMEM(all_keys.shape, all_keys.dtype), pltpu.VMEM(beside.shape, beside.dtype))
        + (jax.ShapeDtypeStruct((rows + SIDE, heads * width), jnp.bfloat16),) * groups,
        in_specs=[SMEM] * 3 + [VMEM] + [HBM] * 4 + [VMEM] * 2,
        out_specs=(VMEM,) * (groups + 2),
        input_output_aliases={8: 0, 9: 1},
        scratch_shapes=[
            pltpu.VMEM((heads * local, 2 * width), jnp.float32),
            pltpu.VMEM((heads * local, width), jnp.float32),
            pltpu.VMEM((most, width), jnp.bfloat16),
            pltpu.VMEM((most, 2 * width), jnp.float32),
            pltpu.VMEM((heads * min(FEW_ROWS, local), width), jnp.float32),
            pltpu.VMEM((4, cache, width), jnp.bfloat16),
            pltpu.SemaphoreType.DMA((4,)),
        ],
        compiler_params=pltpu.CompilerParams(vmem_limit_bytes=28 * MIB),
        cost_estimate=pl.CostEstimate(
            flops=local * heads * cache * width * 4, bytes_accessed=24 * MIB, transcendentals=0
        ),
        name="attend",
    )(plan, *norms, stack, *fetched, all_keys, beside)
    return payloads


def merge_kernel(heads, there_at, plan_ref, *refs):
    parts, out_ref = refs[:-1], refs[-1]
    rows = out_ref.shape[0]
    width = out_ref.shape[1] // heads
    logs = [
        jnp.where(plan_ref[there_at + at] == 1, part[rows:, :rows].astype(jnp.float32), 0.0) for at, part in enumerate(parts)
    ]
    spare = LANES - SIDE * len(parts)
    if spare:
        logs.append(jnp.zeros((spare, rows), jnp.float32))
    terms = jnp.concatenate(logs, axis=0).T
    total = terms + pltpu.roll(terms, LANES - heads, 1)
    top = pltpu.roll(terms, LANES - 2 * heads, 1) + pltpu.roll(terms, LANES - 3 * heads, 1)
    lane = lax.broadcasted_iota(jnp.int32, (rows, LANES), 1)
    used = (lax.rem(lane, SIDE) < heads) & (lane < SIDE * len(parts)) & (total > 0.0)
    top = jnp.where(used, top, NEG)
    biggest = top
    for shift in (16, 32, 64):
        biggest = jnp.maximum(biggest, pltpu.roll(biggest, shift, 1))
    share = jnp.where(used, jnp.exp2(top - biggest), 0.0)
    weight = share * jnp.where(used, total, 0.0)
    for shift in (16, 32, 64):
        weight = weight + pltpu.roll(weight, shift, 1)
    share = share / weight
    for head in range(heads):
        own = slice(head * width, (head + 1) * width)
        mixed = jnp.zeros((rows, width), jnp.float32)
        for at, part in enumerate(parts):
            lane_at = at * SIDE + head
            mixed = mixed + part[:rows, own].astype(jnp.float32) * share[:, lane_at:lane_at + 1]
        out_ref[:, own] = mixed.astype(out_ref.dtype)


def merge(places, plan, parts, heads):
    rows = parts[0].shape[0] - SIDE
    return pl.pallas_call(
        functools.partial(merge_kernel, heads, places["there"]),
        out_shape=jax.ShapeDtypeStruct((rows, parts[0].shape[1]), jnp.bfloat16),
        in_specs=[SMEM] + [VMEM] * len(parts),
        out_specs=VMEM,
        compiler_params=pltpu.CompilerParams(vmem_limit_bytes=12 * MIB),
        name="merge",
    )(plan, *parts)


def project_kernel(pieces, from_at, plan_ref, *refs):
    w_ref, out_ref, whole = refs[pieces:]
    deep = refs[0].shape[1]
    block = out_ref.shape[1]

    @pl.when(pl.program_id(0) == 0)
    def _():
        for at, piece in enumerate(refs[:pieces]):
            whole[:, pl.ds(pl.multiple_of(plan_ref[from_at + at] * deep, deep), deep)] = piece[...]

    left = pl.multiple_of(pl.program_id(0) * block, block)
    out_ref[...] = jnp.dot(
        whole[...], w_ref[:, pl.ds(left, block)], preferred_element_type=jnp.float32
    ).astype(out_ref.dtype)


def project(places, plan, pieces, w_out):
    rows, deep = pieces[0].shape
    depth, wide = w_out.shape
    block = min(1024, wide)
    return pl.pallas_call(
        functools.partial(project_kernel, len(pieces), places["from"]),
        out_shape=pltpu.HBM((rows, wide), jnp.bfloat16),
        grid=(wide // block,),
        in_specs=[SMEM] + [VMEM] * (len(pieces) + 1),
        out_specs=pl.BlockSpec((rows, block), lambda at: (0, at)),
        scratch_shapes=[pltpu.VMEM((rows, depth), jnp.bfloat16)],
        compiler_params=pltpu.CompilerParams(vmem_limit_bytes=16 * MIB),
        cost_estimate=pl.CostEstimate(
            flops=2 * rows * depth * wide, bytes_accessed=2 * depth * wide, transcendentals=0
        ),
        name="project",
    )(plan, *pieces, w_out)


def shift_pairs(count, stride, steps):
    groups = count // stride
    return [
        (group * stride + member, (group + steps) % groups * stride + member)
        for group in range(groups)
        for member in range(stride)
    ]


def swap_pairs(count):
    return [(at, at ^ 1) for at in range(count)]


def is_far(groups, one, two):
    low, high = min(one, two), max(one, two)
    return low < groups // 2 and high >= groups - max(1, groups // 4)


def move(value, groups, steps, far):
    pairs = [
        (source, target)
        for source, target in shift_pairs(2 * groups, 2, steps)
        if far or not is_far(groups, source // 2, target // 2)
    ]
    return lax.ppermute(value, "ctx", pairs) if pairs else jnp.zeros_like(value)


def plan_kernel(shape, places, new_ref, prior_ref, at_ref, plan_ref, far_ref):
    groups, chips, rows, cache, step = shape
    device, place = at_ref[0], at_ref[1]
    group, side, chip, core = lax.div(device, 2), lax.rem(device, 2), lax.div(place, 2), lax.rem(place, 2)
    table = request_table(new_ref, prior_ref)

    def rows_before(row):
        block = lax.div(row, rows)
        odd, inside = lax.rem(block, 2), lax.rem(row, rows)
        return lax.div(block, 2) * rows + jnp.where(odd == side, inside, jnp.where(odd == 1, rows, 0))

    for request, (row, key, ahead, row_end, _) in enumerate(table):
        plan_ref[places["first_key"] + request] = key
        plan_ref[places["ahead"] + request] = ahead
        plan_ref[places["begin"] + request] = rows_before(row)
        plan_ref[places["end"] + request] = rows_before(row_end)
    spans = [
        (key_range(table, jnp.int32(2 * rows * at))[0], key_range(table, jnp.int32(2 * rows * (at + 1) - 1))[1])
        for at in range(groups)
    ]
    needed = jnp.int32(0)
    for source in range(groups):
        for target in range(groups):
            if is_far(groups, source, target):
                first, last = spans[source]
                meet = (first < 2 * cache * (target + 1)) & (last >= 2 * cache * target)
                needed = jnp.where(meet, 1, needed)
    far_ref[0] = needed
    plan_ref[places["side"]] = side
    for steps in range(groups):
        plan_ref[places["groups"] + steps] = lax.rem(group + (groups - steps), groups)
        there = jnp.int32(1)
        for at in range(groups):
            if is_far(groups, (at + steps) % groups, at):
                there = jnp.where(group == at, needed, there)
        plan_ref[places["there"] + steps] = there
    other = (device + 1 - 2 * side) * cache
    for part, key in enumerate((device * cache, other)):
        plan_ref[places["lefts"] + part] = jnp.int32(part * cache)
        plan_ref[places["keys"] + part] = key
        plan_ref[places["steps"] + part] = jnp.int32(cache // step)
    for at in range(2 * chips):
        own = core if at < chips else 1 - core
        plan_ref[places["from"] + at] = lax.rem(chip + (chips - at % chips), chips) * 2 + own


def make_plan(shape, new_counts, prior_lengths, at):
    groups, chips = shape[:2]
    requests = new_counts.shape[0]
    sizes = dict(first_key=requests, ahead=requests, begin=requests, end=requests, side=1)
    sizes.update(groups=groups, there=groups, lefts=2, keys=2, steps=2)
    sizes["from"] = 2 * chips
    places, total = {}, 0
    for name, size in sizes.items():
        places[name] = total
        total += size
    plan, far = pl.pallas_call(
        functools.partial(plan_kernel, shape, dict(places)),
        out_shape=(jax.ShapeDtypeStruct((total,), jnp.int32), jax.ShapeDtypeStruct((1,), jnp.int32)),
        in_specs=[SMEM] * 3,
        out_specs=(SMEM, SMEM),
        name="plan",
    )(new_counts, prior_lengths, at)
    return places, plan, far


def body(queries, keys, values, w_out, new_counts, prior_lengths):
    ctx_count, head_count = lax.axis_size("ctx"), lax.axis_size("head")
    rows = queries.shape[0]
    cache = keys.shape[0]
    groups, chips = ctx_count // 2, head_count // 2
    at = jnp.stack([lax.axis_index("ctx"), lax.axis_index("head")]).astype(jnp.int32)
    shape = (groups, chips, rows, cache, min(KEY_TILE, cache // 2))
    places, plan, far = make_plan(shape, new_counts, prior_lengths, at)
    requests = new_counts.shape[0]
    return lax.cond(
        far[0] == 1,
        functools.partial(attend_and_project, places, requests, True),
        functools.partial(attend_and_project, places, requests, False),
        *(queries, keys, values, w_out, plan),
    )


def attend_and_project(places, requests, far, queries, keys, values, w_out, plan):
    ctx_count, head_count = lax.axis_size("ctx"), lax.axis_size("head")
    rows = queries.shape[0]
    width = keys.shape[1]
    heads = queries.shape[1] // width
    groups, chips = ctx_count // 2, head_count // 2

    blocks = [move(queries, groups, steps, far) for steps in range(1, groups)]

    swapped = [
        [((at ^ 1) * head_count + own, at * head_count + own) for at in range(ctx_count) for own in range(core, head_count, 2)]
        for core in range(2)
    ]
    got = [lax.ppermute(array, ("ctx", "head"), pairs) for array, pairs in zip((keys, values), swapped)]
    all_keys, beside, own_norm, near_w = prepare(keys, values, w_out)
    stack, query_norm = stack_queries(places, plan, [queries] + blocks, width)
    got, query_norm, own_norm = lax.optimization_barrier((got, query_norm, own_norm))
    rest = [
        lax.ppermute(array, "head", [(own, own ^ 1) for own in range(core, head_count, 2)])
        for core, array in enumerate(got)
    ]
    fetched = [got[0], rest[0], got[1], rest[1]]
    shape = (groups, rows, heads, requests)
    parts = attend(places, plan, (own_norm, query_norm), stack, fetched, all_keys, beside, shape)
    back = [parts[0]] + [move(parts[steps], groups, groups - steps, far) for steps in range(1, groups)]
    attended = merge(places, plan, back, heads)

    near = [attended] + [
        lax.ppermute(attended, "head", shift_pairs(head_count, 2, steps)) for steps in range(1, chips)
    ]
    paired = [lax.ppermute(piece, "head", swap_pairs(head_count)) for piece in near]
    return project(places, plan, near + paired, near_w)


def solution(mesh):
    return jax.shard_map(
        body,
        mesh=mesh,
        in_specs=(P("ctx", "head"), P("ctx", None), P("ctx", None), P(None, "head"), P(), P()),
        out_specs=P("ctx", "head"),
        check_vma=False,
    )
```

```python
import functools
import math

import jax
import jax.numpy as jnp
from jax import lax
from jax.experimental import pallas as pl
from jax.experimental.pallas import tpu as pltpu
from jax.sharding import PartitionSpec as P

NEG = -1e30
CALM = 60.0
KEY_TILE = 512
FEW_ROWS = 64
SIDE = 16
LANES = 128
STRETCHES = 7
MIB = 1024 * 1024
SMEM = pl.BlockSpec(memory_space=pltpu.SMEM)
VMEM = pl.BlockSpec(memory_space=pltpu.VMEM)
HBM = pl.BlockSpec(memory_space=pltpu.HBM)


def lengths(rows):
    wide = rows.astype(jnp.float32)
    return jnp.sum(wide * wide, axis=1, keepdims=True)


def fill(from_keys, from_values, done, keys_ref, beside_ref):
    count, width = from_keys.shape
    step = min(KEY_TILE, count)

    def turn(at, longest):
        here = pl.ds(pl.multiple_of(at * step, step), step)
        there = pl.ds(pl.multiple_of(done + at * step, step), step)
        keys = from_keys[here, :]
        keys_ref[there, :] = keys
        beside_ref[there, :width] = from_values[here, :]
        beside_ref[there, width:] = jnp.ones((step, width), jnp.bfloat16)
        return jnp.maximum(longest, lengths(keys))

    return jnp.max(lax.fori_loop(0, count // step, turn, jnp.zeros((step, 1), jnp.float32)))


def prepare_kernel(keys_ref, values_ref, far_w, all_keys, beside_ref, longest_ref, near_w, sem):
    fetch = pltpu.make_async_copy(far_w, near_w, sem)
    fetch.start()
    longest_ref[0] = fill(keys_ref, values_ref, 0, all_keys, beside_ref)
    fetch.wait()


def prepare(keys, values, w_out):
    cache, width = keys.shape
    return pl.pallas_call(
        prepare_kernel,
        out_shape=(
            pltpu.VMEM((2 * cache, width), jnp.bfloat16),
            pltpu.VMEM((2 * cache, 2 * width), jnp.bfloat16),
            jax.ShapeDtypeStruct((1,), jnp.float32),
            pltpu.VMEM(w_out.shape, w_out.dtype),
        ),
        in_specs=[VMEM, VMEM, HBM],
        out_specs=(VMEM, VMEM, SMEM, VMEM),
        scratch_shapes=[pltpu.SemaphoreType.DMA],
        compiler_params=pltpu.CompilerParams(vmem_limit_bytes=4 * MIB),
        name="prepare",
    )(keys, values, pltpu.with_memory_space_constraint(w_out, pltpu.HBM))


def stack_kernel(slots, group_at, width, plan_ref, *refs):
    q_refs, (stack_ref, longest_ref, q_all, sems) = refs[:slots], refs[slots:]
    rows = q_refs[0].shape[0]
    heads = q_refs[0].shape[1] // width
    local = slots * rows
    copies = [pltpu.make_async_copy(q_ref, q_all.at[slot], sems.at[slot]) for slot, q_ref in enumerate(q_refs)]
    for copy in copies:
        copy.start()
    longest = jnp.zeros((rows, 1), jnp.float32)
    for slot, copy in enumerate(copies):
        copy.wait()
        start = plan_ref[group_at + slot] * rows
        for head in range(heads):
            part = q_all[slot, :, head * width:(head + 1) * width]
            stack_ref[pl.ds(pl.multiple_of(head * local + start, rows), rows), :] = part
            longest = jnp.maximum(longest, lengths(part))
    longest_ref[0] = jnp.max(longest)


def stack_queries(places, plan, queries, width):
    slots, (rows, wide) = len(queries), queries[0].shape
    return pl.pallas_call(
        functools.partial(stack_kernel, slots, places["groups"], width),
        out_shape=(
            pltpu.VMEM((slots * rows * (wide // width), width), jnp.bfloat16),
            jax.ShapeDtypeStruct((1,), jnp.float32),
        ),
        in_specs=[SMEM] + [HBM] * slots,
        out_specs=(VMEM, SMEM),
        scratch_shapes=[pltpu.VMEM((slots, rows, wide), jnp.bfloat16), pltpu.SemaphoreType.DMA((slots,))],
        compiler_params=pltpu.CompilerParams(vmem_limit_bytes=4 * MIB),
        name="stack",
    )(plan, *queries)


def request_table(new_ref, prior_ref):
    table = []
    row, key = jnp.int32(0), jnp.int32(0)
    for request in range(new_ref.shape[0]):
        new, prior = new_ref[request], prior_ref[request]
        table.append((row, key, key + prior - row, row + new, key + new + prior))
        row, key = row + new, key + new + prior
    return table


def key_range(table, row):
    first, shift = table[0][1], table[0][2]
    for start, key, ahead, _, _ in table[1:]:
        own = row >= start
        first = jnp.where(own, key, first)
        shift = jnp.where(own, ahead, shift)
    return first, row + shift


def attend_kernel(shape, places, *refs):
    groups, rows, heads, requests = shape
    plan_ref, key_norm_ref, query_norm_ref, stack_ref = refs[:4]
    fetched = refs[4:6]
    keys_ref, beside_ref = refs[8:10]
    out_refs = refs[10:10 + groups]
    sums, tops, chunk_q, chunk_sum, chunk_top, arrived, sems = refs[10 + groups:]
    cache, width = keys_ref.shape[0] // 2, keys_ref.shape[1]
    local = groups * rows
    step = min(KEY_TILE, cache // 8)
    scale = width ** (-0.5)
    factor = scale * math.log2(math.e)
    copies = [pltpu.make_async_copy(ref, arrived.at[at], sems.at[at]) for at, ref in enumerate(fetched)]
    for copy in copies:
        copy.start()
    key_norm = key_norm_ref[0]
    for at, copy in enumerate(copies):
        copy.wait()
        part = arrived.at[at]
        longest = fill(part.at[:, :width], part.at[:, width:], cache + at * (cache // 2), keys_ref, beside_ref)
        key_norm = jnp.maximum(key_norm, longest)
    calm = key_norm * query_norm_ref[0] * (scale * scale) <= CALM * CALM
    side = plan_ref[places["side"]]

    def clear(at, carry):
        sums[pl.ds(pl.multiple_of(at * rows, rows), rows), :] = jnp.zeros((rows, 2 * width), jnp.float32)
        return carry

    lax.fori_loop(0, heads * groups, clear, 0)

    def global_row(place):
        whole = place + side * rows
        for group in range(1, groups):
            whole = whole + jnp.where(place >= group * rows, rows, 0)
        return whole

    def one_chunk(count, online, request, begin, end, start):
        first_key = plan_ref[places["first_key"] + request]
        ahead = plan_ref[places["ahead"] + request]
        start = pl.multiple_of(start, SIDE)
        low_key, high_key = global_row(begin) + ahead, global_row(end - 1) + ahead
        total = heads * count
        for head in range(heads):
            chunk_q[head * count:(head + 1) * count, :] = stack_ref[
                pl.ds(pl.multiple_of(head * local + start, SIDE), count), :
            ]
        chunk_sum[:total, :] = jnp.zeros((total, 2 * width), jnp.float32)
        if online:
            chunk_top[:total, :] = jnp.full((total, width), NEG, jnp.float32)
        place = start + lax.broadcasted_iota(jnp.int32, (count, 1), 0)
        last = global_row(place) + ahead

        def scores(part, left):
            return lax.dot_general(
                chunk_q[part, :], keys_ref[pl.ds(left, step), :], (((1,), (1,)), ((), ())),
                preferred_element_type=jnp.float32,
            ) * factor

        def add(left, weights):
            return jnp.dot(
                weights.astype(jnp.bfloat16), beside_ref[pl.ds(left, step), :], preferred_element_type=jnp.float32
            )

        def one_step(left, key):
            def allowed():
                index = key + lax.broadcasted_iota(jnp.int32, (count, step), 1)
                return (index >= first_key) & (index <= last)

            if online:
                mask = allowed()

                def one_head(head, carry):
                    part = pl.ds(pl.multiple_of(head * count, count), count)
                    score = jnp.where(mask, scores(part, left), NEG)
                    old = chunk_top[part, :]
                    new = jnp.maximum(old, jnp.ceil(jnp.max(score, axis=1, keepdims=True)))
                    weights = jnp.where(mask, jnp.exp2(score - new[:, :1]), 0.0)
                    shrink = jnp.exp2(old - new)
                    chunk_sum[part, :width] = chunk_sum[part, :width] * shrink
                    chunk_sum[part, width:] = chunk_sum[part, width:] * shrink
                    chunk_sum[part, :] += add(left, weights)
                    chunk_top[part, :] = new
                    return carry

                lax.fori_loop(0, heads, one_head, 0)
                return

            plain = (key >= first_key) & (key + step - 1 <= low_key)

            @pl.when(plain)
            def _():
                chunk_sum[:total, :] += add(left, jnp.exp2(scores(pl.ds(0, total), left)))

            @pl.when(jnp.logical_not(plain))
            def _():
                mask = allowed()
                weights = jnp.exp2(scores(pl.ds(0, total), left))
                weights = jnp.concatenate([
                    jnp.where(mask, weights[head * count:(head + 1) * count, :], 0.0) for head in range(heads)
                ])
                chunk_sum[:total, :] += add(left, weights)

        def one_part(part, carry):
            left, key, steps = (plan_ref[places[name] + part] for name in ("lefts", "keys", "steps"))
            low = jnp.clip(lax.div(first_key - key, step), 0, steps)
            high = jnp.clip(lax.div(high_key - key + step, step), 0, steps)

            def turn(at, carry):
                one_step(pl.multiple_of(left + at * step, step), key + at * step)
                return carry

            lax.fori_loop(low, high, turn, 0)
            return carry

        lax.fori_loop(0, STRETCHES, one_part, 0)
        own = (place >= begin) & (place < end)
        for head in range(heads):
            here = pl.ds(pl.multiple_of(head * local + start, SIDE), count)
            part = slice(head * count, (head + 1) * count)
            sums[here, :] += jnp.where(own, chunk_sum[part, :], 0.0)
            if online:
                tops[here, :] = jnp.where(own, chunk_top[part, :], tops[here, :])

    def all_chunks(count, online, request, begin, end):
        aligned = lax.div(begin, SIDE) * SIDE

        def turn(at, carry):
            from_row = aligned + at * count
            one_chunk(
                count,
                online,
                request,
                jnp.maximum(begin, from_row),
                jnp.minimum(end, from_row + count),
                jnp.minimum(from_row, local - count),
            )
            return carry

        lax.fori_loop(0, lax.div(end - aligned + (count - 1), count), turn, 0)

    many, few = min(2 * rows + SIDE, local), min(FEW_ROWS, local)

    def one_request(request, carry):
        begin, end = plan_ref[places["begin"] + request], plan_ref[places["end"] + request]
        large = end - lax.div(begin, SIDE) * SIDE > 2 * few

        @pl.when((end > begin) & calm & large)
        def _():
            all_chunks(many, False, request, begin, end)

        @pl.when((end > begin) & calm & jnp.logical_not(large))
        def _():
            all_chunks(few, False, request, begin, end)

        @pl.when((end > begin) & jnp.logical_not(calm))
        def _():
            all_chunks(few, True, request, begin, end)

        return carry

    lax.fori_loop(0, requests, one_request, 0)

    lane = lax.broadcasted_iota(jnp.int32, (LANES, LANES), 1)
    for slot, out_ref in enumerate(out_refs):
        start = plan_ref[places["groups"] + slot] * rows
        out_ref[rows:, :] = jnp.zeros((SIDE, heads * width), jnp.bfloat16)
        for at in range(0, rows, LANES):
            terms = jnp.zeros((LANES, LANES), jnp.float32)
            for head in range(heads):
                here = pl.ds(pl.multiple_of(head * local + start + at, LANES), LANES)
                out_ref[at:at + LANES, head * width:(head + 1) * width] = sums[here, :width].astype(jnp.bfloat16)
                weight = sums[here, width:]
                top = jnp.where(weight > 0.0, jnp.where(calm, 0.0, tops[here, :]), NEG)
                for term, value in enumerate((weight, top)):
                    high = value.astype(jnp.bfloat16).astype(jnp.float32)
                    terms = jnp.where(lane == 2 * term * heads + head, high, terms)
                    terms = jnp.where(lane == (2 * term + 1) * heads + head, value - high, terms)
            out_ref[rows:, at:at + LANES] = terms.T[:SIDE, :].astype(jnp.bfloat16)


def attend(places, plan, norms, stack, fetched, all_keys, beside, shape):
    groups, rows, heads, _ = shape
    cache, width = all_keys.shape[0] // 2, all_keys.shape[1]
    local = groups * rows
    most = heads * min(2 * rows + SIDE, local)
    _, _, *payloads = pl.pallas_call(
        functools.partial(attend_kernel, shape, dict(places)),
        out_shape=(pltpu.VMEM(all_keys.shape, all_keys.dtype), pltpu.VMEM(beside.shape, beside.dtype))
        + (jax.ShapeDtypeStruct((rows + SIDE, heads * width), jnp.bfloat16),) * groups,
        in_specs=[SMEM] * 3 + [VMEM] + [HBM] * 2 + [VMEM] * 2,
        out_specs=(VMEM,) * (groups + 2),
        input_output_aliases={6: 0, 7: 1},
        scratch_shapes=[
            pltpu.VMEM((heads * local, 2 * width), jnp.float32),
            pltpu.VMEM((heads * local, width), jnp.float32),
            pltpu.VMEM((most, width), jnp.bfloat16),
            pltpu.VMEM((most, 2 * width), jnp.float32),
            pltpu.VMEM((heads * min(FEW_ROWS, local), width), jnp.float32),
            pltpu.VMEM((2, cache // 2, 2 * width), jnp.bfloat16),
            pltpu.SemaphoreType.DMA((2,)),
        ],
        compiler_params=pltpu.CompilerParams(vmem_limit_bytes=28 * MIB),
        cost_estimate=pl.CostEstimate(
            flops=local * heads * cache * width * 4, bytes_accessed=24 * MIB, transcendentals=0
        ),
        name="attend",
    )(plan, *norms, stack, *fetched, all_keys, beside)
    return payloads


def merge_kernel(heads, there_at, plan_ref, *refs):
    parts, out_ref = refs[:-1], refs[-1]
    rows = out_ref.shape[0]
    width = out_ref.shape[1] // heads
    logs = [
        jnp.where(plan_ref[there_at + at] == 1, part[rows:, :rows].astype(jnp.float32), 0.0) for at, part in enumerate(parts)
    ]
    spare = LANES - SIDE * len(parts)
    if spare:
        logs.append(jnp.zeros((spare, rows), jnp.float32))
    terms = jnp.concatenate(logs, axis=0).T
    total = terms + pltpu.roll(terms, LANES - heads, 1)
    top = pltpu.roll(terms, LANES - 2 * heads, 1) + pltpu.roll(terms, LANES - 3 * heads, 1)
    lane = lax.broadcasted_iota(jnp.int32, (rows, LANES), 1)
    used = (lax.rem(lane, SIDE) < heads) & (lane < SIDE * len(parts)) & (total > 0.0)
    top = jnp.where(used, top, NEG)
    biggest = top
    for shift in (16, 32, 64):
        biggest = jnp.maximum(biggest, pltpu.roll(biggest, shift, 1))
    share = jnp.where(used, jnp.exp2(top - biggest), 0.0)
    weight = share * jnp.where(used, total, 0.0)
    for shift in (16, 32, 64):
        weight = weight + pltpu.roll(weight, shift, 1)
    share = share / weight
    for head in range(heads):
        own = slice(head * width, (head + 1) * width)
        mixed = jnp.zeros((rows, width), jnp.float32)
        for at, part in enumerate(parts):
            lane_at = at * SIDE + head
            mixed = mixed + part[:rows, own].astype(jnp.float32) * share[:, lane_at:lane_at + 1]
        out_ref[:, own] = mixed.astype(out_ref.dtype)


def merge(places, plan, parts, heads):
    rows = parts[0].shape[0] - SIDE
    return pl.pallas_call(
        functools.partial(merge_kernel, heads, places["there"]),
        out_shape=jax.ShapeDtypeStruct((rows, parts[0].shape[1]), jnp.bfloat16),
        in_specs=[SMEM] + [VMEM] * len(parts),
        out_specs=VMEM,
        compiler_params=pltpu.CompilerParams(vmem_limit_bytes=12 * MIB),
        name="merge",
    )(plan, *parts)


def project_kernel(order, going_on, last, from_at, plan_ref, *refs):
    refs = list(refs)
    before_ref = refs.pop(0) if going_on else None
    piece_refs, (w_ref, out_ref, token_ref) = refs[:len(order)], refs[len(order):]
    deep = piece_refs[0].shape[1]
    block = out_ref.shape[1]
    left = pl.multiple_of(pl.program_id(0) * block, block)
    token_ref[0] = jnp.int32(0)
    total = None
    for at, piece_ref in zip(order, piece_refs):
        own = pl.multiple_of(plan_ref[from_at + at] * deep, deep)
        term = jnp.dot(
            piece_ref[...], w_ref[pl.ds(own, deep), pl.ds(left, block)], preferred_element_type=jnp.float32
        )
        total = term if total is None else total + term
    if going_on:
        total = total + before_ref[:, pl.ds(left, block)]
    out_ref[...] = total.astype(out_ref.dtype)


def project(places, plan, order, pieces, w_out, before, last):
    rows, deep = pieces[0].shape
    depth, wide = w_out.shape
    block = min(1024, wide)
    going_on = before is not None
    return pl.pallas_call(
        functools.partial(project_kernel, order, going_on, last, places["from"]),
        out_shape=(
            pltpu.HBM((rows, wide), jnp.bfloat16) if last else pltpu.VMEM((rows, wide), jnp.float32),
            jax.ShapeDtypeStruct((1,), jnp.int32),
        ),
        grid=(wide // block,),
        in_specs=[SMEM] + [VMEM] * (going_on + len(pieces) + 1),
        out_specs=(pl.BlockSpec((rows, block), lambda at: (0, at)), SMEM),
        compiler_params=pltpu.CompilerParams(vmem_limit_bytes=16 * MIB),
        cost_estimate=pl.CostEstimate(
            flops=4 * rows * deep * len(pieces) * wide, bytes_accessed=2 * depth * wide, transcendentals=0
        ),
        name="project",
    )(plan, *([before] if going_on else []), *pieces, w_out)


def shift_pairs(count, stride, steps):
    groups = count // stride
    return [
        (group * stride + member, (group + steps) % groups * stride + member)
        for group in range(groups)
        for member in range(stride)
    ]


def swap_pairs(count):
    return [(at, at ^ 1) for at in range(count)]


def is_far(groups, one, two):
    low, high = min(one, two), max(one, two)
    return low < groups // 2 and high >= groups - max(1, groups // 4)


def move(value, groups, steps, far):
    pairs = [
        (source, target)
        for source, target in shift_pairs(2 * groups, 2, steps)
        if far or not is_far(groups, source // 2, target // 2)
    ]
    return lax.ppermute(value, "ctx", pairs) if pairs else jnp.zeros_like(value)


def plan_kernel(shape, places, new_ref, prior_ref, at_ref, plan_ref, far_ref):
    groups, chips, rows, cache, step = shape
    device, place = at_ref[0], at_ref[1]
    group, side, chip, core = lax.div(device, 2), lax.rem(device, 2), lax.div(place, 2), lax.rem(place, 2)
    table = request_table(new_ref, prior_ref)

    def rows_before(row):
        block = lax.div(row, rows)
        odd, inside = lax.rem(block, 2), lax.rem(row, rows)
        return lax.div(block, 2) * rows + jnp.where(odd == side, inside, jnp.where(odd == 1, rows, 0))

    for request, (row, key, ahead, row_end, _) in enumerate(table):
        plan_ref[places["first_key"] + request] = key
        plan_ref[places["ahead"] + request] = ahead
        plan_ref[places["begin"] + request] = rows_before(row)
        plan_ref[places["end"] + request] = rows_before(row_end)
    spans = [
        (key_range(table, jnp.int32(2 * rows * at))[0], key_range(table, jnp.int32(2 * rows * (at + 1) - 1))[1])
        for at in range(groups)
    ]
    needed = jnp.int32(0)
    for source in range(groups):
        for target in range(groups):
            if is_far(groups, source, target):
                first, last = spans[source]
                meet = (first < 2 * cache * (target + 1)) & (last >= 2 * cache * target)
                needed = jnp.where(meet, 1, needed)
    far_ref[0] = needed
    plan_ref[places["side"]] = side
    for steps in range(groups):
        plan_ref[places["groups"] + steps] = lax.rem(group + (groups - steps), groups)
        there = jnp.int32(1)
        for at in range(groups):
            if is_far(groups, (at + steps) % groups, at):
                there = jnp.where(group == at, needed, there)
        plan_ref[places["there"] + steps] = there
    other = (device + 1 - 2 * side) * cache
    odd, part = lax.rem(chip, 2), cache // 8
    stretches = [(0, device * cache, cache)]
    for at, own in enumerate((core, 1 - core)):
        left, key = cache + at * 4 * part, other + own * 4 * part
        stretches.append((left, key + odd * 3 * part, part))
        stretches.append((left + part, key + (1 - odd) * 3 * part, part))
        stretches.append((left + 2 * part, key + part, 2 * part))
    for at, (left, key, count) in enumerate(stretches):
        plan_ref[places["lefts"] + at] = jnp.int32(left)
        plan_ref[places["keys"] + at] = key
        plan_ref[places["steps"] + at] = jnp.int32(count // step)
    for at in range(2 * chips):
        own = core if at < chips else 1 - core
        plan_ref[places["from"] + at] = lax.rem(chip + (chips - at % chips), chips) * 2 + own


def make_plan(shape, new_counts, prior_lengths, at):
    groups, chips = shape[:2]
    requests = new_counts.shape[0]
    sizes = dict(first_key=requests, ahead=requests, begin=requests, end=requests, side=1)
    sizes.update(groups=groups, there=groups, lefts=STRETCHES, keys=STRETCHES, steps=STRETCHES)
    sizes["from"] = 2 * chips
    places, total = {}, 0
    for name, size in sizes.items():
        places[name] = total
        total += size
    plan, far = pl.pallas_call(
        functools.partial(plan_kernel, shape, dict(places)),
        out_shape=(jax.ShapeDtypeStruct((total,), jnp.int32), jax.ShapeDtypeStruct((1,), jnp.int32)),
        in_specs=[SMEM] * 3,
        out_specs=(SMEM, SMEM),
        name="plan",
    )(new_counts, prior_lengths, at)
    return places, plan, far


def body(queries, keys, values, w_out, new_counts, prior_lengths):
    ctx_count, head_count = lax.axis_size("ctx"), lax.axis_size("head")
    rows = queries.shape[0]
    cache = keys.shape[0]
    groups, chips = ctx_count // 2, head_count // 2
    at = jnp.stack([lax.axis_index("ctx"), lax.axis_index("head")]).astype(jnp.int32)
    shape = (groups, chips, rows, cache, min(KEY_TILE, cache // 8))
    places, plan, far = make_plan(shape, new_counts, prior_lengths, at)
    requests = new_counts.shape[0]
    return lax.cond(
        far[0] == 1,
        functools.partial(attend_and_project, places, requests, True),
        functools.partial(attend_and_project, places, requests, False),
        *(queries, keys, values, w_out, plan),
    )


def attend_and_project(places, requests, far, queries, keys, values, w_out, plan):
    ctx_count, head_count = lax.axis_size("ctx"), lax.axis_size("head")
    rows = queries.shape[0]
    cache, width = keys.shape
    heads = queries.shape[1] // width
    groups, chips = ctx_count // 2, head_count // 2

    blocks = [move(queries, groups, steps, far) for steps in range(1, groups)]

    place = lax.axis_index("head")
    core, odd, quarter = place % 2, place // 2 % 2, cache // 8

    def rows_of(start, count):
        taken = [lax.dynamic_slice_in_dim(array, start, count, axis=0) for array in (keys, values)]
        return jnp.concatenate(taken, axis=1)

    outer = lax.ppermute(rows_of((4 * core + 3 * odd) * quarter, quarter), "ctx", swap_pairs(ctx_count))
    inner = lax.ppermute(rows_of((4 * core + 1) * quarter, 2 * quarter), "ctx", swap_pairs(ctx_count))
    outer, late_keys = lax.optimization_barrier((outer, keys))
    relayed = lax.ppermute(outer, "head", [(at, at ^ 2) for at in range(head_count)])
    all_keys, beside, own_norm, near_w = prepare(late_keys, values, w_out)
    stack, query_norm = stack_queries(places, plan, [queries] + blocks, width)
    inner, query_norm, own_norm = lax.optimization_barrier((inner, query_norm, own_norm))
    mine = jnp.concatenate([outer, relayed, inner], axis=0)
    fetched = [mine, lax.ppermute(mine, "head", swap_pairs(head_count))]
    shape = (groups, rows, heads, requests)
    parts = attend(places, plan, (own_norm, query_norm), stack, fetched, all_keys, beside, shape)
    back = [parts[0]] + [move(parts[steps], groups, groups - steps, far) for steps in range(1, groups)]
    attended = merge(places, plan, back, heads)

    away = [lax.ppermute(attended, "head", shift_pairs(head_count, 2, steps)) for steps in range(1, chips)]
    pair = lax.ppermute(attended, "head", swap_pairs(head_count))
    mixed, token = project(places, plan, [0, chips], [attended, pair], near_w, None, False)
    away = [piece + token[0].astype(piece.dtype) for piece in away]
    away = away + [lax.ppermute(piece, "head", swap_pairs(head_count)) for piece in away]
    order = [*range(1, chips), *range(chips + 1, 2 * chips)]
    mixed, _ = project(places, plan, order, away, near_w, mixed, True)
    return mixed


def solution(mesh):
    return jax.shard_map(
        body,
        mesh=mesh,
        in_specs=(P("ctx", "head"), P("ctx", None), P("ctx", None), P(None, "head"), P(), P()),
        out_specs=P("ctx", "head"),
        check_vma=False,
    )
```

```python
import functools
import math

import jax
import jax.numpy as jnp
from jax import lax
from jax.experimental import pallas as pl
from jax.experimental.pallas import tpu as pltpu
from jax.sharding import PartitionSpec as P

NEG = -1e30
CALM = 60.0
KEY_TILE = 512
FEW_ROWS = 64
SIDE = 16
LANES = 128
STRETCHES = 3
MIB = 1024 * 1024
SMEM = pl.BlockSpec(memory_space=pltpu.SMEM)
VMEM = pl.BlockSpec(memory_space=pltpu.VMEM)
HBM = pl.BlockSpec(memory_space=pltpu.HBM)


def lengths(rows):
    wide = rows.astype(jnp.float32)
    return jnp.sum(wide * wide, axis=1, keepdims=True)


def fill(from_keys, from_values, done, keys_ref, beside_ref):
    count, width = from_keys.shape
    step = min(KEY_TILE, count)

    def turn(at, longest):
        here = pl.ds(pl.multiple_of(at * step, step), step)
        there = pl.ds(pl.multiple_of(done + at * step, step), step)
        keys = from_keys[here, :]
        keys_ref[there, :] = keys
        beside_ref[there, :width] = from_values[here, :]
        beside_ref[there, width:] = jnp.ones((step, width), jnp.bfloat16)
        return jnp.maximum(longest, lengths(keys))

    return jnp.max(lax.fori_loop(0, count // step, turn, jnp.zeros((step, 1), jnp.float32)))


def prepare_kernel(keys_ref, values_ref, far_w, all_keys, beside_ref, longest_ref, near_w, sem):
    fetch = pltpu.make_async_copy(far_w, near_w, sem)
    fetch.start()
    longest_ref[0] = fill(keys_ref, values_ref, 0, all_keys, beside_ref)
    fetch.wait()


def prepare(keys, values, w_out):
    cache, width = keys.shape
    return pl.pallas_call(
        prepare_kernel,
        out_shape=(
            pltpu.VMEM((2 * cache, width), jnp.bfloat16),
            pltpu.VMEM((2 * cache, 2 * width), jnp.bfloat16),
            jax.ShapeDtypeStruct((1,), jnp.float32),
            pltpu.VMEM(w_out.shape, w_out.dtype),
        ),
        in_specs=[VMEM, VMEM, HBM],
        out_specs=(VMEM, VMEM, SMEM, VMEM),
        scratch_shapes=[pltpu.SemaphoreType.DMA],
        compiler_params=pltpu.CompilerParams(vmem_limit_bytes=4 * MIB),
        name="prepare",
    )(keys, values, pltpu.with_memory_space_constraint(w_out, pltpu.HBM))


def stack_kernel(slots, group_at, width, plan_ref, *refs):
    q_refs, (stack_ref, longest_ref, q_all, sems) = refs[:slots], refs[slots:]
    rows = q_refs[0].shape[0]
    heads = q_refs[0].shape[1] // width
    local = slots * rows
    copies = [pltpu.make_async_copy(q_ref, q_all.at[slot], sems.at[slot]) for slot, q_ref in enumerate(q_refs)]
    for copy in copies:
        copy.start()
    longest = jnp.zeros((rows, 1), jnp.float32)
    for slot, copy in enumerate(copies):
        copy.wait()
        start = plan_ref[group_at + slot] * rows
        for head in range(heads):
            part = q_all[slot, :, head * width:(head + 1) * width]
            stack_ref[pl.ds(pl.multiple_of(head * local + start, rows), rows), :] = part
            longest = jnp.maximum(longest, lengths(part))
    longest_ref[0] = jnp.max(longest)


def stack_queries(places, plan, queries, width):
    slots, (rows, wide) = len(queries), queries[0].shape
    return pl.pallas_call(
        functools.partial(stack_kernel, slots, places["groups"], width),
        out_shape=(
            pltpu.VMEM((slots * rows * (wide // width), width), jnp.bfloat16),
            jax.ShapeDtypeStruct((1,), jnp.float32),
        ),
        in_specs=[SMEM] + [HBM] * slots,
        out_specs=(VMEM, SMEM),
        scratch_shapes=[pltpu.VMEM((slots, rows, wide), jnp.bfloat16), pltpu.SemaphoreType.DMA((slots,))],
        compiler_params=pltpu.CompilerParams(vmem_limit_bytes=4 * MIB),
        name="stack",
    )(plan, *queries)


def request_table(new_ref, prior_ref):
    table = []
    row, key = jnp.int32(0), jnp.int32(0)
    for request in range(new_ref.shape[0]):
        new, prior = new_ref[request], prior_ref[request]
        table.append((row, key, key + prior - row, row + new, key + new + prior))
        row, key = row + new, key + new + prior
    return table


def key_range(table, row):
    first, shift = table[0][1], table[0][2]
    for start, key, ahead, _, _ in table[1:]:
        own = row >= start
        first = jnp.where(own, key, first)
        shift = jnp.where(own, ahead, shift)
    return first, row + shift


def attend_kernel(shape, places, *refs):
    groups, rows, heads, requests = shape
    plan_ref, key_norm_ref, query_norm_ref, stack_ref = refs[:4]
    fetched = refs[4:6]
    keys_ref, beside_ref = refs[8:10]
    out_refs = refs[10:10 + groups]
    sums, tops, chunk_q, chunk_sum, chunk_top, arrived, sems = refs[10 + groups:]
    cache, width = keys_ref.shape[0] // 2, keys_ref.shape[1]
    local = groups * rows
    step = min(KEY_TILE, cache // 2)
    scale = width ** (-0.5)
    factor = scale * math.log2(math.e)
    copies = [pltpu.make_async_copy(ref, arrived.at[at], sems.at[at]) for at, ref in enumerate(fetched)]
    for copy in copies:
        copy.start()
    key_norm = key_norm_ref[0]
    for at, copy in enumerate(copies):
        copy.wait()
        part = arrived.at[at]
        longest = fill(part.at[:, :width], part.at[:, width:], cache + at * (cache // 2), keys_ref, beside_ref)
        key_norm = jnp.maximum(key_norm, longest)
    calm = key_norm * query_norm_ref[0] * (scale * scale) <= CALM * CALM
    side = plan_ref[places["side"]]

    def clear(at, carry):
        sums[pl.ds(pl.multiple_of(at * rows, rows), rows), :] = jnp.zeros((rows, 2 * width), jnp.float32)
        return carry

    lax.fori_loop(0, heads * groups, clear, 0)

    def global_row(place):
        whole = place + side * rows
        for group in range(1, groups):
            whole = whole + jnp.where(place >= group * rows, rows, 0)
        return whole

    def one_chunk(count, online, request, begin, end, start):
        first_key = plan_ref[places["first_key"] + request]
        ahead = plan_ref[places["ahead"] + request]
        start = pl.multiple_of(start, SIDE)
        low_key, high_key = global_row(begin) + ahead, global_row(end - 1) + ahead
        total = heads * count
        for head in range(heads):
            chunk_q[head * count:(head + 1) * count, :] = stack_ref[
                pl.ds(pl.multiple_of(head * local + start, SIDE), count), :
            ]
        chunk_sum[:total, :] = jnp.zeros((total, 2 * width), jnp.float32)
        if online:
            chunk_top[:total, :] = jnp.full((total, width), NEG, jnp.float32)
        place = start + lax.broadcasted_iota(jnp.int32, (count, 1), 0)
        last = global_row(place) + ahead

        def scores(part, left):
            return lax.dot_general(
                chunk_q[part, :], keys_ref[pl.ds(left, step), :], (((1,), (1,)), ((), ())),
                preferred_element_type=jnp.float32,
            ) * factor

        def add(left, weights):
            return jnp.dot(
                weights.astype(jnp.bfloat16), beside_ref[pl.ds(left, step), :], preferred_element_type=jnp.float32
            )

        def one_step(left, key):
            def allowed():
                index = key + lax.broadcasted_iota(jnp.int32, (count, step), 1)
                return (index >= first_key) & (index <= last)

            if online:
                mask = allowed()

                def one_head(head, carry):
                    part = pl.ds(pl.multiple_of(head * count, count), count)
                    score = jnp.where(mask, scores(part, left), NEG)
                    old = chunk_top[part, :]
                    new = jnp.maximum(old, jnp.ceil(jnp.max(score, axis=1, keepdims=True)))
                    weights = jnp.where(mask, jnp.exp2(score - new[:, :1]), 0.0)
                    shrink = jnp.exp2(old - new)
                    chunk_sum[part, :width] = chunk_sum[part, :width] * shrink
                    chunk_sum[part, width:] = chunk_sum[part, width:] * shrink
                    chunk_sum[part, :] += add(left, weights)
                    chunk_top[part, :] = new
                    return carry

                lax.fori_loop(0, heads, one_head, 0)
                return

            plain = (key >= first_key) & (key + step - 1 <= low_key)

            @pl.when(plain)
            def _():
                chunk_sum[:total, :] += add(left, jnp.exp2(scores(pl.ds(0, total), left)))

            @pl.when(jnp.logical_not(plain))
            def _():
                mask = allowed()
                weights = jnp.exp2(scores(pl.ds(0, total), left))
                weights = jnp.concatenate([
                    jnp.where(mask, weights[head * count:(head + 1) * count, :], 0.0) for head in range(heads)
                ])
                chunk_sum[:total, :] += add(left, weights)

        def one_part(part, carry):
            left, key, steps = (plan_ref[places[name] + part] for name in ("lefts", "keys", "steps"))
            low = jnp.clip(lax.div(first_key - key, step), 0, steps)
            high = jnp.clip(lax.div(high_key - key + step, step), 0, steps)

            def turn(at, carry):
                one_step(pl.multiple_of(left + at * step, step), key + at * step)
                return carry

            lax.fori_loop(low, high, turn, 0)
            return carry

        lax.fori_loop(0, STRETCHES, one_part, 0)
        own = (place >= begin) & (place < end)
        for head in range(heads):
            here = pl.ds(pl.multiple_of(head * local + start, SIDE), count)
            part = slice(head * count, (head + 1) * count)
            sums[here, :] += jnp.where(own, chunk_sum[part, :], 0.0)
            if online:
                tops[here, :] = jnp.where(own, chunk_top[part, :], tops[here, :])

    def all_chunks(count, online, request, begin, end):
        aligned = lax.div(begin, SIDE) * SIDE

        def turn(at, carry):
            from_row = aligned + at * count
            one_chunk(
                count,
                online,
                request,
                jnp.maximum(begin, from_row),
                jnp.minimum(end, from_row + count),
                jnp.minimum(from_row, local - count),
            )
            return carry

        lax.fori_loop(0, lax.div(end - aligned + (count - 1), count), turn, 0)

    many, few = min(2 * rows + SIDE, local), min(FEW_ROWS, local)

    def one_request(request, carry):
        begin, end = plan_ref[places["begin"] + request], plan_ref[places["end"] + request]
        large = end - lax.div(begin, SIDE) * SIDE > 2 * few

        @pl.when((end > begin) & calm & large)
        def _():
            all_chunks(many, False, request, begin, end)

        @pl.when((end > begin) & calm & jnp.logical_not(large))
        def _():
            all_chunks(few, False, request, begin, end)

        @pl.when((end > begin) & jnp.logical_not(calm))
        def _():
            all_chunks(few, True, request, begin, end)

        return carry

    lax.fori_loop(0, requests, one_request, 0)

    lane = lax.broadcasted_iota(jnp.int32, (LANES, LANES), 1)
    for slot, out_ref in enumerate(out_refs):
        start = plan_ref[places["groups"] + slot] * rows
        out_ref[rows:, :] = jnp.zeros((SIDE, heads * width), jnp.bfloat16)
        for at in range(0, rows, LANES):
            terms = jnp.zeros((LANES, LANES), jnp.float32)
            for head in range(heads):
                here = pl.ds(pl.multiple_of(head * local + start + at, LANES), LANES)
                out_ref[at:at + LANES, head * width:(head + 1) * width] = sums[here, :width].astype(jnp.bfloat16)
                weight = sums[here, width:]
                top = jnp.where(weight > 0.0, jnp.where(calm, 0.0, tops[here, :]), NEG)
                for term, value in enumerate((weight, top)):
                    high = value.astype(jnp.bfloat16).astype(jnp.float32)
                    terms = jnp.where(lane == 2 * term * heads + head, high, terms)
                    terms = jnp.where(lane == (2 * term + 1) * heads + head, value - high, terms)
            out_ref[rows:, at:at + LANES] = terms.T[:SIDE, :].astype(jnp.bfloat16)


def attend(places, plan, norms, stack, fetched, all_keys, beside, shape):
    groups, rows, heads, _ = shape
    cache, width = all_keys.shape[0] // 2, all_keys.shape[1]
    local = groups * rows
    most = heads * min(2 * rows + SIDE, local)
    _, _, *payloads = pl.pallas_call(
        functools.partial(attend_kernel, shape, dict(places)),
        out_shape=(pltpu.VMEM(all_keys.shape, all_keys.dtype), pltpu.VMEM(beside.shape, beside.dtype))
        + (jax.ShapeDtypeStruct((rows + SIDE, heads * width), jnp.bfloat16),) * groups,
        in_specs=[SMEM] * 3 + [VMEM] + [HBM] * 2 + [VMEM] * 2,
        out_specs=(VMEM,) * (groups + 2),
        input_output_aliases={6: 0, 7: 1},
        scratch_shapes=[
            pltpu.VMEM((heads * local, 2 * width), jnp.float32),
            pltpu.VMEM((heads * local, width), jnp.float32),
            pltpu.VMEM((most, width), jnp.bfloat16),
            pltpu.VMEM((most, 2 * width), jnp.float32),
            pltpu.VMEM((heads * min(FEW_ROWS, local), width), jnp.float32),
            pltpu.VMEM((2, cache // 2, 2 * width), jnp.bfloat16),
            pltpu.SemaphoreType.DMA((2,)),
        ],
        compiler_params=pltpu.CompilerParams(vmem_limit_bytes=28 * MIB),
        cost_estimate=pl.CostEstimate(
            flops=local * heads * cache * width * 4, bytes_accessed=24 * MIB, transcendentals=0
        ),
        name="attend",
    )(plan, *norms, stack, *fetched, all_keys, beside)
    return payloads


def merge_kernel(heads, there_at, plan_ref, *refs):
    parts, out_ref = refs[:-1], refs[-1]
    rows = out_ref.shape[0]
    width = out_ref.shape[1] // heads
    logs = [
        jnp.where(plan_ref[there_at + at] == 1, part[rows:, :rows].astype(jnp.float32), 0.0) for at, part in enumerate(parts)
    ]
    spare = LANES - SIDE * len(parts)
    if spare:
        logs.append(jnp.zeros((spare, rows), jnp.float32))
    terms = jnp.concatenate(logs, axis=0).T
    total = terms + pltpu.roll(terms, LANES - heads, 1)
    top = pltpu.roll(terms, LANES - 2 * heads, 1) + pltpu.roll(terms, LANES - 3 * heads, 1)
    lane = lax.broadcasted_iota(jnp.int32, (rows, LANES), 1)
    used = (lax.rem(lane, SIDE) < heads) & (lane < SIDE * len(parts)) & (total > 0.0)
    top = jnp.where(used, top, NEG)
    biggest = top
    for shift in (16, 32, 64):
        biggest = jnp.maximum(biggest, pltpu.roll(biggest, shift, 1))
    share = jnp.where(used, jnp.exp2(top - biggest), 0.0)
    weight = share * jnp.where(used, total, 0.0)
    for shift in (16, 32, 64):
        weight = weight + pltpu.roll(weight, shift, 1)
    share = share / weight
    for head in range(heads):
        own = slice(head * width, (head + 1) * width)
        mixed = jnp.zeros((rows, width), jnp.float32)
        for at, part in enumerate(parts):
            lane_at = at * SIDE + head
            mixed = mixed + part[:rows, own].astype(jnp.float32) * share[:, lane_at:lane_at + 1]
        out_ref[:, own] = mixed.astype(out_ref.dtype)


def merge(places, plan, parts, heads):
    rows = parts[0].shape[0] - SIDE
    return pl.pallas_call(
        functools.partial(merge_kernel, heads, places["there"]),
        out_shape=jax.ShapeDtypeStruct((rows, parts[0].shape[1]), jnp.bfloat16),
        in_specs=[SMEM] + [VMEM] * len(parts),
        out_specs=VMEM,
        compiler_params=pltpu.CompilerParams(vmem_limit_bytes=12 * MIB),
        name="merge",
    )(plan, *parts)


def project_kernel(order, going_on, last, from_at, plan_ref, *refs):
    refs = list(refs)
    before_ref = refs.pop(0) if going_on else None
    piece_refs, (w_ref, out_ref, token_ref) = refs[:len(order)], refs[len(order):]
    deep = piece_refs[0].shape[1]
    block = out_ref.shape[1]
    left = pl.multiple_of(pl.program_id(0) * block, block)
    token_ref[0] = jnp.int32(0)
    total = None
    for at, piece_ref in zip(order, piece_refs):
        own = pl.multiple_of(plan_ref[from_at + at] * deep, deep)
        term = jnp.dot(
            piece_ref[...], w_ref[pl.ds(own, deep), pl.ds(left, block)], preferred_element_type=jnp.float32
        )
        total = term if total is None else total + term
    if going_on:
        total = total + before_ref[:, pl.ds(left, block)]
    out_ref[...] = total.astype(out_ref.dtype)


def project(places, plan, order, pieces, w_out, before, last):
    rows, deep = pieces[0].shape
    depth, wide = w_out.shape
    block = min(1024, wide)
    going_on = before is not None
    return pl.pallas_call(
        functools.partial(project_kernel, order, going_on, last, places["from"]),
        out_shape=(
            pltpu.HBM((rows, wide), jnp.bfloat16) if last else pltpu.VMEM((rows, wide), jnp.float32),
            jax.ShapeDtypeStruct((1,), jnp.int32),
        ),
        grid=(wide // block,),
        in_specs=[SMEM] + [VMEM] * (going_on + len(pieces) + 1),
        out_specs=(pl.BlockSpec((rows, block), lambda at: (0, at)), SMEM),
        compiler_params=pltpu.CompilerParams(vmem_limit_bytes=16 * MIB),
        cost_estimate=pl.CostEstimate(
            flops=4 * rows * deep * len(pieces) * wide, bytes_accessed=2 * depth * wide, transcendentals=0
        ),
        name="project",
    )(plan, *([before] if going_on else []), *pieces, w_out)


def shift_pairs(count, stride, steps):
    groups = count // stride
    return [
        (group * stride + member, (group + steps) % groups * stride + member)
        for group in range(groups)
        for member in range(stride)
    ]


def swap_pairs(count):
    return [(at, at ^ 1) for at in range(count)]


def is_far(groups, one, two):
    low, high = min(one, two), max(one, two)
    return low < groups // 2 and high >= groups - max(1, groups // 4)


def move(value, groups, steps, far):
    pairs = [
        (source, target)
        for source, target in shift_pairs(2 * groups, 2, steps)
        if far or not is_far(groups, source // 2, target // 2)
    ]
    return lax.ppermute(value, "ctx", pairs) if pairs else jnp.zeros_like(value)


def plan_kernel(shape, places, new_ref, prior_ref, at_ref, plan_ref, far_ref):
    groups, chips, rows, cache, step = shape
    device, place = at_ref[0], at_ref[1]
    group, side, chip, core = lax.div(device, 2), lax.rem(device, 2), lax.div(place, 2), lax.rem(place, 2)
    table = request_table(new_ref, prior_ref)

    def rows_before(row):
        block = lax.div(row, rows)
        odd, inside = lax.rem(block, 2), lax.rem(row, rows)
        return lax.div(block, 2) * rows + jnp.where(odd == side, inside, jnp.where(odd == 1, rows, 0))

    for request, (row, key, ahead, row_end, _) in enumerate(table):
        plan_ref[places["first_key"] + request] = key
        plan_ref[places["ahead"] + request] = ahead
        plan_ref[places["begin"] + request] = rows_before(row)
        plan_ref[places["end"] + request] = rows_before(row_end)
    spans = [
        (key_range(table, jnp.int32(2 * rows * at))[0], key_range(table, jnp.int32(2 * rows * (at + 1) - 1))[1])
        for at in range(groups)
    ]
    needed = jnp.int32(0)
    for source in range(groups):
        for target in range(groups):
            if is_far(groups, source, target):
                first, last = spans[source]
                meet = (first < 2 * cache * (target + 1)) & (last >= 2 * cache * target)
                needed = jnp.where(meet, 1, needed)
    far_ref[0] = needed
    plan_ref[places["side"]] = side
    for steps in range(groups):
        plan_ref[places["groups"] + steps] = lax.rem(group + (groups - steps), groups)
        there = jnp.int32(1)
        for at in range(groups):
            if is_far(groups, (at + steps) % groups, at):
                there = jnp.where(group == at, needed, there)
        plan_ref[places["there"] + steps] = there
    other = (device + 1 - 2 * side) * cache
    half = cache // 2
    stretches = [
        (0, device * cache, cache), (cache, other + core * half, half), (cache + half, other + (1 - core) * half, half)
    ]
    for at, (left, key, count) in enumerate(stretches):
        plan_ref[places["lefts"] + at] = jnp.int32(left)
        plan_ref[places["keys"] + at] = key
        plan_ref[places["steps"] + at] = jnp.int32(count // step)
    for at in range(2 * chips):
        own = core if at < chips else 1 - core
        plan_ref[places["from"] + at] = lax.rem(chip + (chips - at % chips), chips) * 2 + own


def make_plan(shape, new_counts, prior_lengths, at):
    groups, chips = shape[:2]
    requests = new_counts.shape[0]
    sizes = dict(first_key=requests, ahead=requests, begin=requests, end=requests, side=1)
    sizes.update(groups=groups, there=groups, lefts=STRETCHES, keys=STRETCHES, steps=STRETCHES)
    sizes["from"] = 2 * chips
    places, total = {}, 0
    for name, size in sizes.items():
        places[name] = total
        total += size
    plan, far = pl.pallas_call(
        functools.partial(plan_kernel, shape, dict(places)),
        out_shape=(jax.ShapeDtypeStruct((total,), jnp.int32), jax.ShapeDtypeStruct((1,), jnp.int32)),
        in_specs=[SMEM] * 3,
        out_specs=(SMEM, SMEM),
        name="plan",
    )(new_counts, prior_lengths, at)
    return places, plan, far


def body(queries, keys, values, w_out, new_counts, prior_lengths):
    ctx_count, head_count = lax.axis_size("ctx"), lax.axis_size("head")
    rows = queries.shape[0]
    cache = keys.shape[0]
    groups, chips = ctx_count // 2, head_count // 2
    at = jnp.stack([lax.axis_index("ctx"), lax.axis_index("head")]).astype(jnp.int32)
    shape = (groups, chips, rows, cache, min(KEY_TILE, cache // 2))
    places, plan, far = make_plan(shape, new_counts, prior_lengths, at)
    requests = new_counts.shape[0]
    return lax.cond(
        far[0] == 1,
        functools.partial(attend_and_project, places, requests, True),
        functools.partial(attend_and_project, places, requests, False),
        *(queries, keys, values, w_out, plan),
    )


def attend_and_project(places, requests, far, queries, keys, values, w_out, plan):
    ctx_count, head_count = lax.axis_size("ctx"), lax.axis_size("head")
    rows = queries.shape[0]
    cache, width = keys.shape
    heads = queries.shape[1] // width
    groups, chips = ctx_count // 2, head_count // 2

    blocks = [move(queries, groups, steps, far) for steps in range(1, groups)]

    place = lax.axis_index("head")
    core, odd, eighth = place % 2, place // 2 % 2, cache // 16

    def rows_of(start, count):
        taken = [lax.dynamic_slice_in_dim(array, start * eighth, count * eighth, axis=0) for array in (keys, values)]
        return jnp.concatenate(taken, axis=1)

    outer = lax.ppermute(rows_of(8 * core + 5 * odd, 3), "ctx", swap_pairs(ctx_count))
    inner = lax.ppermute(rows_of(8 * core + 3, 2), "ctx", swap_pairs(ctx_count))
    outer, late_keys = lax.optimization_barrier((outer, keys))
    relayed = lax.ppermute(outer, "head", [(at, at ^ 2) for at in range(head_count)])
    all_keys, beside, own_norm, near_w = prepare(late_keys, values, w_out)
    stack, query_norm = stack_queries(places, plan, [queries] + blocks, width)
    inner, query_norm, own_norm = lax.optimization_barrier((inner, query_norm, own_norm))
    first, last = jnp.where(odd == 0, outer, relayed), jnp.where(odd == 0, relayed, outer)
    mine = jnp.concatenate([first, inner, last], axis=0)
    fetched = [mine, lax.ppermute(mine, "head", swap_pairs(head_count))]
    shape = (groups, rows, heads, requests)
    parts = attend(places, plan, (own_norm, query_norm), stack, fetched, all_keys, beside, shape)
    back = [parts[0]] + [move(parts[steps], groups, groups - steps, far) for steps in range(1, groups)]
    attended = merge(places, plan, back, heads)

    away = [lax.ppermute(attended, "head", shift_pairs(head_count, 2, steps)) for steps in range(1, chips)]
    pair = lax.ppermute(attended, "head", swap_pairs(head_count))
    mixed, token = project(places, plan, [0, chips], [attended, pair], near_w, None, False)
    away = [piece + token[0].astype(piece.dtype) for piece in away]
    away = away + [lax.ppermute(piece, "head", swap_pairs(head_count)) for piece in away]
    order = [*range(1, chips), *range(chips + 1, 2 * chips)]
    mixed, _ = project(places, plan, order, away, near_w, mixed, True)
    return mixed


def solution(mesh):
    return jax.shard_map(
        body,
        mesh=mesh,
        in_specs=(P("ctx", "head"), P("ctx", None), P("ctx", None), P(None, "head"), P(), P()),
        out_specs=P("ctx", "head"),
        check_vma=False,
    )
```

```python
import functools
import math

import jax
import jax.numpy as jnp
from jax import lax
from jax.experimental import pallas as pl
from jax.experimental.pallas import tpu as pltpu
from jax.sharding import PartitionSpec as P

NEG = -1e30
CALM = 60.0
KEY_TILE = 512
FEW_ROWS = 64
SIDE = 16
LANES = 128
STRETCHES = 3
MIB = 1024 * 1024
SMEM = pl.BlockSpec(memory_space=pltpu.SMEM)
VMEM = pl.BlockSpec(memory_space=pltpu.VMEM)
HBM = pl.BlockSpec(memory_space=pltpu.HBM)


def lengths(rows):
    wide = rows.astype(jnp.float32)
    return jnp.sum(wide * wide, axis=1, keepdims=True)


def fill(from_keys, from_values, done, keys_ref, beside_ref):
    count, width = from_keys.shape
    step = min(KEY_TILE, count)

    def turn(at, longest):
        here = pl.ds(pl.multiple_of(at * step, step), step)
        there = pl.ds(pl.multiple_of(done + at * step, step), step)
        keys = from_keys[here, :]
        keys_ref[there, :] = keys
        beside_ref[there, :width] = from_values[here, :]
        beside_ref[there, width:] = jnp.ones((step, width), jnp.bfloat16)
        return jnp.maximum(longest, lengths(keys))

    return jnp.max(lax.fori_loop(0, count // step, turn, jnp.zeros((step, 1), jnp.float32)))


def prepare_kernel(keys_ref, values_ref, all_keys, beside_ref, longest_ref):
    longest_ref[0] = fill(keys_ref, values_ref, 0, all_keys, beside_ref)


def prepare(keys, values):
    cache, width = keys.shape
    return pl.pallas_call(
        prepare_kernel,
        out_shape=(
            pltpu.VMEM((2 * cache, width), jnp.bfloat16),
            pltpu.VMEM((2 * cache, 2 * width), jnp.bfloat16),
            jax.ShapeDtypeStruct((1,), jnp.float32),
        ),
        in_specs=[VMEM, VMEM],
        out_specs=(VMEM, VMEM, SMEM),
        compiler_params=pltpu.CompilerParams(vmem_limit_bytes=4 * MIB),
        name="prepare",
    )(keys, values)


def stack_kernel(slots, group_at, width, plan_ref, *refs):
    q_refs, (stack_ref, longest_ref, q_all, sems) = refs[:slots], refs[slots:]
    rows = q_refs[0].shape[0]
    heads = q_refs[0].shape[1] // width
    local = slots * rows
    copies = [pltpu.make_async_copy(q_ref, q_all.at[slot], sems.at[slot]) for slot, q_ref in enumerate(q_refs)]
    for copy in copies:
        copy.start()
    longest = jnp.zeros((rows, 1), jnp.float32)
    for slot, copy in enumerate(copies):
        copy.wait()
        start = plan_ref[group_at + slot] * rows
        for head in range(heads):
            part = q_all[slot, :, head * width:(head + 1) * width]
            stack_ref[pl.ds(pl.multiple_of(head * local + start, rows), rows), :] = part
            longest = jnp.maximum(longest, lengths(part))
    longest_ref[0] = jnp.max(longest)


def stack_queries(places, plan, queries, width):
    slots, (rows, wide) = len(queries), queries[0].shape
    return pl.pallas_call(
        functools.partial(stack_kernel, slots, places["groups"], width),
        out_shape=(
            pltpu.VMEM((slots * rows * (wide // width), width), jnp.bfloat16),
            jax.ShapeDtypeStruct((1,), jnp.float32),
        ),
        in_specs=[SMEM] + [HBM] * slots,
        out_specs=(VMEM, SMEM),
        scratch_shapes=[pltpu.VMEM((slots, rows, wide), jnp.bfloat16), pltpu.SemaphoreType.DMA((slots,))],
        compiler_params=pltpu.CompilerParams(vmem_limit_bytes=4 * MIB),
        name="stack",
    )(plan, *queries)


def request_table(new_ref, prior_ref):
    table = []
    row, key = jnp.int32(0), jnp.int32(0)
    for request in range(new_ref.shape[0]):
        new, prior = new_ref[request], prior_ref[request]
        table.append((row, key, key + prior - row, row + new, key + new + prior))
        row, key = row + new, key + new + prior
    return table


def key_range(table, row):
    first, shift = table[0][1], table[0][2]
    for start, key, ahead, _, _ in table[1:]:
        own = row >= start
        first = jnp.where(own, key, first)
        shift = jnp.where(own, ahead, shift)
    return first, row + shift


def attend_kernel(shape, places, *refs):
    groups, rows, heads, requests = shape
    plan_ref, key_norm_ref, query_norm_ref, stack_ref = refs[:4]
    fetched, far_w = refs[4:6], refs[6]
    keys_ref, beside_ref, near_w = refs[9:12]
    out_refs = refs[12:12 + groups]
    sums, tops, chunk_q, chunk_sum, chunk_top, arrived, sems, w_sem = refs[12 + groups:]
    cache, width = keys_ref.shape[0] // 2, keys_ref.shape[1]
    local = groups * rows
    step = min(KEY_TILE, cache // 2)
    scale = width ** (-0.5)
    factor = scale * math.log2(math.e)
    copies = [pltpu.make_async_copy(ref, arrived.at[at], sems.at[at]) for at, ref in enumerate(fetched)]
    for copy in copies:
        copy.start()
    fetch = pltpu.make_async_copy(far_w, near_w, w_sem)
    fetch.start()
    key_norm = key_norm_ref[0]
    for at, copy in enumerate(copies):
        copy.wait()
        part = arrived.at[at]
        longest = fill(part.at[:, :width], part.at[:, width:], cache + at * (cache // 2), keys_ref, beside_ref)
        key_norm = jnp.maximum(key_norm, longest)
    calm = key_norm * query_norm_ref[0] * (scale * scale) <= CALM * CALM
    side = plan_ref[places["side"]]

    def clear(at, carry):
        sums[pl.ds(pl.multiple_of(at * rows, rows), rows), :] = jnp.zeros((rows, 2 * width), jnp.float32)
        return carry

    lax.fori_loop(0, heads * groups, clear, 0)

    def global_row(place):
        whole = place + side * rows
        for group in range(1, groups):
            whole = whole + jnp.where(place >= group * rows, rows, 0)
        return whole

    def one_chunk(count, online, request, begin, end, start):
        first_key = plan_ref[places["first_key"] + request]
        ahead = plan_ref[places["ahead"] + request]
        start = pl.multiple_of(start, SIDE)
        low_key, high_key = global_row(begin) + ahead, global_row(end - 1) + ahead
        total = heads * count
        for head in range(heads):
            chunk_q[head * count:(head + 1) * count, :] = stack_ref[
                pl.ds(pl.multiple_of(head * local + start, SIDE), count), :
            ]
        chunk_sum[:total, :] = jnp.zeros((total, 2 * width), jnp.float32)
        if online:
            chunk_top[:total, :] = jnp.full((total, width), NEG, jnp.float32)
        place = start + lax.broadcasted_iota(jnp.int32, (count, 1), 0)
        last = global_row(place) + ahead

        def scores(part, left):
            return lax.dot_general(
                chunk_q[part, :], keys_ref[pl.ds(left, step), :], (((1,), (1,)), ((), ())),
                preferred_element_type=jnp.float32,
            ) * factor

        def add(left, weights):
            return jnp.dot(
                weights.astype(jnp.bfloat16), beside_ref[pl.ds(left, step), :], preferred_element_type=jnp.float32
            )

        def one_step(left, key):
            def allowed():
                index = key + lax.broadcasted_iota(jnp.int32, (count, step), 1)
                return (index >= first_key) & (index <= last)

            if online:
                mask = allowed()

                def one_head(head, carry):
                    part = pl.ds(pl.multiple_of(head * count, count), count)
                    score = jnp.where(mask, scores(part, left), NEG)
                    old = chunk_top[part, :]
                    new = jnp.maximum(old, jnp.ceil(jnp.max(score, axis=1, keepdims=True)))
                    weights = jnp.where(mask, jnp.exp2(score - new[:, :1]), 0.0)
                    shrink = jnp.exp2(old - new)
                    chunk_sum[part, :width] = chunk_sum[part, :width] * shrink
                    chunk_sum[part, width:] = chunk_sum[part, width:] * shrink
                    chunk_sum[part, :] += add(left, weights)
                    chunk_top[part, :] = new
                    return carry

                lax.fori_loop(0, heads, one_head, 0)
                return

            mask = allowed()
            weights = jnp.exp2(scores(pl.ds(0, total), left))
            weights = jnp.concatenate([
                jnp.where(mask, weights[head * count:(head + 1) * count, :], 0.0) for head in range(heads)
            ])
            chunk_sum[:total, :] += add(left, weights)

        def two_steps(left):
            one, two = scores(pl.ds(0, total), left), scores(pl.ds(0, total), left + step)
            chunk_sum[:total, :] += add(left, jnp.exp2(one)) + add(left + step, jnp.exp2(two))

        def one_part(part, carry):
            left, key, steps = (plan_ref[places[name] + part] for name in ("lefts", "keys", "steps"))
            low = jnp.clip(lax.div(first_key - key, step), 0, steps)
            high = jnp.clip(lax.div(high_key - key + step, step), 0, steps)
            plain = jnp.clip(lax.div(first_key - key + (step - 1), step), low, high)
            pairs = lax.div(jnp.clip(lax.div(low_key + 1 - key, step), plain, high) - plain, 2)
            if online:
                pairs = 0

            def turn(at, carry):
                @pl.when((at < plain) | (at >= plain + 2 * pairs))
                def _():
                    one_step(pl.multiple_of(left + at * step, step), key + at * step)

                return carry

            lax.fori_loop(low, high, turn, 0)
            if not online:

                def pair(at, carry):
                    two_steps(pl.multiple_of(left + (plain + 2 * at) * step, step))
                    return carry

                lax.fori_loop(0, pairs, pair, 0)
            return carry

        lax.fori_loop(0, STRETCHES, one_part, 0)
        own = (place >= begin) & (place < end)
        for head in range(heads):
            here = pl.ds(pl.multiple_of(head * local + start, SIDE), count)
            part = slice(head * count, (head + 1) * count)
            sums[here, :] += jnp.where(own, chunk_sum[part, :], 0.0)
            if online:
                tops[here, :] = jnp.where(own, chunk_top[part, :], tops[here, :])

    def all_chunks(count, online, request, begin, end):
        aligned = lax.div(begin, SIDE) * SIDE

        def turn(at, carry):
            from_row = aligned + at * count
            one_chunk(
                count,
                online,
                request,
                jnp.maximum(begin, from_row),
                jnp.minimum(end, from_row + count),
                jnp.minimum(from_row, local - count),
            )
            return carry

        lax.fori_loop(0, lax.div(end - aligned + (count - 1), count), turn, 0)

    many, few = min(2 * rows + SIDE, local), min(FEW_ROWS, local)

    def one_request(request, carry):
        begin, end = plan_ref[places["begin"] + request], plan_ref[places["end"] + request]
        large = end - lax.div(begin, SIDE) * SIDE > 2 * few

        @pl.when((end > begin) & calm & large)
        def _():
            all_chunks(many, False, request, begin, end)

        @pl.when((end > begin) & calm & jnp.logical_not(large))
        def _():
            all_chunks(few, False, request, begin, end)

        @pl.when((end > begin) & jnp.logical_not(calm))
        def _():
            all_chunks(few, True, request, begin, end)

        return carry

    lax.fori_loop(0, requests, one_request, 0)

    lane = lax.broadcasted_iota(jnp.int32, (LANES, LANES), 1)
    for slot, out_ref in enumerate(out_refs):
        start = plan_ref[places["groups"] + slot] * rows
        out_ref[rows:, :] = jnp.zeros((SIDE, heads * width), jnp.bfloat16)
        for at in range(0, rows, LANES):
            terms = jnp.zeros((LANES, LANES), jnp.float32)
            for head in range(heads):
                here = pl.ds(pl.multiple_of(head * local + start + at, LANES), LANES)
                out_ref[at:at + LANES, head * width:(head + 1) * width] = sums[here, :width].astype(jnp.bfloat16)
                weight = sums[here, width:]
                top = jnp.where(weight > 0.0, jnp.where(calm, 0.0, tops[here, :]), NEG)
                for term, value in enumerate((weight, top)):
                    high = value.astype(jnp.bfloat16).astype(jnp.float32)
                    terms = jnp.where(lane == 2 * term * heads + head, high, terms)
                    terms = jnp.where(lane == (2 * term + 1) * heads + head, value - high, terms)
            out_ref[rows:, at:at + LANES] = terms.T[:SIDE, :].astype(jnp.bfloat16)
    fetch.wait()


def attend(places, plan, norms, stack, fetched, all_keys, beside, w_out, shape):
    groups, rows, heads, _ = shape
    cache, width = all_keys.shape[0] // 2, all_keys.shape[1]
    local = groups * rows
    most = heads * min(2 * rows + SIDE, local)
    _, _, near_w, *payloads = pl.pallas_call(
        functools.partial(attend_kernel, shape, dict(places)),
        out_shape=tuple(pltpu.VMEM(array.shape, array.dtype) for array in (all_keys, beside, w_out))
        + (jax.ShapeDtypeStruct((rows + SIDE, heads * width), jnp.bfloat16),) * groups,
        in_specs=[SMEM] * 3 + [VMEM] + [HBM] * 3 + [VMEM] * 2,
        out_specs=(VMEM,) * (groups + 3),
        input_output_aliases={7: 0, 8: 1},
        scratch_shapes=[
            pltpu.VMEM((heads * local, 2 * width), jnp.float32),
            pltpu.VMEM((heads * local, width), jnp.float32),
            pltpu.VMEM((most, width), jnp.bfloat16),
            pltpu.VMEM((most, 2 * width), jnp.float32),
            pltpu.VMEM((heads * min(FEW_ROWS, local), width), jnp.float32),
            pltpu.VMEM((2, cache // 2, 2 * width), jnp.bfloat16),
            pltpu.SemaphoreType.DMA((2,)),
            pltpu.SemaphoreType.DMA,
        ],
        compiler_params=pltpu.CompilerParams(vmem_limit_bytes=30 * MIB),
        cost_estimate=pl.CostEstimate(
            flops=local * heads * cache * width * 4, bytes_accessed=24 * MIB, transcendentals=0
        ),
        name="attend",
    )(plan, *norms, stack, *fetched, pltpu.with_memory_space_constraint(w_out, pltpu.HBM), all_keys, beside)
    return payloads, near_w


def merge_kernel(heads, there_at, plan_ref, *refs):
    parts, out_ref = refs[:-1], refs[-1]
    rows = out_ref.shape[0]
    width = out_ref.shape[1] // heads
    logs = [
        jnp.where(plan_ref[there_at + at] == 1, part[rows:, :rows].astype(jnp.float32), 0.0) for at, part in enumerate(parts)
    ]
    spare = LANES - SIDE * len(parts)
    if spare:
        logs.append(jnp.zeros((spare, rows), jnp.float32))
    terms = jnp.concatenate(logs, axis=0).T
    total = terms + pltpu.roll(terms, LANES - heads, 1)
    top = pltpu.roll(terms, LANES - 2 * heads, 1) + pltpu.roll(terms, LANES - 3 * heads, 1)
    lane = lax.broadcasted_iota(jnp.int32, (rows, LANES), 1)
    used = (lax.rem(lane, SIDE) < heads) & (lane < SIDE * len(parts)) & (total > 0.0)
    top = jnp.where(used, top, NEG)
    biggest = top
    for shift in (16, 32, 64):
        biggest = jnp.maximum(biggest, pltpu.roll(biggest, shift, 1))
    share = jnp.where(used, jnp.exp2(top - biggest), 0.0)
    weight = share * jnp.where(used, total, 0.0)
    for shift in (16, 32, 64):
        weight = weight + pltpu.roll(weight, shift, 1)
    share = share / weight
    for head in range(heads):
        own = slice(head * width, (head + 1) * width)
        mixed = jnp.zeros((rows, width), jnp.float32)
        for at, part in enumerate(parts):
            lane_at = at * SIDE + head
            mixed = mixed + part[:rows, own].astype(jnp.float32) * share[:, lane_at:lane_at + 1]
        out_ref[:, own] = mixed.astype(out_ref.dtype)


def merge(places, plan, parts, heads):
    rows = parts[0].shape[0] - SIDE
    return pl.pallas_call(
        functools.partial(merge_kernel, heads, places["there"]),
        out_shape=jax.ShapeDtypeStruct((rows, parts[0].shape[1]), jnp.bfloat16),
        in_specs=[SMEM] + [VMEM] * len(parts),
        out_specs=VMEM,
        compiler_params=pltpu.CompilerParams(vmem_limit_bytes=12 * MIB),
        name="merge",
    )(plan, *parts)


def project_kernel(order, going_on, last, from_at, plan_ref, *refs):
    refs = list(refs)
    before_ref = refs.pop(0) if going_on else None
    piece_refs, (w_ref, out_ref, token_ref) = refs[:len(order)], refs[len(order):]
    deep = piece_refs[0].shape[1]
    block = out_ref.shape[1]
    left = pl.multiple_of(pl.program_id(0) * block, block)
    token_ref[0] = jnp.int32(0)
    total = None
    for at, piece_ref in zip(order, piece_refs):
        own = pl.multiple_of(plan_ref[from_at + at] * deep, deep)
        term = jnp.dot(
            piece_ref[...], w_ref[pl.ds(own, deep), pl.ds(left, block)], preferred_element_type=jnp.float32
        )
        total = term if total is None else total + term
    if going_on:
        total = total + before_ref[:, pl.ds(left, block)]
    out_ref[...] = total.astype(out_ref.dtype)


def project(places, plan, order, pieces, w_out, before, last):
    rows, deep = pieces[0].shape
    depth, wide = w_out.shape
    block = min(1024, wide)
    going_on = before is not None
    return pl.pallas_call(
        functools.partial(project_kernel, order, going_on, last, places["from"]),
        out_shape=(
            pltpu.HBM((rows, wide), jnp.bfloat16) if last else pltpu.VMEM((rows, wide), jnp.float32),
            jax.ShapeDtypeStruct((1,), jnp.int32),
        ),
        grid=(wide // block,),
        in_specs=[SMEM] + [VMEM] * (going_on + len(pieces) + 1),
        out_specs=(pl.BlockSpec((rows, block), lambda at: (0, at)), SMEM),
        compiler_params=pltpu.CompilerParams(vmem_limit_bytes=16 * MIB),
        cost_estimate=pl.CostEstimate(
            flops=4 * rows * deep * len(pieces) * wide, bytes_accessed=2 * depth * wide, transcendentals=0
        ),
        name="project",
    )(plan, *([before] if going_on else []), *pieces, w_out)


def shift_pairs(count, stride, steps):
    groups = count // stride
    return [
        (group * stride + member, (group + steps) % groups * stride + member)
        for group in range(groups)
        for member in range(stride)
    ]


def swap_pairs(count):
    return [(at, at ^ 1) for at in range(count)]


def is_far(groups, one, two):
    low, high = min(one, two), max(one, two)
    return low < groups // 2 and high >= groups - max(1, groups // 4)


def move(value, groups, steps, far):
    pairs = [
        (source, target)
        for source, target in shift_pairs(2 * groups, 2, steps)
        if far or not is_far(groups, source // 2, target // 2)
    ]
    return lax.ppermute(value, "ctx", pairs) if pairs else jnp.zeros_like(value)


def plan_kernel(shape, places, new_ref, prior_ref, at_ref, plan_ref, far_ref):
    groups, chips, rows, cache, step = shape
    device, place = at_ref[0], at_ref[1]
    group, side, chip, core = lax.div(device, 2), lax.rem(device, 2), lax.div(place, 2), lax.rem(place, 2)
    table = request_table(new_ref, prior_ref)

    def rows_before(row):
        block = lax.div(row, rows)
        odd, inside = lax.rem(block, 2), lax.rem(row, rows)
        return lax.div(block, 2) * rows + jnp.where(odd == side, inside, jnp.where(odd == 1, rows, 0))

    for request, (row, key, ahead, row_end, _) in enumerate(table):
        plan_ref[places["first_key"] + request] = key
        plan_ref[places["ahead"] + request] = ahead
        plan_ref[places["begin"] + request] = rows_before(row)
        plan_ref[places["end"] + request] = rows_before(row_end)
    spans = [
        (key_range(table, jnp.int32(2 * rows * at))[0], key_range(table, jnp.int32(2 * rows * (at + 1) - 1))[1])
        for at in range(groups)
    ]
    needed = jnp.int32(0)
    for source in range(groups):
        for target in range(groups):
            if is_far(groups, source, target):
                first, last = spans[source]
                meet = (first < 2 * cache * (target + 1)) & (last >= 2 * cache * target)
                needed = jnp.where(meet, 1, needed)
    far_ref[0] = needed
    plan_ref[places["side"]] = side
    for steps in range(groups):
        plan_ref[places["groups"] + steps] = lax.rem(group + (groups - steps), groups)
        there = jnp.int32(1)
        for at in range(groups):
            if is_far(groups, (at + steps) % groups, at):
                there = jnp.where(group == at, needed, there)
        plan_ref[places["there"] + steps] = there
    other = (device + 1 - 2 * side) * cache
    half = cache // 2
    stretches = [
        (0, device * cache, cache), (cache, other + core * half, half), (cache + half, other + (1 - core) * half, half)
    ]
    for at, (left, key, count) in enumerate(stretches):
        plan_ref[places["lefts"] + at] = jnp.int32(left)
        plan_ref[places["keys"] + at] = key
        plan_ref[places["steps"] + at] = jnp.int32(count // step)
    for at in range(2 * chips):
        own = core if at < chips else 1 - core
        plan_ref[places["from"] + at] = lax.rem(chip + (chips - at % chips), chips) * 2 + own


def make_plan(shape, new_counts, prior_lengths, at):
    groups, chips = shape[:2]
    requests = new_counts.shape[0]
    sizes = dict(first_key=requests, ahead=requests, begin=requests, end=requests, side=1)
    sizes.update(groups=groups, there=groups, lefts=STRETCHES, keys=STRETCHES, steps=STRETCHES)
    sizes["from"] = 2 * chips
    places, total = {}, 0
    for name, size in sizes.items():
        places[name] = total
        total += size
    plan, far = pl.pallas_call(
        functools.partial(plan_kernel, shape, dict(places)),
        out_shape=(jax.ShapeDtypeStruct((total,), jnp.int32), jax.ShapeDtypeStruct((1,), jnp.int32)),
        in_specs=[SMEM] * 3,
        out_specs=(SMEM, SMEM),
        name="plan",
    )(new_counts, prior_lengths, at)
    return places, plan, far


def body(queries, keys, values, w_out, new_counts, prior_lengths):
    ctx_count, head_count = lax.axis_size("ctx"), lax.axis_size("head")
    rows = queries.shape[0]
    cache = keys.shape[0]
    groups, chips = ctx_count // 2, head_count // 2
    at = jnp.stack([lax.axis_index("ctx"), lax.axis_index("head")]).astype(jnp.int32)
    shape = (groups, chips, rows, cache, min(KEY_TILE, cache // 2))
    places, plan, far = make_plan(shape, new_counts, prior_lengths, at)
    requests = new_counts.shape[0]
    return lax.cond(
        far[0] == 1,
        functools.partial(attend_and_project, places, requests, True),
        functools.partial(attend_and_project, places, requests, False),
        *(queries, keys, values, w_out, plan),
    )


def attend_and_project(places, requests, far, queries, keys, values, w_out, plan):
    ctx_count, head_count = lax.axis_size("ctx"), lax.axis_size("head")
    rows = queries.shape[0]
    cache, width = keys.shape
    heads = queries.shape[1] // width
    groups, chips = ctx_count // 2, head_count // 2

    blocks = [move(queries, groups, steps, far) for steps in range(1, groups)]

    place = lax.axis_index("head")
    core, odd, eighth = place % 2, place // 2 % 2, cache // 16

    def rows_of(start, count):
        taken = [lax.dynamic_slice_in_dim(array, start * eighth, count * eighth, axis=0) for array in (keys, values)]
        return jnp.concatenate(taken, axis=1)

    outer = lax.ppermute(rows_of(8 * core + 5 * odd, 3), "ctx", swap_pairs(ctx_count))
    inner = lax.ppermute(rows_of(8 * core + 3, 2), "ctx", swap_pairs(ctx_count))
    relayed = lax.ppermute(outer, "head", [(at, at ^ 2) for at in range(head_count)])
    all_keys, beside, own_norm = prepare(keys, values)
    stack, query_norm = stack_queries(places, plan, [queries] + blocks, width)
    first, last = jnp.where(odd == 0, outer, relayed), jnp.where(odd == 0, relayed, outer)
    mine = jnp.concatenate([first, inner, last], axis=0)
    fetched = [mine, lax.ppermute(mine, "head", swap_pairs(head_count))]
    shape = (groups, rows, heads, requests)
    parts, near_w = attend(
        places, plan, (own_norm, query_norm), stack, fetched, all_keys, beside, w_out, shape
    )
    back = [parts[0]] + [move(parts[steps], groups, groups - steps, far) for steps in range(1, groups)]
    attended = merge(places, plan, back, heads)

    away = [lax.ppermute(attended, "head", shift_pairs(head_count, 2, steps)) for steps in range(1, chips)]
    pair = lax.ppermute(attended, "head", swap_pairs(head_count))
    mixed, token = project(places, plan, [0, chips], [attended, pair], near_w, None, False)
    away = [piece + token[0].astype(piece.dtype) for piece in away]
    away = away + [lax.ppermute(piece, "head", swap_pairs(head_count)) for piece in away]
    order = [*range(1, chips), *range(chips + 1, 2 * chips)]
    mixed, _ = project(places, plan, order, away, near_w, mixed, True)
    return mixed


def solution(mesh):
    return jax.shard_map(
        body,
        mesh=mesh,
        in_specs=(P("ctx", "head"), P("ctx", None), P("ctx", None), P(None, "head"), P(), P()),
        out_specs=P("ctx", "head"),
        check_vma=False,
    )
```

```python
import functools
import math

import jax
import jax.numpy as jnp
from jax import lax
from jax.experimental import pallas as pl
from jax.experimental.pallas import tpu as pltpu
from jax.sharding import PartitionSpec as P

NEG = -1e30
CALM = 60.0
KEY_TILE = 512
FEW_ROWS = 64
SIDE = 16
LANES = 128
STRETCHES = 3
MIB = 1024 * 1024
SMEM = pl.BlockSpec(memory_space=pltpu.SMEM)
VMEM = pl.BlockSpec(memory_space=pltpu.VMEM)
HBM = pl.BlockSpec(memory_space=pltpu.HBM)


def lengths(rows):
    wide = rows.astype(jnp.float32)
    return jnp.sum(wide * wide, axis=1, keepdims=True)


def fill(from_keys, from_values, done, keys_ref, beside_ref):
    count, width = from_keys.shape
    step = min(KEY_TILE, count)

    def turn(at, longest):
        here = pl.ds(pl.multiple_of(at * step, step), step)
        there = pl.ds(pl.multiple_of(done + at * step, step), step)
        keys = from_keys[here, :]
        keys_ref[there, :] = keys
        beside_ref[there, :width] = from_values[here, :]
        beside_ref[there, width:] = jnp.ones((step, width), jnp.bfloat16)
        return jnp.maximum(longest, lengths(keys))

    return jnp.max(lax.fori_loop(0, count // step, turn, jnp.zeros((step, 1), jnp.float32)))


def prepare_kernel(keys_ref, values_ref, far_w, all_keys, beside_ref, longest_ref, near_w, sem):
    fetch = pltpu.make_async_copy(far_w, near_w, sem)
    fetch.start()
    longest_ref[0] = fill(keys_ref, values_ref, 0, all_keys, beside_ref)
    fetch.wait()


def prepare(keys, values, w_out):
    cache, width = keys.shape
    return pl.pallas_call(
        prepare_kernel,
        out_shape=(
            pltpu.VMEM((2 * cache, width), jnp.bfloat16),
            pltpu.VMEM((2 * cache, 2 * width), jnp.bfloat16),
            jax.ShapeDtypeStruct((1,), jnp.float32),
            pltpu.VMEM(w_out.shape, w_out.dtype),
        ),
        in_specs=[VMEM, VMEM, HBM],
        out_specs=(VMEM, VMEM, SMEM, VMEM),
        scratch_shapes=[pltpu.SemaphoreType.DMA],
        compiler_params=pltpu.CompilerParams(vmem_limit_bytes=4 * MIB),
        name="prepare",
    )(keys, values, pltpu.with_memory_space_constraint(w_out, pltpu.HBM))


def stack_kernel(slots, group_at, width, plan_ref, *refs):
    q_refs, (stack_ref, longest_ref, q_all, sems) = refs[:slots], refs[slots:]
    rows = q_refs[0].shape[0]
    heads = q_refs[0].shape[1] // width
    local = slots * rows
    copies = [pltpu.make_async_copy(q_ref, q_all.at[slot], sems.at[slot]) for slot, q_ref in enumerate(q_refs)]
    for copy in copies:
        copy.start()
    longest = jnp.zeros((rows, 1), jnp.float32)
    for slot, copy in enumerate(copies):
        copy.wait()
        start = plan_ref[group_at + slot] * rows
        for head in range(heads):
            part = q_all[slot, :, head * width:(head + 1) * width]
            stack_ref[pl.ds(pl.multiple_of(head * local + start, rows), rows), :] = part
            longest = jnp.maximum(longest, lengths(part))
    longest_ref[0] = jnp.max(longest)


def stack_queries(places, plan, queries, width):
    slots, (rows, wide) = len(queries), queries[0].shape
    return pl.pallas_call(
        functools.partial(stack_kernel, slots, places["groups"], width),
        out_shape=(
            pltpu.VMEM((slots * rows * (wide // width), width), jnp.bfloat16),
            jax.ShapeDtypeStruct((1,), jnp.float32),
        ),
        in_specs=[SMEM] + [HBM] * slots,
        out_specs=(VMEM, SMEM),
        scratch_shapes=[pltpu.VMEM((slots, rows, wide), jnp.bfloat16), pltpu.SemaphoreType.DMA((slots,))],
        compiler_params=pltpu.CompilerParams(vmem_limit_bytes=4 * MIB),
        name="stack",
    )(plan, *queries)


def request_table(new_ref, prior_ref):
    table = []
    row, key = jnp.int32(0), jnp.int32(0)
    for request in range(new_ref.shape[0]):
        new, prior = new_ref[request], prior_ref[request]
        table.append((row, key, key + prior - row, row + new, key + new + prior))
        row, key = row + new, key + new + prior
    return table


def key_range(table, row):
    first, shift = table[0][1], table[0][2]
    for start, key, ahead, _, _ in table[1:]:
        own = row >= start
        first = jnp.where(own, key, first)
        shift = jnp.where(own, ahead, shift)
    return first, row + shift


def attend_kernel(shape, places, *refs):
    groups, rows, heads, requests = shape
    plan_ref, key_norm_ref, query_norm_ref, stack_ref = refs[:4]
    fetched = refs[4:6]
    keys_ref, beside_ref = refs[8:10]
    out_refs = refs[10:10 + groups]
    sums, tops, chunk_q, chunk_sum, chunk_top, arrived, sems = refs[10 + groups:]
    cache, width = keys_ref.shape[0] // 2, keys_ref.shape[1]
    local = groups * rows
    step = min(KEY_TILE, cache // 2)
    scale = width ** (-0.5)
    factor = scale * math.log2(math.e)
    copies = [pltpu.make_async_copy(ref, arrived.at[at], sems.at[at]) for at, ref in enumerate(fetched)]
    for copy in copies:
        copy.start()
    key_norm = key_norm_ref[0]
    for at, copy in enumerate(copies):
        copy.wait()
        part = arrived.at[at]
        longest = fill(part.at[:, :width], part.at[:, width:], cache + at * (cache // 2), keys_ref, beside_ref)
        key_norm = jnp.maximum(key_norm, longest)
    calm = key_norm * query_norm_ref[0] * (scale * scale) <= CALM * CALM
    side = plan_ref[places["side"]]

    def clear(at, carry):
        sums[pl.ds(pl.multiple_of(at * rows, rows), rows), :] = jnp.zeros((rows, 2 * width), jnp.float32)
        return carry

    lax.fori_loop(0, heads * groups, clear, 0)

    def global_row(place):
        whole = place + side * rows
        for group in range(1, groups):
            whole = whole + jnp.where(place >= group * rows, rows, 0)
        return whole

    def one_chunk(count, online, request, begin, end, start):
        first_key = plan_ref[places["first_key"] + request]
        ahead = plan_ref[places["ahead"] + request]
        start = pl.multiple_of(start, SIDE)
        low_key, high_key = global_row(begin) + ahead, global_row(end - 1) + ahead
        total = heads * count
        for head in range(heads):
            chunk_q[head * count:(head + 1) * count, :] = stack_ref[
                pl.ds(pl.multiple_of(head * local + start, SIDE), count), :
            ]
        chunk_sum[:total, :] = jnp.zeros((total, 2 * width), jnp.float32)
        if online:
            chunk_top[:total, :] = jnp.full((total, width), NEG, jnp.float32)
        place = start + lax.broadcasted_iota(jnp.int32, (count, 1), 0)
        last = global_row(place) + ahead

        def scores(part, left):
            return lax.dot_general(
                chunk_q[part, :], keys_ref[pl.ds(left, step), :], (((1,), (1,)), ((), ())),
                preferred_element_type=jnp.float32,
            ) * factor

        def add(left, weights):
            return jnp.dot(
                weights.astype(jnp.bfloat16), beside_ref[pl.ds(left, step), :], preferred_element_type=jnp.float32
            )

        def one_step(left, key):
            def allowed():
                index = key + lax.broadcasted_iota(jnp.int32, (count, step), 1)
                return (index >= first_key) & (index <= last)

            if online:
                mask = allowed()

                def one_head(head, carry):
                    part = pl.ds(pl.multiple_of(head * count, count), count)
                    score = jnp.where(mask, scores(part, left), NEG)
                    old = chunk_top[part, :]
                    new = jnp.maximum(old, jnp.ceil(jnp.max(score, axis=1, keepdims=True)))
                    weights = jnp.where(mask, jnp.exp2(score - new[:, :1]), 0.0)
                    shrink = jnp.exp2(old - new)
                    chunk_sum[part, :width] = chunk_sum[part, :width] * shrink
                    chunk_sum[part, width:] = chunk_sum[part, width:] * shrink
                    chunk_sum[part, :] += add(left, weights)
                    chunk_top[part, :] = new
                    return carry

                lax.fori_loop(0, heads, one_head, 0)
                return

            plain = (key >= first_key) & (key + step - 1 <= low_key)

            @pl.when(plain)
            def _():
                chunk_sum[:total, :] += add(left, jnp.exp2(scores(pl.ds(0, total), left)))

            @pl.when(jnp.logical_not(plain))
            def _():
                mask = allowed()
                weights = jnp.exp2(scores(pl.ds(0, total), left))
                weights = jnp.concatenate([
                    jnp.where(mask, weights[head * count:(head + 1) * count, :], 0.0) for head in range(heads)
                ])
                chunk_sum[:total, :] += add(left, weights)

        def one_part(part, carry):
            left, key, steps = (plan_ref[places[name] + part] for name in ("lefts", "keys", "steps"))
            low = jnp.clip(lax.div(first_key - key, step), 0, steps)
            high = jnp.clip(lax.div(high_key - key + step, step), 0, steps)

            def turn(at, carry):
                one_step(pl.multiple_of(left + at * step, step), key + at * step)
                return carry

            lax.fori_loop(low, high, turn, 0)
            return carry

        lax.fori_loop(0, STRETCHES, one_part, 0)
        own = (place >= begin) & (place < end)
        for head in range(heads):
            here = pl.ds(pl.multiple_of(head * local + start, SIDE), count)
            part = slice(head * count, (head + 1) * count)
            sums[here, :] += jnp.where(own, chunk_sum[part, :], 0.0)
            if online:
                tops[here, :] = jnp.where(own, chunk_top[part, :], tops[here, :])

    def all_chunks(count, online, request, begin, end):
        aligned = lax.div(begin, SIDE) * SIDE

        def turn(at, carry):
            from_row = aligned + at * count
            one_chunk(
                count,
                online,
                request,
                jnp.maximum(begin, from_row),
                jnp.minimum(end, from_row + count),
                jnp.minimum(from_row, local - count),
            )
            return carry

        lax.fori_loop(0, lax.div(end - aligned + (count - 1), count), turn, 0)

    many, few = min(2 * rows + SIDE, local), min(FEW_ROWS, local)

    def one_request(request, carry):
        begin, end = plan_ref[places["begin"] + request], plan_ref[places["end"] + request]
        large = end - lax.div(begin, SIDE) * SIDE > 2 * few

        @pl.when((end > begin) & calm & large)
        def _():
            all_chunks(many, False, request, begin, end)

        @pl.when((end > begin) & calm & jnp.logical_not(large))
        def _():
            all_chunks(few, False, request, begin, end)

        @pl.when((end > begin) & jnp.logical_not(calm))
        def _():
            all_chunks(few, True, request, begin, end)

        return carry

    lax.fori_loop(0, requests, one_request, 0)

    lane = lax.broadcasted_iota(jnp.int32, (LANES, LANES), 1)
    for slot, out_ref in enumerate(out_refs):
        start = plan_ref[places["groups"] + slot] * rows
        out_ref[rows:, :] = jnp.zeros((SIDE, heads * width), jnp.bfloat16)
        for at in range(0, rows, LANES):
            terms = jnp.zeros((LANES, LANES), jnp.float32)
            for head in range(heads):
                here = pl.ds(pl.multiple_of(head * local + start + at, LANES), LANES)
                out_ref[at:at + LANES, head * width:(head + 1) * width] = sums[here, :width].astype(jnp.bfloat16)
                weight = sums[here, width:]
                top = jnp.where(weight > 0.0, jnp.where(calm, 0.0, tops[here, :]), NEG)
                for term, value in enumerate((weight, top)):
                    high = value.astype(jnp.bfloat16).astype(jnp.float32)
                    terms = jnp.where(lane == 2 * term * heads + head, high, terms)
                    terms = jnp.where(lane == (2 * term + 1) * heads + head, value - high, terms)
            out_ref[rows:, at:at + LANES] = terms.T[:SIDE, :].astype(jnp.bfloat16)


def attend(places, plan, norms, stack, fetched, all_keys, beside, shape):
    groups, rows, heads, _ = shape
    cache, width = all_keys.shape[0] // 2, all_keys.shape[1]
    local = groups * rows
    most = heads * min(2 * rows + SIDE, local)
    _, _, *payloads = pl.pallas_call(
        functools.partial(attend_kernel, shape, dict(places)),
        out_shape=(pltpu.VMEM(all_keys.shape, all_keys.dtype), pltpu.VMEM(beside.shape, beside.dtype))
        + (jax.ShapeDtypeStruct((rows + SIDE, heads * width), jnp.bfloat16),) * groups,
        in_specs=[SMEM] * 3 + [VMEM] + [HBM] * 2 + [VMEM] * 2,
        out_specs=(VMEM,) * (groups + 2),
        input_output_aliases={6: 0, 7: 1},
        scratch_shapes=[
            pltpu.VMEM((heads * local, 2 * width), jnp.float32),
            pltpu.VMEM((heads * local, width), jnp.float32),
            pltpu.VMEM((most, width), jnp.bfloat16),
            pltpu.VMEM((most, 2 * width), jnp.float32),
            pltpu.VMEM((heads * min(FEW_ROWS, local), width), jnp.float32),
            pltpu.VMEM((2, cache // 2, 2 * width), jnp.bfloat16),
            pltpu.SemaphoreType.DMA((2,)),
        ],
        compiler_params=pltpu.CompilerParams(vmem_limit_bytes=28 * MIB),
        cost_estimate=pl.CostEstimate(
            flops=local * heads * cache * width * 4, bytes_accessed=24 * MIB, transcendentals=0
        ),
        name="attend",
    )(plan, *norms, stack, *fetched, all_keys, beside)
    return payloads


def merge_kernel(heads, there_at, plan_ref, *refs):
    parts, out_ref = refs[:-1], refs[-1]
    rows = out_ref.shape[0]
    width = out_ref.shape[1] // heads
    logs = [
        jnp.where(plan_ref[there_at + at] == 1, part[rows:, :rows].astype(jnp.float32), 0.0) for at, part in enumerate(parts)
    ]
    spare = LANES - SIDE * len(parts)
    if spare:
        logs.append(jnp.zeros((spare, rows), jnp.float32))
    terms = jnp.concatenate(logs, axis=0).T
    total = terms + pltpu.roll(terms, LANES - heads, 1)
    top = pltpu.roll(terms, LANES - 2 * heads, 1) + pltpu.roll(terms, LANES - 3 * heads, 1)
    lane = lax.broadcasted_iota(jnp.int32, (rows, LANES), 1)
    used = (lax.rem(lane, SIDE) < heads) & (lane < SIDE * len(parts)) & (total > 0.0)
    top = jnp.where(used, top, NEG)
    biggest = top
    for shift in (16, 32, 64):
        biggest = jnp.maximum(biggest, pltpu.roll(biggest, shift, 1))
    share = jnp.where(used, jnp.exp2(top - biggest), 0.0)
    weight = share * jnp.where(used, total, 0.0)
    for shift in (16, 32, 64):
        weight = weight + pltpu.roll(weight, shift, 1)
    share = share / weight
    for head in range(heads):
        own = slice(head * width, (head + 1) * width)
        mixed = jnp.zeros((rows, width), jnp.float32)
        for at, part in enumerate(parts):
            lane_at = at * SIDE + head
            mixed = mixed + part[:rows, own].astype(jnp.float32) * share[:, lane_at:lane_at + 1]
        out_ref[:, own] = mixed.astype(out_ref.dtype)


def merge(places, plan, parts, heads):
    rows = parts[0].shape[0] - SIDE
    return pl.pallas_call(
        functools.partial(merge_kernel, heads, places["there"]),
        out_shape=jax.ShapeDtypeStruct((rows, parts[0].shape[1]), jnp.bfloat16),
        in_specs=[SMEM] + [VMEM] * len(parts),
        out_specs=VMEM,
        compiler_params=pltpu.CompilerParams(vmem_limit_bytes=12 * MIB),
        name="merge",
    )(plan, *parts)


def project_kernel(order, going_on, last, from_at, plan_ref, *refs):
    refs = list(refs)
    before_ref = refs.pop(0) if going_on else None
    piece_refs, (w_ref, out_ref, token_ref) = refs[:len(order)], refs[len(order):]
    deep = piece_refs[0].shape[1]
    block = out_ref.shape[1]
    left = pl.multiple_of(pl.program_id(0) * block, block)
    token_ref[0] = jnp.int32(0)
    total = None
    for at, piece_ref in zip(order, piece_refs):
        own = pl.multiple_of(plan_ref[from_at + at] * deep, deep)
        term = jnp.dot(
            piece_ref[...], w_ref[pl.ds(own, deep), pl.ds(left, block)], preferred_element_type=jnp.float32
        )
        total = term if total is None else total + term
    if going_on:
        total = total + before_ref[:, pl.ds(left, block)]
    out_ref[...] = total.astype(out_ref.dtype)


def project(places, plan, order, pieces, w_out, before, last):
    rows, deep = pieces[0].shape
    depth, wide = w_out.shape
    block = min(1024, wide)
    going_on = before is not None
    return pl.pallas_call(
        functools.partial(project_kernel, order, going_on, last, places["from"]),
        out_shape=(
            pltpu.HBM((rows, wide), jnp.bfloat16) if last else pltpu.VMEM((rows, wide), jnp.float32),
            jax.ShapeDtypeStruct((1,), jnp.int32),
        ),
        grid=(wide // block,),
        in_specs=[SMEM] + [VMEM] * (going_on + len(pieces) + 1),
        out_specs=(pl.BlockSpec((rows, block), lambda at: (0, at)), SMEM),
        compiler_params=pltpu.CompilerParams(vmem_limit_bytes=16 * MIB),
        cost_estimate=pl.CostEstimate(
            flops=4 * rows * deep * len(pieces) * wide, bytes_accessed=2 * depth * wide, transcendentals=0
        ),
        name="project",
    )(plan, *([before] if going_on else []), *pieces, w_out)


def shift_pairs(count, stride, steps):
    groups = count // stride
    return [
        (group * stride + member, (group + steps) % groups * stride + member)
        for group in range(groups)
        for member in range(stride)
    ]


def swap_pairs(count):
    return [(at, at ^ 1) for at in range(count)]


def is_far(groups, one, two):
    low, high = min(one, two), max(one, two)
    return low < groups // 2 and high >= groups - max(1, groups // 4)


def move(value, groups, steps, far):
    pairs = [
        (source, target)
        for source, target in shift_pairs(2 * groups, 2, steps)
        if far or not is_far(groups, source // 2, target // 2)
    ]
    return lax.ppermute(value, "ctx", pairs) if pairs else jnp.zeros_like(value)


def plan_kernel(shape, places, new_ref, prior_ref, at_ref, plan_ref, far_ref):
    groups, chips, rows, cache, step = shape
    device, place = at_ref[0], at_ref[1]
    group, side, chip, core = lax.div(device, 2), lax.rem(device, 2), lax.div(place, 2), lax.rem(place, 2)
    table = request_table(new_ref, prior_ref)

    def rows_before(row):
        block = lax.div(row, rows)
        odd, inside = lax.rem(block, 2), lax.rem(row, rows)
        return lax.div(block, 2) * rows + jnp.where(odd == side, inside, jnp.where(odd == 1, rows, 0))

    for request, (row, key, ahead, row_end, _) in enumerate(table):
        plan_ref[places["first_key"] + request] = key
        plan_ref[places["ahead"] + request] = ahead
        plan_ref[places["begin"] + request] = rows_before(row)
        plan_ref[places["end"] + request] = rows_before(row_end)
    spans = [
        (key_range(table, jnp.int32(2 * rows * at))[0], key_range(table, jnp.int32(2 * rows * (at + 1) - 1))[1])
        for at in range(groups)
    ]
    needed = jnp.int32(0)
    for source in range(groups):
        for target in range(groups):
            if is_far(groups, source, target):
                first, last = spans[source]
                meet = (first < 2 * cache * (target + 1)) & (last >= 2 * cache * target)
                needed = jnp.where(meet, 1, needed)
    far_ref[0] = needed
    plan_ref[places["side"]] = side
    for steps in range(groups):
        plan_ref[places["groups"] + steps] = lax.rem(group + (groups - steps), groups)
        there = jnp.int32(1)
        for at in range(groups):
            if is_far(groups, (at + steps) % groups, at):
                there = jnp.where(group == at, needed, there)
        plan_ref[places["there"] + steps] = there
    other = (device + 1 - 2 * side) * cache
    half = cache // 2
    stretches = [
        (0, device * cache, cache), (cache, other + core * half, half), (cache + half, other + (1 - core) * half, half)
    ]
    for at, (left, key, count) in enumerate(stretches):
        plan_ref[places["lefts"] + at] = jnp.int32(left)
        plan_ref[places["keys"] + at] = key
        plan_ref[places["steps"] + at] = jnp.int32(count // step)
    for at in range(2 * chips):
        own = core if at < chips else 1 - core
        plan_ref[places["from"] + at] = lax.rem(chip + (chips - at % chips), chips) * 2 + own


def make_plan(shape, new_counts, prior_lengths, at):
    groups, chips = shape[:2]
    requests = new_counts.shape[0]
    sizes = dict(first_key=requests, ahead=requests, begin=requests, end=requests, side=1)
    sizes.update(groups=groups, there=groups, lefts=STRETCHES, keys=STRETCHES, steps=STRETCHES)
    sizes["from"] = 2 * chips
    places, total = {}, 0
    for name, size in sizes.items():
        places[name] = total
        total += size
    plan, far = pl.pallas_call(
        functools.partial(plan_kernel, shape, dict(places)),
        out_shape=(jax.ShapeDtypeStruct((total,), jnp.int32), jax.ShapeDtypeStruct((1,), jnp.int32)),
        in_specs=[SMEM] * 3,
        out_specs=(SMEM, SMEM),
        name="plan",
    )(new_counts, prior_lengths, at)
    return places, plan, far


def body(queries, keys, values, w_out, new_counts, prior_lengths):
    ctx_count, head_count = lax.axis_size("ctx"), lax.axis_size("head")
    rows = queries.shape[0]
    cache = keys.shape[0]
    groups, chips = ctx_count // 2, head_count // 2
    at = jnp.stack([lax.axis_index("ctx"), lax.axis_index("head")]).astype(jnp.int32)
    shape = (groups, chips, rows, cache, min(KEY_TILE, cache // 2))
    places, plan, far = make_plan(shape, new_counts, prior_lengths, at)
    requests = new_counts.shape[0]
    return lax.cond(
        far[0] == 1,
        functools.partial(attend_and_project, places, requests, True),
        functools.partial(attend_and_project, places, requests, False),
        *(queries, keys, values, w_out, plan),
    )


def attend_and_project(places, requests, far, queries, keys, values, w_out, plan):
    ctx_count, head_count = lax.axis_size("ctx"), lax.axis_size("head")
    rows = queries.shape[0]
    cache, width = keys.shape
    heads = queries.shape[1] // width
    groups, chips = ctx_count // 2, head_count // 2

    blocks = [move(queries, groups, steps, far) for steps in range(1, groups)]

    half = cache // 2
    start = lax.axis_index("head") % 2 * half
    mine = [lax.dynamic_slice_in_dim(array, start, half, axis=0) for array in (keys, values)]
    got = lax.ppermute(jnp.concatenate(mine, axis=1), "ctx", swap_pairs(ctx_count))
    all_keys, beside, own_norm, near_w = prepare(keys, values, w_out)
    stack, query_norm = stack_queries(places, plan, [queries] + blocks, width)
    got, query_norm, own_norm = lax.optimization_barrier((got, query_norm, own_norm))
    fetched = [got, lax.ppermute(got, "head", swap_pairs(head_count))]
    shape = (groups, rows, heads, requests)
    parts = attend(places, plan, (own_norm, query_norm), stack, fetched, all_keys, beside, shape)
    back = [parts[0]] + [move(parts[steps], groups, groups - steps, far) for steps in range(1, groups)]
    attended = merge(places, plan, back, heads)

    away = [lax.ppermute(attended, "head", shift_pairs(head_count, 2, steps)) for steps in range(1, chips)]
    pair = lax.ppermute(attended, "head", swap_pairs(head_count))
    mixed, token = project(places, plan, [0, chips], [attended, pair], near_w, None, False)
    away = [piece + token[0].astype(piece.dtype) for piece in away]
    away = away + [lax.ppermute(piece, "head", swap_pairs(head_count)) for piece in away]
    order = [*range(1, chips), *range(chips + 1, 2 * chips)]
    mixed, _ = project(places, plan, order, away, near_w, mixed, True)
    return mixed


def solution(mesh):
    return jax.shard_map(
        body,
        mesh=mesh,
        in_specs=(P("ctx", "head"), P("ctx", None), P("ctx", None), P(None, "head"), P(), P()),
        out_specs=P("ctx", "head"),
        check_vma=False,
    )
```

```python
import functools
import math

import jax
import jax.numpy as jnp
from jax import lax
from jax.experimental import pallas as pl
from jax.experimental.pallas import tpu as pltpu
from jax.sharding import PartitionSpec as P

NEG = -1e30
CALM = 60.0
KEY_TILE = 512
FEW_ROWS = 64
SIDE = 16
LANES = 128
STRETCHES = 3
MIB = 1024 * 1024
SMEM = pl.BlockSpec(memory_space=pltpu.SMEM)
VMEM = pl.BlockSpec(memory_space=pltpu.VMEM)
HBM = pl.BlockSpec(memory_space=pltpu.HBM)


def lengths(rows):
    wide = rows.astype(jnp.float32)
    return jnp.sum(wide * wide, axis=1, keepdims=True)


def fill(from_keys, from_values, done, keys_ref, beside_ref):
    count, width = from_keys.shape
    step = min(KEY_TILE, count)

    def turn(at, longest):
        here = pl.ds(pl.multiple_of(at * step, step), step)
        there = pl.ds(pl.multiple_of(done + at * step, step), step)
        keys = from_keys[here, :]
        keys_ref[there, :] = keys
        beside_ref[there, :width] = from_values[here, :]
        beside_ref[there, width:] = jnp.ones((step, width), jnp.bfloat16)
        return jnp.maximum(longest, lengths(keys))

    return jnp.max(lax.fori_loop(0, count // step, turn, jnp.zeros((step, 1), jnp.float32)))


def prepare_kernel(keys_ref, values_ref, far_w, all_keys, beside_ref, longest_ref, near_w, sem):
    fetch = pltpu.make_async_copy(far_w, near_w, sem)
    fetch.start()
    longest_ref[0] = fill(keys_ref, values_ref, 0, all_keys, beside_ref)
    fetch.wait()


def prepare(keys, values, w_out):
    cache, width = keys.shape
    return pl.pallas_call(
        prepare_kernel,
        out_shape=(
            pltpu.VMEM((2 * cache, width), jnp.bfloat16),
            pltpu.VMEM((2 * cache, 2 * width), jnp.bfloat16),
            jax.ShapeDtypeStruct((1,), jnp.float32),
            pltpu.VMEM(w_out.shape, w_out.dtype),
        ),
        in_specs=[VMEM, VMEM, HBM],
        out_specs=(VMEM, VMEM, SMEM, VMEM),
        scratch_shapes=[pltpu.SemaphoreType.DMA],
        compiler_params=pltpu.CompilerParams(vmem_limit_bytes=4 * MIB),
        name="prepare",
    )(keys, values, pltpu.with_memory_space_constraint(w_out, pltpu.HBM))


def stack_kernel(slots, group_at, width, plan_ref, *refs):
    q_refs, (stack_ref, longest_ref, q_all, sems) = refs[:slots], refs[slots:]
    rows = q_refs[0].shape[0]
    heads = q_refs[0].shape[1] // width
    local = slots * rows
    copies = [pltpu.make_async_copy(q_ref, q_all.at[slot], sems.at[slot]) for slot, q_ref in enumerate(q_refs)]
    for copy in copies:
        copy.start()
    longest = jnp.zeros((rows, 1), jnp.float32)
    for slot, copy in enumerate(copies):
        copy.wait()
        start = plan_ref[group_at + slot] * rows
        for head in range(heads):
            part = q_all[slot, :, head * width:(head + 1) * width]
            stack_ref[pl.ds(pl.multiple_of(head * local + start, rows), rows), :] = part
            longest = jnp.maximum(longest, lengths(part))
    longest_ref[0] = jnp.max(longest)


def stack_queries(places, plan, queries, width):
    slots, (rows, wide) = len(queries), queries[0].shape
    return pl.pallas_call(
        functools.partial(stack_kernel, slots, places["groups"], width),
        out_shape=(
            pltpu.VMEM((slots * rows * (wide // width), width), jnp.bfloat16),
            jax.ShapeDtypeStruct((1,), jnp.float32),
        ),
        in_specs=[SMEM] + [HBM] * slots,
        out_specs=(VMEM, SMEM),
        scratch_shapes=[pltpu.VMEM((slots, rows, wide), jnp.bfloat16), pltpu.SemaphoreType.DMA((slots,))],
        compiler_params=pltpu.CompilerParams(vmem_limit_bytes=4 * MIB),
        name="stack",
    )(plan, *queries)


def request_table(new_ref, prior_ref):
    table = []
    row, key = jnp.int32(0), jnp.int32(0)
    for request in range(new_ref.shape[0]):
        new, prior = new_ref[request], prior_ref[request]
        table.append((row, key, key + prior - row, row + new, key + new + prior))
        row, key = row + new, key + new + prior
    return table


def key_range(table, row):
    first, shift = table[0][1], table[0][2]
    for start, key, ahead, _, _ in table[1:]:
        own = row >= start
        first = jnp.where(own, key, first)
        shift = jnp.where(own, ahead, shift)
    return first, row + shift


def attend_kernel(shape, places, *refs):
    groups, rows, heads, requests = shape
    plan_ref, key_norm_ref, query_norm_ref, stack_ref = refs[:4]
    fetched = refs[4:6]
    keys_ref, beside_ref = refs[8:10]
    out_refs = refs[10:10 + groups]
    sums, tops, chunk_q, chunk_sum, chunk_top, arrived, sems = refs[10 + groups:]
    cache, width = keys_ref.shape[0] // 2, keys_ref.shape[1]
    local = groups * rows
    step = min(KEY_TILE, cache // 2)
    scale = width ** (-0.5)
    factor = scale * math.log2(math.e)
    copies = [pltpu.make_async_copy(ref, arrived.at[at], sems.at[at]) for at, ref in enumerate(fetched)]
    for copy in copies:
        copy.start()
    key_norm = key_norm_ref[0]
    for at, copy in enumerate(copies):
        copy.wait()
        part = arrived.at[at]
        longest = fill(part.at[:, :width], part.at[:, width:], cache + at * (cache // 2), keys_ref, beside_ref)
        key_norm = jnp.maximum(key_norm, longest)
    calm = key_norm * query_norm_ref[0] * (scale * scale) <= CALM * CALM
    side = plan_ref[places["side"]]

    def clear(at, carry):
        sums[pl.ds(pl.multiple_of(at * rows, rows), rows), :] = jnp.zeros((rows, 2 * width), jnp.float32)
        return carry

    lax.fori_loop(0, heads * groups, clear, 0)

    def global_row(place):
        whole = place + side * rows
        for group in range(1, groups):
            whole = whole + jnp.where(place >= group * rows, rows, 0)
        return whole

    def one_chunk(count, online, request, begin, end, start):
        first_key = plan_ref[places["first_key"] + request]
        ahead = plan_ref[places["ahead"] + request]
        start = pl.multiple_of(start, SIDE)
        low_key, high_key = global_row(begin) + ahead, global_row(end - 1) + ahead
        total = heads * count
        for head in range(heads):
            chunk_q[head * count:(head + 1) * count, :] = stack_ref[
                pl.ds(pl.multiple_of(head * local + start, SIDE), count), :
            ]
        chunk_sum[:total, :] = jnp.zeros((total, 2 * width), jnp.float32)
        if online:
            chunk_top[:total, :] = jnp.full((total, width), NEG, jnp.float32)
        place = start + lax.broadcasted_iota(jnp.int32, (count, 1), 0)
        last = global_row(place) + ahead

        def scores(part, left):
            return lax.dot_general(
                chunk_q[part, :], keys_ref[pl.ds(left, step), :], (((1,), (1,)), ((), ())),
                preferred_element_type=jnp.float32,
            ) * factor

        def add(left, weights):
            return jnp.dot(
                weights.astype(jnp.bfloat16), beside_ref[pl.ds(left, step), :], preferred_element_type=jnp.float32
            )

        def one_step(left, key):
            def allowed():
                index = key + lax.broadcasted_iota(jnp.int32, (count, step), 1)
                return (index >= first_key) & (index <= last)

            if online:
                mask = allowed()

                def one_head(head, carry):
                    part = pl.ds(pl.multiple_of(head * count, count), count)
                    score = jnp.where(mask, scores(part, left), NEG)
                    old = chunk_top[part, :]
                    new = jnp.maximum(old, jnp.ceil(jnp.max(score, axis=1, keepdims=True)))
                    weights = jnp.where(mask, jnp.exp2(score - new[:, :1]), 0.0)
                    shrink = jnp.exp2(old - new)
                    chunk_sum[part, :width] = chunk_sum[part, :width] * shrink
                    chunk_sum[part, width:] = chunk_sum[part, width:] * shrink
                    chunk_sum[part, :] += add(left, weights)
                    chunk_top[part, :] = new
                    return carry

                lax.fori_loop(0, heads, one_head, 0)
                return

            plain = (key >= first_key) & (key + step - 1 <= low_key)

            @pl.when(plain)
            def _():
                for head in range(heads):
                    part = pl.ds(head * count, count)
                    chunk_sum[part, :] += add(left, jnp.exp2(scores(part, left)))

            @pl.when(jnp.logical_not(plain))
            def _():
                mask = allowed()
                weights = jnp.exp2(scores(pl.ds(0, total), left))
                weights = jnp.concatenate([
                    jnp.where(mask, weights[head * count:(head + 1) * count, :], 0.0) for head in range(heads)
                ])
                chunk_sum[:total, :] += add(left, weights)

        def one_part(part, carry):
            left, key, steps = (plan_ref[places[name] + part] for name in ("lefts", "keys", "steps"))
            low = jnp.clip(lax.div(first_key - key, step), 0, steps)
            high = jnp.clip(lax.div(high_key - key + step, step), 0, steps)

            def turn(at, carry):
                one_step(pl.multiple_of(left + at * step, step), key + at * step)
                return carry

            lax.fori_loop(low, high, turn, 0)
            return carry

        lax.fori_loop(0, STRETCHES, one_part, 0)
        own = (place >= begin) & (place < end)
        for head in range(heads):
            here = pl.ds(pl.multiple_of(head * local + start, SIDE), count)
            part = slice(head * count, (head + 1) * count)
            sums[here, :] += jnp.where(own, chunk_sum[part, :], 0.0)
            if online:
                tops[here, :] = jnp.where(own, chunk_top[part, :], tops[here, :])

    def all_chunks(count, online, request, begin, end):
        aligned = lax.div(begin, SIDE) * SIDE

        def turn(at, carry):
            from_row = aligned + at * count
            one_chunk(
                count,
                online,
                request,
                jnp.maximum(begin, from_row),
                jnp.minimum(end, from_row + count),
                jnp.minimum(from_row, local - count),
            )
            return carry

        lax.fori_loop(0, lax.div(end - aligned + (count - 1), count), turn, 0)

    many, few = min(2 * rows + SIDE, local), min(FEW_ROWS, local)

    def one_request(request, carry):
        begin, end = plan_ref[places["begin"] + request], plan_ref[places["end"] + request]
        large = end - lax.div(begin, SIDE) * SIDE > 2 * few

        @pl.when((end > begin) & calm & large)
        def _():
            all_chunks(many, False, request, begin, end)

        @pl.when((end > begin) & calm & jnp.logical_not(large))
        def _():
            all_chunks(few, False, request, begin, end)

        @pl.when((end > begin) & jnp.logical_not(calm))
        def _():
            all_chunks(few, True, request, begin, end)

        return carry

    lax.fori_loop(0, requests, one_request, 0)

    lane = lax.broadcasted_iota(jnp.int32, (LANES, LANES), 1)
    for slot, out_ref in enumerate(out_refs):
        start = plan_ref[places["groups"] + slot] * rows
        out_ref[rows:, :] = jnp.zeros((SIDE, heads * width), jnp.bfloat16)
        for at in range(0, rows, LANES):
            terms = jnp.zeros((LANES, LANES), jnp.float32)
            for head in range(heads):
                here = pl.ds(pl.multiple_of(head * local + start + at, LANES), LANES)
                out_ref[at:at + LANES, head * width:(head + 1) * width] = sums[here, :width].astype(jnp.bfloat16)
                weight = sums[here, width:]
                top = jnp.where(weight > 0.0, jnp.where(calm, 0.0, tops[here, :]), NEG)
                for term, value in enumerate((weight, top)):
                    high = value.astype(jnp.bfloat16).astype(jnp.float32)
                    terms = jnp.where(lane == 2 * term * heads + head, high, terms)
                    terms = jnp.where(lane == (2 * term + 1) * heads + head, value - high, terms)
            out_ref[rows:, at:at + LANES] = terms.T[:SIDE, :].astype(jnp.bfloat16)


def attend(places, plan, norms, stack, fetched, all_keys, beside, shape):
    groups, rows, heads, _ = shape
    cache, width = all_keys.shape[0] // 2, all_keys.shape[1]
    local = groups * rows
    most = heads * min(2 * rows + SIDE, local)
    _, _, *payloads = pl.pallas_call(
        functools.partial(attend_kernel, shape, dict(places)),
        out_shape=(pltpu.VMEM(all_keys.shape, all_keys.dtype), pltpu.VMEM(beside.shape, beside.dtype))
        + (jax.ShapeDtypeStruct((rows + SIDE, heads * width), jnp.bfloat16),) * groups,
        in_specs=[SMEM] * 3 + [VMEM] + [HBM] * 2 + [VMEM] * 2,
        out_specs=(VMEM,) * (groups + 2),
        input_output_aliases={6: 0, 7: 1},
        scratch_shapes=[
            pltpu.VMEM((heads * local, 2 * width), jnp.float32),
            pltpu.VMEM((heads * local, width), jnp.float32),
            pltpu.VMEM((most, width), jnp.bfloat16),
            pltpu.VMEM((most, 2 * width), jnp.float32),
            pltpu.VMEM((heads * min(FEW_ROWS, local), width), jnp.float32),
            pltpu.VMEM((2, cache // 2, 2 * width), jnp.bfloat16),
            pltpu.SemaphoreType.DMA((2,)),
        ],
        compiler_params=pltpu.CompilerParams(vmem_limit_bytes=28 * MIB),
        cost_estimate=pl.CostEstimate(
            flops=local * heads * cache * width * 4, bytes_accessed=24 * MIB, transcendentals=0
        ),
        name="attend",
    )(plan, *norms, stack, *fetched, all_keys, beside)
    return payloads


def merge_kernel(heads, there_at, plan_ref, *refs):
    parts, out_ref = refs[:-1], refs[-1]
    rows = out_ref.shape[0]
    width = out_ref.shape[1] // heads
    logs = [
        jnp.where(plan_ref[there_at + at] == 1, part[rows:, :rows].astype(jnp.float32), 0.0) for at, part in enumerate(parts)
    ]
    spare = LANES - SIDE * len(parts)
    if spare:
        logs.append(jnp.zeros((spare, rows), jnp.float32))
    terms = jnp.concatenate(logs, axis=0).T
    total = terms + pltpu.roll(terms, LANES - heads, 1)
    top = pltpu.roll(terms, LANES - 2 * heads, 1) + pltpu.roll(terms, LANES - 3 * heads, 1)
    lane = lax.broadcasted_iota(jnp.int32, (rows, LANES), 1)
    used = (lax.rem(lane, SIDE) < heads) & (lane < SIDE * len(parts)) & (total > 0.0)
    top = jnp.where(used, top, NEG)
    biggest = top
    for shift in (16, 32, 64):
        biggest = jnp.maximum(biggest, pltpu.roll(biggest, shift, 1))
    share = jnp.where(used, jnp.exp2(top - biggest), 0.0)
    weight = share * jnp.where(used, total, 0.0)
    for shift in (16, 32, 64):
        weight = weight + pltpu.roll(weight, shift, 1)
    share = share / weight
    for head in range(heads):
        own = slice(head * width, (head + 1) * width)
        mixed = jnp.zeros((rows, width), jnp.float32)
        for at, part in enumerate(parts):
            lane_at = at * SIDE + head
            mixed = mixed + part[:rows, own].astype(jnp.float32) * share[:, lane_at:lane_at + 1]
        out_ref[:, own] = mixed.astype(out_ref.dtype)


def merge(places, plan, parts, heads):
    rows = parts[0].shape[0] - SIDE
    return pl.pallas_call(
        functools.partial(merge_kernel, heads, places["there"]),
        out_shape=jax.ShapeDtypeStruct((rows, parts[0].shape[1]), jnp.bfloat16),
        in_specs=[SMEM] + [VMEM] * len(parts),
        out_specs=VMEM,
        compiler_params=pltpu.CompilerParams(vmem_limit_bytes=12 * MIB),
        name="merge",
    )(plan, *parts)


def project_kernel(order, going_on, last, from_at, plan_ref, *refs):
    refs = list(refs)
    before_ref = refs.pop(0) if going_on else None
    piece_refs, (w_ref, out_ref, token_ref) = refs[:len(order)], refs[len(order):]
    deep = piece_refs[0].shape[1]
    block = out_ref.shape[1]
    left = pl.multiple_of(pl.program_id(0) * block, block)
    token_ref[0] = jnp.int32(0)
    total = None
    for at, piece_ref in zip(order, piece_refs):
        own = pl.multiple_of(plan_ref[from_at + at] * deep, deep)
        term = jnp.dot(
            piece_ref[...], w_ref[pl.ds(own, deep), pl.ds(left, block)], preferred_element_type=jnp.float32
        )
        total = term if total is None else total + term
    if going_on:
        total = total + before_ref[:, pl.ds(left, block)]
    out_ref[...] = total.astype(out_ref.dtype)


def project(places, plan, order, pieces, w_out, before, last):
    rows, deep = pieces[0].shape
    depth, wide = w_out.shape
    block = min(1024, wide)
    going_on = before is not None
    return pl.pallas_call(
        functools.partial(project_kernel, order, going_on, last, places["from"]),
        out_shape=(
            pltpu.HBM((rows, wide), jnp.bfloat16) if last else pltpu.VMEM((rows, wide), jnp.float32),
            jax.ShapeDtypeStruct((1,), jnp.int32),
        ),
        grid=(wide // block,),
        in_specs=[SMEM] + [VMEM] * (going_on + len(pieces) + 1),
        out_specs=(pl.BlockSpec((rows, block), lambda at: (0, at)), SMEM),
        compiler_params=pltpu.CompilerParams(vmem_limit_bytes=16 * MIB),
        cost_estimate=pl.CostEstimate(
            flops=4 * rows * deep * len(pieces) * wide, bytes_accessed=2 * depth * wide, transcendentals=0
        ),
        name="project",
    )(plan, *([before] if going_on else []), *pieces, w_out)


def shift_pairs(count, stride, steps):
    groups = count // stride
    return [
        (group * stride + member, (group + steps) % groups * stride + member)
        for group in range(groups)
        for member in range(stride)
    ]


def swap_pairs(count):
    return [(at, at ^ 1) for at in range(count)]


def is_far(groups, one, two):
    low, high = min(one, two), max(one, two)
    return low < groups // 2 and high >= groups - max(1, groups // 4)


def move(value, groups, steps, far):
    pairs = [
        (source, target)
        for source, target in shift_pairs(2 * groups, 2, steps)
        if far or not is_far(groups, source // 2, target // 2)
    ]
    return lax.ppermute(value, "ctx", pairs) if pairs else jnp.zeros_like(value)


def plan_kernel(shape, places, new_ref, prior_ref, at_ref, plan_ref, far_ref):
    groups, chips, rows, cache, step = shape
    device, place = at_ref[0], at_ref[1]
    group, side, chip, core = lax.div(device, 2), lax.rem(device, 2), lax.div(place, 2), lax.rem(place, 2)
    table = request_table(new_ref, prior_ref)

    def rows_before(row):
        block = lax.div(row, rows)
        odd, inside = lax.rem(block, 2), lax.rem(row, rows)
        return lax.div(block, 2) * rows + jnp.where(odd == side, inside, jnp.where(odd == 1, rows, 0))

    for request, (row, key, ahead, row_end, _) in enumerate(table):
        plan_ref[places["first_key"] + request] = key
        plan_ref[places["ahead"] + request] = ahead
        plan_ref[places["begin"] + request] = rows_before(row)
        plan_ref[places["end"] + request] = rows_before(row_end)
    spans = [
        (key_range(table, jnp.int32(2 * rows * at))[0], key_range(table, jnp.int32(2 * rows * (at + 1) - 1))[1])
        for at in range(groups)
    ]
    needed = jnp.int32(0)
    for source in range(groups):
        for target in range(groups):
            if is_far(groups, source, target):
                first, last = spans[source]
                meet = (first < 2 * cache * (target + 1)) & (last >= 2 * cache * target)
                needed = jnp.where(meet, 1, needed)
    far_ref[0] = needed
    plan_ref[places["side"]] = side
    for steps in range(groups):
        plan_ref[places["groups"] + steps] = lax.rem(group + (groups - steps), groups)
        there = jnp.int32(1)
        for at in range(groups):
            if is_far(groups, (at + steps) % groups, at):
                there = jnp.where(group == at, needed, there)
        plan_ref[places["there"] + steps] = there
    other = (device + 1 - 2 * side) * cache
    half = cache // 2
    stretches = [
        (0, device * cache, cache), (cache, other + core * half, half), (cache + half, other + (1 - core) * half, half)
    ]
    for at, (left, key, count) in enumerate(stretches):
        plan_ref[places["lefts"] + at] = jnp.int32(left)
        plan_ref[places["keys"] + at] = key
        plan_ref[places["steps"] + at] = jnp.int32(count // step)
    for at in range(2 * chips):
        own = core if at < chips else 1 - core
        plan_ref[places["from"] + at] = lax.rem(chip + (chips - at % chips), chips) * 2 + own


def make_plan(shape, new_counts, prior_lengths, at):
    groups, chips = shape[:2]
    requests = new_counts.shape[0]
    sizes = dict(first_key=requests, ahead=requests, begin=requests, end=requests, side=1)
    sizes.update(groups=groups, there=groups, lefts=STRETCHES, keys=STRETCHES, steps=STRETCHES)
    sizes["from"] = 2 * chips
    places, total = {}, 0
    for name, size in sizes.items():
        places[name] = total
        total += size
    plan, far = pl.pallas_call(
        functools.partial(plan_kernel, shape, dict(places)),
        out_shape=(jax.ShapeDtypeStruct((total,), jnp.int32), jax.ShapeDtypeStruct((1,), jnp.int32)),
        in_specs=[SMEM] * 3,
        out_specs=(SMEM, SMEM),
        name="plan",
    )(new_counts, prior_lengths, at)
    return places, plan, far


def body(queries, keys, values, w_out, new_counts, prior_lengths):
    ctx_count, head_count = lax.axis_size("ctx"), lax.axis_size("head")
    rows = queries.shape[0]
    cache = keys.shape[0]
    groups, chips = ctx_count // 2, head_count // 2
    at = jnp.stack([lax.axis_index("ctx"), lax.axis_index("head")]).astype(jnp.int32)
    shape = (groups, chips, rows, cache, min(KEY_TILE, cache // 2))
    places, plan, far = make_plan(shape, new_counts, prior_lengths, at)
    requests = new_counts.shape[0]
    return lax.cond(
        far[0] == 1,
        functools.partial(attend_and_project, places, requests, True),
        functools.partial(attend_and_project, places, requests, False),
        *(queries, keys, values, w_out, plan),
    )


def attend_and_project(places, requests, far, queries, keys, values, w_out, plan):
    ctx_count, head_count = lax.axis_size("ctx"), lax.axis_size("head")
    rows = queries.shape[0]
    cache, width = keys.shape
    heads = queries.shape[1] // width
    groups, chips = ctx_count // 2, head_count // 2

    blocks = [move(queries, groups, steps, far) for steps in range(1, groups)]

    half = cache // 2
    start = lax.axis_index("head") % 2 * half
    mine = [lax.dynamic_slice_in_dim(array, start, half, axis=0) for array in (keys, values)]
    got = lax.ppermute(jnp.concatenate(mine, axis=1), "ctx", swap_pairs(ctx_count))
    all_keys, beside, own_norm, near_w = prepare(keys, values, w_out)
    stack, query_norm = stack_queries(places, plan, [queries] + blocks, width)
    got, query_norm, own_norm = lax.optimization_barrier((got, query_norm, own_norm))
    fetched = [got, lax.ppermute(got, "head", swap_pairs(head_count))]
    shape = (groups, rows, heads, requests)
    parts = attend(places, plan, (own_norm, query_norm), stack, fetched, all_keys, beside, shape)
    back = [parts[0]] + [move(parts[steps], groups, groups - steps, far) for steps in range(1, groups)]
    attended = merge(places, plan, back, heads)

    away = [lax.ppermute(attended, "head", shift_pairs(head_count, 2, steps)) for steps in range(1, chips)]
    pair = lax.ppermute(attended, "head", swap_pairs(head_count))
    mixed, token = project(places, plan, [0, chips], [attended, pair], near_w, None, False)
    away = [piece + token[0].astype(piece.dtype) for piece in away]
    away = away + [lax.ppermute(piece, "head", swap_pairs(head_count)) for piece in away]
    order = [*range(1, chips), *range(chips + 1, 2 * chips)]
    mixed, _ = project(places, plan, order, away, near_w, mixed, True)
    return mixed


def solution(mesh):
    return jax.shard_map(
        body,
        mesh=mesh,
        in_specs=(P("ctx", "head"), P("ctx", None), P("ctx", None), P(None, "head"), P(), P()),
        out_specs=P("ctx", "head"),
        check_vma=False,
    )
```

```python
import functools
import math

import jax
import jax.numpy as jnp
from jax import lax
from jax.experimental import pallas as pl
from jax.experimental.pallas import tpu as pltpu
from jax.sharding import PartitionSpec as P

NEG = -1e30
CALM = 60.0
KEY_TILE = 512
RUN = 4
FEW_ROWS = 64
SIDE = 16
LANES = 128
STRETCHES = 3
MIB = 1024 * 1024
SMEM = pl.BlockSpec(memory_space=pltpu.SMEM)
VMEM = pl.BlockSpec(memory_space=pltpu.VMEM)
HBM = pl.BlockSpec(memory_space=pltpu.HBM)


def lengths(rows):
    wide = rows.astype(jnp.float32)
    return jnp.sum(wide * wide, axis=1, keepdims=True)


def fill(from_keys, from_values, done, keys_ref, beside_ref):
    count, width = from_keys.shape
    step = min(KEY_TILE, count)

    def turn(at, longest):
        here = pl.ds(pl.multiple_of(at * step, step), step)
        there = pl.ds(pl.multiple_of(done + at * step, step), step)
        keys = from_keys[here, :]
        keys_ref[there, :] = keys
        beside_ref[there, :width] = from_values[here, :]
        beside_ref[there, width:] = jnp.ones((step, width), jnp.bfloat16)
        return jnp.maximum(longest, lengths(keys))

    return jnp.max(lax.fori_loop(0, count // step, turn, jnp.zeros((step, 1), jnp.float32)))


def prepare_kernel(keys_ref, values_ref, far_w, all_keys, beside_ref, longest_ref, near_w, sem):
    fetch = pltpu.make_async_copy(far_w, near_w, sem)
    fetch.start()
    longest_ref[0] = fill(keys_ref, values_ref, 0, all_keys, beside_ref)
    fetch.wait()


def prepare(keys, values, w_out):
    cache, width = keys.shape
    return pl.pallas_call(
        prepare_kernel,
        out_shape=(
            pltpu.VMEM((2 * cache, width), jnp.bfloat16),
            pltpu.VMEM((2 * cache, 2 * width), jnp.bfloat16),
            jax.ShapeDtypeStruct((1,), jnp.float32),
            pltpu.VMEM(w_out.shape, w_out.dtype),
        ),
        in_specs=[VMEM, VMEM, HBM],
        out_specs=(VMEM, VMEM, SMEM, VMEM),
        scratch_shapes=[pltpu.SemaphoreType.DMA],
        compiler_params=pltpu.CompilerParams(vmem_limit_bytes=4 * MIB),
        name="prepare",
    )(keys, values, pltpu.with_memory_space_constraint(w_out, pltpu.HBM))


def stack_kernel(slots, group_at, width, plan_ref, *refs):
    q_refs, (stack_ref, longest_ref, q_all, sems) = refs[:slots], refs[slots:]
    rows = q_refs[0].shape[0]
    heads = q_refs[0].shape[1] // width
    local = slots * rows
    copies = [pltpu.make_async_copy(q_ref, q_all.at[slot], sems.at[slot]) for slot, q_ref in enumerate(q_refs)]
    for copy in copies:
        copy.start()
    longest = jnp.zeros((rows, 1), jnp.float32)
    for slot, copy in enumerate(copies):
        copy.wait()
        start = plan_ref[group_at + slot] * rows
        for head in range(heads):
            part = q_all[slot, :, head * width:(head + 1) * width]
            stack_ref[pl.ds(pl.multiple_of(head * local + start, rows), rows), :] = part
            longest = jnp.maximum(longest, lengths(part))
    longest_ref[0] = jnp.max(longest)


def stack_queries(places, plan, queries, width):
    slots, (rows, wide) = len(queries), queries[0].shape
    return pl.pallas_call(
        functools.partial(stack_kernel, slots, places["groups"], width),
        out_shape=(
            pltpu.VMEM((slots * rows * (wide // width), width), jnp.bfloat16),
            jax.ShapeDtypeStruct((1,), jnp.float32),
        ),
        in_specs=[SMEM] + [HBM] * slots,
        out_specs=(VMEM, SMEM),
        scratch_shapes=[pltpu.VMEM((slots, rows, wide), jnp.bfloat16), pltpu.SemaphoreType.DMA((slots,))],
        compiler_params=pltpu.CompilerParams(vmem_limit_bytes=4 * MIB),
        name="stack",
    )(plan, *queries)


def request_table(new_ref, prior_ref):
    table = []
    row, key = jnp.int32(0), jnp.int32(0)
    for request in range(new_ref.shape[0]):
        new, prior = new_ref[request], prior_ref[request]
        table.append((row, key, key + prior - row, row + new, key + new + prior))
        row, key = row + new, key + new + prior
    return table


def key_range(table, row):
    first, shift = table[0][1], table[0][2]
    for start, key, ahead, _, _ in table[1:]:
        own = row >= start
        first = jnp.where(own, key, first)
        shift = jnp.where(own, ahead, shift)
    return first, row + shift


def attend_kernel(shape, places, *refs):
    groups, rows, heads, requests = shape
    plan_ref, key_norm_ref, query_norm_ref, stack_ref = refs[:4]
    fetched = refs[4:6]
    keys_ref, beside_ref = refs[8:10]
    out_refs = refs[10:10 + groups]
    sums, tops, chunk_q, chunk_sum, chunk_top, arrived, sems = refs[10 + groups:]
    cache, width = keys_ref.shape[0] // 2, keys_ref.shape[1]
    local = groups * rows
    step = min(KEY_TILE, cache // 2)
    scale = width ** (-0.5)
    factor = scale * math.log2(math.e)
    copies = [pltpu.make_async_copy(ref, arrived.at[at], sems.at[at]) for at, ref in enumerate(fetched)]
    for copy in copies:
        copy.start()
    key_norm = key_norm_ref[0]
    for at, copy in enumerate(copies):
        copy.wait()
        part = arrived.at[at]
        longest = fill(part.at[:, :width], part.at[:, width:], cache + at * (cache // 2), keys_ref, beside_ref)
        key_norm = jnp.maximum(key_norm, longest)
    calm = key_norm * query_norm_ref[0] * (scale * scale) <= CALM * CALM
    side = plan_ref[places["side"]]

    def clear(at, carry):
        sums[pl.ds(pl.multiple_of(at * rows, rows), rows), :] = jnp.zeros((rows, 2 * width), jnp.float32)
        return carry

    lax.fori_loop(0, heads * groups, clear, 0)

    def global_row(place):
        whole = place + side * rows
        for group in range(1, groups):
            whole = whole + jnp.where(place >= group * rows, rows, 0)
        return whole

    def one_chunk(count, online, request, begin, end, start):
        first_key = plan_ref[places["first_key"] + request]
        ahead = plan_ref[places["ahead"] + request]
        start = pl.multiple_of(start, SIDE)
        low_key, high_key = global_row(begin) + ahead, global_row(end - 1) + ahead
        total = heads * count
        for head in range(heads):
            chunk_q[head * count:(head + 1) * count, :] = stack_ref[
                pl.ds(pl.multiple_of(head * local + start, SIDE), count), :
            ]
        chunk_sum[:total, :] = jnp.zeros((total, 2 * width), jnp.float32)
        if online:
            chunk_top[:total, :] = jnp.full((total, width), NEG, jnp.float32)
        place = start + lax.broadcasted_iota(jnp.int32, (count, 1), 0)
        last = global_row(place) + ahead

        def scores(part, left, keys):
            return lax.dot_general(
                chunk_q[part, :], keys_ref[pl.ds(left, keys), :], (((1,), (1,)), ((), ())),
                preferred_element_type=jnp.float32,
            ) * factor

        def add(part, left, weights):
            chunk_sum[part, :] += jnp.dot(
                weights.astype(jnp.bfloat16),
                beside_ref[pl.ds(left, weights.shape[1]), :],
                preferred_element_type=jnp.float32,
            )

        at_once = heads if count <= FEW_ROWS else 1

        def by_heads(work):
            def turn(at, carry):
                work(pl.ds(pl.multiple_of(at * (at_once * count), SIDE), at_once * count))
                return carry

            lax.fori_loop(0, heads // at_once, turn, 0)

        def plain_steps(left, steps):
            by_heads(lambda part: add(part, left, jnp.exp2(scores(part, left, steps * step))))

        def masked_step(left, key):
            index = key + lax.broadcasted_iota(jnp.int32, (count, step), 1)
            mask = (index >= first_key) & (index <= last)

            def work(part):
                weights = jnp.exp2(scores(part, left, step))
                weights = jnp.concatenate([
                    jnp.where(mask, weights[at * count:(at + 1) * count, :], 0.0) for at in range(at_once)
                ])
                add(part, left, weights)

            by_heads(work)

        def online_step(left, key):
            index = key + lax.broadcasted_iota(jnp.int32, (count, step), 1)
            mask = (index >= first_key) & (index <= last)

            def one_head(head, carry):
                part = pl.ds(pl.multiple_of(head * count, count), count)
                score = jnp.where(mask, scores(part, left, step), NEG)
                old = chunk_top[part, :]
                new = jnp.maximum(old, jnp.ceil(jnp.max(score, axis=1, keepdims=True)))
                weights = jnp.where(mask, jnp.exp2(score - new[:, :1]), 0.0)
                shrink = jnp.exp2(old - new)
                chunk_sum[part, :width] = chunk_sum[part, :width] * shrink
                chunk_sum[part, width:] = chunk_sum[part, width:] * shrink
                add(part, left, weights)
                chunk_top[part, :] = new
                return carry

            lax.fori_loop(0, heads, one_head, 0)

        def one_part(part, carry):
            left, key, steps = (plan_ref[places[name] + part] for name in ("lefts", "keys", "steps"))
            low = jnp.clip(lax.div(first_key - key, step), 0, steps)
            high = jnp.clip(lax.div(high_key - key + step, step), 0, steps)

            if online:

                def turn_online(at, carry):
                    online_step(pl.multiple_of(left + at * step, step), key + at * step)
                    return carry

                lax.fori_loop(low, high, turn_online, 0)
                return carry

            plain = jnp.clip(lax.div(first_key - key + (step - 1), step), low, high)
            plain_end = jnp.clip(lax.div(low_key + 1 - key, step), plain, high)
            runs = lax.div(plain_end - plain, RUN)

            def turn(at, carry):
                here, its_key = pl.multiple_of(left + at * step, step), key + at * step
                inside = (at >= plain) & (at < plain_end)

                @pl.when(inside & (at >= plain + RUN * runs))
                def _():
                    plain_steps(here, 1)

                @pl.when(jnp.logical_not(inside))
                def _():
                    masked_step(here, its_key)

                return carry

            lax.fori_loop(low, high, turn, 0)

            def run(at, carry):
                plain_steps(pl.multiple_of(left + (plain + RUN * at) * step, step), RUN)
                return carry

            lax.fori_loop(0, runs, run, 0)
            return carry

        lax.fori_loop(0, STRETCHES, one_part, 0)
        own = (place >= begin) & (place < end)
        for head in range(heads):
            here = pl.ds(pl.multiple_of(head * local + start, SIDE), count)
            part = slice(head * count, (head + 1) * count)
            sums[here, :] += jnp.where(own, chunk_sum[part, :], 0.0)
            if online:
                tops[here, :] = jnp.where(own, chunk_top[part, :], tops[here, :])

    def all_chunks(count, online, request, begin, end):
        aligned = lax.div(begin, SIDE) * SIDE

        def turn(at, carry):
            from_row = aligned + at * count
            one_chunk(
                count,
                online,
                request,
                jnp.maximum(begin, from_row),
                jnp.minimum(end, from_row + count),
                jnp.minimum(from_row, local - count),
            )
            return carry

        lax.fori_loop(0, lax.div(end - aligned + (count - 1), count), turn, 0)

    many, few = min(2 * rows + SIDE, local), min(FEW_ROWS, local)

    def one_request(request, carry):
        begin, end = plan_ref[places["begin"] + request], plan_ref[places["end"] + request]
        large = end - lax.div(begin, SIDE) * SIDE > 2 * few

        @pl.when((end > begin) & calm & large)
        def _():
            all_chunks(many, False, request, begin, end)

        @pl.when((end > begin) & calm & jnp.logical_not(large))
        def _():
            all_chunks(few, False, request, begin, end)

        @pl.when((end > begin) & jnp.logical_not(calm))
        def _():
            all_chunks(few, True, request, begin, end)

        return carry

    lax.fori_loop(0, requests, one_request, 0)

    lane = lax.broadcasted_iota(jnp.int32, (LANES, LANES), 1)
    for slot, out_ref in enumerate(out_refs):
        start = plan_ref[places["groups"] + slot] * rows
        out_ref[rows:, :] = jnp.zeros((SIDE, heads * width), jnp.bfloat16)
        for at in range(0, rows, LANES):
            terms = jnp.zeros((LANES, LANES), jnp.float32)
            for head in range(heads):
                here = pl.ds(pl.multiple_of(head * local + start + at, LANES), LANES)
                out_ref[at:at + LANES, head * width:(head + 1) * width] = sums[here, :width].astype(jnp.bfloat16)
                weight = sums[here, width:]
                top = jnp.where(weight > 0.0, jnp.where(calm, 0.0, tops[here, :]), NEG)
                for term, value in enumerate((weight, top)):
                    high = value.astype(jnp.bfloat16).astype(jnp.float32)
                    terms = jnp.where(lane == 2 * term * heads + head, high, terms)
                    terms = jnp.where(lane == (2 * term + 1) * heads + head, value - high, terms)
            out_ref[rows:, at:at + LANES] = terms.T[:SIDE, :].astype(jnp.bfloat16)


def attend(places, plan, norms, stack, fetched, all_keys, beside, shape):
    groups, rows, heads, _ = shape
    cache, width = all_keys.shape[0] // 2, all_keys.shape[1]
    local = groups * rows
    most = heads * min(2 * rows + SIDE, local)
    _, _, *payloads = pl.pallas_call(
        functools.partial(attend_kernel, shape, dict(places)),
        out_shape=(pltpu.VMEM(all_keys.shape, all_keys.dtype), pltpu.VMEM(beside.shape, beside.dtype))
        + (jax.ShapeDtypeStruct((rows + SIDE, heads * width), jnp.bfloat16),) * groups,
        in_specs=[SMEM] * 3 + [VMEM] + [HBM] * 2 + [VMEM] * 2,
        out_specs=(VMEM,) * (groups + 2),
        input_output_aliases={6: 0, 7: 1},
        scratch_shapes=[
            pltpu.VMEM((heads * local, 2 * width), jnp.float32),
            pltpu.VMEM((heads * local, width), jnp.float32),
            pltpu.VMEM((most, width), jnp.bfloat16),
            pltpu.VMEM((most, 2 * width), jnp.float32),
            pltpu.VMEM((heads * min(FEW_ROWS, local), width), jnp.float32),
            pltpu.VMEM((2, cache // 2, 2 * width), jnp.bfloat16),
            pltpu.SemaphoreType.DMA((2,)),
        ],
        compiler_params=pltpu.CompilerParams(vmem_limit_bytes=28 * MIB),
        cost_estimate=pl.CostEstimate(
            flops=local * heads * cache * width * 4, bytes_accessed=24 * MIB, transcendentals=0
        ),
        name="attend",
    )(plan, *norms, stack, *fetched, all_keys, beside)
    return payloads


def merge_kernel(heads, there_at, plan_ref, *refs):
    parts, out_ref = refs[:-1], refs[-1]
    rows = out_ref.shape[0]
    width = out_ref.shape[1] // heads
    logs = [
        jnp.where(plan_ref[there_at + at] == 1, part[rows:, :rows].astype(jnp.float32), 0.0) for at, part in enumerate(parts)
    ]
    spare = LANES - SIDE * len(parts)
    if spare:
        logs.append(jnp.zeros((spare, rows), jnp.float32))
    terms = jnp.concatenate(logs, axis=0).T
    total = terms + pltpu.roll(terms, LANES - heads, 1)
    top = pltpu.roll(terms, LANES - 2 * heads, 1) + pltpu.roll(terms, LANES - 3 * heads, 1)
    lane = lax.broadcasted_iota(jnp.int32, (rows, LANES), 1)
    used = (lax.rem(lane, SIDE) < heads) & (lane < SIDE * len(parts)) & (total > 0.0)
    top = jnp.where(used, top, NEG)
    biggest = top
    for shift in (16, 32, 64):
        biggest = jnp.maximum(biggest, pltpu.roll(biggest, shift, 1))
    share = jnp.where(used, jnp.exp2(top - biggest), 0.0)
    weight = share * jnp.where(used, total, 0.0)
    for shift in (16, 32, 64):
        weight = weight + pltpu.roll(weight, shift, 1)
    share = share / weight
    for head in range(heads):
        own = slice(head * width, (head + 1) * width)
        mixed = jnp.zeros((rows, width), jnp.float32)
        for at, part in enumerate(parts):
            lane_at = at * SIDE + head
            mixed = mixed + part[:rows, own].astype(jnp.float32) * share[:, lane_at:lane_at + 1]
        out_ref[:, own] = mixed.astype(out_ref.dtype)


def merge(places, plan, parts, heads):
    rows = parts[0].shape[0] - SIDE
    return pl.pallas_call(
        functools.partial(merge_kernel, heads, places["there"]),
        out_shape=jax.ShapeDtypeStruct((rows, parts[0].shape[1]), jnp.bfloat16),
        in_specs=[SMEM] + [VMEM] * len(parts),
        out_specs=VMEM,
        compiler_params=pltpu.CompilerParams(vmem_limit_bytes=12 * MIB),
        name="merge",
    )(plan, *parts)


def project_kernel(order, going_on, last, from_at, plan_ref, *refs):
    refs = list(refs)
    before_ref = refs.pop(0) if going_on else None
    piece_refs, (w_ref, out_ref, token_ref) = refs[:len(order)], refs[len(order):]
    deep = piece_refs[0].shape[1]
    block = out_ref.shape[1]
    left = pl.multiple_of(pl.program_id(0) * block, block)
    token_ref[0] = jnp.int32(0)
    total = None
    for at, piece_ref in zip(order, piece_refs):
        own = pl.multiple_of(plan_ref[from_at + at] * deep, deep)
        term = jnp.dot(
            piece_ref[...], w_ref[pl.ds(own, deep), pl.ds(left, block)], preferred_element_type=jnp.float32
        )
        total = term if total is None else total + term
    if going_on:
        total = total + before_ref[:, pl.ds(left, block)]
    out_ref[...] = total.astype(out_ref.dtype)


def project(places, plan, order, pieces, w_out, before, last):
    rows, deep = pieces[0].shape
    depth, wide = w_out.shape
    block = min(1024, wide)
    going_on = before is not None
    return pl.pallas_call(
        functools.partial(project_kernel, order, going_on, last, places["from"]),
        out_shape=(
            pltpu.HBM((rows, wide), jnp.bfloat16) if last else pltpu.VMEM((rows, wide), jnp.float32),
            jax.ShapeDtypeStruct((1,), jnp.int32),
        ),
        grid=(wide // block,),
        in_specs=[SMEM] + [VMEM] * (going_on + len(pieces) + 1),
        out_specs=(pl.BlockSpec((rows, block), lambda at: (0, at)), SMEM),
        compiler_params=pltpu.CompilerParams(vmem_limit_bytes=16 * MIB),
        cost_estimate=pl.CostEstimate(
            flops=4 * rows * deep * len(pieces) * wide, bytes_accessed=2 * depth * wide, transcendentals=0
        ),
        name="project",
    )(plan, *([before] if going_on else []), *pieces, w_out)


def shift_pairs(count, stride, steps):
    groups = count // stride
    return [
        (group * stride + member, (group + steps) % groups * stride + member)
        for group in range(groups)
        for member in range(stride)
    ]


def swap_pairs(count):
    return [(at, at ^ 1) for at in range(count)]


def is_far(groups, one, two):
    low, high = min(one, two), max(one, two)
    return low < groups // 2 and high >= groups - max(1, groups // 4)


def move(value, groups, steps, far):
    pairs = [
        (source, target)
        for source, target in shift_pairs(2 * groups, 2, steps)
        if far or not is_far(groups, source // 2, target // 2)
    ]
    return lax.ppermute(value, "ctx", pairs) if pairs else jnp.zeros_like(value)


def plan_kernel(shape, places, new_ref, prior_ref, at_ref, plan_ref, far_ref):
    groups, chips, rows, cache, step = shape
    device, place = at_ref[0], at_ref[1]
    group, side, chip, core = lax.div(device, 2), lax.rem(device, 2), lax.div(place, 2), lax.rem(place, 2)
    table = request_table(new_ref, prior_ref)

    def rows_before(row):
        block = lax.div(row, rows)
        odd, inside = lax.rem(block, 2), lax.rem(row, rows)
        return lax.div(block, 2) * rows + jnp.where(odd == side, inside, jnp.where(odd == 1, rows, 0))

    for request, (row, key, ahead, row_end, _) in enumerate(table):
        plan_ref[places["first_key"] + request] = key
        plan_ref[places["ahead"] + request] = ahead
        plan_ref[places["begin"] + request] = rows_before(row)
        plan_ref[places["end"] + request] = rows_before(row_end)
    spans = [
        (key_range(table, jnp.int32(2 * rows * at))[0], key_range(table, jnp.int32(2 * rows * (at + 1) - 1))[1])
        for at in range(groups)
    ]
    needed = jnp.int32(0)
    for source in range(groups):
        for target in range(groups):
            if is_far(groups, source, target):
                first, last = spans[source]
                meet = (first < 2 * cache * (target + 1)) & (last >= 2 * cache * target)
                needed = jnp.where(meet, 1, needed)
    far_ref[0] = needed
    plan_ref[places["side"]] = side
    for steps in range(groups):
        plan_ref[places["groups"] + steps] = lax.rem(group + (groups - steps), groups)
        there = jnp.int32(1)
        for at in range(groups):
            if is_far(groups, (at + steps) % groups, at):
                there = jnp.where(group == at, needed, there)
        plan_ref[places["there"] + steps] = there
    other = (device + 1 - 2 * side) * cache
    half = cache // 2
    stretches = [
        (0, device * cache, cache), (cache, other + core * half, half), (cache + half, other + (1 - core) * half, half)
    ]
    for at, (left, key, count) in enumerate(stretches):
        plan_ref[places["lefts"] + at] = jnp.int32(left)
        plan_ref[places["keys"] + at] = key
        plan_ref[places["steps"] + at] = jnp.int32(count // step)
    for at in range(2 * chips):
        own = core if at < chips else 1 - core
        plan_ref[places["from"] + at] = lax.rem(chip + (chips - at % chips), chips) * 2 + own


def make_plan(shape, new_counts, prior_lengths, at):
    groups, chips = shape[:2]
    requests = new_counts.shape[0]
    sizes = dict(first_key=requests, ahead=requests, begin=requests, end=requests, side=1)
    sizes.update(groups=groups, there=groups, lefts=STRETCHES, keys=STRETCHES, steps=STRETCHES)
    sizes["from"] = 2 * chips
    places, total = {}, 0
    for name, size in sizes.items():
        places[name] = total
        total += size
    plan, far = pl.pallas_call(
        functools.partial(plan_kernel, shape, dict(places)),
        out_shape=(jax.ShapeDtypeStruct((total,), jnp.int32), jax.ShapeDtypeStruct((1,), jnp.int32)),
        in_specs=[SMEM] * 3,
        out_specs=(SMEM, SMEM),
        name="plan",
    )(new_counts, prior_lengths, at)
    return places, plan, far


def body(queries, keys, values, w_out, new_counts, prior_lengths):
    ctx_count, head_count = lax.axis_size("ctx"), lax.axis_size("head")
    rows = queries.shape[0]
    cache = keys.shape[0]
    groups, chips = ctx_count // 2, head_count // 2
    at = jnp.stack([lax.axis_index("ctx"), lax.axis_index("head")]).astype(jnp.int32)
    shape = (groups, chips, rows, cache, min(KEY_TILE, cache // 2))
    places, plan, far = make_plan(shape, new_counts, prior_lengths, at)
    requests = new_counts.shape[0]
    return lax.cond(
        far[0] == 1,
        functools.partial(attend_and_project, places, requests, True),
        functools.partial(attend_and_project, places, requests, False),
        *(queries, keys, values, w_out, plan),
    )


def attend_and_project(places, requests, far, queries, keys, values, w_out, plan):
    ctx_count, head_count = lax.axis_size("ctx"), lax.axis_size("head")
    rows = queries.shape[0]
    cache, width = keys.shape
    heads = queries.shape[1] // width
    groups, chips = ctx_count // 2, head_count // 2

    blocks = [move(queries, groups, steps, far) for steps in range(1, groups)]

    half = cache // 2
    start = lax.axis_index("head") % 2 * half
    mine = [lax.dynamic_slice_in_dim(array, start, half, axis=0) for array in (keys, values)]
    got = lax.ppermute(jnp.concatenate(mine, axis=1), "ctx", swap_pairs(ctx_count))
    all_keys, beside, own_norm, near_w = prepare(keys, values, w_out)
    stack, query_norm = stack_queries(places, plan, [queries] + blocks, width)
    got, query_norm, own_norm = lax.optimization_barrier((got, query_norm, own_norm))
    fetched = [got, lax.ppermute(got, "head", swap_pairs(head_count))]
    shape = (groups, rows, heads, requests)
    parts = attend(places, plan, (own_norm, query_norm), stack, fetched, all_keys, beside, shape)
    back = [parts[0]] + [move(parts[steps], groups, groups - steps, far) for steps in range(1, groups)]
    attended = merge(places, plan, back, heads)

    away = [lax.ppermute(attended, "head", shift_pairs(head_count, 2, steps)) for steps in range(1, chips)]
    pair = lax.ppermute(attended, "head", swap_pairs(head_count))
    mixed, token = project(places, plan, [0, chips], [attended, pair], near_w, None, False)
    away = [piece + token[0].astype(piece.dtype) for piece in away]
    away = away + [lax.ppermute(piece, "head", swap_pairs(head_count)) for piece in away]
    order = [*range(1, chips), *range(chips + 1, 2 * chips)]
    mixed, _ = project(places, plan, order, away, near_w, mixed, True)
    return mixed


def solution(mesh):
    return jax.shard_map(
        body,
        mesh=mesh,
        in_specs=(P("ctx", "head"), P("ctx", None), P("ctx", None), P(None, "head"), P(), P()),
        out_specs=P("ctx", "head"),
        check_vma=False,
    )
```

```python
import functools
import math

import jax
import jax.numpy as jnp
from jax import lax
from jax.experimental import pallas as pl
from jax.experimental.pallas import tpu as pltpu
from jax.sharding import PartitionSpec as P

NEG = -1e30
CALM = 60.0
KEY_TILE = 512
FEW_ROWS = 64
SIDE = 16
LANES = 128
STRETCHES = 3
MIB = 1024 * 1024
SMEM = pl.BlockSpec(memory_space=pltpu.SMEM)
VMEM = pl.BlockSpec(memory_space=pltpu.VMEM)
HBM = pl.BlockSpec(memory_space=pltpu.HBM)


def lengths(rows):
    wide = rows.astype(jnp.float32)
    return jnp.sum(wide * wide, axis=1, keepdims=True)


def fill(from_keys, from_values, done, keys_ref, beside_ref):
    count, width = from_keys.shape
    step = min(KEY_TILE, count)

    def turn(at, longest):
        here = pl.ds(pl.multiple_of(at * step, step), step)
        there = pl.ds(pl.multiple_of(done + at * step, step), step)
        keys = from_keys[here, :]
        keys_ref[there, :] = keys
        beside_ref[there, :width] = from_values[here, :]
        beside_ref[there, width:] = jnp.ones((step, width), jnp.bfloat16)
        return jnp.maximum(longest, lengths(keys))

    return jnp.max(lax.fori_loop(0, count // step, turn, jnp.zeros((step, 1), jnp.float32)))


def prepare_kernel(keys_ref, values_ref, far_w, all_keys, beside_ref, longest_ref, near_w, sem):
    fetch = pltpu.make_async_copy(far_w, near_w, sem)
    fetch.start()
    longest_ref[0] = fill(keys_ref, values_ref, 0, all_keys, beside_ref)
    fetch.wait()


def prepare(keys, values, w_out):
    cache, width = keys.shape
    return pl.pallas_call(
        prepare_kernel,
        out_shape=(
            pltpu.VMEM((2 * cache, width), jnp.bfloat16),
            pltpu.VMEM((2 * cache, 2 * width), jnp.bfloat16),
            jax.ShapeDtypeStruct((1,), jnp.float32),
            pltpu.VMEM(w_out.shape, w_out.dtype),
        ),
        in_specs=[VMEM, VMEM, HBM],
        out_specs=(VMEM, VMEM, SMEM, VMEM),
        scratch_shapes=[pltpu.SemaphoreType.DMA],
        compiler_params=pltpu.CompilerParams(vmem_limit_bytes=4 * MIB),
        name="prepare",
    )(keys, values, pltpu.with_memory_space_constraint(w_out, pltpu.HBM))


def stack_kernel(order, group_at, width, plan_ref, *refs):
    slots = len(order)
    q_refs, (stack_ref, longest_ref, q_all, sems) = refs[:slots], refs[slots:]
    rows = q_refs[0].shape[0]
    heads = q_refs[0].shape[1] // width
    local = slots * rows
    copies = [pltpu.make_async_copy(q_ref, q_all.at[slot], sems.at[slot]) for slot, q_ref in enumerate(q_refs)]
    for copy in copies:
        copy.start()
    longest = jnp.zeros((rows, 1), jnp.float32)
    for slot, copy in enumerate(copies):
        copy.wait()
        start = plan_ref[group_at + order[slot]] * rows
        for head in range(heads):
            part = q_all[slot, :, head * width:(head + 1) * width]
            stack_ref[pl.ds(pl.multiple_of(head * local + start, rows), rows), :] = part
            longest = jnp.maximum(longest, lengths(part))
    longest_ref[0] = jnp.max(longest)


def stack_queries(places, plan, order, queries, width):
    slots, (rows, wide) = len(queries), queries[0].shape
    return pl.pallas_call(
        functools.partial(stack_kernel, order, places["groups"], width),
        out_shape=(
            pltpu.VMEM((slots * rows * (wide // width), width), jnp.bfloat16),
            jax.ShapeDtypeStruct((1,), jnp.float32),
        ),
        in_specs=[SMEM] + [HBM] * slots,
        out_specs=(VMEM, SMEM),
        scratch_shapes=[pltpu.VMEM((slots, rows, wide), jnp.bfloat16), pltpu.SemaphoreType.DMA((slots,))],
        compiler_params=pltpu.CompilerParams(vmem_limit_bytes=4 * MIB),
        name="stack",
    )(plan, *queries)


def request_table(new_ref, prior_ref):
    table = []
    row, key = jnp.int32(0), jnp.int32(0)
    for request in range(new_ref.shape[0]):
        new, prior = new_ref[request], prior_ref[request]
        table.append((row, key, key + prior - row, row + new, key + new + prior))
        row, key = row + new, key + new + prior
    return table


def key_range(table, row):
    first, shift = table[0][1], table[0][2]
    for start, key, ahead, _, _ in table[1:]:
        own = row >= start
        first = jnp.where(own, key, first)
        shift = jnp.where(own, ahead, shift)
    return first, row + shift


def attend_kernel(shape, places, *refs):
    groups, rows, heads, requests = shape
    plan_ref, key_norm_ref, query_norm_ref, stack_ref = refs[:4]
    fetched = refs[4:6]
    keys_ref, beside_ref = refs[8:10]
    out_refs = refs[10:10 + groups]
    sums, tops, chunk_q, chunk_sum, chunk_top, arrived, sems = refs[10 + groups:]
    cache, width = keys_ref.shape[0] // 2, keys_ref.shape[1]
    local = groups * rows
    step = min(KEY_TILE, cache // 2)
    scale = width ** (-0.5)
    factor = scale * math.log2(math.e)
    copies = [pltpu.make_async_copy(ref, arrived.at[at], sems.at[at]) for at, ref in enumerate(fetched)]
    for copy in copies:
        copy.start()
    key_norm = key_norm_ref[0]
    for at, copy in enumerate(copies):
        copy.wait()
        part = arrived.at[at]
        longest = fill(part.at[:, :width], part.at[:, width:], cache + at * (cache // 2), keys_ref, beside_ref)
        key_norm = jnp.maximum(key_norm, longest)
    calm = key_norm * query_norm_ref[0] * (scale * scale) <= CALM * CALM
    side = plan_ref[places["side"]]

    def clear(at, carry):
        sums[pl.ds(pl.multiple_of(at * rows, rows), rows), :] = jnp.zeros((rows, 2 * width), jnp.float32)
        return carry

    lax.fori_loop(0, heads * groups, clear, 0)

    def global_row(place):
        whole = place + side * rows
        for group in range(1, groups):
            whole = whole + jnp.where(place >= group * rows, rows, 0)
        return whole

    def one_chunk(count, online, request, begin, end, start):
        first_key = plan_ref[places["first_key"] + request]
        ahead = plan_ref[places["ahead"] + request]
        start = pl.multiple_of(start, SIDE)
        low_key, high_key = global_row(begin) + ahead, global_row(end - 1) + ahead
        total = heads * count
        for head in range(heads):
            chunk_q[head * count:(head + 1) * count, :] = stack_ref[
                pl.ds(pl.multiple_of(head * local + start, SIDE), count), :
            ]
        chunk_sum[:total, :] = jnp.zeros((total, 2 * width), jnp.float32)
        if online:
            chunk_top[:total, :] = jnp.full((total, width), NEG, jnp.float32)
        place = start + lax.broadcasted_iota(jnp.int32, (count, 1), 0)
        last = global_row(place) + ahead

        def scores(part, left):
            return lax.dot_general(
                chunk_q[part, :], keys_ref[pl.ds(left, step), :], (((1,), (1,)), ((), ())),
                preferred_element_type=jnp.float32,
            ) * factor

        def add(left, weights):
            return jnp.dot(
                weights.astype(jnp.bfloat16), beside_ref[pl.ds(left, step), :], preferred_element_type=jnp.float32
            )

        def one_step(left, key):
            def allowed():
                index = key + lax.broadcasted_iota(jnp.int32, (count, step), 1)
                return (index >= first_key) & (index <= last)

            if online:
                mask = allowed()

                def one_head(head, carry):
                    part = pl.ds(pl.multiple_of(head * count, count), count)
                    score = jnp.where(mask, scores(part, left), NEG)
                    old = chunk_top[part, :]
                    new = jnp.maximum(old, jnp.ceil(jnp.max(score, axis=1, keepdims=True)))
                    weights = jnp.where(mask, jnp.exp2(score - new[:, :1]), 0.0)
                    shrink = jnp.exp2(old - new)
                    chunk_sum[part, :width] = chunk_sum[part, :width] * shrink
                    chunk_sum[part, width:] = chunk_sum[part, width:] * shrink
                    chunk_sum[part, :] += add(left, weights)
                    chunk_top[part, :] = new
                    return carry

                lax.fori_loop(0, heads, one_head, 0)
                return

            plain = (key >= first_key) & (key + step - 1 <= low_key)

            @pl.when(plain)
            def _():
                for head in range(heads):
                    part = pl.ds(head * count, count)
                    chunk_sum[part, :] += add(left, jnp.exp2(scores(part, left)))

            @pl.when(jnp.logical_not(plain))
            def _():
                mask = allowed()
                weights = jnp.exp2(scores(pl.ds(0, total), left))
                weights = jnp.concatenate([
                    jnp.where(mask, weights[head * count:(head + 1) * count, :], 0.0) for head in range(heads)
                ])
                chunk_sum[:total, :] += add(left, weights)

        def one_part(part, carry):
            left, key, steps = (plan_ref[places[name] + part] for name in ("lefts", "keys", "steps"))
            low = jnp.clip(lax.div(first_key - key, step), 0, steps)
            high = jnp.clip(lax.div(high_key - key + step, step), 0, steps)

            def turn(at, carry):
                one_step(pl.multiple_of(left + at * step, step), key + at * step)
                return carry

            lax.fori_loop(low, high, turn, 0)
            return carry

        lax.fori_loop(0, STRETCHES, one_part, 0)
        own = (place >= begin) & (place < end)
        for head in range(heads):
            here = pl.ds(pl.multiple_of(head * local + start, SIDE), count)
            part = slice(head * count, (head + 1) * count)
            sums[here, :] += jnp.where(own, chunk_sum[part, :], 0.0)
            if online:
                tops[here, :] = jnp.where(own, chunk_top[part, :], tops[here, :])

    def all_chunks(count, online, request, begin, end):
        aligned = lax.div(begin, SIDE) * SIDE

        def turn(at, carry):
            from_row = aligned + at * count
            one_chunk(
                count,
                online,
                request,
                jnp.maximum(begin, from_row),
                jnp.minimum(end, from_row + count),
                jnp.minimum(from_row, local - count),
            )
            return carry

        lax.fori_loop(0, lax.div(end - aligned + (count - 1), count), turn, 0)

    many, few = min(2 * rows + SIDE, local), min(FEW_ROWS, local)

    def one_request(request, carry):
        begin, end = plan_ref[places["begin"] + request], plan_ref[places["end"] + request]
        large = end - lax.div(begin, SIDE) * SIDE > 2 * few

        @pl.when((end > begin) & calm & large)
        def _():
            all_chunks(many, False, request, begin, end)

        @pl.when((end > begin) & calm & jnp.logical_not(large))
        def _():
            all_chunks(few, False, request, begin, end)

        @pl.when((end > begin) & jnp.logical_not(calm))
        def _():
            all_chunks(few, True, request, begin, end)

        return carry

    lax.fori_loop(0, requests, one_request, 0)

    lane = lax.broadcasted_iota(jnp.int32, (LANES, LANES), 1)
    for slot, out_ref in enumerate(out_refs):
        start = plan_ref[places["groups"] + slot] * rows
        out_ref[rows:, :] = jnp.zeros((SIDE, heads * width), jnp.bfloat16)
        for at in range(0, rows, LANES):
            terms = jnp.zeros((LANES, LANES), jnp.float32)
            for head in range(heads):
                here = pl.ds(pl.multiple_of(head * local + start + at, LANES), LANES)
                out_ref[at:at + LANES, head * width:(head + 1) * width] = sums[here, :width].astype(jnp.bfloat16)
                weight = sums[here, width:]
                top = jnp.where(weight > 0.0, jnp.where(calm, 0.0, tops[here, :]), NEG)
                for term, value in enumerate((weight, top)):
                    high = value.astype(jnp.bfloat16).astype(jnp.float32)
                    terms = jnp.where(lane == 2 * term * heads + head, high, terms)
                    terms = jnp.where(lane == (2 * term + 1) * heads + head, value - high, terms)
            out_ref[rows:, at:at + LANES] = terms.T[:SIDE, :].astype(jnp.bfloat16)


def attend(places, plan, norms, stack, fetched, all_keys, beside, shape):
    groups, rows, heads, _ = shape
    cache, width = all_keys.shape[0] // 2, all_keys.shape[1]
    local = groups * rows
    most = heads * min(2 * rows + SIDE, local)
    _, _, *payloads = pl.pallas_call(
        functools.partial(attend_kernel, shape, dict(places)),
        out_shape=(pltpu.VMEM(all_keys.shape, all_keys.dtype), pltpu.VMEM(beside.shape, beside.dtype))
        + (jax.ShapeDtypeStruct((rows + SIDE, heads * width), jnp.bfloat16),) * groups,
        in_specs=[SMEM] * 3 + [VMEM] + [HBM] * 2 + [VMEM] * 2,
        out_specs=(VMEM,) * (groups + 2),
        input_output_aliases={6: 0, 7: 1},
        scratch_shapes=[
            pltpu.VMEM((heads * local, 2 * width), jnp.float32),
            pltpu.VMEM((heads * local, width), jnp.float32),
            pltpu.VMEM((most, width), jnp.bfloat16),
            pltpu.VMEM((most, 2 * width), jnp.float32),
            pltpu.VMEM((heads * min(FEW_ROWS, local), width), jnp.float32),
            pltpu.VMEM((2, cache // 2, 2 * width), jnp.bfloat16),
            pltpu.SemaphoreType.DMA((2,)),
        ],
        compiler_params=pltpu.CompilerParams(vmem_limit_bytes=28 * MIB),
        cost_estimate=pl.CostEstimate(
            flops=local * heads * cache * width * 4, bytes_accessed=24 * MIB, transcendentals=0
        ),
        name="attend",
    )(plan, *norms, stack, *fetched, all_keys, beside)
    return payloads


def merge_kernel(heads, order, there_at, plan_ref, *refs):
    parts, out_ref = refs[:-1], refs[-1]
    rows = out_ref.shape[0]
    width = out_ref.shape[1] // heads
    logs = [
        jnp.where(plan_ref[there_at + order[at]] == 1, part[rows:, :rows].astype(jnp.float32), 0.0) for at, part in enumerate(parts)
    ]
    spare = LANES - SIDE * len(parts)
    if spare:
        logs.append(jnp.zeros((spare, rows), jnp.float32))
    terms = jnp.concatenate(logs, axis=0).T
    total = terms + pltpu.roll(terms, LANES - heads, 1)
    top = pltpu.roll(terms, LANES - 2 * heads, 1) + pltpu.roll(terms, LANES - 3 * heads, 1)
    lane = lax.broadcasted_iota(jnp.int32, (rows, LANES), 1)
    used = (lax.rem(lane, SIDE) < heads) & (lane < SIDE * len(parts)) & (total > 0.0)
    top = jnp.where(used, top, NEG)
    biggest = top
    for shift in (16, 32, 64):
        biggest = jnp.maximum(biggest, pltpu.roll(biggest, shift, 1))
    share = jnp.where(used, jnp.exp2(top - biggest), 0.0)
    weight = share * jnp.where(used, total, 0.0)
    for shift in (16, 32, 64):
        weight = weight + pltpu.roll(weight, shift, 1)
    share = share / weight
    for head in range(heads):
        own = slice(head * width, (head + 1) * width)
        mixed = jnp.zeros((rows, width), jnp.float32)
        for at, part in enumerate(parts):
            lane_at = at * SIDE + head
            mixed = mixed + part[:rows, own].astype(jnp.float32) * share[:, lane_at:lane_at + 1]
        out_ref[:, own] = mixed.astype(out_ref.dtype)


def merge(places, plan, order, parts, heads):
    rows = parts[0].shape[0] - SIDE
    return pl.pallas_call(
        functools.partial(merge_kernel, heads, order, places["there"]),
        out_shape=jax.ShapeDtypeStruct((rows, parts[0].shape[1]), jnp.bfloat16),
        in_specs=[SMEM] + [VMEM] * len(parts),
        out_specs=VMEM,
        compiler_params=pltpu.CompilerParams(vmem_limit_bytes=12 * MIB),
        name="merge",
    )(plan, *parts)


def project_kernel(order, going_on, last, from_at, plan_ref, *refs):
    refs = list(refs)
    before_ref = refs.pop(0) if going_on else None
    piece_refs, (w_ref, out_ref, token_ref) = refs[:len(order)], refs[len(order):]
    deep = piece_refs[0].shape[1]
    block = out_ref.shape[1]
    left = pl.multiple_of(pl.program_id(0) * block, block)
    token_ref[0] = jnp.int32(0)
    total = None
    for at, piece_ref in zip(order, piece_refs):
        own = pl.multiple_of(plan_ref[from_at + at] * deep, deep)
        term = jnp.dot(
            piece_ref[...], w_ref[pl.ds(own, deep), pl.ds(left, block)], preferred_element_type=jnp.float32
        )
        total = term if total is None else total + term
    if going_on:
        total = total + before_ref[:, pl.ds(left, block)]
    out_ref[...] = total.astype(out_ref.dtype)


def project(places, plan, order, pieces, w_out, before, last):
    rows, deep = pieces[0].shape
    depth, wide = w_out.shape
    block = min(1024, wide)
    going_on = before is not None
    return pl.pallas_call(
        functools.partial(project_kernel, order, going_on, last, places["from"]),
        out_shape=(
            pltpu.HBM((rows, wide), jnp.bfloat16) if last else pltpu.VMEM((rows, wide), jnp.float32),
            jax.ShapeDtypeStruct((1,), jnp.int32),
        ),
        grid=(wide // block,),
        in_specs=[SMEM] + [VMEM] * (going_on + len(pieces) + 1),
        out_specs=(pl.BlockSpec((rows, block), lambda at: (0, at)), SMEM),
        compiler_params=pltpu.CompilerParams(vmem_limit_bytes=16 * MIB),
        cost_estimate=pl.CostEstimate(
            flops=4 * rows * deep * len(pieces) * wide, bytes_accessed=2 * depth * wide, transcendentals=0
        ),
        name="project",
    )(plan, *([before] if going_on else []), *pieces, w_out)


def shift_pairs(count, stride, steps):
    groups = count // stride
    return [
        (group * stride + member, (group + steps) % groups * stride + member)
        for group in range(groups)
        for member in range(stride)
    ]


def swap_pairs(count):
    return [(at, at ^ 1) for at in range(count)]


def is_far(groups, one, two):
    low, high = min(one, two), max(one, two)
    return low < groups // 2 and high >= groups - max(1, groups // 4)


def move(value, groups, steps, far):
    pairs = [
        (source, target)
        for source, target in shift_pairs(2 * groups, 2, steps)
        if far or not is_far(groups, source // 2, target // 2)
    ]
    return lax.ppermute(value, "ctx", pairs) if pairs else jnp.zeros_like(value)


def plan_kernel(shape, places, new_ref, prior_ref, at_ref, keys_ref, values_ref, plan_ref, far_ref, mine_ref, sems):
    groups, chips, rows, cache, step = shape
    device, place = at_ref[0], at_ref[1]
    group, side, chip, core = lax.div(device, 2), lax.rem(device, 2), lax.div(place, 2), lax.rem(place, 2)
    half, width = mine_ref.shape[0], keys_ref.shape[1]
    here = pl.ds(pl.multiple_of(core * half, half), half)
    copies = [
        pltpu.make_async_copy(ref.at[here, :], mine_ref.at[:, at * width:(at + 1) * width], sems.at[at])
        for at, ref in enumerate((keys_ref, values_ref))
    ]
    for copy in copies:
        copy.start()
    table = request_table(new_ref, prior_ref)

    def rows_before(row):
        block = lax.div(row, rows)
        odd, inside = lax.rem(block, 2), lax.rem(row, rows)
        return lax.div(block, 2) * rows + jnp.where(odd == side, inside, jnp.where(odd == 1, rows, 0))

    for request, (row, key, ahead, row_end, _) in enumerate(table):
        plan_ref[places["first_key"] + request] = key
        plan_ref[places["ahead"] + request] = ahead
        plan_ref[places["begin"] + request] = rows_before(row)
        plan_ref[places["end"] + request] = rows_before(row_end)
    spans = [
        (key_range(table, jnp.int32(2 * rows * at))[0], key_range(table, jnp.int32(2 * rows * (at + 1) - 1))[1])
        for at in range(groups)
    ]
    needed = jnp.int32(0)
    for source in range(groups):
        for target in range(groups):
            if is_far(groups, source, target):
                first, last = spans[source]
                meet = (first < 2 * cache * (target + 1)) & (last >= 2 * cache * target)
                needed = jnp.where(meet, 1, needed)
    far_ref[0] = needed
    plan_ref[places["side"]] = side
    for steps in range(groups):
        plan_ref[places["groups"] + steps] = lax.rem(group + (groups - steps), groups)
        there = jnp.int32(1)
        for at in range(groups):
            if is_far(groups, (at + steps) % groups, at):
                there = jnp.where(group == at, needed, there)
        plan_ref[places["there"] + steps] = there
    other = (device + 1 - 2 * side) * cache
    half = cache // 2
    stretches = [
        (0, device * cache, cache), (cache, other + core * half, half), (cache + half, other + (1 - core) * half, half)
    ]
    for at, (left, key, count) in enumerate(stretches):
        plan_ref[places["lefts"] + at] = jnp.int32(left)
        plan_ref[places["keys"] + at] = key
        plan_ref[places["steps"] + at] = jnp.int32(count // step)
    for at in range(2 * chips):
        own = core if at < chips else 1 - core
        plan_ref[places["from"] + at] = lax.rem(chip + (chips - at % chips), chips) * 2 + own
    for copy in copies:
        copy.wait()


def make_plan(shape, new_counts, prior_lengths, at, keys, values):
    groups, chips = shape[:2]
    requests = new_counts.shape[0]
    sizes = dict(first_key=requests, ahead=requests, begin=requests, end=requests, side=1)
    sizes.update(groups=groups, there=groups, lefts=STRETCHES, keys=STRETCHES, steps=STRETCHES)
    sizes["from"] = 2 * chips
    places, total = {}, 0
    for name, size in sizes.items():
        places[name] = total
        total += size
    plan, far, mine = pl.pallas_call(
        functools.partial(plan_kernel, shape, dict(places)),
        out_shape=(
            jax.ShapeDtypeStruct((total,), jnp.int32),
            jax.ShapeDtypeStruct((1,), jnp.int32),
            pltpu.HBM((keys.shape[0] // 2, 2 * keys.shape[1]), keys.dtype),
        ),
        in_specs=[SMEM] * 3 + [HBM] * 2,
        out_specs=(SMEM, SMEM, HBM),
        scratch_shapes=[pltpu.SemaphoreType.DMA((2,))],
        name="plan",
    )(new_counts, prior_lengths, at, keys, values)
    return places, plan, far, mine


def body(queries, keys, values, w_out, new_counts, prior_lengths):
    ctx_count, head_count = lax.axis_size("ctx"), lax.axis_size("head")
    rows = queries.shape[0]
    cache = keys.shape[0]
    groups, chips = ctx_count // 2, head_count // 2
    at = jnp.stack([lax.axis_index("ctx"), lax.axis_index("head")]).astype(jnp.int32)
    shape = (groups, chips, rows, cache, min(KEY_TILE, cache // 2))
    places, plan, far, mine = make_plan(shape, new_counts, prior_lengths, at, keys, values)
    requests = new_counts.shape[0]
    return lax.cond(
        far[0] == 1,
        functools.partial(attend_and_project, places, requests, True),
        functools.partial(attend_and_project, places, requests, False),
        *(queries, keys, values, w_out, plan, mine),
    )


def attend_and_project(places, requests, far, queries, keys, values, w_out, plan, mine):
    ctx_count, head_count = lax.axis_size("ctx"), lax.axis_size("head")
    rows = queries.shape[0]
    cache, width = keys.shape
    heads = queries.shape[1] // width
    groups, chips = ctx_count // 2, head_count // 2

    nearest = sorted(range(1, groups), key=lambda steps: min(steps, groups - steps))
    blocks = [move(queries, groups, steps, far) for steps in reversed(nearest)]

    got = lax.ppermute(mine, "ctx", swap_pairs(ctx_count))
    all_keys, beside, own_norm, near_w = prepare(keys, values, w_out)
    stack, query_norm = stack_queries(places, plan, [0, *reversed(nearest)], [queries] + blocks, width)
    got, query_norm, own_norm = lax.optimization_barrier((got, query_norm, own_norm))
    fetched = [got, lax.ppermute(got, "head", swap_pairs(head_count))]
    shape = (groups, rows, heads, requests)
    parts = attend(places, plan, (own_norm, query_norm), stack, fetched, all_keys, beside, shape)
    back = [parts[0]] + [move(parts[steps], groups, groups - steps, far) for steps in nearest]
    attended = merge(places, plan, [0, *nearest], back, heads)

    away = [lax.ppermute(attended, "head", shift_pairs(head_count, 2, steps)) for steps in range(1, chips)]
    pair = lax.ppermute(attended, "head", swap_pairs(head_count))
    mixed, token = project(places, plan, [0, chips], [attended, pair], near_w, None, False)
    away = [piece + token[0].astype(piece.dtype) for piece in away]
    away = away + [lax.ppermute(piece, "head", swap_pairs(head_count)) for piece in away]
    order = [*range(1, chips), *range(chips + 1, 2 * chips)]
    mixed, _ = project(places, plan, order, away, near_w, mixed, True)
    return mixed


def solution(mesh):
    return jax.shard_map(
        body,
        mesh=mesh,
        in_specs=(P("ctx", "head"), P("ctx", None), P("ctx", None), P(None, "head"), P(), P()),
        out_specs=P("ctx", "head"),
        check_vma=False,
    )
```

```python
import functools
import math

import jax
import jax.numpy as jnp
from jax import lax
from jax.experimental import pallas as pl
from jax.experimental.pallas import tpu as pltpu
from jax.sharding import PartitionSpec as P

NEG = -1e30
CALM = 60.0
KEY_TILE = 512
FEW_ROWS = 64
SIDE = 16
LANES = 128
STRETCHES = 3
MIB = 1024 * 1024
SMEM = pl.BlockSpec(memory_space=pltpu.SMEM)
VMEM = pl.BlockSpec(memory_space=pltpu.VMEM)
HBM = pl.BlockSpec(memory_space=pltpu.HBM)


def lengths(rows):
    wide = rows.astype(jnp.float32)
    return jnp.sum(wide * wide, axis=1, keepdims=True)


def fill(from_keys, from_values, done, keys_ref, beside_ref):
    count, width = from_keys.shape
    step = min(KEY_TILE, count)

    def turn(at, longest):
        here = pl.ds(pl.multiple_of(at * step, step), step)
        there = pl.ds(pl.multiple_of(done + at * step, step), step)
        keys = from_keys[here, :]
        keys_ref[there, :] = keys
        beside_ref[there, :width] = from_values[here, :]
        beside_ref[there, width:] = jnp.ones((step, width), jnp.bfloat16)
        return jnp.maximum(longest, lengths(keys))

    return jnp.max(lax.fori_loop(0, count // step, turn, jnp.zeros((step, 1), jnp.float32)))


def prepare_kernel(keys_ref, values_ref, far_w, all_keys, beside_ref, longest_ref, near_w, sem):
    fetch = pltpu.make_async_copy(far_w, near_w, sem)
    fetch.start()
    longest_ref[0] = fill(keys_ref, values_ref, 0, all_keys, beside_ref)
    fetch.wait()


def prepare(keys, values, w_out):
    cache, width = keys.shape
    return pl.pallas_call(
        prepare_kernel,
        out_shape=(
            pltpu.VMEM((2 * cache, width), jnp.bfloat16),
            pltpu.VMEM((2 * cache, 2 * width), jnp.bfloat16),
            jax.ShapeDtypeStruct((1,), jnp.float32),
            pltpu.VMEM(w_out.shape, w_out.dtype),
        ),
        in_specs=[VMEM, VMEM, HBM],
        out_specs=(VMEM, VMEM, SMEM, VMEM),
        scratch_shapes=[pltpu.SemaphoreType.DMA],
        compiler_params=pltpu.CompilerParams(vmem_limit_bytes=4 * MIB),
        name="prepare",
    )(keys, values, pltpu.with_memory_space_constraint(w_out, pltpu.HBM))


def stack_kernel(order, group_at, width, plan_ref, *refs):
    slots = len(order)
    q_refs, (stack_ref, longest_ref, q_all, sems) = refs[:slots], refs[slots:]
    rows = q_refs[0].shape[0]
    heads = q_refs[0].shape[1] // width
    local = slots * rows
    copies = [pltpu.make_async_copy(q_ref, q_all.at[slot], sems.at[slot]) for slot, q_ref in enumerate(q_refs)]
    for copy in copies:
        copy.start()
    longest = jnp.zeros((rows, 1), jnp.float32)
    for slot, copy in enumerate(copies):
        copy.wait()
        start = plan_ref[group_at + order[slot]] * rows
        for head in range(heads):
            part = q_all[slot, :, head * width:(head + 1) * width]
            stack_ref[pl.ds(pl.multiple_of(head * local + start, rows), rows), :] = part
            longest = jnp.maximum(longest, lengths(part))
    longest_ref[0] = jnp.max(longest)


def stack_queries(places, plan, order, queries, width):
    slots, (rows, wide) = len(queries), queries[0].shape
    return pl.pallas_call(
        functools.partial(stack_kernel, order, places["groups"], width),
        out_shape=(
            pltpu.VMEM((slots * rows * (wide // width), width), jnp.bfloat16),
            jax.ShapeDtypeStruct((1,), jnp.float32),
        ),
        in_specs=[SMEM] + [HBM] * slots,
        out_specs=(VMEM, SMEM),
        scratch_shapes=[pltpu.VMEM((slots, rows, wide), jnp.bfloat16), pltpu.SemaphoreType.DMA((slots,))],
        compiler_params=pltpu.CompilerParams(vmem_limit_bytes=4 * MIB),
        name="stack",
    )(plan, *queries)


def request_table(new_ref, prior_ref):
    table = []
    row, key = jnp.int32(0), jnp.int32(0)
    for request in range(new_ref.shape[0]):
        new, prior = new_ref[request], prior_ref[request]
        table.append((row, key, key + prior - row, row + new, key + new + prior))
        row, key = row + new, key + new + prior
    return table


def key_range(table, row):
    first, shift = table[0][1], table[0][2]
    for start, key, ahead, _, _ in table[1:]:
        own = row >= start
        first = jnp.where(own, key, first)
        shift = jnp.where(own, ahead, shift)
    return first, row + shift


def attend_kernel(shape, places, *refs):
    groups, rows, heads, requests = shape
    plan_ref, key_norm_ref, query_norm_ref, stack_ref = refs[:4]
    fetched = refs[4:6]
    keys_ref, beside_ref = refs[8:10]
    out_refs = refs[10:10 + groups]
    sums, tops, chunk_q, chunk_sum, chunk_top, arrived, sems = refs[10 + groups:]
    cache, width = keys_ref.shape[0] // 2, keys_ref.shape[1]
    local = groups * rows
    step = min(KEY_TILE, cache // 2)
    scale = width ** (-0.5)
    factor = scale * math.log2(math.e)
    copies = [pltpu.make_async_copy(ref, arrived.at[at], sems.at[at]) for at, ref in enumerate(fetched)]
    for copy in copies:
        copy.start()
    key_norm = key_norm_ref[0]
    for at, copy in enumerate(copies):
        copy.wait()
        part = arrived.at[at]
        longest = fill(part.at[:, :width], part.at[:, width:], cache + at * (cache // 2), keys_ref, beside_ref)
        key_norm = jnp.maximum(key_norm, longest)
    calm = key_norm * query_norm_ref[0] * (scale * scale) <= CALM * CALM
    side = plan_ref[places["side"]]

    def clear(at, carry):
        sums[pl.ds(pl.multiple_of(at * rows, rows), rows), :] = jnp.zeros((rows, 2 * width), jnp.float32)
        return carry

    lax.fori_loop(0, heads * groups, clear, 0)

    def global_row(place):
        whole = place + side * rows
        for group in range(1, groups):
            whole = whole + jnp.where(place >= group * rows, rows, 0)
        return whole

    def one_chunk(count, online, request, begin, end, start):
        first_key = plan_ref[places["first_key"] + request]
        ahead = plan_ref[places["ahead"] + request]
        start = pl.multiple_of(start, SIDE)
        low_key, high_key = global_row(begin) + ahead, global_row(end - 1) + ahead
        total = heads * count
        for head in range(heads):
            chunk_q[head * count:(head + 1) * count, :] = stack_ref[
                pl.ds(pl.multiple_of(head * local + start, SIDE), count), :
            ]
        chunk_sum[:total, :] = jnp.zeros((total, 2 * width), jnp.float32)
        if online:
            chunk_top[:total, :] = jnp.full((total, width), NEG, jnp.float32)
        place = start + lax.broadcasted_iota(jnp.int32, (count, 1), 0)
        last = global_row(place) + ahead

        def scores(part, left):
            return lax.dot_general(
                chunk_q[part, :], keys_ref[pl.ds(left, step), :], (((1,), (1,)), ((), ())),
                preferred_element_type=jnp.float32,
            ) * factor

        def add(left, weights):
            return jnp.dot(
                weights.astype(jnp.bfloat16), beside_ref[pl.ds(left, step), :], preferred_element_type=jnp.float32
            )

        def one_step(left, key):
            def allowed():
                index = key + lax.broadcasted_iota(jnp.int32, (count, step), 1)
                return (index >= first_key) & (index <= last)

            if online:
                mask = allowed()

                def one_head(head, carry):
                    part = pl.ds(pl.multiple_of(head * count, count), count)
                    score = jnp.where(mask, scores(part, left), NEG)
                    old = chunk_top[part, :]
                    new = jnp.maximum(old, jnp.ceil(jnp.max(score, axis=1, keepdims=True)))
                    weights = jnp.where(mask, jnp.exp2(score - new[:, :1]), 0.0)
                    shrink = jnp.exp2(old - new)
                    chunk_sum[part, :width] = chunk_sum[part, :width] * shrink
                    chunk_sum[part, width:] = chunk_sum[part, width:] * shrink
                    chunk_sum[part, :] += add(left, weights)
                    chunk_top[part, :] = new
                    return carry

                lax.fori_loop(0, heads, one_head, 0)
                return

            plain = (key >= first_key) & (key + step - 1 <= low_key)

            @pl.when(plain)
            def _():
                for head in range(heads):
                    part = pl.ds(head * count, count)
                    chunk_sum[part, :] += add(left, jnp.exp2(scores(part, left)))

            @pl.when(jnp.logical_not(plain))
            def _():
                mask = allowed()
                weights = jnp.exp2(scores(pl.ds(0, total), left))
                weights = jnp.concatenate([
                    jnp.where(mask, weights[head * count:(head + 1) * count, :], 0.0) for head in range(heads)
                ])
                chunk_sum[:total, :] += add(left, weights)

        def one_part(part, carry):
            left, key, steps = (plan_ref[places[name] + part] for name in ("lefts", "keys", "steps"))
            low = jnp.clip(lax.div(first_key - key, step), 0, steps)
            high = jnp.clip(lax.div(high_key - key + step, step), 0, steps)

            def turn(at, carry):
                one_step(pl.multiple_of(left + at * step, step), key + at * step)
                return carry

            lax.fori_loop(low, high, turn, 0)
            return carry

        lax.fori_loop(0, STRETCHES, one_part, 0)
        own = (place >= begin) & (place < end)
        for head in range(heads):
            here = pl.ds(pl.multiple_of(head * local + start, SIDE), count)
            part = slice(head * count, (head + 1) * count)
            sums[here, :] += jnp.where(own, chunk_sum[part, :], 0.0)
            if online:
                tops[here, :] = jnp.where(own, chunk_top[part, :], tops[here, :])

    def all_chunks(count, online, request, begin, end):
        aligned = lax.div(begin, SIDE) * SIDE

        def turn(at, carry):
            from_row = aligned + at * count
            one_chunk(
                count,
                online,
                request,
                jnp.maximum(begin, from_row),
                jnp.minimum(end, from_row + count),
                jnp.minimum(from_row, local - count),
            )
            return carry

        lax.fori_loop(0, lax.div(end - aligned + (count - 1), count), turn, 0)

    many, few = min(2 * rows + SIDE, local), min(FEW_ROWS, local)

    def one_request(request, carry):
        begin, end = plan_ref[places["begin"] + request], plan_ref[places["end"] + request]
        low = plan_ref[places["low"]]
        first_key = plan_ref[places["first_key"] + request]
        last_key = global_row(end - 1) + plan_ref[places["ahead"] + request]
        here = (end > begin) & (first_key < low + 2 * cache) & (last_key >= low)
        large = end - lax.div(begin, SIDE) * SIDE > 2 * few

        @pl.when(here & calm & large)
        def _():
            all_chunks(many, False, request, begin, end)

        @pl.when(here & calm & jnp.logical_not(large))
        def _():
            all_chunks(few, False, request, begin, end)

        @pl.when(here & jnp.logical_not(calm))
        def _():
            all_chunks(few, True, request, begin, end)

        return carry

    lax.fori_loop(0, requests, one_request, 0)

    lane = lax.broadcasted_iota(jnp.int32, (LANES, LANES), 1)
    for slot, out_ref in enumerate(out_refs):
        start = plan_ref[places["groups"] + slot] * rows
        out_ref[rows:, :] = jnp.zeros((SIDE, heads * width), jnp.bfloat16)
        for at in range(0, rows, LANES):
            terms = jnp.zeros((LANES, LANES), jnp.float32)
            for head in range(heads):
                here = pl.ds(pl.multiple_of(head * local + start + at, LANES), LANES)
                out_ref[at:at + LANES, head * width:(head + 1) * width] = sums[here, :width].astype(jnp.bfloat16)
                weight = sums[here, width:]
                top = jnp.where(weight > 0.0, jnp.where(calm, 0.0, tops[here, :]), NEG)
                for term, value in enumerate((weight, top)):
                    high = value.astype(jnp.bfloat16).astype(jnp.float32)
                    terms = jnp.where(lane == 2 * term * heads + head, high, terms)
                    terms = jnp.where(lane == (2 * term + 1) * heads + head, value - high, terms)
            out_ref[rows:, at:at + LANES] = terms.T[:SIDE, :].astype(jnp.bfloat16)


def attend(places, plan, norms, stack, fetched, all_keys, beside, shape):
    groups, rows, heads, _ = shape
    cache, width = all_keys.shape[0] // 2, all_keys.shape[1]
    local = groups * rows
    most = heads * min(2 * rows + SIDE, local)
    _, _, *payloads = pl.pallas_call(
        functools.partial(attend_kernel, shape, dict(places)),
        out_shape=(pltpu.VMEM(all_keys.shape, all_keys.dtype), pltpu.VMEM(beside.shape, beside.dtype))
        + (jax.ShapeDtypeStruct((rows + SIDE, heads * width), jnp.bfloat16),) * groups,
        in_specs=[SMEM] * 3 + [VMEM] + [HBM] * 2 + [VMEM] * 2,
        out_specs=(VMEM,) * (groups + 2),
        input_output_aliases={6: 0, 7: 1},
        scratch_shapes=[
            pltpu.VMEM((heads * local, 2 * width), jnp.float32),
            pltpu.VMEM((heads * local, width), jnp.float32),
            pltpu.VMEM((most, width), jnp.bfloat16),
            pltpu.VMEM((most, 2 * width), jnp.float32),
            pltpu.VMEM((heads * min(FEW_ROWS, local), width), jnp.float32),
            pltpu.VMEM((2, cache // 2, 2 * width), jnp.bfloat16),
            pltpu.SemaphoreType.DMA((2,)),
        ],
        compiler_params=pltpu.CompilerParams(vmem_limit_bytes=28 * MIB),
        cost_estimate=pl.CostEstimate(
            flops=local * heads * cache * width * 4, bytes_accessed=24 * MIB, transcendentals=0
        ),
        name="attend",
    )(plan, *norms, stack, *fetched, all_keys, beside)
    return payloads


def merge_kernel(heads, order, there_at, plan_ref, *refs):
    parts, out_ref = refs[:-1], refs[-1]
    rows = out_ref.shape[0]
    width = out_ref.shape[1] // heads
    logs = [
        jnp.where(plan_ref[there_at + order[at]] == 1, part[rows:, :rows].astype(jnp.float32), 0.0) for at, part in enumerate(parts)
    ]
    spare = LANES - SIDE * len(parts)
    if spare:
        logs.append(jnp.zeros((spare, rows), jnp.float32))
    terms = jnp.concatenate(logs, axis=0).T
    total = terms + pltpu.roll(terms, LANES - heads, 1)
    top = pltpu.roll(terms, LANES - 2 * heads, 1) + pltpu.roll(terms, LANES - 3 * heads, 1)
    lane = lax.broadcasted_iota(jnp.int32, (rows, LANES), 1)
    used = (lax.rem(lane, SIDE) < heads) & (lane < SIDE * len(parts)) & (total > 0.0)
    top = jnp.where(used, top, NEG)
    biggest = top
    for shift in (16, 32, 64):
        biggest = jnp.maximum(biggest, pltpu.roll(biggest, shift, 1))
    share = jnp.where(used, jnp.exp2(top - biggest), 0.0)
    weight = share * jnp.where(used, total, 0.0)
    for shift in (16, 32, 64):
        weight = weight + pltpu.roll(weight, shift, 1)
    share = share / weight
    for head in range(heads):
        own = slice(head * width, (head + 1) * width)
        mixed = jnp.zeros((rows, width), jnp.float32)
        for at, part in enumerate(parts):
            lane_at = at * SIDE + head
            mixed = mixed + part[:rows, own].astype(jnp.float32) * share[:, lane_at:lane_at + 1]
        out_ref[:, own] = mixed.astype(out_ref.dtype)


def merge(places, plan, order, parts, heads):
    rows = parts[0].shape[0] - SIDE
    return pl.pallas_call(
        functools.partial(merge_kernel, heads, order, places["there"]),
        out_shape=jax.ShapeDtypeStruct((rows, parts[0].shape[1]), jnp.bfloat16),
        in_specs=[SMEM] + [VMEM] * len(parts),
        out_specs=VMEM,
        compiler_params=pltpu.CompilerParams(vmem_limit_bytes=12 * MIB),
        name="merge",
    )(plan, *parts)


def project_kernel(order, going_on, last, from_at, plan_ref, *refs):
    refs = list(refs)
    before_ref = refs.pop(0) if going_on else None
    piece_refs, (w_ref, out_ref, token_ref) = refs[:len(order)], refs[len(order):]
    deep = piece_refs[0].shape[1]
    block = out_ref.shape[1]
    left = pl.multiple_of(pl.program_id(0) * block, block)
    token_ref[0] = jnp.int32(0)
    total = None
    for at, piece_ref in zip(order, piece_refs):
        own = pl.multiple_of(plan_ref[from_at + at] * deep, deep)
        term = jnp.dot(
            piece_ref[...], w_ref[pl.ds(own, deep), pl.ds(left, block)], preferred_element_type=jnp.float32
        )
        total = term if total is None else total + term
    if going_on:
        total = total + before_ref[:, pl.ds(left, block)]
    out_ref[...] = total.astype(out_ref.dtype)


def project(places, plan, order, pieces, w_out, before, last):
    rows, deep = pieces[0].shape
    depth, wide = w_out.shape
    block = min(1024, wide)
    going_on = before is not None
    return pl.pallas_call(
        functools.partial(project_kernel, order, going_on, last, places["from"]),
        out_shape=(
            pltpu.HBM((rows, wide), jnp.bfloat16) if last else pltpu.VMEM((rows, wide), jnp.float32),
            jax.ShapeDtypeStruct((1,), jnp.int32),
        ),
        grid=(wide // block,),
        in_specs=[SMEM] + [VMEM] * (going_on + len(pieces) + 1),
        out_specs=(pl.BlockSpec((rows, block), lambda at: (0, at)), SMEM),
        compiler_params=pltpu.CompilerParams(vmem_limit_bytes=16 * MIB),
        cost_estimate=pl.CostEstimate(
            flops=4 * rows * deep * len(pieces) * wide, bytes_accessed=2 * depth * wide, transcendentals=0
        ),
        name="project",
    )(plan, *([before] if going_on else []), *pieces, w_out)


def shift_pairs(count, stride, steps):
    groups = count // stride
    return [
        (group * stride + member, (group + steps) % groups * stride + member)
        for group in range(groups)
        for member in range(stride)
    ]


def swap_pairs(count):
    return [(at, at ^ 1) for at in range(count)]


def is_far(groups, one, two):
    low, high = min(one, two), max(one, two)
    return low < groups // 2 and high >= groups - max(1, groups // 4)


def move(value, groups, steps, far):
    pairs = [
        (source, target)
        for source, target in shift_pairs(2 * groups, 2, steps)
        if far or not is_far(groups, source // 2, target // 2)
    ]
    return lax.ppermute(value, "ctx", pairs) if pairs else jnp.zeros_like(value)


def plan_kernel(shape, places, new_ref, prior_ref, at_ref, plan_ref, far_ref):
    groups, chips, rows, cache, step = shape
    device, place = at_ref[0], at_ref[1]
    group, side, chip, core = lax.div(device, 2), lax.rem(device, 2), lax.div(place, 2), lax.rem(place, 2)
    table = request_table(new_ref, prior_ref)

    def rows_before(row):
        block = lax.div(row, rows)
        odd, inside = lax.rem(block, 2), lax.rem(row, rows)
        return lax.div(block, 2) * rows + jnp.where(odd == side, inside, jnp.where(odd == 1, rows, 0))

    for request, (row, key, ahead, row_end, _) in enumerate(table):
        plan_ref[places["first_key"] + request] = key
        plan_ref[places["ahead"] + request] = ahead
        plan_ref[places["begin"] + request] = rows_before(row)
        plan_ref[places["end"] + request] = rows_before(row_end)
    spans = [
        (key_range(table, jnp.int32(2 * rows * at))[0], key_range(table, jnp.int32(2 * rows * (at + 1) - 1))[1])
        for at in range(groups)
    ]
    needed = jnp.int32(0)
    for source in range(groups):
        for target in range(groups):
            if is_far(groups, source, target):
                first, last = spans[source]
                meet = (first < 2 * cache * (target + 1)) & (last >= 2 * cache * target)
                needed = jnp.where(meet, 1, needed)
    far_ref[0] = needed
    plan_ref[places["side"]] = side
    plan_ref[places["low"]] = group * 2 * cache
    for steps in range(groups):
        plan_ref[places["groups"] + steps] = lax.rem(group + (groups - steps), groups)
        there = jnp.int32(1)
        for at in range(groups):
            if is_far(groups, (at + steps) % groups, at):
                there = jnp.where(group == at, needed, there)
        plan_ref[places["there"] + steps] = there
    other = (device + 1 - 2 * side) * cache
    half = cache // 2
    stretches = [
        (0, device * cache, cache), (cache, other + core * half, half), (cache + half, other + (1 - core) * half, half)
    ]
    for at, (left, key, count) in enumerate(stretches):
        plan_ref[places["lefts"] + at] = jnp.int32(left)
        plan_ref[places["keys"] + at] = key
        plan_ref[places["steps"] + at] = jnp.int32(count // step)
    for at in range(2 * chips):
        own = core if at < chips else 1 - core
        plan_ref[places["from"] + at] = lax.rem(chip + (chips - at % chips), chips) * 2 + own


def make_plan(shape, new_counts, prior_lengths, at):
    groups, chips = shape[:2]
    requests = new_counts.shape[0]
    sizes = dict(first_key=requests, ahead=requests, begin=requests, end=requests, side=1, low=1)
    sizes.update(groups=groups, there=groups, lefts=STRETCHES, keys=STRETCHES, steps=STRETCHES)
    sizes["from"] = 2 * chips
    places, total = {}, 0
    for name, size in sizes.items():
        places[name] = total
        total += size
    plan, far = pl.pallas_call(
        functools.partial(plan_kernel, shape, dict(places)),
        out_shape=(jax.ShapeDtypeStruct((total,), jnp.int32), jax.ShapeDtypeStruct((1,), jnp.int32)),
        in_specs=[SMEM] * 3,
        out_specs=(SMEM, SMEM),
        name="plan",
    )(new_counts, prior_lengths, at)
    return places, plan, far


def body(queries, keys, values, w_out, new_counts, prior_lengths):
    ctx_count, head_count = lax.axis_size("ctx"), lax.axis_size("head")
    rows = queries.shape[0]
    cache = keys.shape[0]
    groups, chips = ctx_count // 2, head_count // 2
    at = jnp.stack([lax.axis_index("ctx"), lax.axis_index("head")]).astype(jnp.int32)
    shape = (groups, chips, rows, cache, min(KEY_TILE, cache // 2))
    places, plan, far = make_plan(shape, new_counts, prior_lengths, at)
    requests = new_counts.shape[0]
    return lax.cond(
        far[0] == 1,
        functools.partial(attend_and_project, places, requests, True),
        functools.partial(attend_and_project, places, requests, False),
        *(queries, keys, values, w_out, plan),
    )


def attend_and_project(places, requests, far, queries, keys, values, w_out, plan):
    ctx_count, head_count = lax.axis_size("ctx"), lax.axis_size("head")
    rows = queries.shape[0]
    cache, width = keys.shape
    heads = queries.shape[1] // width
    groups, chips = ctx_count // 2, head_count // 2

    nearest = sorted(range(1, groups), key=lambda steps: min(steps, groups - steps))
    blocks = [move(queries, groups, steps, far) for steps in reversed(nearest)]

    half = cache // 2
    start = lax.axis_index("head") % 2 * half
    mine = [lax.dynamic_slice_in_dim(array, start, half, axis=0) for array in (keys, values)]
    got = lax.ppermute(jnp.concatenate(mine, axis=1), "ctx", swap_pairs(ctx_count))
    all_keys, beside, own_norm, near_w = prepare(keys, values, w_out)
    stack, query_norm = stack_queries(places, plan, [0, *reversed(nearest)], [queries] + blocks, width)
    got, query_norm, own_norm = lax.optimization_barrier((got, query_norm, own_norm))
    fetched = [got, lax.ppermute(got, "head", swap_pairs(head_count))]
    shape = (groups, rows, heads, requests)
    parts = attend(places, plan, (own_norm, query_norm), stack, fetched, all_keys, beside, shape)
    back = [parts[0]] + [move(parts[steps], groups, groups - steps, far) for steps in nearest]
    attended = merge(places, plan, [0, *nearest], back, heads)

    away = [lax.ppermute(attended, "head", shift_pairs(head_count, 2, steps)) for steps in range(1, chips)]
    pair = lax.ppermute(attended, "head", swap_pairs(head_count))
    mixed, token = project(places, plan, [0, chips], [attended, pair], near_w, None, False)
    away = [piece + token[0].astype(piece.dtype) for piece in away]
    away = away + [lax.ppermute(piece, "head", swap_pairs(head_count)) for piece in away]
    order = [*range(1, chips), *range(chips + 1, 2 * chips)]
    mixed, _ = project(places, plan, order, away, near_w, mixed, True)
    return mixed


def solution(mesh):
    return jax.shard_map(
        body,
        mesh=mesh,
        in_specs=(P("ctx", "head"), P("ctx", None), P("ctx", None), P(None, "head"), P(), P()),
        out_specs=P("ctx", "head"),
        check_vma=False,
    )
```

```python
import functools
import math

import jax
import jax.numpy as jnp
from jax import lax
from jax.experimental import pallas as pl
from jax.experimental.pallas import tpu as pltpu
from jax.sharding import PartitionSpec as P

NEG = -1e30
CALM = 60.0
KEY_TILE = 512
FEW_ROWS = 64
SIDE = 16
LANES = 128
STRETCHES = 3
MIB = 1024 * 1024
SMEM = pl.BlockSpec(memory_space=pltpu.SMEM)
VMEM = pl.BlockSpec(memory_space=pltpu.VMEM)
HBM = pl.BlockSpec(memory_space=pltpu.HBM)


def lengths(rows):
    wide = rows.astype(jnp.float32)
    return jnp.sum(wide * wide, axis=1, keepdims=True)


def fill(from_keys, from_values, done, keys_ref, beside_ref):
    count, width = from_keys.shape
    step = min(KEY_TILE, count)

    def turn(at, longest):
        here = pl.ds(pl.multiple_of(at * step, step), step)
        there = pl.ds(pl.multiple_of(done + at * step, step), step)
        keys = from_keys[here, :]
        keys_ref[there, :] = keys
        beside_ref[there, :width] = from_values[here, :]
        beside_ref[there, width:] = jnp.ones((step, width), jnp.bfloat16)
        return jnp.maximum(longest, lengths(keys))

    return jnp.max(lax.fori_loop(0, count // step, turn, jnp.zeros((step, 1), jnp.float32)))


def prepare_kernel(keys_ref, values_ref, far_w, all_keys, beside_ref, longest_ref, near_w, sem):
    fetch = pltpu.make_async_copy(far_w, near_w, sem)
    fetch.start()
    longest_ref[0] = fill(keys_ref, values_ref, 0, all_keys, beside_ref)
    fetch.wait()


def prepare(keys, values, w_out):
    cache, width = keys.shape
    return pl.pallas_call(
        prepare_kernel,
        out_shape=(
            pltpu.VMEM((2 * cache, width), jnp.bfloat16),
            pltpu.VMEM((2 * cache, 2 * width), jnp.bfloat16),
            jax.ShapeDtypeStruct((1,), jnp.float32),
            pltpu.VMEM(w_out.shape, w_out.dtype),
        ),
        in_specs=[VMEM, VMEM, HBM],
        out_specs=(VMEM, VMEM, SMEM, VMEM),
        scratch_shapes=[pltpu.SemaphoreType.DMA],
        compiler_params=pltpu.CompilerParams(vmem_limit_bytes=4 * MIB),
        name="prepare",
    )(keys, values, pltpu.with_memory_space_constraint(w_out, pltpu.HBM))


def stack_kernel(order, group_at, width, plan_ref, *refs):
    slots = len(order)
    q_refs, (stack_ref, longest_ref, q_all, sems) = refs[:slots], refs[slots:]
    rows = q_refs[0].shape[0]
    heads = q_refs[0].shape[1] // width
    local = slots * rows
    copies = [pltpu.make_async_copy(q_ref, q_all.at[slot], sems.at[slot]) for slot, q_ref in enumerate(q_refs)]
    for copy in copies:
        copy.start()
    longest = jnp.zeros((rows, 1), jnp.float32)
    for slot, copy in enumerate(copies):
        copy.wait()
        start = plan_ref[group_at + order[slot]] * rows
        for head in range(heads):
            part = q_all[slot, :, head * width:(head + 1) * width]
            stack_ref[pl.ds(pl.multiple_of(head * local + start, rows), rows), :] = part
            longest = jnp.maximum(longest, lengths(part))
    longest_ref[0] = jnp.max(longest)


def stack_queries(places, plan, order, queries, width):
    slots, (rows, wide) = len(queries), queries[0].shape
    return pl.pallas_call(
        functools.partial(stack_kernel, order, places["groups"], width),
        out_shape=(
            pltpu.VMEM((slots * rows * (wide // width), width), jnp.bfloat16),
            jax.ShapeDtypeStruct((1,), jnp.float32),
        ),
        in_specs=[SMEM] + [HBM] * slots,
        out_specs=(VMEM, SMEM),
        scratch_shapes=[pltpu.VMEM((slots, rows, wide), jnp.bfloat16), pltpu.SemaphoreType.DMA((slots,))],
        compiler_params=pltpu.CompilerParams(vmem_limit_bytes=4 * MIB),
        name="stack",
    )(plan, *queries)


def request_table(new_ref, prior_ref):
    table = []
    row, key = jnp.int32(0), jnp.int32(0)
    for request in range(new_ref.shape[0]):
        new, prior = new_ref[request], prior_ref[request]
        table.append((row, key, key + prior - row, row + new, key + new + prior))
        row, key = row + new, key + new + prior
    return table


def key_range(table, row):
    first, shift = table[0][1], table[0][2]
    for start, key, ahead, _, _ in table[1:]:
        own = row >= start
        first = jnp.where(own, key, first)
        shift = jnp.where(own, ahead, shift)
    return first, row + shift


def attend_kernel(shape, places, *refs):
    groups, rows, heads, requests = shape
    plan_ref, key_norm_ref, query_norm_ref, stack_ref = refs[:4]
    fetched = refs[4:6]
    keys_ref, beside_ref = refs[8:10]
    out_refs = refs[10:10 + groups]
    sums, tops, chunk_q, chunk_sum, chunk_top, arrived, sems = refs[10 + groups:]
    cache, width = keys_ref.shape[0] // 2, keys_ref.shape[1]
    local = groups * rows
    step = min(KEY_TILE, cache // 2)
    scale = width ** (-0.5)
    factor = scale * math.log2(math.e)
    copies = [pltpu.make_async_copy(ref, arrived.at[at], sems.at[at]) for at, ref in enumerate(fetched)]
    for copy in copies:
        copy.start()
    key_norm = key_norm_ref[0]
    for at, copy in enumerate(copies):
        copy.wait()
        part = arrived.at[at]
        longest = fill(part.at[:, :width], part.at[:, width:], cache + at * (cache // 2), keys_ref, beside_ref)
        key_norm = jnp.maximum(key_norm, longest)
    calm = key_norm * query_norm_ref[0] * (scale * scale) <= CALM * CALM
    side = plan_ref[places["side"]]

    def clear(at, carry):
        sums[pl.ds(pl.multiple_of(at * rows, rows), rows), :] = jnp.zeros((rows, 2 * width), jnp.float32)
        return carry

    lax.fori_loop(0, heads * groups, clear, 0)

    def global_row(place):
        whole = place + side * rows
        for group in range(1, groups):
            whole = whole + jnp.where(place >= group * rows, rows, 0)
        return whole

    def one_chunk(count, online, request, begin, end, start):
        first_key = plan_ref[places["first_key"] + request]
        ahead = plan_ref[places["ahead"] + request]
        start = pl.multiple_of(start, SIDE)
        low_key, high_key = global_row(begin) + ahead, global_row(end - 1) + ahead
        total = heads * count
        for head in range(heads):
            chunk_q[head * count:(head + 1) * count, :] = stack_ref[
                pl.ds(pl.multiple_of(head * local + start, SIDE), count), :
            ]
        chunk_sum[:total, :] = jnp.zeros((total, 2 * width), jnp.float32)
        if online:
            chunk_top[:total, :] = jnp.full((total, width), NEG, jnp.float32)
        place = start + lax.broadcasted_iota(jnp.int32, (count, 1), 0)
        last = global_row(place) + ahead

        def scores(part, left):
            return lax.dot_general(
                chunk_q[part, :], keys_ref[pl.ds(left, step), :], (((1,), (1,)), ((), ())),
                preferred_element_type=jnp.float32,
            ) * factor

        def add(left, weights):
            return jnp.dot(
                weights.astype(jnp.bfloat16), beside_ref[pl.ds(left, step), :], preferred_element_type=jnp.float32
            )

        def one_step(left, key):
            def allowed():
                index = key + lax.broadcasted_iota(jnp.int32, (count, step), 1)
                return (index >= first_key) & (index <= last)

            if online:
                mask = allowed()

                def one_head(head, carry):
                    part = pl.ds(pl.multiple_of(head * count, count), count)
                    score = jnp.where(mask, scores(part, left), NEG)
                    old = chunk_top[part, :]
                    new = jnp.maximum(old, jnp.ceil(jnp.max(score, axis=1, keepdims=True)))
                    weights = jnp.where(mask, jnp.exp2(score - new[:, :1]), 0.0)
                    shrink = jnp.exp2(old - new)
                    chunk_sum[part, :width] = chunk_sum[part, :width] * shrink
                    chunk_sum[part, width:] = chunk_sum[part, width:] * shrink
                    chunk_sum[part, :] += add(left, weights)
                    chunk_top[part, :] = new
                    return carry

                lax.fori_loop(0, heads, one_head, 0)
                return

            plain = (key >= first_key) & (key + step - 1 <= low_key)

            @pl.when(plain)
            def _():
                for head in range(heads):
                    part = pl.ds(head * count, count)
                    chunk_sum[part, :] += add(left, jnp.exp2(scores(part, left)))

            @pl.when(jnp.logical_not(plain))
            def _():
                mask = allowed()
                weights = jnp.exp2(scores(pl.ds(0, total), left))
                weights = jnp.concatenate([
                    jnp.where(mask, weights[head * count:(head + 1) * count, :], 0.0) for head in range(heads)
                ])
                chunk_sum[:total, :] += add(left, weights)

        def one_part(part, carry):
            left, key, steps = (plan_ref[places[name] + part] for name in ("lefts", "keys", "steps"))
            low = jnp.clip(lax.div(first_key - key, step), 0, steps)
            high = jnp.clip(lax.div(high_key - key + step, step), 0, steps)

            def turn(at, carry):
                one_step(pl.multiple_of(left + at * step, step), key + at * step)
                return carry

            lax.fori_loop(low, high, turn, 0)
            return carry

        lax.fori_loop(0, STRETCHES, one_part, 0)
        own = (place >= begin) & (place < end)
        for head in range(heads):
            here = pl.ds(pl.multiple_of(head * local + start, SIDE), count)
            part = slice(head * count, (head + 1) * count)
            sums[here, :] += jnp.where(own, chunk_sum[part, :], 0.0)
            if online:
                tops[here, :] = jnp.where(own, chunk_top[part, :], tops[here, :])

    def all_chunks(count, online, request, begin, end):
        aligned = lax.div(begin, SIDE) * SIDE

        def turn(at, carry):
            from_row = aligned + at * count
            one_chunk(
                count,
                online,
                request,
                jnp.maximum(begin, from_row),
                jnp.minimum(end, from_row + count),
                jnp.minimum(from_row, local - count),
            )
            return carry

        lax.fori_loop(0, lax.div(end - aligned + (count - 1), count), turn, 0)

    many, few = min(2 * rows + SIDE, local), min(FEW_ROWS, local)

    def one_request(request, carry):
        begin, end = plan_ref[places["begin"] + request], plan_ref[places["end"] + request]
        low = plan_ref[places["low"]]
        first_key = plan_ref[places["first_key"] + request]
        last_key = global_row(end - 1) + plan_ref[places["ahead"] + request]
        here = (end > begin) & (first_key < low + 2 * cache) & (last_key >= low)
        large = end - lax.div(begin, SIDE) * SIDE > 2 * few

        @pl.when(here & calm & large)
        def _():
            all_chunks(many, False, request, begin, end)

        @pl.when(here & calm & jnp.logical_not(large))
        def _():
            all_chunks(few, False, request, begin, end)

        @pl.when(here & jnp.logical_not(calm))
        def _():
            all_chunks(few, True, request, begin, end)

        return carry

    lax.fori_loop(0, requests, one_request, 0)

    lane = lax.broadcasted_iota(jnp.int32, (LANES, LANES), 1)
    for slot, out_ref in enumerate(out_refs):
        start = plan_ref[places["groups"] + slot] * rows
        out_ref[rows:, :] = jnp.zeros((SIDE, heads * width), jnp.bfloat16)
        for at in range(0, rows, LANES):
            terms = jnp.zeros((LANES, LANES), jnp.float32)
            for head in range(heads):
                here = pl.ds(pl.multiple_of(head * local + start + at, LANES), LANES)
                out_ref[at:at + LANES, head * width:(head + 1) * width] = sums[here, :width].astype(jnp.bfloat16)
                weight = sums[here, width:]
                top = jnp.where(weight > 0.0, jnp.where(calm, 0.0, tops[here, :]), NEG)
                for term, value in enumerate((weight, top)):
                    high = value.astype(jnp.bfloat16).astype(jnp.float32)
                    terms = jnp.where(lane == 2 * term * heads + head, high, terms)
                    terms = jnp.where(lane == (2 * term + 1) * heads + head, value - high, terms)
            out_ref[rows:, at:at + LANES] = terms.T[:SIDE, :].astype(jnp.bfloat16)


def attend(places, plan, norms, stack, fetched, all_keys, beside, shape):
    groups, rows, heads, _ = shape
    cache, width = all_keys.shape[0] // 2, all_keys.shape[1]
    local = groups * rows
    most = heads * min(2 * rows + SIDE, local)
    _, _, *payloads = pl.pallas_call(
        functools.partial(attend_kernel, shape, dict(places)),
        out_shape=(pltpu.VMEM(all_keys.shape, all_keys.dtype), pltpu.VMEM(beside.shape, beside.dtype))
        + (jax.ShapeDtypeStruct((rows + SIDE, heads * width), jnp.bfloat16),) * groups,
        in_specs=[SMEM] * 3 + [VMEM] + [HBM] * 2 + [VMEM] * 2,
        out_specs=(VMEM,) * (groups + 2),
        input_output_aliases={6: 0, 7: 1},
        scratch_shapes=[
            pltpu.VMEM((heads * local, 2 * width), jnp.float32),
            pltpu.VMEM((heads * local, width), jnp.float32),
            pltpu.VMEM((most, width), jnp.bfloat16),
            pltpu.VMEM((most, 2 * width), jnp.float32),
            pltpu.VMEM((heads * min(FEW_ROWS, local), width), jnp.float32),
            pltpu.VMEM((2, cache // 2, 2 * width), jnp.bfloat16),
            pltpu.SemaphoreType.DMA((2,)),
        ],
        compiler_params=pltpu.CompilerParams(vmem_limit_bytes=28 * MIB),
        cost_estimate=pl.CostEstimate(
            flops=local * heads * cache * width * 4, bytes_accessed=24 * MIB, transcendentals=0
        ),
        name="attend",
    )(plan, *norms, stack, *fetched, all_keys, beside)
    return payloads


def merge_kernel(heads, order, there_at, plan_ref, *refs):
    parts, out_ref = refs[:-1], refs[-1]
    rows = out_ref.shape[0]
    width = out_ref.shape[1] // heads
    logs = [
        jnp.where(plan_ref[there_at + order[at]] == 1, part[rows:, :rows].astype(jnp.float32), 0.0) for at, part in enumerate(parts)
    ]
    spare = LANES - SIDE * len(parts)
    if spare:
        logs.append(jnp.zeros((spare, rows), jnp.float32))
    terms = jnp.concatenate(logs, axis=0).T
    total = terms + pltpu.roll(terms, LANES - heads, 1)
    top = pltpu.roll(terms, LANES - 2 * heads, 1) + pltpu.roll(terms, LANES - 3 * heads, 1)
    lane = lax.broadcasted_iota(jnp.int32, (rows, LANES), 1)
    used = (lax.rem(lane, SIDE) < heads) & (lane < SIDE * len(parts)) & (total > 0.0)
    top = jnp.where(used, top, NEG)
    biggest = top
    for shift in (16, 32, 64):
        biggest = jnp.maximum(biggest, pltpu.roll(biggest, shift, 1))
    share = jnp.where(used, jnp.exp2(top - biggest), 0.0)
    weight = share * jnp.where(used, total, 0.0)
    for shift in (16, 32, 64):
        weight = weight + pltpu.roll(weight, shift, 1)
    share = share / weight
    for head in range(heads):
        own = slice(head * width, (head + 1) * width)
        mixed = jnp.zeros((rows, width), jnp.float32)
        for at, part in enumerate(parts):
            lane_at = at * SIDE + head
            mixed = mixed + part[:rows, own].astype(jnp.float32) * share[:, lane_at:lane_at + 1]
        out_ref[:, own] = mixed.astype(out_ref.dtype)


def merge(places, plan, order, parts, heads):
    rows = parts[0].shape[0] - SIDE
    return pl.pallas_call(
        functools.partial(merge_kernel, heads, order, places["there"]),
        out_shape=jax.ShapeDtypeStruct((rows, parts[0].shape[1]), jnp.bfloat16),
        in_specs=[SMEM] + [VMEM] * len(parts),
        out_specs=VMEM,
        compiler_params=pltpu.CompilerParams(vmem_limit_bytes=12 * MIB),
        name="merge",
    )(plan, *parts)


def project_kernel(order, going_on, last, from_at, plan_ref, *refs):
    refs = list(refs)
    before_ref = refs.pop(0) if going_on else None
    piece_refs, (w_ref, out_ref, token_ref) = refs[:len(order)], refs[len(order):]
    deep = piece_refs[0].shape[1]
    token_ref[0] = jnp.int32(0)

    def one_block(left, block):
        total = None
        for at, piece_ref in zip(order, piece_refs):
            own = pl.multiple_of(plan_ref[from_at + at] * deep, deep)
            term = jnp.dot(
                piece_ref[...], w_ref[pl.ds(own, deep), pl.ds(left, block)], preferred_element_type=jnp.float32
            )
            total = term if total is None else total + term
        return total

    if last:
        block = out_ref.shape[1]
        left = pl.multiple_of(pl.program_id(0) * block, block)
        total = one_block(left, block)
        if going_on:
            total = total + before_ref[:, pl.ds(left, block)]
        out_ref[...] = total.astype(out_ref.dtype)
        return

    block = min(1024, out_ref.shape[1])

    def turn(at, carry):
        left = pl.multiple_of(at * block, block)
        out_ref[:, pl.ds(left, block)] = one_block(left, block)
        return carry

    lax.fori_loop(0, out_ref.shape[1] // block, turn, 0)


def project(places, plan, order, pieces, w_out, before, last):
    rows, deep = pieces[0].shape
    depth, wide = w_out.shape
    block = min(1024, wide)
    going_on = before is not None
    return pl.pallas_call(
        functools.partial(project_kernel, order, going_on, last, places["from"]),
        out_shape=(
            pltpu.HBM((rows, wide), jnp.bfloat16) if last else pltpu.VMEM((rows, wide), jnp.float32),
            jax.ShapeDtypeStruct((1,), jnp.int32),
        ),
        grid=(wide // block,) if last else (),
        in_specs=[SMEM] + [VMEM] * (going_on + len(pieces) + 1),
        out_specs=(pl.BlockSpec((rows, block), lambda at: (0, at)) if last else VMEM, SMEM),
        compiler_params=pltpu.CompilerParams(vmem_limit_bytes=16 * MIB),
        cost_estimate=pl.CostEstimate(
            flops=4 * rows * deep * len(pieces) * wide, bytes_accessed=2 * depth * wide, transcendentals=0
        ),
        name="project",
    )(plan, *([before] if going_on else []), *pieces, w_out)


def shift_pairs(count, stride, steps):
    groups = count // stride
    return [
        (group * stride + member, (group + steps) % groups * stride + member)
        for group in range(groups)
        for member in range(stride)
    ]


def swap_pairs(count):
    return [(at, at ^ 1) for at in range(count)]


def is_far(groups, one, two):
    low, high = min(one, two), max(one, two)
    return low < groups // 2 and high >= groups - max(1, groups // 4)


def move(value, groups, steps, far):
    pairs = [
        (source, target)
        for source, target in shift_pairs(2 * groups, 2, steps)
        if far or not is_far(groups, source // 2, target // 2)
    ]
    return lax.ppermute(value, "ctx", pairs) if pairs else jnp.zeros_like(value)


def plan_kernel(shape, places, new_ref, prior_ref, at_ref, plan_ref, far_ref):
    groups, chips, rows, cache, step = shape
    device, place = at_ref[0], at_ref[1]
    group, side, chip, core = lax.div(device, 2), lax.rem(device, 2), lax.div(place, 2), lax.rem(place, 2)
    table = request_table(new_ref, prior_ref)

    def rows_before(row):
        block = lax.div(row, rows)
        odd, inside = lax.rem(block, 2), lax.rem(row, rows)
        return lax.div(block, 2) * rows + jnp.where(odd == side, inside, jnp.where(odd == 1, rows, 0))

    for request, (row, key, ahead, row_end, _) in enumerate(table):
        plan_ref[places["first_key"] + request] = key
        plan_ref[places["ahead"] + request] = ahead
        plan_ref[places["begin"] + request] = rows_before(row)
        plan_ref[places["end"] + request] = rows_before(row_end)
    spans = [
        (key_range(table, jnp.int32(2 * rows * at))[0], key_range(table, jnp.int32(2 * rows * (at + 1) - 1))[1])
        for at in range(groups)
    ]
    needed = jnp.int32(0)
    for source in range(groups):
        for target in range(groups):
            if is_far(groups, source, target):
                first, last = spans[source]
                meet = (first < 2 * cache * (target + 1)) & (last >= 2 * cache * target)
                needed = jnp.where(meet, 1, needed)
    far_ref[0] = needed
    plan_ref[places["side"]] = side
    plan_ref[places["low"]] = group * 2 * cache
    for steps in range(groups):
        plan_ref[places["groups"] + steps] = lax.rem(group + (groups - steps), groups)
        there = jnp.int32(1)
        for at in range(groups):
            if is_far(groups, (at + steps) % groups, at):
                there = jnp.where(group == at, needed, there)
        plan_ref[places["there"] + steps] = there
    other = (device + 1 - 2 * side) * cache
    half = cache // 2
    stretches = [
        (0, device * cache, cache), (cache, other + core * half, half), (cache + half, other + (1 - core) * half, half)
    ]
    for at, (left, key, count) in enumerate(stretches):
        plan_ref[places["lefts"] + at] = jnp.int32(left)
        plan_ref[places["keys"] + at] = key
        plan_ref[places["steps"] + at] = jnp.int32(count // step)
    for at in range(2 * chips):
        own = core if at < chips else 1 - core
        plan_ref[places["from"] + at] = lax.rem(chip + (chips - at % chips), chips) * 2 + own


def make_plan(shape, new_counts, prior_lengths, at):
    groups, chips = shape[:2]
    requests = new_counts.shape[0]
    sizes = dict(first_key=requests, ahead=requests, begin=requests, end=requests, side=1, low=1)
    sizes.update(groups=groups, there=groups, lefts=STRETCHES, keys=STRETCHES, steps=STRETCHES)
    sizes["from"] = 2 * chips
    places, total = {}, 0
    for name, size in sizes.items():
        places[name] = total
        total += size
    plan, far = pl.pallas_call(
        functools.partial(plan_kernel, shape, dict(places)),
        out_shape=(jax.ShapeDtypeStruct((total,), jnp.int32), jax.ShapeDtypeStruct((1,), jnp.int32)),
        in_specs=[SMEM] * 3,
        out_specs=(SMEM, SMEM),
        name="plan",
    )(new_counts, prior_lengths, at)
    return places, plan, far


def body(queries, keys, values, w_out, new_counts, prior_lengths):
    ctx_count, head_count = lax.axis_size("ctx"), lax.axis_size("head")
    rows = queries.shape[0]
    cache = keys.shape[0]
    groups, chips = ctx_count // 2, head_count // 2
    at = jnp.stack([lax.axis_index("ctx"), lax.axis_index("head")]).astype(jnp.int32)
    shape = (groups, chips, rows, cache, min(KEY_TILE, cache // 2))
    places, plan, far = make_plan(shape, new_counts, prior_lengths, at)
    requests = new_counts.shape[0]
    return lax.cond(
        far[0] == 1,
        functools.partial(attend_and_project, places, requests, True),
        functools.partial(attend_and_project, places, requests, False),
        *(queries, keys, values, w_out, plan),
    )


def attend_and_project(places, requests, far, queries, keys, values, w_out, plan):
    ctx_count, head_count = lax.axis_size("ctx"), lax.axis_size("head")
    rows = queries.shape[0]
    cache, width = keys.shape
    heads = queries.shape[1] // width
    groups, chips = ctx_count // 2, head_count // 2

    nearest = sorted(range(1, groups), key=lambda steps: min(steps, groups - steps))
    blocks = [move(queries, groups, steps, far) for steps in reversed(nearest)]

    half = cache // 2
    start = lax.axis_index("head") % 2 * half
    mine = [lax.dynamic_slice_in_dim(array, start, half, axis=0) for array in (keys, values)]
    got = lax.ppermute(jnp.concatenate(mine, axis=1), "ctx", swap_pairs(ctx_count))
    all_keys, beside, own_norm, near_w = prepare(keys, values, w_out)
    stack, query_norm = stack_queries(places, plan, [0, *reversed(nearest)], [queries] + blocks, width)
    got, query_norm, own_norm = lax.optimization_barrier((got, query_norm, own_norm))
    fetched = [got, lax.ppermute(got, "head", swap_pairs(head_count))]
    shape = (groups, rows, heads, requests)
    parts = attend(places, plan, (own_norm, query_norm), stack, fetched, all_keys, beside, shape)
    back = [parts[0]] + [move(parts[steps], groups, groups - steps, far) for steps in nearest]
    attended = merge(places, plan, [0, *nearest], back, heads)

    away = [lax.ppermute(attended, "head", shift_pairs(head_count, 2, steps)) for steps in range(1, chips)]
    pair = lax.ppermute(attended, "head", swap_pairs(head_count))
    mixed, token = project(places, plan, [0, chips], [attended, pair], near_w, None, False)
    away = [piece + token[0].astype(piece.dtype) for piece in away]
    away = away + [lax.ppermute(piece, "head", swap_pairs(head_count)) for piece in away]
    order = [*range(1, chips), *range(chips + 1, 2 * chips)]
    mixed, _ = project(places, plan, order, away, near_w, mixed, True)
    return mixed


def solution(mesh):
    return jax.shard_map(
        body,
        mesh=mesh,
        in_specs=(P("ctx", "head"), P("ctx", None), P("ctx", None), P(None, "head"), P(), P()),
        out_specs=P("ctx", "head"),
        check_vma=False,
    )
```

```python
import functools
import math

import jax
import jax.numpy as jnp
from jax import lax
from jax.experimental import pallas as pl
from jax.experimental.pallas import tpu as pltpu
from jax.sharding import PartitionSpec as P

NEG = -1e30
CALM = 60.0
KEY_TILE = 512
FEW_ROWS = 64
SIDE = 16
LANES = 128
STRETCHES = 3
MIB = 1024 * 1024
SMEM = pl.BlockSpec(memory_space=pltpu.SMEM)
VMEM = pl.BlockSpec(memory_space=pltpu.VMEM)
HBM = pl.BlockSpec(memory_space=pltpu.HBM)


def lengths(rows):
    wide = rows.astype(jnp.float32)
    return jnp.sum(wide * wide, axis=1, keepdims=True)


def fill(from_keys, from_values, done, keys_ref, beside_ref):
    count, width = from_keys.shape
    step = min(KEY_TILE, count)

    def turn(at, longest):
        here = pl.ds(pl.multiple_of(at * step, step), step)
        there = pl.ds(pl.multiple_of(done + at * step, step), step)
        keys = from_keys[here, :]
        keys_ref[there, :] = keys
        beside_ref[there, :width] = from_values[here, :]
        beside_ref[there, width:] = jnp.ones((step, width), jnp.bfloat16)
        return jnp.maximum(longest, lengths(keys))

    return jnp.max(lax.fori_loop(0, count // step, turn, jnp.zeros((step, 1), jnp.float32)))


def prepare_kernel(keys_ref, values_ref, far_w, all_keys, beside_ref, longest_ref, near_w, sem):
    fetch = pltpu.make_async_copy(far_w, near_w, sem)
    fetch.start()
    longest_ref[0] = fill(keys_ref, values_ref, 0, all_keys, beside_ref)
    fetch.wait()


def prepare(keys, values, w_out):
    cache, width = keys.shape
    return pl.pallas_call(
        prepare_kernel,
        out_shape=(
            pltpu.VMEM((2 * cache, width), jnp.bfloat16),
            pltpu.VMEM((2 * cache, 2 * width), jnp.bfloat16),
            jax.ShapeDtypeStruct((1,), jnp.float32),
            pltpu.VMEM(w_out.shape, w_out.dtype),
        ),
        in_specs=[VMEM, VMEM, HBM],
        out_specs=(VMEM, VMEM, SMEM, VMEM),
        scratch_shapes=[pltpu.SemaphoreType.DMA],
        compiler_params=pltpu.CompilerParams(vmem_limit_bytes=4 * MIB),
        name="prepare",
    )(keys, values, pltpu.with_memory_space_constraint(w_out, pltpu.HBM))


def join_kernel(got_ref, own_ref, keys_in, beside_in, all_keys, beside_ref, longest_ref):
    del keys_in, beside_in
    half, width = got_ref.shape[0], all_keys.shape[1]
    longest = fill(got_ref.at[:, :width], got_ref.at[:, width:], 2 * half, all_keys, beside_ref)
    longest_ref[0] = jnp.maximum(own_ref[0], longest)


def join(got, own_longest, all_keys, beside):
    return pl.pallas_call(
        join_kernel,
        out_shape=(
            pltpu.VMEM(all_keys.shape, all_keys.dtype),
            pltpu.VMEM(beside.shape, beside.dtype),
            jax.ShapeDtypeStruct((1,), jnp.float32),
        ),
        in_specs=[VMEM, SMEM, VMEM, VMEM],
        out_specs=(VMEM, VMEM, SMEM),
        input_output_aliases={2: 0, 3: 1},
        compiler_params=pltpu.CompilerParams(vmem_limit_bytes=4 * MIB),
        name="join",
    )(got, own_longest, all_keys, beside)


def stack_kernel(order, group_at, width, plan_ref, *refs):
    slots = len(order)
    q_refs, (stack_ref, longest_ref, q_all, sems) = refs[:slots], refs[slots:]
    rows = q_refs[0].shape[0]
    heads = q_refs[0].shape[1] // width
    local = slots * rows
    copies = [pltpu.make_async_copy(q_ref, q_all.at[slot], sems.at[slot]) for slot, q_ref in enumerate(q_refs)]
    for copy in copies:
        copy.start()
    longest = jnp.zeros((rows, 1), jnp.float32)
    for slot, copy in enumerate(copies):
        copy.wait()
        start = plan_ref[group_at + order[slot]] * rows
        for head in range(heads):
            part = q_all[slot, :, head * width:(head + 1) * width]
            stack_ref[pl.ds(pl.multiple_of(head * local + start, rows), rows), :] = part
            longest = jnp.maximum(longest, lengths(part))
    longest_ref[0] = jnp.max(longest)


def stack_queries(places, plan, order, queries, width):
    slots, (rows, wide) = len(queries), queries[0].shape
    return pl.pallas_call(
        functools.partial(stack_kernel, order, places["groups"], width),
        out_shape=(
            pltpu.VMEM((slots * rows * (wide // width), width), jnp.bfloat16),
            jax.ShapeDtypeStruct((1,), jnp.float32),
        ),
        in_specs=[SMEM] + [HBM] * slots,
        out_specs=(VMEM, SMEM),
        scratch_shapes=[pltpu.VMEM((slots, rows, wide), jnp.bfloat16), pltpu.SemaphoreType.DMA((slots,))],
        compiler_params=pltpu.CompilerParams(vmem_limit_bytes=4 * MIB),
        name="stack",
    )(plan, *queries)


def request_table(new_ref, prior_ref):
    table = []
    row, key = jnp.int32(0), jnp.int32(0)
    for request in range(new_ref.shape[0]):
        new, prior = new_ref[request], prior_ref[request]
        table.append((row, key, key + prior - row, row + new, key + new + prior))
        row, key = row + new, key + new + prior
    return table


def key_range(table, row):
    first, shift = table[0][1], table[0][2]
    for start, key, ahead, _, _ in table[1:]:
        own = row >= start
        first = jnp.where(own, key, first)
        shift = jnp.where(own, ahead, shift)
    return first, row + shift


def attend_kernel(shape, places, *refs):
    groups, rows, heads, requests = shape
    plan_ref, key_norm_ref, query_norm_ref, stack_ref = refs[:4]
    rest_ref = refs[4]
    keys_ref, beside_ref = refs[7:9]
    out_refs = refs[9:9 + groups]
    sums, tops, chunk_q, chunk_sum, chunk_top, arrived, sem = refs[9 + groups:]
    cache, width = keys_ref.shape[0] // 2, keys_ref.shape[1]
    local = groups * rows
    step = min(KEY_TILE, cache // 2)
    scale = width ** (-0.5)
    factor = scale * math.log2(math.e)
    copy = pltpu.make_async_copy(rest_ref, arrived, sem)
    copy.start()
    copy.wait()
    half = cache // 2
    longest = fill(arrived.at[:, :width], arrived.at[:, width:], cache + half, keys_ref, beside_ref)
    key_norm = jnp.maximum(key_norm_ref[0], longest)
    calm = key_norm * query_norm_ref[0] * (scale * scale) <= CALM * CALM
    side = plan_ref[places["side"]]

    def clear(at, carry):
        sums[pl.ds(pl.multiple_of(at * rows, rows), rows), :] = jnp.zeros((rows, 2 * width), jnp.float32)
        return carry

    lax.fori_loop(0, heads * groups, clear, 0)

    def global_row(place):
        whole = place + side * rows
        for group in range(1, groups):
            whole = whole + jnp.where(place >= group * rows, rows, 0)
        return whole

    def one_chunk(count, online, request, begin, end, start):
        first_key = plan_ref[places["first_key"] + request]
        ahead = plan_ref[places["ahead"] + request]
        start = pl.multiple_of(start, SIDE)
        low_key, high_key = global_row(begin) + ahead, global_row(end - 1) + ahead
        total = heads * count
        for head in range(heads):
            chunk_q[head * count:(head + 1) * count, :] = stack_ref[
                pl.ds(pl.multiple_of(head * local + start, SIDE), count), :
            ]
        chunk_sum[:total, :] = jnp.zeros((total, 2 * width), jnp.float32)
        if online:
            chunk_top[:total, :] = jnp.full((total, width), NEG, jnp.float32)
        place = start + lax.broadcasted_iota(jnp.int32, (count, 1), 0)
        last = global_row(place) + ahead

        def scores(part, left):
            return lax.dot_general(
                chunk_q[part, :], keys_ref[pl.ds(left, step), :], (((1,), (1,)), ((), ())),
                preferred_element_type=jnp.float32,
            ) * factor

        def add(left, weights):
            return jnp.dot(
                weights.astype(jnp.bfloat16), beside_ref[pl.ds(left, step), :], preferred_element_type=jnp.float32
            )

        def one_step(left, key):
            def allowed():
                index = key + lax.broadcasted_iota(jnp.int32, (count, step), 1)
                return (index >= first_key) & (index <= last)

            if online:
                mask = allowed()

                def one_head(head, carry):
                    part = pl.ds(pl.multiple_of(head * count, count), count)
                    score = jnp.where(mask, scores(part, left), NEG)
                    old = chunk_top[part, :]
                    new = jnp.maximum(old, jnp.ceil(jnp.max(score, axis=1, keepdims=True)))
                    weights = jnp.where(mask, jnp.exp2(score - new[:, :1]), 0.0)
                    shrink = jnp.exp2(old - new)
                    chunk_sum[part, :width] = chunk_sum[part, :width] * shrink
                    chunk_sum[part, width:] = chunk_sum[part, width:] * shrink
                    chunk_sum[part, :] += add(left, weights)
                    chunk_top[part, :] = new
                    return carry

                lax.fori_loop(0, heads, one_head, 0)
                return

            plain = (key >= first_key) & (key + step - 1 <= low_key)

            @pl.when(plain)
            def _():
                for head in range(heads):
                    part = pl.ds(head * count, count)
                    chunk_sum[part, :] += add(left, jnp.exp2(scores(part, left)))

            @pl.when(jnp.logical_not(plain))
            def _():
                mask = allowed()
                weights = jnp.exp2(scores(pl.ds(0, total), left))
                weights = jnp.concatenate([
                    jnp.where(mask, weights[head * count:(head + 1) * count, :], 0.0) for head in range(heads)
                ])
                chunk_sum[:total, :] += add(left, weights)

        def one_part(part, carry):
            left, key, steps = (plan_ref[places[name] + part] for name in ("lefts", "keys", "steps"))
            low = jnp.clip(lax.div(first_key - key, step), 0, steps)
            high = jnp.clip(lax.div(high_key - key + step, step), 0, steps)

            def turn(at, carry):
                one_step(pl.multiple_of(left + at * step, step), key + at * step)
                return carry

            lax.fori_loop(low, high, turn, 0)
            return carry

        lax.fori_loop(0, STRETCHES, one_part, 0)
        own = (place >= begin) & (place < end)
        for head in range(heads):
            here = pl.ds(pl.multiple_of(head * local + start, SIDE), count)
            part = slice(head * count, (head + 1) * count)
            sums[here, :] += jnp.where(own, chunk_sum[part, :], 0.0)
            if online:
                tops[here, :] = jnp.where(own, chunk_top[part, :], tops[here, :])

    def all_chunks(count, online, request, begin, end):
        aligned = lax.div(begin, SIDE) * SIDE

        def turn(at, carry):
            from_row = aligned + at * count
            one_chunk(
                count,
                online,
                request,
                jnp.maximum(begin, from_row),
                jnp.minimum(end, from_row + count),
                jnp.minimum(from_row, local - count),
            )
            return carry

        lax.fori_loop(0, lax.div(end - aligned + (count - 1), count), turn, 0)

    many, few = min(2 * rows + SIDE, local), min(FEW_ROWS, local)

    def one_request(request, carry):
        begin, end = plan_ref[places["begin"] + request], plan_ref[places["end"] + request]
        low = plan_ref[places["low"]]
        first_key = plan_ref[places["first_key"] + request]
        last_key = global_row(end - 1) + plan_ref[places["ahead"] + request]
        here = (end > begin) & (first_key < low + 2 * cache) & (last_key >= low)
        large = end - lax.div(begin, SIDE) * SIDE > 2 * few

        @pl.when(here & calm & large)
        def _():
            all_chunks(many, False, request, begin, end)

        @pl.when(here & calm & jnp.logical_not(large))
        def _():
            all_chunks(few, False, request, begin, end)

        @pl.when(here & jnp.logical_not(calm))
        def _():
            all_chunks(few, True, request, begin, end)

        return carry

    lax.fori_loop(0, requests, one_request, 0)

    lane = lax.broadcasted_iota(jnp.int32, (LANES, LANES), 1)
    for slot, out_ref in enumerate(out_refs):
        start = plan_ref[places["groups"] + slot] * rows
        out_ref[rows:, :] = jnp.zeros((SIDE, heads * width), jnp.bfloat16)
        for at in range(0, rows, LANES):
            terms = jnp.zeros((LANES, LANES), jnp.float32)
            for head in range(heads):
                here = pl.ds(pl.multiple_of(head * local + start + at, LANES), LANES)
                out_ref[at:at + LANES, head * width:(head + 1) * width] = sums[here, :width].astype(jnp.bfloat16)
                weight = sums[here, width:]
                top = jnp.where(weight > 0.0, jnp.where(calm, 0.0, tops[here, :]), NEG)
                for term, value in enumerate((weight, top)):
                    high = value.astype(jnp.bfloat16).astype(jnp.float32)
                    terms = jnp.where(lane == 2 * term * heads + head, high, terms)
                    terms = jnp.where(lane == (2 * term + 1) * heads + head, value - high, terms)
            out_ref[rows:, at:at + LANES] = terms.T[:SIDE, :].astype(jnp.bfloat16)


def attend(places, plan, norms, stack, rest, all_keys, beside, shape):
    groups, rows, heads, _ = shape
    cache, width = all_keys.shape[0] // 2, all_keys.shape[1]
    local = groups * rows
    most = heads * min(2 * rows + SIDE, local)
    _, _, *payloads = pl.pallas_call(
        functools.partial(attend_kernel, shape, dict(places)),
        out_shape=(pltpu.VMEM(all_keys.shape, all_keys.dtype), pltpu.VMEM(beside.shape, beside.dtype))
        + (jax.ShapeDtypeStruct((rows + SIDE, heads * width), jnp.bfloat16),) * groups,
        in_specs=[SMEM] * 3 + [VMEM, HBM] + [VMEM] * 2,
        out_specs=(VMEM,) * (groups + 2),
        input_output_aliases={5: 0, 6: 1},
        scratch_shapes=[
            pltpu.VMEM((heads * local, 2 * width), jnp.float32),
            pltpu.VMEM((heads * local, width), jnp.float32),
            pltpu.VMEM((most, width), jnp.bfloat16),
            pltpu.VMEM((most, 2 * width), jnp.float32),
            pltpu.VMEM((heads * min(FEW_ROWS, local), width), jnp.float32),
            pltpu.VMEM((cache // 2, 2 * width), jnp.bfloat16),
            pltpu.SemaphoreType.DMA,
        ],
        compiler_params=pltpu.CompilerParams(vmem_limit_bytes=28 * MIB),
        cost_estimate=pl.CostEstimate(
            flops=local * heads * cache * width * 4, bytes_accessed=24 * MIB, transcendentals=0
        ),
        name="attend",
    )(plan, *norms, stack, rest, all_keys, beside)
    return payloads


def merge_kernel(heads, order, there_at, plan_ref, *refs):
    parts, out_ref = refs[:-1], refs[-1]
    rows = out_ref.shape[0]
    width = out_ref.shape[1] // heads
    logs = [
        jnp.where(plan_ref[there_at + order[at]] == 1, part[rows:, :rows].astype(jnp.float32), 0.0) for at, part in enumerate(parts)
    ]
    spare = LANES - SIDE * len(parts)
    if spare:
        logs.append(jnp.zeros((spare, rows), jnp.float32))
    terms = jnp.concatenate(logs, axis=0).T
    total = terms + pltpu.roll(terms, LANES - heads, 1)
    top = pltpu.roll(terms, LANES - 2 * heads, 1) + pltpu.roll(terms, LANES - 3 * heads, 1)
    lane = lax.broadcasted_iota(jnp.int32, (rows, LANES), 1)
    used = (lax.rem(lane, SIDE) < heads) & (lane < SIDE * len(parts)) & (total > 0.0)
    top = jnp.where(used, top, NEG)
    biggest = top
    for shift in (16, 32, 64):
        biggest = jnp.maximum(biggest, pltpu.roll(biggest, shift, 1))
    share = jnp.where(used, jnp.exp2(top - biggest), 0.0)
    weight = share * jnp.where(used, total, 0.0)
    for shift in (16, 32, 64):
        weight = weight + pltpu.roll(weight, shift, 1)
    share = share / weight
    for head in range(heads):
        own = slice(head * width, (head + 1) * width)
        mixed = jnp.zeros((rows, width), jnp.float32)
        for at, part in enumerate(parts):
            lane_at = at * SIDE + head
            mixed = mixed + part[:rows, own].astype(jnp.float32) * share[:, lane_at:lane_at + 1]
        out_ref[:, own] = mixed.astype(out_ref.dtype)


def merge(places, plan, order, parts, heads):
    rows = parts[0].shape[0] - SIDE
    return pl.pallas_call(
        functools.partial(merge_kernel, heads, order, places["there"]),
        out_shape=jax.ShapeDtypeStruct((rows, parts[0].shape[1]), jnp.bfloat16),
        in_specs=[SMEM] + [VMEM] * len(parts),
        out_specs=VMEM,
        compiler_params=pltpu.CompilerParams(vmem_limit_bytes=12 * MIB),
        name="merge",
    )(plan, *parts)


def project_kernel(order, going_on, last, from_at, plan_ref, *refs):
    refs = list(refs)
    before_ref = refs.pop(0) if going_on else None
    piece_refs, (w_ref, out_ref, token_ref) = refs[:len(order)], refs[len(order):]
    deep = piece_refs[0].shape[1]
    token_ref[0] = jnp.int32(0)

    def one_block(left, block):
        total = None
        for at, piece_ref in zip(order, piece_refs):
            own = pl.multiple_of(plan_ref[from_at + at] * deep, deep)
            term = jnp.dot(
                piece_ref[...], w_ref[pl.ds(own, deep), pl.ds(left, block)], preferred_element_type=jnp.float32
            )
            total = term if total is None else total + term
        return total

    if last:
        block = out_ref.shape[1]
        left = pl.multiple_of(pl.program_id(0) * block, block)
        total = one_block(left, block)
        if going_on:
            total = total + before_ref[:, pl.ds(left, block)]
        out_ref[...] = total.astype(out_ref.dtype)
        return

    block = min(1024, out_ref.shape[1])

    def turn(at, carry):
        left = pl.multiple_of(at * block, block)
        out_ref[:, pl.ds(left, block)] = one_block(left, block)
        return carry

    lax.fori_loop(0, out_ref.shape[1] // block, turn, 0)


def project(places, plan, order, pieces, w_out, before, last):
    rows, deep = pieces[0].shape
    depth, wide = w_out.shape
    block = min(1024, wide)
    going_on = before is not None
    return pl.pallas_call(
        functools.partial(project_kernel, order, going_on, last, places["from"]),
        out_shape=(
            pltpu.HBM((rows, wide), jnp.bfloat16) if last else pltpu.VMEM((rows, wide), jnp.float32),
            jax.ShapeDtypeStruct((1,), jnp.int32),
        ),
        grid=(wide // block,) if last else (),
        in_specs=[SMEM] + [VMEM] * (going_on + len(pieces) + 1),
        out_specs=(pl.BlockSpec((rows, block), lambda at: (0, at)) if last else VMEM, SMEM),
        compiler_params=pltpu.CompilerParams(vmem_limit_bytes=16 * MIB),
        cost_estimate=pl.CostEstimate(
            flops=4 * rows * deep * len(pieces) * wide, bytes_accessed=2 * depth * wide, transcendentals=0
        ),
        name="project",
    )(plan, *([before] if going_on else []), *pieces, w_out)


def shift_pairs(count, stride, steps):
    groups = count // stride
    return [
        (group * stride + member, (group + steps) % groups * stride + member)
        for group in range(groups)
        for member in range(stride)
    ]


def swap_pairs(count):
    return [(at, at ^ 1) for at in range(count)]


def is_far(groups, one, two):
    low, high = min(one, two), max(one, two)
    return low < groups // 2 and high >= groups - max(1, groups // 4)


def move(value, groups, steps, far):
    pairs = [
        (source, target)
        for source, target in shift_pairs(2 * groups, 2, steps)
        if far or not is_far(groups, source // 2, target // 2)
    ]
    return lax.ppermute(value, "ctx", pairs) if pairs else jnp.zeros_like(value)


def plan_kernel(shape, places, new_ref, prior_ref, at_ref, plan_ref, far_ref):
    groups, chips, rows, cache, step = shape
    device, place = at_ref[0], at_ref[1]
    group, side, chip, core = lax.div(device, 2), lax.rem(device, 2), lax.div(place, 2), lax.rem(place, 2)
    table = request_table(new_ref, prior_ref)

    def rows_before(row):
        block = lax.div(row, rows)
        odd, inside = lax.rem(block, 2), lax.rem(row, rows)
        return lax.div(block, 2) * rows + jnp.where(odd == side, inside, jnp.where(odd == 1, rows, 0))

    for request, (row, key, ahead, row_end, _) in enumerate(table):
        plan_ref[places["first_key"] + request] = key
        plan_ref[places["ahead"] + request] = ahead
        plan_ref[places["begin"] + request] = rows_before(row)
        plan_ref[places["end"] + request] = rows_before(row_end)
    spans = [
        (key_range(table, jnp.int32(2 * rows * at))[0], key_range(table, jnp.int32(2 * rows * (at + 1) - 1))[1])
        for at in range(groups)
    ]
    needed = jnp.int32(0)
    for source in range(groups):
        for target in range(groups):
            if is_far(groups, source, target):
                first, last = spans[source]
                meet = (first < 2 * cache * (target + 1)) & (last >= 2 * cache * target)
                needed = jnp.where(meet, 1, needed)
    far_ref[0] = needed
    plan_ref[places["side"]] = side
    plan_ref[places["low"]] = group * 2 * cache
    for steps in range(groups):
        plan_ref[places["groups"] + steps] = lax.rem(group + (groups - steps), groups)
        there = jnp.int32(1)
        for at in range(groups):
            if is_far(groups, (at + steps) % groups, at):
                there = jnp.where(group == at, needed, there)
        plan_ref[places["there"] + steps] = there
    other = (device + 1 - 2 * side) * cache
    half = cache // 2
    stretches = [
        (0, device * cache, cache), (cache, other + core * half, half), (cache + half, other + (1 - core) * half, half)
    ]
    for at, (left, key, count) in enumerate(stretches):
        plan_ref[places["lefts"] + at] = jnp.int32(left)
        plan_ref[places["keys"] + at] = key
        plan_ref[places["steps"] + at] = jnp.int32(count // step)
    for at in range(2 * chips):
        own = core if at < chips else 1 - core
        plan_ref[places["from"] + at] = lax.rem(chip + (chips - at % chips), chips) * 2 + own


def make_plan(shape, new_counts, prior_lengths, at):
    groups, chips = shape[:2]
    requests = new_counts.shape[0]
    sizes = dict(first_key=requests, ahead=requests, begin=requests, end=requests, side=1, low=1)
    sizes.update(groups=groups, there=groups, lefts=STRETCHES, keys=STRETCHES, steps=STRETCHES)
    sizes["from"] = 2 * chips
    places, total = {}, 0
    for name, size in sizes.items():
        places[name] = total
        total += size
    plan, far = pl.pallas_call(
        functools.partial(plan_kernel, shape, dict(places)),
        out_shape=(jax.ShapeDtypeStruct((total,), jnp.int32), jax.ShapeDtypeStruct((1,), jnp.int32)),
        in_specs=[SMEM] * 3,
        out_specs=(SMEM, SMEM),
        name="plan",
    )(new_counts, prior_lengths, at)
    return places, plan, far


def body(queries, keys, values, w_out, new_counts, prior_lengths):
    ctx_count, head_count = lax.axis_size("ctx"), lax.axis_size("head")
    rows = queries.shape[0]
    cache = keys.shape[0]
    groups, chips = ctx_count // 2, head_count // 2
    at = jnp.stack([lax.axis_index("ctx"), lax.axis_index("head")]).astype(jnp.int32)
    shape = (groups, chips, rows, cache, min(KEY_TILE, cache // 2))
    places, plan, far = make_plan(shape, new_counts, prior_lengths, at)
    requests = new_counts.shape[0]
    return lax.cond(
        far[0] == 1,
        functools.partial(attend_and_project, places, requests, True),
        functools.partial(attend_and_project, places, requests, False),
        *(queries, keys, values, w_out, plan),
    )


def attend_and_project(places, requests, far, queries, keys, values, w_out, plan):
    ctx_count, head_count = lax.axis_size("ctx"), lax.axis_size("head")
    rows = queries.shape[0]
    cache, width = keys.shape
    heads = queries.shape[1] // width
    groups, chips = ctx_count // 2, head_count // 2

    nearest = sorted(range(1, groups), key=lambda steps: min(steps, groups - steps))
    blocks = [move(queries, groups, steps, far) for steps in reversed(nearest)]

    half = cache // 2
    start = lax.axis_index("head") % 2 * half
    mine = [lax.dynamic_slice_in_dim(array, start, half, axis=0) for array in (keys, values)]
    got = lax.ppermute(jnp.concatenate(mine, axis=1), "ctx", swap_pairs(ctx_count))
    all_keys, beside, own_norm, near_w = prepare(keys, values, w_out)
    stack, query_norm = stack_queries(places, plan, [0, *reversed(nearest)], [queries] + blocks, width)
    got, query_norm, own_norm = lax.optimization_barrier((got, query_norm, own_norm))
    rest = lax.ppermute(got, "head", swap_pairs(head_count))
    all_keys, beside, key_norm = join(got, own_norm, all_keys, beside)
    shape = (groups, rows, heads, requests)
    parts = attend(places, plan, (key_norm, query_norm), stack, rest, all_keys, beside, shape)
    back = [parts[0]] + [move(parts[steps], groups, groups - steps, far) for steps in nearest]
    attended = merge(places, plan, [0, *nearest], back, heads)

    away = [lax.ppermute(attended, "head", shift_pairs(head_count, 2, steps)) for steps in range(1, chips)]
    pair = lax.ppermute(attended, "head", swap_pairs(head_count))
    mixed, token = project(places, plan, [0, chips], [attended, pair], near_w, None, False)
    away = [piece + token[0].astype(piece.dtype) for piece in away]
    away = away + [lax.ppermute(piece, "head", swap_pairs(head_count)) for piece in away]
    order = [*range(1, chips), *range(chips + 1, 2 * chips)]
    mixed, _ = project(places, plan, order, away, near_w, mixed, True)
    return mixed


def solution(mesh):
    return jax.shard_map(
        body,
        mesh=mesh,
        in_specs=(P("ctx", "head"), P("ctx", None), P("ctx", None), P(None, "head"), P(), P()),
        out_specs=P("ctx", "head"),
        check_vma=False,
    )
```
